32 devices in a mesh: gcm: 4 (over y, core), crm: 8 (over z, x).
Axes of the slice: x: 2, y: 2, z: 4, core: 2. Of those that a mesh axis runs over, the one named last changes fastest.
Arguments:
- tracer: float32 [72, 32, 2048], P(None, 'gcm', 'crm'), may hold values from -6 to 6
- wind_x: float32 [72, 32, 2048], P(None, 'gcm', 'crm'), may hold values from -4 to 4
- wind_y: float32 [72, 32, 2048], P(None, 'gcm', 'crm'), may hold values from -4 to 4
- drops: bfloat16 [4096, 33, 256], P(('gcm', 'crm')), may hold values from 0 to 1
- owner: int32 [4096, 1], P(('gcm', 'crm')), may hold values from 0 to 31, as said below
- counts: int32 [4096], P(('gcm', 'crm')), may hold values from 0 to 4, as said below
- collision: bfloat16 [33, 1089], replicated, may hold values from -0.1875 to 0.1875
- growth: float32 [33], replicated, may hold values from -4 to 4
Outputs:
- tracer_next: float32 [72, 32, 2048], P(None, 'gcm', 'crm')
- drops_next: bfloat16 [4096, 33, 256], P(('gcm', 'crm'))
- power: float32 [16, 8192], P(None, ('gcm', 'crm'))
The draws below stay inside these ranges and needn't reach their ends.
Inputs may be any that keep to these rules, and one draw needn't show every extreme that they name: Owner index in gcm-then-crm device order; among the 128 columns of one device no owner appears more than 8 times, and some owner appears exactly 8 times. `counts`: how cloudy the columns are differs from device to device.
All inputs are finite; a program needn't handle non-finite values.
Results may differ from the reference program's by a relative error of at most 0.0018.
Values may be sent and summed in bfloat16 or wider, within the bound.
No kernel may reach another device: no remote copies, remote signals or barrier semaphores. Data moves between devices by JAX's collectives and lax.ppermute only.
A program may use at most 128 MiB of HBM per device.

```python
import jax
import jax.numpy as jnp
import numpy as np
from jax import lax

NPTS = 4
LEV = 72
BINS = 33
CRM_X = 16
CRM_LEV = 16
SUB_MAX = 4
DYN_STEPS = 2
SLOT_BLOCK = 16
EX_DEV = 2
EY_DEV = 64
CELLS = 256
COL_DEV = 128
CAP = 8
SLOTS = 256
COLS = 4096
N_GCM = 4
N_CRM = 8


def draw_owner(key, part):
    devices = COLS // COL_DEV
    order_key, choose_key = jax.random.split(jax.random.fold_in(key, 17), 2)
    device_keys = jax.random.split(order_key, devices)
    choose_keys = jax.random.split(choose_key, devices)
    orders = jax.vmap(lambda k: jax.random.permutation(k, COL_DEV))(device_keys)
    picks = jax.vmap(lambda k: jax.random.permutation(k, devices))(choose_keys)
    groups = (orders.astype(jnp.int32) // CAP).astype(jnp.int32)
    values = jnp.take_along_axis(picks.astype(jnp.int32), groups, axis=1)
    return values.reshape(COLS, 1).astype(jnp.int32)


def draw_counts(key, part):
    devices = COLS // COL_DEV
    flag_key, pick_key, cloudy_key, clear_key = jax.random.split(key, 4)
    flagged = jax.random.randint(flag_key, (devices, 1), 0, 8) == 0
    chosen = jax.random.randint(pick_key, (), 0, devices)
    flagged = flagged | (jnp.arange(devices)[:, None] == chosen)
    column_index = jnp.arange(COL_DEV)[None, :]
    lowered = (jax.random.randint(cloudy_key, (devices, COL_DEV), 0, 4) == 0) & (column_index > 0)
    cloudy_values = SUB_MAX - lowered.astype(jnp.int32)
    clear_values = jax.random.randint(clear_key, (devices, COL_DEV), 0, 2)
    values = jnp.where(flagged, cloudy_values, clear_values)
    return values.reshape(COLS).astype(jnp.int32)


def steps_of(stream_key, shape, cuts, smallest, high):
    def one(axis_at, shards_of):
        draws = jax.random.uniform(jax.random.fold_in(jax.random.fold_in(stream_key, 6), axis_at), (shards_of,), jnp.float32, smallest / len(cuts), high / len(cuts))
        return jnp.repeat(jnp.exp(draws), shape[axis_at] // shards_of).reshape((-1,) + (1,) * (len(shape) - axis_at - 1))

    gain = one(*cuts[0])
    for cut in cuts[1:]:
        gain = gain * one(*cut)
    return gain


def normal_values(own_key, extent, scale, most, cuts=(), kind=jnp.bfloat16):
    values = jax.random.normal(own_key, extent, jnp.float32) * scale
    if len(cuts) > 0:
        values = steps_of(own_key, extent, cuts, -0.22, 0.18) * values
    return jnp.clip(values, min=-most, max=most).astype(kind)


def setup_inputs(seed: int = 0) -> dict:
    splits = jax.random.split(jax.random.key(seed), 9)
    tracer = normal_values(splits[0], (LEV, NPTS * EX_DEV * N_GCM, NPTS * EY_DEV * N_CRM), 1.0, 6.0, ((1, 4), (2, 8)), jnp.float32)
    wind_x = normal_values(splits[1], (LEV, NPTS * EX_DEV * N_GCM, NPTS * EY_DEV * N_CRM), 1.0, 4.0, ((1, 4), (2, 8)), jnp.float32)
    wind_y = normal_values(splits[2], (LEV, NPTS * EX_DEV * N_GCM, NPTS * EY_DEV * N_CRM), 1.0, 4.0, ((1, 4), (2, 8)), jnp.float32)
    drops = jnp.clip(1.0 * jax.random.uniform(splits[3], (COLS, BINS, CELLS), jnp.float32) ** steps_of(splits[3], (COLS, BINS, CELLS), ((0, 32),), -0.2, 0.2), 0.0, 1.0).astype(jnp.bfloat16)
    owner = draw_owner(jax.random.fold_in(splits[8], 71), 0)
    counts = draw_counts(jax.random.fold_in(splits[8], 71), 0)
    collision = normal_values(splits[6], (BINS, BINS * BINS), (BINS * BINS) ** -0.5, 0.1875)
    growth = normal_values(splits[7], (BINS,), 1.0, 4.0, (), jnp.float32)
    return dict(tracer=tracer, wind_x=wind_x, wind_y=wind_y, drops=drops, owner=owner, counts=counts, collision=collision, growth=growth)


DT_DYN = 0.04
DT_CRM = 0.05
DT_PHYS = 0.5
HIGH = lax.Precision.HIGHEST

def gll_tables():
    inv_root = 1.0 / np.sqrt(5.0)
    gll_nodes = np.array([-1.0, -inv_root, inv_root, 1.0])
    weights = np.array([1.0, 5.0, 5.0, 1.0]) / 6.0
    legendre = (5.0 * gll_nodes ** 3 - 3.0 * gll_nodes) / 2.0
    derivative = np.zeros((4, 4))
    for i in range(4):
        for j in range(4):
            if i != j:
                derivative[i, j] = legendre[i] / (legendre[j] * (gll_nodes[i] - gll_nodes[j]))
    derivative[0, 0] = -3.0
    derivative[3, 3] = 3.0
    return (2.0 * derivative, weights)

def level_tables(levels, crm_levels):
    spacing = levels / crm_levels
    centres = (np.arange(crm_levels) + 0.5) * spacing - 0.5
    hats = np.maximum(0.0, 1.0 - np.abs(np.arange(levels)[None, :] - centres[:, None]) / spacing)
    down_map = hats / hats.sum(axis=1, keepdims=True)
    up_map = hats.T / hats.T.sum(axis=1, keepdims=True)
    return (down_map, up_map)

def sum_rows(padded):
    row_count = padded.shape[1] - 2
    phase = (jnp.arange(row_count) % 4)[None, :, None]
    middle = padded[:, 1:-1]
    return middle + jnp.where(phase == 3, padded[:, 2:], 0.0) + jnp.where(phase == 0, padded[:, :-2], 0.0)

def sum_cols(padded):
    col_count = padded.shape[2] - 2
    phase = (jnp.arange(col_count) % 4)[None, None, :]
    middle = padded[:, :, 1:-1]
    return middle + jnp.where(phase == 3, padded[:, :, 2:], 0.0) + jnp.where(phase == 0, padded[:, :, :-2], 0.0)

def wrap_sum(field):
    return sum_cols(sum_rows(jnp.pad(field, ((0, 0), (1, 1), (1, 1)), mode='wrap')))

def advect(tracer, wind_x, wind_y, derivative):
    levels, row_count, col_count = tracer.shape
    by_rows = tracer.reshape(levels, row_count // 4, 4, col_count)
    grad_x = jnp.einsum('ij,lejc->leic', derivative, by_rows, precision=HIGH).reshape(tracer.shape)
    by_cols = tracer.reshape(levels, row_count, col_count // 4, 4)
    grad_y = jnp.einsum('ij,lrej->lrei', derivative, by_cols, precision=HIGH).reshape(tracer.shape)
    return -(wind_x * grad_x + wind_y * grad_y)

def crm_substep(state, cell_forcing, growth, collision):
    grown = state + DT_CRM * cell_forcing[:, None, :] * growth[None, :, None]
    slot_count, bin_count, cell_count = grown.shape
    pairs = (grown[:, :, None, :] * grown[:, None, :, :]).reshape(slot_count, bin_count * bin_count, cell_count)
    pairs = lax.optimization_barrier(pairs.astype(jnp.bfloat16)).astype(state.dtype)
    change = jnp.einsum('kq,sqc->skc', collision.astype(state.dtype), pairs)
    return grown + DT_CRM * change

def summarize(final, initial):
    slot_count, bin_count, cell_count = final.shape
    mass = (jnp.arange(bin_count).astype(final.dtype) + 1.0) / bin_count
    heat = jnp.einsum('b,sbc->sc', mass, final - initial, precision=HIGH)
    echo = jnp.einsum('b,sbc->sc', mass * mass, final * final, precision=HIGH)
    heat = heat.reshape(slot_count, cell_count // CRM_X, CRM_X).mean(axis=2)
    echo = echo.reshape(slot_count, cell_count // CRM_X, CRM_X).mean(axis=2)
    return (heat, jnp.log(1.0 + echo))

def reference(tracer, wind_x, wind_y, drops, owner, counts, collision, growth):
    ftype = tracer.dtype
    devices = N_GCM * N_CRM
    derivative, gll_weights = gll_tables()
    derivative = jnp.asarray(derivative, ftype)
    gll_weights = jnp.asarray(gll_weights, ftype)
    levels, row_count, col_count = tracer.shape
    mass_pattern = jnp.outer(jnp.tile(gll_weights, row_count // 4), jnp.tile(gll_weights, col_count // 4))[None]
    denominator = wrap_sum(mass_pattern)
    state = tracer
    for step in range(DYN_STEPS):
        state = state + DT_DYN * wrap_sum(advect(state, wind_x, wind_y, derivative) * mass_pattern) / denominator
    blocks = ((state - tracer) / (DYN_STEPS * DT_DYN)).reshape(levels, row_count // 4, 4, col_count // 4, 4)
    means = jnp.einsum('laibj,i,j->abl', blocks, gll_weights, gll_weights, precision=HIGH) / 4.0
    means = means.reshape(N_GCM, EX_DEV, N_CRM, EY_DEV, levels).transpose(0, 2, 1, 3, 4).reshape(COLS, levels)
    down_map, up_map = level_tables(levels, CRM_LEV)
    forcing = jnp.dot(means, jnp.asarray(down_map.T, ftype), precision=HIGH).astype(jnp.bfloat16)

    def run_block(block):
        block_drops, block_forcing, block_counts = block
        initial = block_drops.astype(ftype)
        cell_forcing = jnp.repeat(block_forcing.astype(ftype), CRM_X, axis=1)

        def advance(step, current):
            moved = crm_substep(current, cell_forcing, growth, collision)
            return jnp.where((step < block_counts)[:, None, None], moved, current)
        final = lax.fori_loop(jnp.int32(0), jnp.max(block_counts).astype(jnp.int32), advance, initial)
        heat, echo_power = summarize(final, initial)
        return (final.astype(jnp.bfloat16), heat.astype(jnp.bfloat16), echo_power)
    nblock = COLS // SLOT_BLOCK
    finals, heats, powers = lax.map(run_block, (drops.reshape((nblock, SLOT_BLOCK) + drops.shape[1:]), forcing.reshape(nblock, SLOT_BLOCK, CRM_LEV), counts.reshape(nblock, SLOT_BLOCK)))
    drops_next = finals.reshape(drops.shape)
    heat = lax.optimization_barrier(heats.reshape(COLS, CRM_LEV)).astype(ftype)
    echo_power = powers.reshape(COLS, CRM_LEV)
    back = jnp.dot(heat, jnp.asarray(up_map.T, ftype), precision=HIGH)
    back = back.reshape(N_GCM, N_CRM, EX_DEV, EY_DEV, levels).transpose(0, 2, 1, 3, 4).reshape(EX_DEV * N_GCM, EY_DEV * N_CRM, levels)
    grid = jnp.transpose(back, (2, 0, 1))[:, :, None, :, None]
    spread = jnp.broadcast_to(grid, (levels, row_count // 4, 4, col_count // 4, 4)).reshape(tracer.shape)
    tracer_next = wrap_sum((state + DT_PHYS * spread) * mass_pattern) / denominator
    owners = owner[:, 0]
    onehot = (owners.reshape(devices, COL_DEV)[:, :, None] == jnp.arange(devices, dtype=jnp.int32)[None, None, :]).astype(jnp.int32)
    earlier = jnp.cumsum(onehot, axis=1) - onehot
    position = lax.optimization_barrier(jnp.sum(earlier * onehot, axis=2)).reshape(COLS)
    sources = (jnp.arange(COLS, dtype=jnp.int32) // COL_DEV).astype(jnp.int32)
    slot_index = (owners * SLOTS + sources * CAP + position).astype(jnp.int32)
    power = jnp.zeros((CRM_LEV, devices * SLOTS), ftype).at[:, slot_index].set(echo_power.T)
    return (tracer_next, drops_next, power)
```

```python
import functools

import jax
import jax.numpy as jnp
import numpy as np
from jax import lax
from jax.experimental import pallas as pl
from jax.experimental.pallas import tpu as pltpu
from jax.sharding import PartitionSpec as P

CRM_X = 16
CRM_LEV = 16
DYN_STEPS = 2

DT_DYN = 0.04
DT_CRM = 0.05
DT_PHYS = 0.5
HIGH = lax.Precision.HIGHEST
F32 = jnp.float32
BF16 = jnp.bfloat16
GROUP = 8
CHUNK = 8
MIB = 1024 * 1024


def gll_tables():
    inv_root = 1.0 / np.sqrt(5.0)
    gll_nodes = np.array([-1.0, -inv_root, inv_root, 1.0])
    weights = np.array([1.0, 5.0, 5.0, 1.0]) / 6.0
    legendre = (5.0 * gll_nodes**3 - 3.0 * gll_nodes) / 2.0
    derivative = np.zeros((4, 4))
    for i in range(4):
        for j in range(4):
            if i != j:
                derivative[i, j] = legendre[i] / (legendre[j] * (gll_nodes[i] - gll_nodes[j]))
    derivative[0, 0] = -3.0
    derivative[3, 3] = 3.0
    return (2.0 * derivative, weights)


def level_tables(levels, crm_levels):
    spacing = levels / crm_levels
    centres = (np.arange(crm_levels) + 0.5) * spacing - 0.5
    hats = np.maximum(0.0, 1.0 - np.abs(np.arange(levels)[None, :] - centres[:, None]) / spacing)
    down_map = hats / hats.sum(axis=1, keepdims=True)
    up_map = hats.T / hats.T.sum(axis=1, keepdims=True)
    return (down_map, up_map)


DERIV, WEIGHTS = gll_tables()


def iota(shape, axis):
    return lax.broadcasted_iota(jnp.int32, shape, axis)


def derivative_terms(shape, axis):
    phase = iota(shape, axis) % 4
    terms = []
    for shift in range(-3, 4):
        value = jnp.zeros(shape, F32)
        for i in range(4):
            if 0 <= i + shift < 4:
                value = jnp.where(phase == i, F32(DERIV[i, i + shift]), value)
        terms.append((shift, value))
    return terms


def along(x, terms, axis):
    size = x.shape[axis]
    total = None
    for shift, value in terms:
        moved = x if shift == 0 else pltpu.roll(x, (-shift) % size, axis)
        part = value[None] * moved
        total = part if total is None else total + part
    return total


def tendency(x, u, v, row_terms, col_terms):
    halves = []
    for h in range(2):
        cut = slice(128 * h, 128 * h + 128)
        q = x[:, :, cut]
        grad_x = along(q, row_terms, 1)
        grad_y = along(q, col_terms, 2)
        halves.append(-(u[:, :, cut] * grad_x + v[:, :, cut] * grad_y))
    return jnp.concatenate(halves, axis=2)


def column_lanes(fields):
    rows = fields[0].shape[0] * 8
    lane = iota((rows, 128), 1)
    out = jnp.zeros((rows, 128), F32)
    for i, x in enumerate(fields):
        first = x[:, :, 0:128].reshape(rows, 128)
        last = x[:, :, 128:256].reshape(rows, 128)
        if i:
            first = pltpu.roll(first, 2 * i, 1)
        last = pltpu.roll(last, 2 * i + 2, 1)
        out = jnp.where(lane == 2 * i, first, jnp.where(lane == 2 * i + 1, last, out))
    return out


def put_edges(chunk, fields, top_ref, bot_ref, lanes_ref):
    levels = pl.ds(pl.multiple_of(chunk * CHUNK, CHUNK), CHUNK)
    for i, x in enumerate(fields):
        top_ref[i, levels, :] = x[:, 0, :]
        bot_ref[i, levels, :] = x[:, 7, :]
    rows = pl.ds(pl.multiple_of(chunk * CHUNK * 8, CHUNK * 8), CHUNK * 8)
    lanes_ref[rows, :] = column_lanes(fields)


def first_kernel(q_ref, u_ref, v_ref, tend_ref, top_ref, bot_ref, col_ref, lanes_ref):
    row_terms = derivative_terms((8, 128), 0)
    col_terms = derivative_terms((8, 128), 1)
    total = q_ref.shape[0] * 8
    lanes_ref[total:, :] = jnp.zeros((lanes_ref.shape[0] - total, 128), F32)

    def body(chunk, carry):
        levels = pl.ds(chunk * CHUNK, CHUNK)
        q = q_ref[levels]
        tend = tendency(q, u_ref[levels], v_ref[levels], row_terms, col_terms)
        tend_ref[levels] = tend
        put_edges(chunk, (tend, q), top_ref, bot_ref, lanes_ref)
        return carry

    lax.fori_loop(0, q_ref.shape[0] // CHUNK, body, 0)
    col_ref[...] = lanes_ref[...].T[0:8]


def halo_columns(halo, field, lanes_ref):
    left, right, up_left, up_right, down_left, down_right = [r[...] for r in halo]
    width = left.shape[1]
    row = iota((8, width), 0)
    odd = row % 2 == 1
    own = jnp.where(odd, pltpu.roll(right, 1, 0), pltpu.roll(left, 7, 0))
    above = jnp.where(odd, pltpu.roll(up_right, 1, 0), pltpu.roll(up_left, 7, 0))
    below = jnp.where(odd, pltpu.roll(down_right, 1, 0), pltpu.roll(down_left, 7, 0))
    place = iota((8, width), 1) % 8
    partner = jnp.where(
        place == 0,
        pltpu.roll(above, width - 7, 1),
        jnp.where(
            place == 7,
            pltpu.roll(below, 7, 1),
            jnp.where(place == 3, pltpu.roll(own, width - 1, 1), pltpu.roll(own, 1, 1)),
        ),
    )
    edge = (place % 4 == 0) | (place % 4 == 3)
    lanes_ref[...] = jnp.where(edge, 0.5 * (own + partner), own).T


def assemble_chunk(x, up, down, left, right):
    shape = x.shape
    row = iota(shape, 1)
    partner = jnp.where(
        row == 0,
        jnp.broadcast_to(up[:, None, :], shape),
        jnp.where(
            row == 7,
            jnp.broadcast_to(down[:, None, :], shape),
            jnp.where(row == 3, pltpu.roll(x, 7, 1), pltpu.roll(x, 1, 1)),
        ),
    )
    x = jnp.where((row % 4 == 0) | (row % 4 == 3), 0.5 * (x + partner), x)
    col = iota(shape, 2)
    sides = jnp.concatenate(
        [
            jnp.broadcast_to(left, (shape[0] * 8, 128)).reshape(shape[0], 8, 128),
            jnp.broadcast_to(right, (shape[0] * 8, 128)).reshape(shape[0], 8, 128),
        ],
        axis=2,
    )
    partner = jnp.where(
        (col == 0) | (col == 255),
        sides,
        jnp.where(col % 4 == 3, pltpu.roll(x, 255, 2), pltpu.roll(x, 1, 2)),
    )
    return jnp.where((col % 4 == 0) | (col % 4 == 3), 0.5 * (x + partner), x)


def second_kernel(
    q_ref, u_ref, v_ref, tend_ref, up_ref, down_ref,
    left, right, up_left, up_right, down_left, down_right,
    state_ref, smooth_ref, next_ref, top_ref, bot_ref, col_ref, halo_ref, lanes_ref,
):
    row_terms = derivative_terms((8, 128), 0)
    col_terms = derivative_terms((8, 128), 1)
    total = q_ref.shape[0] * 8
    lanes_ref[total:, :] = jnp.zeros((lanes_ref.shape[0] - total, 128), F32)
    halo_columns((left, right, up_left, up_right, down_left, down_right), 2, halo_ref)

    def body(chunk, carry):
        levels = pl.ds(pl.multiple_of(chunk * CHUNK, CHUNK), CHUNK)
        sides = halo_ref[pl.ds(pl.multiple_of(chunk * CHUNK * 8, CHUNK * 8), CHUNK * 8), :]
        q = q_ref[levels]
        change = assemble_chunk(
            tend_ref[levels], up_ref[0, levels, :], down_ref[0, levels, :],
            sides[:, 0:1], sides[:, 1:2],
        )
        smooth_ref[levels] = assemble_chunk(
            q, up_ref[1, levels, :], down_ref[1, levels, :], sides[:, 2:3], sides[:, 3:4]
        )
        state = q + DT_DYN * change
        state_ref[levels] = state
        tend = tendency(state, u_ref[levels], v_ref[levels], row_terms, col_terms)
        next_ref[levels] = tend
        put_edges(chunk, (tend,), top_ref, bot_ref, lanes_ref)
        return carry

    lax.fori_loop(0, q_ref.shape[0] // CHUNK, body, 0)
    col_ref[...] = lanes_ref[...].T[0:8]


def third_kernel(
    q_ref, state_ref, smooth_ref, tend_ref, up_ref, down_ref,
    left, right, up_left, up_right, down_left, down_right, down_map_ref,
    base_ref, cell_ref, halo_ref, near_ref, far_ref,
):
    halo_columns((left, right, up_left, up_right, down_left, down_right), 1, halo_ref)
    cols = cell_ref.shape[0]
    half = cols // 2
    phase = iota((8, 256), 0) % 4
    row_weight = jnp.where((phase == 0) | (phase == 3), F32(WEIGHTS[0]), F32(WEIGHTS[1]))
    near_rows = jnp.where(iota((8, 256), 0) < 4, row_weight, 0.0)
    far_rows = row_weight - near_rows

    def body(chunk, carry):
        levels = pl.ds(pl.multiple_of(chunk * CHUNK, CHUNK), CHUNK)
        sides = halo_ref[pl.ds(pl.multiple_of(chunk * CHUNK * 8, CHUNK * 8), CHUNK * 8), :]
        change = assemble_chunk(
            tend_ref[levels], up_ref[0, levels, :], down_ref[0, levels, :],
            sides[:, 0:1], sides[:, 1:2],
        )
        moved = (state_ref[levels] + DT_DYN * change) - q_ref[levels]
        base_ref[levels] = smooth_ref[levels] + moved
        near_ref[levels, :] = jnp.sum(moved * near_rows[None], axis=1)
        far_ref[levels, :] = jnp.sum(moved * far_rows[None], axis=1)
        return carry

    lax.fori_loop(0, q_ref.shape[0] // CHUNK, body, 0)
    point = iota((256, cols), 0)
    element = iota((256, cols), 1)
    weight = jnp.where(
        (point % 4 == 0) | (point % 4 == 3), F32(WEIGHTS[0]), F32(WEIGHTS[1])
    ) * F32(0.25 / (DYN_STEPS * DT_DYN))
    near_cols = jnp.where(point // 4 == element, weight, 0.0)
    far_cols = jnp.where(point // 4 + half == element, weight, 0.0)
    means = jnp.dot(near_ref[...], near_cols, precision=HIGH, preferred_element_type=F32)
    means += jnp.dot(far_ref[...], far_cols, precision=HIGH, preferred_element_type=F32)
    forcing = jnp.dot(down_map_ref[...], means, precision=HIGH, preferred_element_type=F32)
    forcing = forcing.T.astype(BF16)
    cells = cell_ref.shape[1]
    spread = (iota((CRM_LEV, cells), 1) // CRM_X == iota((CRM_LEV, cells), 0)).astype(BF16)
    cell_ref[...] = DT_CRM * jnp.dot(forcing, spread, preferred_element_type=F32)


def crm_kernel(
    order_ref, count_ref, drops_ref, cell_ref, slot_ref, coef_ref, growth_ref,
    final_ref, heat_ref, power_ref, state_ref, pair_ref, heat_cell_ref, echo_cell_ref,
):
    bins = drops_ref.shape[1]
    cells = drops_ref.shape[2]
    cols = drops_ref.shape[0]
    coef = coef_ref[...]
    growth = growth_ref[...]
    state_ref[...] = jnp.zeros(state_ref.shape, F32)
    pair_ref[...] = jnp.zeros(pair_ref.shape, BF16)
    mass = (iota((40, cells), 0) + 1).astype(F32) / F32(bins)

    def substep(k, which, active):
        current = state_ref[k]
        grown = current + growth * cell_ref[pl.ds(which, 1), :]
        for h in range(cells // 128):
            cut = slice(128 * h, 128 * h + 128)
            g = grown[0:32, cut]
            last = grown[32:40, cut]
            for s in range(8):
                rolled = g if s == 0 else pltpu.roll(g, 32 - s, 0)
                for a in range(2):
                    other = rolled
                    if a:
                        other = jnp.concatenate([rolled[8:], rolled[:8]], axis=0)
                    d = 8 * a + s
                    pair_ref[k, 32 * d : 32 * d + 32, cut] = (g * other).astype(BF16)
            pair_ref[k, 512:528, cut] = (g[0:16] * g[16:32]).astype(BF16)
            pair_ref[k, 528:560, cut] = (g * last[0:1]).astype(BF16)
            tail = jnp.concatenate([last * last, jnp.zeros((8, 128), F32)], axis=0)
            pair_ref[k, 560:576, cut] = tail.astype(BF16)
        change = jnp.dot(coef, pair_ref[k], preferred_element_type=F32)
        moved = grown + (change[0:40] + change[40:80])
        state_ref[k] = jnp.where(active, moved, current)

    def group(index, carry):
        base = index * GROUP
        which = [order_ref[base + k] for k in range(GROUP)]
        count = [count_ref[base + k] for k in range(GROUP)]
        for k in range(GROUP):
            state_ref[k, 0:bins, :] = drops_ref[which[k]].astype(F32)

        def step(s, c):
            for k in range(GROUP):
                substep(k, which[k], s < count[k])
            return c

        lax.fori_loop(0, count[0], step, 0)
        for k in range(GROUP):
            final = state_ref[k, 0:bins, :]
            initial = drops_ref[which[k]].astype(F32)
            final_ref[which[k]] = final.astype(BF16)
            weighted = mass[0:bins] * final
            heat = jnp.sum(mass[0:bins] * (final - initial), axis=0, keepdims=True)
            echo = jnp.sum(weighted * weighted, axis=0, keepdims=True)
            heat_cell_ref[pl.ds(which[k], 1), :] = heat
            echo_cell_ref[pl.ds(which[k], 1), :] = echo
        return carry

    lax.fori_loop(0, cols // GROUP, group, 0)
    means = jnp.where(
        iota((CRM_LEV, cells), 1) // CRM_X == iota((CRM_LEV, cells), 0), F32(1.0 / CRM_X), 0.0
    )
    contract = (((1,), (1,)), ((), ()))
    heat = lax.dot_general(
        means, heat_cell_ref[...], contract, precision=HIGH, preferred_element_type=F32
    )
    heat_ref[...] = heat.astype(BF16).astype(F32)
    echo = lax.dot_general(
        echo_cell_ref[...], means, contract, precision=HIGH, preferred_element_type=F32
    )
    echo = jnp.log(1.0 + echo)
    slots = power_ref.shape[0]
    onehot = (slot_ref[...] == iota((slots, cols), 0)).astype(F32)
    power_ref[...] = jnp.dot(onehot, echo, precision=HIGH, preferred_element_type=F32)


def last_kernel(
    base_ref, own, up, down, left, right, up_left, up_right, down_left, down_right, up_map_ref,
    out_ref, *back_refs,
):
    cols = own.shape[1]
    half = cols // 2
    element = iota((cols, 256), 0)
    col = iota((cols, 256), 1)
    phase = col % 4
    edge = (phase == 0) | (phase == 3)
    other = jnp.where(phase == 0, col // 4 - 1, col // 4 + 1)

    def spread(row, centre, west, east):
        start = row * half
        inside = jnp.where(element == col // 4 + start, jnp.where(edge, 0.5, 1.0), 0.0)
        beside = edge & (element == other + start) & (other >= 0) & (other < half)
        middle = jnp.where(beside, 0.5, inside).astype(BF16)
        from_west = jnp.where((col == 0) & (element == start + half - 1), 0.5, 0.0).astype(BF16)
        from_east = jnp.where((col == 255) & (element == start), 0.5, 0.0).astype(BF16)
        total = jnp.dot(centre[...].astype(BF16), middle, preferred_element_type=F32)
        total += jnp.dot(west[...].astype(BF16), from_west, preferred_element_type=F32)
        total += jnp.dot(east[...].astype(BF16), from_east, preferred_element_type=F32)
        return total

    above = spread(1, up, up_left, up_right)
    near = spread(0, own, left, right)
    far = spread(1, own, left, right)
    below = spread(0, down, down_left, down_right)
    parts = (
        0.5 * (above + near), near, 0.5 * (near + far), far, 0.5 * (far + below),
    )
    up_map = up_map_ref[...]
    for part, ref in zip(parts, back_refs):
        ref[...] = DT_PHYS * jnp.dot(up_map, part, precision=HIGH, preferred_element_type=F32)

    def body(chunk, carry):
        levels = pl.ds(pl.multiple_of(chunk * CHUNK, CHUNK), CHUNK)
        shape = (CHUNK, 8, 256)
        row = iota(shape, 1)
        wide = [jnp.broadcast_to(ref[levels, :][:, None, :], shape) for ref in back_refs]
        back = jnp.where(
            row == 0,
            wide[0],
            jnp.where(
                row < 3,
                wide[1],
                jnp.where(row < 5, wide[2], jnp.where(row < 7, wide[3], wide[4])),
            ),
        )
        out_ref[levels] = base_ref[levels] + back
        return carry

    lax.fori_loop(0, base_ref.shape[0] // CHUNK, body, 0)


def call(kernel, outs, args, scratch, flops=10_000_000):
    smem = pl.BlockSpec(memory_space=pltpu.SMEM)
    vmem = pl.BlockSpec(memory_space=pltpu.VMEM)
    return pl.pallas_call(
        kernel,
        out_shape=[jax.ShapeDtypeStruct(s, t) for s, t in outs],
        in_specs=[smem if kind == "s" else vmem for kind, _ in args],
        out_specs=[vmem] * len(outs),
        scratch_shapes=[pltpu.VMEM(s, t) for s, t in scratch],
        compiler_params=pltpu.CompilerParams(vmem_limit_bytes=40 * MIB),
        cost_estimate=pl.CostEstimate(flops=flops, bytes_accessed=4_000_000, transcendentals=0),
    )(*[value for _, value in args])


def v(*values):
    return [("v", value) for value in values]


def shift(value, rows, cols):
    n_gcm = lax.axis_size("gcm")
    n_crm = lax.axis_size("crm")
    pairs = []
    for g in range(n_gcm):
        for c in range(n_crm):
            target = ((g + rows) % n_gcm) * n_crm + (c + cols) % n_crm
            pairs.append((g * n_crm + c, target))
    return lax.ppermute(value, ("gcm", "crm"), pairs)


def neighbours(top, bot, side):
    return [
        shift(bot, 1, 0), shift(top, -1, 0), shift(side, 0, 1), shift(side, 0, -1),
        shift(side, 1, 1), shift(side, 1, -1), shift(side, -1, 1), shift(side, -1, -1),
    ]


def pair_table(bins):
    table = np.zeros((bins * bins, 576), np.float32)

    def put(column, i, j):
        table[i * bins + j, column] = 1.0
        table[j * bins + i, column] = 1.0

    for d in range(16):
        for b in range(32):
            put(32 * d + b, b, (b + d) % 32)
    for b in range(16):
        put(512 + b, b, b + 16)
    for b in range(32):
        put(528 + b, b, 32)
    put(560, 32, 32)
    return table


def rank_order(counts):
    total = counts.shape[0]
    index = jnp.arange(total, dtype=jnp.int32)
    ahead = (counts[None, :] > counts[:, None]) | (
        (counts[None, :] == counts[:, None]) & (index[None, :] < index[:, None])
    )
    rank = jnp.sum(ahead.astype(jnp.int32), axis=1)
    match = rank[None, :] == index[:, None]
    order = jnp.sum(jnp.where(match, index[None, :], 0), axis=1)
    ordered = jnp.sum(jnp.where(match, counts[None, :], 0), axis=1)
    return order, ordered


def shards(tracer, wind_x, wind_y, drops, owner, counts, collision, growth):
    devices = lax.axis_size("gcm") * lax.axis_size("crm")
    levels, row_count, col_count = tracer.shape
    col_total, bins, cells = drops.shape
    field = (tracer.shape, F32)
    width = -(-levels * 8 // 128) * 128
    lanes = ((width, 128), F32)
    side = ((8, width), F32)
    down_map, up_map = level_tables(levels, CRM_LEV)

    tend, top, bot, col = call(
        first_kernel,
        [field, ((2, levels, col_count), F32), ((2, levels, col_count), F32), side],
        v(tracer, wind_x, wind_y),
        [lanes],
    )
    halo = neighbours(top, bot, col)
    state, smooth, tend, top, bot, col = call(
        second_kernel,
        [field, field, field, ((1, levels, col_count), F32), ((1, levels, col_count), F32), side],
        v(tracer, wind_x, wind_y, tend, *halo),
        [((width, 8), F32), lanes],
    )
    halo = neighbours(top, bot, col)
    base, cell_forcing = call(
        third_kernel,
        [field, ((col_total, cells), F32)],
        v(tracer, state, smooth, tend, *halo, jnp.asarray(down_map, F32)),
        [((width, 8), F32), ((levels, col_count), F32), ((levels, col_count), F32)],
    )

    capacity = 2 * col_total // devices
    owners = owner[:, 0]
    index = jnp.arange(col_total, dtype=jnp.int32)
    same = (owners[:, None] == owners[None, :]) & (index[:, None] < index[None, :])
    slot_of = owners * capacity + jnp.sum(same.astype(jnp.int32), axis=0)
    order, ordered = rank_order(counts)
    table = jnp.asarray(pair_table(bins), BF16)
    coef = DT_CRM * jnp.dot(collision, table, preferred_element_type=F32)
    coarse = lax.reduce_precision(coef, 8, 7)
    fine = coef - coarse
    pad = ((0, 40 - bins), (0, 0))
    coef = jnp.concatenate([jnp.pad(coarse, pad), jnp.pad(fine, pad)], axis=0).astype(BF16)
    growth_rows = jnp.broadcast_to(jnp.pad(growth, (0, 40 - bins))[:, None], (40, cells))

    final, heat, packed = call(
        crm_kernel,
        [((col_total, bins, cells), BF16), ((CRM_LEV, col_total), F32),
         ((devices * capacity, CRM_LEV), F32)],
        [("s", order), ("s", ordered)]
        + v(drops, cell_forcing, slot_of[None, :], coef, growth_rows),
        [((GROUP, 40, cells), F32), ((GROUP, 576, cells), BF16),
         ((col_total, cells), F32), ((col_total, cells), F32)],
        flops=10_000_000_000,
    )
    around = [
        shift(heat, *way)
        for way in ((1, 0), (-1, 0), (0, 1), (0, -1), (1, 1), (1, -1), (-1, 1), (-1, -1))
    ]
    power = lax.all_to_all(packed, ("gcm", "crm"), split_axis=0, concat_axis=0, tiled=True).T
    (tracer_next,) = call(
        last_kernel,
        [field],
        v(base, heat, *around, jnp.asarray(up_map, F32)),
        [((levels, col_count), F32)] * 5,
    )
    return (tracer_next, final, power)


def solution(mesh):
    return jax.shard_map(
        shards,
        mesh=mesh,
        in_specs=(
            P(None, "gcm", "crm"),
            P(None, "gcm", "crm"),
            P(None, "gcm", "crm"),
            P(("gcm", "crm"), None, None),
            P(("gcm", "crm"), None),
            P(("gcm", "crm")),
            P(),
            P(),
        ),
        out_specs=(P(None, "gcm", "crm"), P(("gcm", "crm"), None, None), P(None, ("gcm", "crm"))),
        check_vma=False,
    )
```

```python
import functools

import jax
import jax.numpy as jnp
import numpy as np
from jax import lax
from jax.experimental import pallas as pl
from jax.experimental.pallas import tpu as pltpu
from jax.sharding import PartitionSpec as P

CRM_X = 16
CRM_LEV = 16
DYN_STEPS = 2

DT_DYN = 0.04
DT_CRM = 0.05
DT_PHYS = 0.5
HIGH = lax.Precision.HIGHEST
F32 = jnp.float32
BF16 = jnp.bfloat16
GROUP = 8
CHUNK = 8
MIB = 1024 * 1024


def gll_tables():
    inv_root = 1.0 / np.sqrt(5.0)
    gll_nodes = np.array([-1.0, -inv_root, inv_root, 1.0])
    weights = np.array([1.0, 5.0, 5.0, 1.0]) / 6.0
    legendre = (5.0 * gll_nodes**3 - 3.0 * gll_nodes) / 2.0
    derivative = np.zeros((4, 4))
    for i in range(4):
        for j in range(4):
            if i != j:
                derivative[i, j] = legendre[i] / (legendre[j] * (gll_nodes[i] - gll_nodes[j]))
    derivative[0, 0] = -3.0
    derivative[3, 3] = 3.0
    return (2.0 * derivative, weights)


def level_tables(levels, crm_levels):
    spacing = levels / crm_levels
    centres = (np.arange(crm_levels) + 0.5) * spacing - 0.5
    hats = np.maximum(0.0, 1.0 - np.abs(np.arange(levels)[None, :] - centres[:, None]) / spacing)
    down_map = hats / hats.sum(axis=1, keepdims=True)
    up_map = hats.T / hats.T.sum(axis=1, keepdims=True)
    return (down_map, up_map)


DERIV, WEIGHTS = gll_tables()


def iota(shape, axis):
    return lax.broadcasted_iota(jnp.int32, shape, axis)


def derivative_terms(shape, axis):
    phase = iota(shape, axis) % 4
    terms = []
    for shift in range(-3, 4):
        value = jnp.zeros(shape, F32)
        for i in range(4):
            if 0 <= i + shift < 4:
                value = jnp.where(phase == i, F32(DERIV[i, i + shift]), value)
        terms.append((shift, value))
    return terms


def along(x, terms, axis):
    size = x.shape[axis]
    total = None
    for shift, value in terms:
        moved = x if shift == 0 else pltpu.roll(x, (-shift) % size, axis)
        part = value[None] * moved
        total = part if total is None else total + part
    return total


def tendency(x, u, v, row_terms, col_terms):
    halves = []
    for h in range(x.shape[2] // 128):
        cut = slice(128 * h, 128 * h + 128)
        q = x[:, :, cut]
        grad_x = along(q, row_terms, 1)
        grad_y = along(q, col_terms, 2)
        halves.append(-(u[:, :, cut] * grad_x + v[:, :, cut] * grad_y))
    return jnp.concatenate(halves, axis=2)


def pack_kernel(q_hbm, u_hbm, v_hbm, right_ref, left_ref, q_ref, u_ref, v_ref, sems):
    copies = []
    for i, (src, dst) in enumerate(((q_hbm, q_ref), (u_hbm, u_ref), (v_hbm, v_ref))):
        copies.append(pltpu.make_async_copy(src, dst, sems.at[i]))
    for copy in copies:
        copy.start()
    for copy in copies:
        copy.wait()
    lane = iota((8, 128), 1)

    def body(group, carry):
        right = jnp.zeros((8, 128), F32)
        left = jnp.zeros((8, 128), F32)
        for j in range(4):
            for f, ref in enumerate((q_ref, u_ref, v_ref)):
                start = 32 * j + 8 * f
                here = (lane >= start) & (lane < start + 8)
                x = ref[group * 4 + j]
                right = jnp.where(here, pltpu.roll(x[:, 128:256], (start - 120) % 128, 1), right)
                first = x[:, 0:128]
                if start:
                    first = pltpu.roll(first, start, 1)
                left = jnp.where(here, first, left)
        right_ref[group] = right
        left_ref[group] = left
        return carry

    lax.fori_loop(0, right_ref.shape[0], body, 0)


def put_rows(x, levels, top_ref, bot_ref, i):
    top_ref[i, levels, :] = x[:, 0, :]
    bot_ref[i, levels, :] = x[:, 7, :]


def first_kernel(q_ref, u_ref, v_ref, tend_ref, top_ref, bot_ref):
    row_terms = derivative_terms((8, 128), 0)
    col_terms = derivative_terms((8, 128), 1)

    def body(chunk, carry):
        levels = pl.ds(pl.multiple_of(chunk * CHUNK, CHUNK), CHUNK)
        q = q_ref[levels]
        tend = tendency(q, u_ref[levels], v_ref[levels], row_terms, col_terms)
        tend_ref[levels] = tend
        put_rows(tend, levels, top_ref, bot_ref, 0)
        put_rows(q, levels, top_ref, bot_ref, 1)
        return carry

    lax.fori_loop(0, q_ref.shape[0] // CHUNK, body, 0)


def strip_kernel(
    left_ref, right_ref, top_main, bot_main,
    q_ref, u_ref, v_ref, tend_ref, top_ref, bot_ref,
):
    row_terms = derivative_terms((8, 128), 0)
    col_terms = derivative_terms((8, 128), 1)
    lane = iota((8, 128), 1)
    top_ref[:, :, 0:256] = top_main[...]
    bot_ref[:, :, 0:256] = bot_main[...]

    def body(chunk, carry):
        tiles = [[], [], []]
        for half in range(CHUNK // 4):
            west = left_ref[chunk * (CHUNK // 4) + half]
            east = right_ref[chunk * (CHUNK // 4) + half]
            for j in range(4):
                for f in range(3):
                    start = 32 * j + 8 * f
                    a = pltpu.roll(east, 128 - start, 1) if start else east
                    b = pltpu.roll(west, (120 - start) % 128, 1)
                    tiles[f].append(jnp.where(lane < 8, a, jnp.where(lane >= 120, b, 0.0)))
        q, u, v = [jnp.stack(tile, axis=0) for tile in tiles]
        levels = pl.ds(pl.multiple_of(chunk * CHUNK, CHUNK), CHUNK)
        q_ref[levels] = q
        u_ref[levels] = u
        v_ref[levels] = v
        tend = tendency(q, u, v, row_terms, col_terms)
        tend_ref[levels] = tend
        for i, x in enumerate((tend, q)):
            top_ref[i, levels, 256:384] = x[:, 0, :]
            bot_ref[i, levels, 256:384] = x[:, 7, :]
        return carry

    lax.fori_loop(0, q_ref.shape[0] // CHUNK, body, 0)


def assemble_chunk(x, up, down):
    shape = x.shape
    row = iota(shape, 1)
    partner = jnp.where(
        row == 0,
        jnp.broadcast_to(up[:, None, :], shape),
        jnp.where(
            row == 7,
            jnp.broadcast_to(down[:, None, :], shape),
            jnp.where(row == 3, pltpu.roll(x, 7, 1), pltpu.roll(x, 1, 1)),
        ),
    )
    x = jnp.where((row % 4 == 0) | (row % 4 == 3), 0.5 * (x + partner), x)
    col = iota(shape, 2)
    partner = jnp.where(
        col % 4 == 3, pltpu.roll(x, shape[2] - 1, 2), pltpu.roll(x, 1, 2)
    )
    return jnp.where((col % 4 == 0) | (col % 4 == 3), 0.5 * (x + partner), x)


def join(main, strip):
    return jnp.concatenate([main, strip], axis=2)


def second_kernel(
    q_ref, u_ref, v_ref, tend_ref, q_strip, u_strip, v_strip, tend_strip, up_ref, down_ref,
    state_ref, smooth_ref, next_ref, top_ref, bot_ref,
):
    row_terms = derivative_terms((8, 128), 0)
    col_terms = derivative_terms((8, 128), 1)

    def body(chunk, carry):
        levels = pl.ds(pl.multiple_of(chunk * CHUNK, CHUNK), CHUNK)
        q = join(q_ref[levels], q_strip[levels])
        change = assemble_chunk(
            join(tend_ref[levels], tend_strip[levels]), up_ref[0, levels, :], down_ref[0, levels, :]
        )
        smooth = assemble_chunk(q, up_ref[1, levels, :], down_ref[1, levels, :])
        smooth_ref[levels] = smooth[:, :, 0:256]
        state = q + DT_DYN * change
        state_ref[levels] = state[:, :, 0:256]
        tend = tendency(
            state, join(u_ref[levels], u_strip[levels]), join(v_ref[levels], v_strip[levels]),
            row_terms, col_terms,
        )
        next_ref[levels] = tend
        put_rows(tend, levels, top_ref, bot_ref, 0)
        return carry

    lax.fori_loop(0, q_ref.shape[0] // CHUNK, body, 0)


def third_kernel(
    q_ref, state_ref, smooth_ref, tend_ref, up_ref, down_ref, down_map_ref,
    base_ref, cell_ref, near_ref, far_ref,
):
    cols = cell_ref.shape[0]
    half = cols // 2
    phase = iota((8, 256), 0) % 4
    row_weight = jnp.where((phase == 0) | (phase == 3), F32(WEIGHTS[0]), F32(WEIGHTS[1]))
    near_rows = jnp.where(iota((8, 256), 0) < 4, row_weight, 0.0)
    far_rows = row_weight - near_rows

    def body(chunk, carry):
        levels = pl.ds(pl.multiple_of(chunk * CHUNK, CHUNK), CHUNK)
        change = assemble_chunk(tend_ref[levels], up_ref[0, levels, :], down_ref[0, levels, :])
        moved = (state_ref[levels] + DT_DYN * change[:, :, 0:256]) - q_ref[levels]
        base_ref[levels] = smooth_ref[levels] + moved
        near_ref[levels, :] = jnp.sum(moved * near_rows[None], axis=1)
        far_ref[levels, :] = jnp.sum(moved * far_rows[None], axis=1)
        return carry

    lax.fori_loop(0, q_ref.shape[0] // CHUNK, body, 0)
    point = iota((256, cols), 0)
    element = iota((256, cols), 1)
    weight = jnp.where(
        (point % 4 == 0) | (point % 4 == 3), F32(WEIGHTS[0]), F32(WEIGHTS[1])
    ) * F32(0.25 / (DYN_STEPS * DT_DYN))
    near_cols = jnp.where(point // 4 == element, weight, 0.0)
    far_cols = jnp.where(point // 4 + half == element, weight, 0.0)
    means = jnp.dot(near_ref[...], near_cols, precision=HIGH, preferred_element_type=F32)
    means += jnp.dot(far_ref[...], far_cols, precision=HIGH, preferred_element_type=F32)
    forcing = jnp.dot(down_map_ref[...], means, precision=HIGH, preferred_element_type=F32)
    forcing = forcing.T.astype(BF16)
    cells = cell_ref.shape[1]
    spread = (iota((CRM_LEV, cells), 1) // CRM_X == iota((CRM_LEV, cells), 0)).astype(BF16)
    cell_ref[...] = DT_CRM * jnp.dot(forcing, spread, preferred_element_type=F32)


def crm_kernel(
    order_ref, count_ref, place_ref, drops_ref, cell_ref, slot_ref, coef_ref, tail_coef_ref,
    growth_ref,
    final_ref, heat_ref, send_ref, state_ref, pair_ref, tail_ref, heat_cell_ref, echo_cell_ref,
):
    bins = drops_ref.shape[1]
    cells = drops_ref.shape[2]
    cols = drops_ref.shape[0]
    coef = coef_ref[...]
    tail_coef = tail_coef_ref[...]
    growth = growth_ref[...]
    state_ref[...] = jnp.zeros(state_ref.shape, F32)
    mass = (iota((40, cells), 0) + 1).astype(F32) / F32(bins)

    def grow(k, which):
        grown = state_ref[k] + growth * cell_ref[pl.ds(which, 1), :]
        for h in range(cells // 128):
            cut = slice(128 * h, 128 * h + 128)
            g = grown[0:32, cut]
            last = grown[32:40, cut]
            for s in range(8):
                rolled = g if s == 0 else pltpu.roll(g, 32 - s, 0)
                for a in range(2):
                    other = rolled
                    if a:
                        other = jnp.concatenate([rolled[8:], rolled[:8]], axis=0)
                    d = 8 * a + s
                    pair_ref[k, 32 * d : 32 * d + 32, cut] = (g * other).astype(BF16)
            at = 64 * (k % 4)
            tail_ref[k // 4, at : at + 16, cut] = (g[0:16] * g[16:32]).astype(BF16)
            tail_ref[k // 4, at + 16 : at + 48, cut] = (g * last[0:1]).astype(BF16)
            tail = jnp.concatenate([last * last, jnp.zeros((8, 128), F32)], axis=0)
            tail_ref[k // 4, at + 48 : at + 64, cut] = tail.astype(BF16)
        return grown

    def group(index, carry):
        base = index * GROUP
        which = [order_ref[base + k] for k in range(GROUP)]
        count = [count_ref[base + k] for k in range(GROUP)]
        for k in range(GROUP):
            state_ref[k, 0:bins, :] = drops_ref[which[k]].astype(F32)

        def step(s, c):
            for q in range(GROUP // 4):
                grown = [grow(4 * q + k, which[4 * q + k]) for k in range(4)]
                tails = jnp.dot(tail_coef, tail_ref[q], preferred_element_type=F32)
                for k in range(4):
                    slot = 4 * q + k
                    change = jnp.dot(coef, pair_ref[slot], preferred_element_type=F32)
                    change = change + tails[80 * k : 80 * k + 80]
                    moved = grown[k] + (change[0:40] + change[40:80])
                    state_ref[slot] = jnp.where(s < count[slot], moved, state_ref[slot])
            return c

        lax.fori_loop(0, count[0], step, 0)
        for k in range(GROUP):
            final = state_ref[k, 0:bins, :]
            initial = drops_ref[which[k]].astype(F32)
            final_ref[which[k]] = final.astype(BF16)
            weighted = mass[0:bins] * final
            heat = jnp.sum(mass[0:bins] * (final - initial), axis=0, keepdims=True)
            echo = jnp.sum(weighted * weighted, axis=0, keepdims=True)
            heat_cell_ref[pl.ds(which[k], 1), :] = heat
            echo_cell_ref[pl.ds(which[k], 1), :] = echo
        return carry

    lax.fori_loop(0, cols // GROUP, group, 0)
    means = jnp.where(
        iota((CRM_LEV, cells), 1) // CRM_X == iota((CRM_LEV, cells), 0), F32(1.0 / CRM_X), 0.0
    )
    contract = (((1,), (1,)), ((), ()))
    heat = lax.dot_general(
        means, heat_cell_ref[...], contract, precision=HIGH, preferred_element_type=F32
    )
    heat = heat.astype(BF16).astype(F32)
    heat_ref[...] = heat
    echo = lax.dot_general(
        means, echo_cell_ref[...], contract, precision=HIGH, preferred_element_type=F32
    )
    echo = jnp.log(1.0 + echo)

    devices = send_ref.shape[0]
    slots = 2 * cols
    capacity = slots // devices
    onehot = (slot_ref[...] == iota((slots, cols), 0)).astype(F32)
    packed = lax.dot_general(echo, onehot, contract, precision=HIGH, preferred_element_type=F32)
    coarse = packed.astype(BF16).astype(F32)
    rest = packed - coarse
    middle = rest.astype(BF16).astype(F32)
    pieces = (coarse, middle, rest - middle)
    lane = iota((CRM_LEV, 128), 1)
    near = heat
    far = pltpu.roll(heat, 64, 1)
    sides = jnp.where(
        lane == 1, pltpu.roll(heat, 65, 1), jnp.where(lane == 62, pltpu.roll(heat, 63, 1), heat)
    )
    n_gcm = place_ref[1]
    n_crm = place_ref[2]
    for d in range(devices):
        away = d // n_crm - place_ref[0]
        below = (away == 1) | (away == 1 - n_gcm)
        above = (away == -1) | (away == n_gcm - 1)
        block = jnp.where(below, far, jnp.where(above, near, sides))
        tile, offset = divmod(d * capacity, 128)
        for i, piece in enumerate(pieces):
            moved = pltpu.roll(
                piece[:, 128 * tile : 128 * tile + 128], (64 + i * capacity - offset) % 128, 1
            )
            start = 64 + i * capacity
            block = jnp.where((lane >= start) & (lane < start + capacity), moved, block)
        send_ref[d] = block.astype(BF16)


def last_kernel(around_ref, base_ref, own_ref, got_ref, up_map_ref, out_ref, power_ref, *back_refs):
    cols = own_ref.shape[1]
    half = cols // 2
    element = iota((cols, 256), 0)
    col = iota((cols, 256), 1)
    phase = col % 4
    edge = (phase == 0) | (phase == 3)
    other = jnp.where(phase == 0, col // 4 - 1, col // 4 + 1)

    def spread(centre, start, west, west_lane, east, east_lane):
        inside = jnp.where(element == col // 4 + start, jnp.where(edge, 0.5, 1.0), 0.0)
        beside = edge & (element == other + start) & (other >= 0) & (other < half)
        middle = jnp.where(beside, 0.5, inside).astype(BF16)
        from_west = jnp.where((col == 0) & (element == west_lane), 0.5, 0.0).astype(BF16)
        from_east = jnp.where((col == 255) & (element == east_lane), 0.5, 0.0).astype(BF16)
        total = jnp.dot(centre, middle, preferred_element_type=F32)
        total += jnp.dot(west, from_west, preferred_element_type=F32)
        total += jnp.dot(east, from_east, preferred_element_type=F32)
        return total

    own = own_ref[...].astype(BF16)
    up, down, left, right, up_left, up_right, down_left, down_right = [
        got_ref[around_ref[i]] for i in range(8)
    ]
    above = spread(up, 0, up_left, half - 1, up_right, 0)
    near = spread(own, 0, left, half - 1, right, 0)
    far = spread(own, half, left, half - 2, right, 1)
    below = spread(down, 0, down_left, half - 1, down_right, 0)
    parts = (
        0.5 * (above + near), near, 0.5 * (near + far), far, 0.5 * (far + below),
    )
    up_map = up_map_ref[...]
    for part, ref in zip(parts, back_refs):
        ref[...] = DT_PHYS * jnp.dot(up_map, part, precision=HIGH, preferred_element_type=F32)

    devices = got_ref.shape[0]
    slots = power_ref.shape[1]
    capacity = slots // devices
    lane = iota((CRM_LEV, 128), 1)
    tiles = [jnp.zeros((CRM_LEV, 128), F32) for _ in range(slots // 128)]
    for d in range(devices):
        block = got_ref[d].astype(F32)
        fine = pltpu.roll(block, 128 - 2 * capacity, 1) + pltpu.roll(block, 128 - capacity, 1)
        tile, offset = divmod(d * capacity, 128)
        moved = pltpu.roll(block + fine, (offset - 64) % 128, 1)
        tiles[tile] = jnp.where((lane >= offset) & (lane < offset + capacity), moved, tiles[tile])
    power_ref[...] = jnp.concatenate(tiles, axis=1)

    def body(chunk, carry):
        levels = pl.ds(pl.multiple_of(chunk * CHUNK, CHUNK), CHUNK)
        shape = (CHUNK, 8, 256)
        row = iota(shape, 1)
        wide = [jnp.broadcast_to(ref[levels, :][:, None, :], shape) for ref in back_refs]
        back = jnp.where(
            row == 0,
            wide[0],
            jnp.where(
                row < 3,
                wide[1],
                jnp.where(row < 5, wide[2], jnp.where(row < 7, wide[3], wide[4])),
            ),
        )
        out_ref[levels] = base_ref[levels] + back
        return carry

    lax.fori_loop(0, base_ref.shape[0] // CHUNK, body, 0)


def call(kernel, outs, args, scratch=(), sems=(), flops=10_000_000):
    spaces = {
        "s": pl.BlockSpec(memory_space=pltpu.SMEM),
        "v": pl.BlockSpec(memory_space=pltpu.VMEM),
        "h": pl.BlockSpec(memory_space=pl.ANY),
    }
    return pl.pallas_call(
        kernel,
        out_shape=[jax.ShapeDtypeStruct(s, t) for s, t in outs],
        in_specs=[spaces[kind] for kind, _ in args],
        out_specs=[spaces["v"]] * len(outs),
        scratch_shapes=[pltpu.VMEM(s, t) for s, t in scratch] + list(sems),
        compiler_params=pltpu.CompilerParams(vmem_limit_bytes=40 * MIB),
        cost_estimate=pl.CostEstimate(flops=flops, bytes_accessed=4_000_000, transcendentals=0),
    )(*[value for _, value in args])


def v(*values):
    return [("v", value) for value in values]


def shift(value, rows, cols):
    n_gcm = lax.axis_size("gcm")
    n_crm = lax.axis_size("crm")
    pairs = []
    for g in range(n_gcm):
        for c in range(n_crm):
            target = ((g + rows) % n_gcm) * n_crm + (c + cols) % n_crm
            pairs.append((g * n_crm + c, target))
    return lax.ppermute(value, ("gcm", "crm"), pairs)


def pair_table(bins):
    table = np.zeros((bins * bins, 576), np.float32)

    def put(column, i, j):
        table[i * bins + j, column] = 1.0
        table[j * bins + i, column] = 1.0

    for d in range(16):
        for b in range(32):
            put(32 * d + b, b, (b + d) % 32)
    for b in range(16):
        put(512 + b, b, b + 16)
    for b in range(32):
        put(528 + b, b, 32)
    put(560, 32, 32)
    return table


def rank_order(counts):
    total = counts.shape[0]
    index = jnp.arange(total, dtype=jnp.int32)
    ahead = (counts[None, :] > counts[:, None]) | (
        (counts[None, :] == counts[:, None]) & (index[None, :] < index[:, None])
    )
    rank = jnp.sum(ahead.astype(jnp.int32), axis=1)
    match = rank[None, :] == index[:, None]
    order = jnp.sum(jnp.where(match, index[None, :], 0), axis=1)
    ordered = jnp.sum(jnp.where(match, counts[None, :], 0), axis=1)
    return order, ordered


def shards(tracer, wind_x, wind_y, drops, owner, counts, collision, growth):
    devices = lax.axis_size("gcm") * lax.axis_size("crm")
    levels, row_count, col_count = tracer.shape
    col_total, bins, cells = drops.shape
    field = (tracer.shape, F32)
    strip = ((levels, row_count, 128), F32)
    rows = ((2, levels, col_count), F32)
    wide = col_count + 128
    down_map, up_map = level_tables(levels, CRM_LEV)

    to_right, to_left = call(
        pack_kernel,
        [((levels // 4, 8, 128), F32)] * 2,
        [("h", tracer), ("h", wind_x), ("h", wind_y)],
        [field] * 3,
        [pltpu.SemaphoreType.DMA((3,))],
    )
    from_left = shift(to_right, 0, 1)
    from_right = shift(to_left, 0, -1)
    tend, top, bot = call(first_kernel, [field, rows, rows], v(tracer, wind_x, wind_y))
    q_strip, u_strip, v_strip, tend_strip, top, bot = call(
        strip_kernel,
        [strip] * 4 + [((2, levels, wide), F32)] * 2,
        v(from_left, from_right, top, bot),
    )
    state, smooth, tend, top, bot = call(
        second_kernel,
        [field, field, ((levels, row_count, wide), F32)] + [((1, levels, wide), F32)] * 2,
        v(tracer, wind_x, wind_y, tend, q_strip, u_strip, v_strip, tend_strip)
        + v(shift(bot, 1, 0), shift(top, -1, 0)),
    )
    base, cell_forcing = call(
        third_kernel,
        [field, ((col_total, cells), F32)],
        v(tracer, state, smooth, tend, shift(bot, 1, 0), shift(top, -1, 0))
        + v(jnp.asarray(down_map, F32)),
        [((levels, col_count), F32), ((levels, col_count), F32)],
    )

    capacity = 2 * col_total // devices
    owners = owner[:, 0]
    index = jnp.arange(col_total, dtype=jnp.int32)
    same = (owners[:, None] == owners[None, :]) & (index[:, None] < index[None, :])
    slot_of = owners * capacity + jnp.sum(same.astype(jnp.int32), axis=0)
    order, ordered = rank_order(counts)
    table = jnp.asarray(pair_table(bins), BF16)
    coef = DT_CRM * jnp.dot(collision, table, preferred_element_type=F32)
    coarse = lax.reduce_precision(coef, 8, 7)
    fine = coef - coarse
    pad = ((0, 40 - bins), (0, 0))
    coef = jnp.concatenate([jnp.pad(coarse, pad), jnp.pad(fine, pad)], axis=0).astype(BF16)
    tail = coef[:, 512:]
    tail_coef = jnp.concatenate(
        [jnp.pad(tail, ((0, 0), (64 * k, 192 - 64 * k))) for k in range(4)], axis=0
    )
    growth_rows = jnp.broadcast_to(jnp.pad(growth, (0, 40 - bins))[:, None], (40, cells))
    n_gcm = lax.axis_size("gcm")
    n_crm = lax.axis_size("crm")
    g = lax.axis_index("gcm").astype(jnp.int32)
    c = lax.axis_index("crm").astype(jnp.int32)
    place = jnp.stack([g, jnp.int32(n_gcm), jnp.int32(n_crm)])

    final, heat, send = call(
        crm_kernel,
        [((col_total, bins, cells), BF16), ((CRM_LEV, col_total), F32),
         ((devices, CRM_LEV, 128), BF16)],
        [("s", order), ("s", ordered), ("s", place)]
        + v(drops, cell_forcing, slot_of[None, :], coef[:, :512], tail_coef, growth_rows),
        [((GROUP, 40, cells), F32), ((GROUP, 512, cells), BF16),
         ((GROUP // 4, 256, cells), BF16),
         ((col_total, cells), F32), ((col_total, cells), F32)],
        flops=10_000_000_000,
    )
    got = lax.all_to_all(send, ("gcm", "crm"), split_axis=0, concat_axis=0, tiled=True)
    up = (g + n_gcm - 1) % n_gcm * n_crm
    same_row = g * n_crm
    down = (g + 1) % n_gcm * n_crm
    west = (c + n_crm - 1) % n_crm
    east = (c + 1) % n_crm
    around = jnp.stack(
        [up + c, down + c, same_row + west, same_row + east,
         up + west, up + east, down + west, down + east]
    )
    tracer_next, power = call(
        last_kernel,
        [field, ((CRM_LEV, devices * capacity), F32)],
        [("s", around)] + v(base, heat, got, jnp.asarray(up_map, F32)),
        [((levels, col_count), F32)] * 5,
    )
    return (tracer_next, final, power)


def solution(mesh):
    return jax.shard_map(
        shards,
        mesh=mesh,
        in_specs=(
            P(None, "gcm", "crm"),
            P(None, "gcm", "crm"),
            P(None, "gcm", "crm"),
            P(("gcm", "crm"), None, None),
            P(("gcm", "crm"), None),
            P(("gcm", "crm")),
            P(),
            P(),
        ),
        out_specs=(P(None, "gcm", "crm"), P(("gcm", "crm"), None, None), P(None, ("gcm", "crm"))),
        check_vma=False,
    )
```

```python
import functools

import jax
import jax.numpy as jnp
import numpy as np
from jax import lax
from jax.experimental import pallas as pl
from jax.experimental.pallas import tpu as pltpu
from jax.sharding import PartitionSpec as P

CRM_X = 16
CRM_LEV = 16
DYN_STEPS = 2

DT_DYN = 0.04
DT_CRM = 0.05
DT_PHYS = 0.5
HIGH = lax.Precision.HIGHEST
F32 = jnp.float32
BF16 = jnp.bfloat16
GROUP = 8
CHUNK = 8
MIB = 1024 * 1024


def gll_tables():
    inv_root = 1.0 / np.sqrt(5.0)
    gll_nodes = np.array([-1.0, -inv_root, inv_root, 1.0])
    weights = np.array([1.0, 5.0, 5.0, 1.0]) / 6.0
    legendre = (5.0 * gll_nodes**3 - 3.0 * gll_nodes) / 2.0
    derivative = np.zeros((4, 4))
    for i in range(4):
        for j in range(4):
            if i != j:
                derivative[i, j] = legendre[i] / (legendre[j] * (gll_nodes[i] - gll_nodes[j]))
    derivative[0, 0] = -3.0
    derivative[3, 3] = 3.0
    return (2.0 * derivative, weights)


def level_tables(levels, crm_levels):
    spacing = levels / crm_levels
    centres = (np.arange(crm_levels) + 0.5) * spacing - 0.5
    hats = np.maximum(0.0, 1.0 - np.abs(np.arange(levels)[None, :] - centres[:, None]) / spacing)
    down_map = hats / hats.sum(axis=1, keepdims=True)
    up_map = hats.T / hats.T.sum(axis=1, keepdims=True)
    return (down_map, up_map)


DERIV, WEIGHTS = gll_tables()


def iota(shape, axis):
    return lax.broadcasted_iota(jnp.int32, shape, axis)


def derivative_terms(shape, axis):
    phase = iota(shape, axis) % 4
    terms = []
    for shift in range(-3, 4):
        value = jnp.zeros(shape, F32)
        for i in range(4):
            if 0 <= i + shift < 4:
                value = jnp.where(phase == i, F32(DERIV[i, i + shift]), value)
        terms.append((shift, value))
    return terms


def along(x, terms, axis):
    size = x.shape[axis]
    total = None
    for shift, value in terms:
        moved = x if shift == 0 else pltpu.roll(x, (-shift) % size, axis)
        part = value[None] * moved
        total = part if total is None else total + part
    return total


def tendency(x, u, v, row_terms, col_terms):
    halves = []
    for h in range(x.shape[2] // 128):
        cut = slice(128 * h, 128 * h + 128)
        q = x[:, :, cut]
        grad_x = along(q, row_terms, 1)
        grad_y = along(q, col_terms, 2)
        halves.append(-(u[:, :, cut] * grad_x + v[:, :, cut] * grad_y))
    return jnp.concatenate(halves, axis=2)


def pack_kernel(q_hbm, u_hbm, v_hbm, right_ref, left_ref, q_ref, u_ref, v_ref, sems):
    copies = []
    for i, (src, dst) in enumerate(((q_hbm, q_ref), (u_hbm, u_ref), (v_hbm, v_ref))):
        copies.append(pltpu.make_async_copy(src, dst, sems.at[i]))
    for copy in copies:
        copy.start()
    for copy in copies:
        copy.wait()
    lane = iota((8, 128), 1)

    def body(group, carry):
        right = jnp.zeros((8, 128), F32)
        left = jnp.zeros((8, 128), F32)
        for j in range(4):
            for f, ref in enumerate((q_ref, u_ref, v_ref)):
                start = 32 * j + 8 * f
                here = (lane >= start) & (lane < start + 8)
                x = ref[group * 4 + j]
                right = jnp.where(here, pltpu.roll(x[:, 128:256], (start - 120) % 128, 1), right)
                first = x[:, 0:128]
                if start:
                    first = pltpu.roll(first, start, 1)
                left = jnp.where(here, first, left)
        right_ref[group] = right
        left_ref[group] = left
        return carry

    lax.fori_loop(0, right_ref.shape[0], body, 0)


def put_rows(x, levels, top_ref, bot_ref, i):
    top_ref[i, levels, :] = x[:, 0, :]
    bot_ref[i, levels, :] = x[:, 7, :]


def first_kernel(q_ref, u_ref, v_ref, tend_ref, top_ref, bot_ref):
    row_terms = derivative_terms((8, 128), 0)
    col_terms = derivative_terms((8, 128), 1)

    def body(chunk, carry):
        levels = pl.ds(pl.multiple_of(chunk * CHUNK, CHUNK), CHUNK)
        q = q_ref[levels]
        tend = tendency(q, u_ref[levels], v_ref[levels], row_terms, col_terms)
        tend_ref[levels] = tend
        put_rows(tend, levels, top_ref, bot_ref, 0)
        put_rows(q, levels, top_ref, bot_ref, 1)
        return carry

    lax.fori_loop(0, q_ref.shape[0] // CHUNK, body, 0)


def strip_kernel(
    left_ref, right_ref, top_main, bot_main,
    q_ref, u_ref, v_ref, tend_ref, top_ref, bot_ref,
):
    row_terms = derivative_terms((8, 128), 0)
    col_terms = derivative_terms((8, 128), 1)
    lane = iota((8, 128), 1)
    top_ref[:, :, 0:256] = top_main[...]
    bot_ref[:, :, 0:256] = bot_main[...]

    def body(chunk, carry):
        tiles = [[], [], []]
        for half in range(CHUNK // 4):
            west = left_ref[chunk * (CHUNK // 4) + half]
            east = right_ref[chunk * (CHUNK // 4) + half]
            for j in range(4):
                for f in range(3):
                    start = 32 * j + 8 * f
                    a = pltpu.roll(east, 128 - start, 1) if start else east
                    b = pltpu.roll(west, (120 - start) % 128, 1)
                    tiles[f].append(jnp.where(lane < 8, a, jnp.where(lane >= 120, b, 0.0)))
        q, u, v = [jnp.stack(tile, axis=0) for tile in tiles]
        levels = pl.ds(pl.multiple_of(chunk * CHUNK, CHUNK), CHUNK)
        q_ref[levels] = q
        u_ref[levels] = u
        v_ref[levels] = v
        tend = tendency(q, u, v, row_terms, col_terms)
        tend_ref[levels] = tend
        for i, x in enumerate((tend, q)):
            top_ref[i, levels, 256:384] = x[:, 0, :]
            bot_ref[i, levels, 256:384] = x[:, 7, :]
        return carry

    lax.fori_loop(0, q_ref.shape[0] // CHUNK, body, 0)


def assemble_chunk(x, up, down):
    shape = x.shape
    row = iota(shape, 1)
    partner = jnp.where(
        row == 0,
        jnp.broadcast_to(up[:, None, :], shape),
        jnp.where(
            row == 7,
            jnp.broadcast_to(down[:, None, :], shape),
            jnp.where(row == 3, pltpu.roll(x, 7, 1), pltpu.roll(x, 1, 1)),
        ),
    )
    x = jnp.where((row % 4 == 0) | (row % 4 == 3), 0.5 * (x + partner), x)
    col = iota(shape, 2)
    partner = jnp.where(
        col % 4 == 3, pltpu.roll(x, shape[2] - 1, 2), pltpu.roll(x, 1, 2)
    )
    return jnp.where((col % 4 == 0) | (col % 4 == 3), 0.5 * (x + partner), x)


def join(main, strip):
    return jnp.concatenate([main, strip], axis=2)


def second_kernel(
    q_ref, u_ref, v_ref, tend_ref, q_strip, u_strip, v_strip, tend_strip, up_ref, down_ref,
    state_ref, smooth_ref, next_ref, top_ref, bot_ref,
):
    row_terms = derivative_terms((8, 128), 0)
    col_terms = derivative_terms((8, 128), 1)

    def body(chunk, carry):
        levels = pl.ds(pl.multiple_of(chunk * CHUNK, CHUNK), CHUNK)
        q = join(q_ref[levels], q_strip[levels])
        change = assemble_chunk(
            join(tend_ref[levels], tend_strip[levels]), up_ref[0, levels, :], down_ref[0, levels, :]
        )
        smooth = assemble_chunk(q, up_ref[1, levels, :], down_ref[1, levels, :])
        smooth_ref[levels] = smooth[:, :, 0:256]
        state = q + DT_DYN * change
        state_ref[levels] = state[:, :, 0:256]
        tend = tendency(
            state, join(u_ref[levels], u_strip[levels]), join(v_ref[levels], v_strip[levels]),
            row_terms, col_terms,
        )
        next_ref[levels] = tend
        put_rows(tend, levels, top_ref, bot_ref, 0)
        return carry

    lax.fori_loop(0, q_ref.shape[0] // CHUNK, body, 0)


def third_kernel(
    q_ref, state_ref, smooth_ref, tend_ref, up_ref, down_ref, down_map_ref,
    base_ref, cell_ref, near_ref, far_ref,
):
    cols = cell_ref.shape[0]
    half = cols // 2
    phase = iota((8, 256), 0) % 4
    row_weight = jnp.where((phase == 0) | (phase == 3), F32(WEIGHTS[0]), F32(WEIGHTS[1]))
    near_rows = jnp.where(iota((8, 256), 0) < 4, row_weight, 0.0)
    far_rows = row_weight - near_rows

    def body(chunk, carry):
        levels = pl.ds(pl.multiple_of(chunk * CHUNK, CHUNK), CHUNK)
        change = assemble_chunk(tend_ref[levels], up_ref[0, levels, :], down_ref[0, levels, :])
        moved = (state_ref[levels] + DT_DYN * change[:, :, 0:256]) - q_ref[levels]
        base_ref[levels] = smooth_ref[levels] + moved
        near_ref[levels, :] = jnp.sum(moved * near_rows[None], axis=1)
        far_ref[levels, :] = jnp.sum(moved * far_rows[None], axis=1)
        return carry

    lax.fori_loop(0, q_ref.shape[0] // CHUNK, body, 0)
    point = iota((256, cols), 0)
    element = iota((256, cols), 1)
    weight = jnp.where(
        (point % 4 == 0) | (point % 4 == 3), F32(WEIGHTS[0]), F32(WEIGHTS[1])
    ) * F32(0.25 / (DYN_STEPS * DT_DYN))
    near_cols = jnp.where(point // 4 == element, weight, 0.0)
    far_cols = jnp.where(point // 4 + half == element, weight, 0.0)
    means = jnp.dot(near_ref[...], near_cols, precision=HIGH, preferred_element_type=F32)
    means += jnp.dot(far_ref[...], far_cols, precision=HIGH, preferred_element_type=F32)
    forcing = jnp.dot(down_map_ref[...], means, precision=HIGH, preferred_element_type=F32)
    forcing = forcing.T.astype(BF16)
    cells = cell_ref.shape[1]
    spread = (iota((CRM_LEV, cells), 1) // CRM_X == iota((CRM_LEV, cells), 0)).astype(BF16)
    cell_ref[...] = DT_CRM * jnp.dot(forcing, spread, preferred_element_type=F32)


def crm_kernel(
    order_ref, count_ref, place_ref, drops_ref, cell_ref, slot_ref, coef_ref, growth_ref,
    final_ref, heat_ref, send_ref, state_ref, pair_ref, twice_ref, heat_cell_ref, echo_cell_ref,
):
    bins = drops_ref.shape[1]
    cells = drops_ref.shape[2]
    cols = drops_ref.shape[0]
    coef = coef_ref[...]
    growth = growth_ref[...]
    state_ref[...] = jnp.zeros(state_ref.shape, F32)
    mass = (iota((40, cells), 0) + 1).astype(F32) / F32(bins)

    def grow(k, which, zero):
        grown = state_ref[k] + growth * cell_ref[pl.ds(which, 1), :]
        for h in range(cells // 128):
            cut = slice(128 * h, 128 * h + 128)
            g = grown[0:32, cut]
            last = grown[32:40, cut]
            twice_ref[2 * k + h, 0:32, :] = g
            twice_ref[2 * k + h, 32:48, :] = g[0:16]
            for d in range(16):
                other = g if d % 8 == 0 else twice_ref[2 * k + h, pl.ds(zero + d, 32), :]
                if d == 8:
                    other = jnp.concatenate([g[8:], g[:8]], axis=0)
                pair_ref[k, 32 * d : 32 * d + 32, cut] = (g * other).astype(BF16)
            pair_ref[k, 512:528, cut] = (g[0:16] * g[16:32]).astype(BF16)
            pair_ref[k, 528:560, cut] = (g * last[0:1]).astype(BF16)
            tail = jnp.concatenate([last * last, jnp.zeros((8, 128), F32)], axis=0)
            pair_ref[k, 560:576, cut] = tail.astype(BF16)
        return grown

    def group(index, carry):
        base = index * GROUP
        which = [order_ref[base + k] for k in range(GROUP)]
        count = [count_ref[base + k] for k in range(GROUP)]
        for k in range(GROUP):
            state_ref[k, 0:bins, :] = drops_ref[which[k]].astype(F32)

        def step(s, c):
            for k in range(GROUP):
                grown = grow(k, which[k], place_ref[3])
                change = jnp.dot(coef, pair_ref[k], preferred_element_type=F32)
                moved = grown + (change[0:40] + change[40:80])
                state_ref[k] = jnp.where(s < count[k], moved, state_ref[k])
            return c

        lax.fori_loop(0, count[0], step, 0)
        for k in range(GROUP):
            final = state_ref[k, 0:bins, :]
            initial = drops_ref[which[k]].astype(F32)
            final_ref[which[k]] = final.astype(BF16)
            weighted = mass[0:bins] * final
            heat = jnp.sum(mass[0:bins] * (final - initial), axis=0, keepdims=True)
            echo = jnp.sum(weighted * weighted, axis=0, keepdims=True)
            heat_cell_ref[pl.ds(which[k], 1), :] = heat
            echo_cell_ref[pl.ds(which[k], 1), :] = echo
        return carry

    lax.fori_loop(0, cols // GROUP, group, 0)
    means = jnp.where(
        iota((CRM_LEV, cells), 1) // CRM_X == iota((CRM_LEV, cells), 0), F32(1.0 / CRM_X), 0.0
    )
    contract = (((1,), (1,)), ((), ()))
    heat = lax.dot_general(
        means, heat_cell_ref[...], contract, precision=HIGH, preferred_element_type=F32
    )
    heat = heat.astype(BF16).astype(F32)
    heat_ref[...] = heat
    echo = lax.dot_general(
        means, echo_cell_ref[...], contract, precision=HIGH, preferred_element_type=F32
    )
    echo = jnp.log(1.0 + echo)

    devices = send_ref.shape[0]
    slots = 2 * cols
    capacity = slots // devices
    onehot = (slot_ref[...] == iota((slots, cols), 0)).astype(F32)
    packed = lax.dot_general(echo, onehot, contract, precision=HIGH, preferred_element_type=F32)
    coarse = packed.astype(BF16).astype(F32)
    rest = packed - coarse
    middle = rest.astype(BF16).astype(F32)
    pieces = (coarse, middle, rest - middle)
    lane = iota((CRM_LEV, 128), 1)
    near = heat
    far = pltpu.roll(heat, 64, 1)
    sides = jnp.where(
        lane == 1, pltpu.roll(heat, 65, 1), jnp.where(lane == 62, pltpu.roll(heat, 63, 1), heat)
    )
    n_gcm = place_ref[1]
    n_crm = place_ref[2]
    for d in range(devices):
        away = d // n_crm - place_ref[0]
        below = (away == 1) | (away == 1 - n_gcm)
        above = (away == -1) | (away == n_gcm - 1)
        block = jnp.where(below, far, jnp.where(above, near, sides))
        tile, offset = divmod(d * capacity, 128)
        for i, piece in enumerate(pieces):
            moved = pltpu.roll(
                piece[:, 128 * tile : 128 * tile + 128], (64 + i * capacity - offset) % 128, 1
            )
            start = 64 + i * capacity
            block = jnp.where((lane >= start) & (lane < start + capacity), moved, block)
        send_ref[d] = block.astype(BF16)


def last_kernel(around_ref, base_ref, own_ref, got_ref, up_map_ref, out_ref, power_ref, *back_refs):
    cols = own_ref.shape[1]
    half = cols // 2
    element = iota((cols, 256), 0)
    col = iota((cols, 256), 1)
    phase = col % 4
    edge = (phase == 0) | (phase == 3)
    other = jnp.where(phase == 0, col // 4 - 1, col // 4 + 1)

    def spread(centre, start, west, west_lane, east, east_lane):
        inside = jnp.where(element == col // 4 + start, jnp.where(edge, 0.5, 1.0), 0.0)
        beside = edge & (element == other + start) & (other >= 0) & (other < half)
        middle = jnp.where(beside, 0.5, inside).astype(BF16)
        from_west = jnp.where((col == 0) & (element == west_lane), 0.5, 0.0).astype(BF16)
        from_east = jnp.where((col == 255) & (element == east_lane), 0.5, 0.0).astype(BF16)
        total = jnp.dot(centre, middle, preferred_element_type=F32)
        total += jnp.dot(west, from_west, preferred_element_type=F32)
        total += jnp.dot(east, from_east, preferred_element_type=F32)
        return total

    own = own_ref[...].astype(BF16)
    up, down, left, right, up_left, up_right, down_left, down_right = [
        got_ref[around_ref[i]] for i in range(8)
    ]
    above = spread(up, 0, up_left, half - 1, up_right, 0)
    near = spread(own, 0, left, half - 1, right, 0)
    far = spread(own, half, left, half - 2, right, 1)
    below = spread(down, 0, down_left, half - 1, down_right, 0)
    parts = (
        0.5 * (above + near), near, 0.5 * (near + far), far, 0.5 * (far + below),
    )
    up_map = up_map_ref[...]
    for part, ref in zip(parts, back_refs):
        ref[...] = DT_PHYS * jnp.dot(up_map, part, precision=HIGH, preferred_element_type=F32)

    devices = got_ref.shape[0]
    slots = power_ref.shape[1]
    capacity = slots // devices
    lane = iota((CRM_LEV, 128), 1)
    tiles = [jnp.zeros((CRM_LEV, 128), F32) for _ in range(slots // 128)]
    for d in range(devices):
        block = got_ref[d].astype(F32)
        fine = pltpu.roll(block, 128 - 2 * capacity, 1) + pltpu.roll(block, 128 - capacity, 1)
        tile, offset = divmod(d * capacity, 128)
        moved = pltpu.roll(block + fine, (offset - 64) % 128, 1)
        tiles[tile] = jnp.where((lane >= offset) & (lane < offset + capacity), moved, tiles[tile])
    power_ref[...] = jnp.concatenate(tiles, axis=1)

    def body(chunk, carry):
        levels = pl.ds(pl.multiple_of(chunk * CHUNK, CHUNK), CHUNK)
        shape = (CHUNK, 8, 256)
        row = iota(shape, 1)
        wide = [jnp.broadcast_to(ref[levels, :][:, None, :], shape) for ref in back_refs]
        back = jnp.where(
            row == 0,
            wide[0],
            jnp.where(
                row < 3,
                wide[1],
                jnp.where(row < 5, wide[2], jnp.where(row < 7, wide[3], wide[4])),
            ),
        )
        out_ref[levels] = base_ref[levels] + back
        return carry

    lax.fori_loop(0, base_ref.shape[0] // CHUNK, body, 0)


def call(kernel, outs, args, scratch=(), sems=(), flops=10_000_000):
    spaces = {
        "s": pl.BlockSpec(memory_space=pltpu.SMEM),
        "v": pl.BlockSpec(memory_space=pltpu.VMEM),
        "h": pl.BlockSpec(memory_space=pl.ANY),
    }
    return pl.pallas_call(
        kernel,
        out_shape=[jax.ShapeDtypeStruct(s, t) for s, t in outs],
        in_specs=[spaces[kind] for kind, _ in args],
        out_specs=[spaces["v"]] * len(outs),
        scratch_shapes=[pltpu.VMEM(s, t) for s, t in scratch] + list(sems),
        compiler_params=pltpu.CompilerParams(vmem_limit_bytes=40 * MIB),
        cost_estimate=pl.CostEstimate(flops=flops, bytes_accessed=4_000_000, transcendentals=0),
    )(*[value for _, value in args])


def v(*values):
    return [("v", value) for value in values]


def shift(value, rows, cols):
    n_gcm = lax.axis_size("gcm")
    n_crm = lax.axis_size("crm")
    pairs = []
    for g in range(n_gcm):
        for c in range(n_crm):
            target = ((g + rows) % n_gcm) * n_crm + (c + cols) % n_crm
            pairs.append((g * n_crm + c, target))
    return lax.ppermute(value, ("gcm", "crm"), pairs)


def pair_table(bins):
    table = np.zeros((bins * bins, 576), np.float32)

    def put(column, i, j):
        table[i * bins + j, column] = 1.0
        table[j * bins + i, column] = 1.0

    for d in range(16):
        for b in range(32):
            put(32 * d + b, b, (b + d) % 32)
    for b in range(16):
        put(512 + b, b, b + 16)
    for b in range(32):
        put(528 + b, b, 32)
    put(560, 32, 32)
    return table


def rank_order(counts):
    total = counts.shape[0]
    index = jnp.arange(total, dtype=jnp.int32)
    ahead = (counts[None, :] > counts[:, None]) | (
        (counts[None, :] == counts[:, None]) & (index[None, :] < index[:, None])
    )
    rank = jnp.sum(ahead.astype(jnp.int32), axis=1)
    match = rank[None, :] == index[:, None]
    order = jnp.sum(jnp.where(match, index[None, :], 0), axis=1)
    ordered = jnp.sum(jnp.where(match, counts[None, :], 0), axis=1)
    return order, ordered


def shards(tracer, wind_x, wind_y, drops, owner, counts, collision, growth):
    devices = lax.axis_size("gcm") * lax.axis_size("crm")
    levels, row_count, col_count = tracer.shape
    col_total, bins, cells = drops.shape
    field = (tracer.shape, F32)
    strip = ((levels, row_count, 128), F32)
    rows = ((2, levels, col_count), F32)
    wide = col_count + 128
    down_map, up_map = level_tables(levels, CRM_LEV)

    to_right, to_left = call(
        pack_kernel,
        [((levels // 4, 8, 128), F32)] * 2,
        [("h", tracer), ("h", wind_x), ("h", wind_y)],
        [field] * 3,
        [pltpu.SemaphoreType.DMA((3,))],
    )
    from_left = shift(to_right, 0, 1)
    from_right = shift(to_left, 0, -1)
    tend, top, bot = call(first_kernel, [field, rows, rows], v(tracer, wind_x, wind_y))
    q_strip, u_strip, v_strip, tend_strip, top, bot = call(
        strip_kernel,
        [strip] * 4 + [((2, levels, wide), F32)] * 2,
        v(from_left, from_right, top, bot),
    )
    state, smooth, tend, top, bot = call(
        second_kernel,
        [field, field, ((levels, row_count, wide), F32)] + [((1, levels, wide), F32)] * 2,
        v(tracer, wind_x, wind_y, tend, q_strip, u_strip, v_strip, tend_strip)
        + v(shift(bot, 1, 0), shift(top, -1, 0)),
    )
    base, cell_forcing = call(
        third_kernel,
        [field, ((col_total, cells), F32)],
        v(tracer, state, smooth, tend, shift(bot, 1, 0), shift(top, -1, 0))
        + v(jnp.asarray(down_map, F32)),
        [((levels, col_count), F32), ((levels, col_count), F32)],
    )

    capacity = 2 * col_total // devices
    owners = owner[:, 0]
    index = jnp.arange(col_total, dtype=jnp.int32)
    same = (owners[:, None] == owners[None, :]) & (index[:, None] < index[None, :])
    slot_of = owners * capacity + jnp.sum(same.astype(jnp.int32), axis=0)
    order, ordered = rank_order(counts)
    table = jnp.asarray(pair_table(bins), BF16)
    coef = DT_CRM * jnp.dot(collision, table, preferred_element_type=F32)
    coarse = lax.reduce_precision(coef, 8, 7)
    fine = coef - coarse
    pad = ((0, 40 - bins), (0, 0))
    coef = jnp.concatenate([jnp.pad(coarse, pad), jnp.pad(fine, pad)], axis=0).astype(BF16)
    growth_rows = jnp.broadcast_to(jnp.pad(growth, (0, 40 - bins))[:, None], (40, cells))
    n_gcm = lax.axis_size("gcm")
    n_crm = lax.axis_size("crm")
    g = lax.axis_index("gcm").astype(jnp.int32)
    c = lax.axis_index("crm").astype(jnp.int32)
    place = jnp.stack([g, jnp.int32(n_gcm), jnp.int32(n_crm), jnp.int32(0)])

    final, heat, send = call(
        crm_kernel,
        [((col_total, bins, cells), BF16), ((CRM_LEV, col_total), F32),
         ((devices, CRM_LEV, 128), BF16)],
        [("s", order), ("s", ordered), ("s", place)]
        + v(drops, cell_forcing, slot_of[None, :], coef, growth_rows),
        [((GROUP, 40, cells), F32), ((GROUP, 576, cells), BF16),
         ((2 * GROUP, 48, 128), F32),
         ((col_total, cells), F32), ((col_total, cells), F32)],
        flops=10_000_000_000,
    )
    got = lax.all_to_all(send, ("gcm", "crm"), split_axis=0, concat_axis=0, tiled=True)
    up = (g + n_gcm - 1) % n_gcm * n_crm
    same_row = g * n_crm
    down = (g + 1) % n_gcm * n_crm
    west = (c + n_crm - 1) % n_crm
    east = (c + 1) % n_crm
    around = jnp.stack(
        [up + c, down + c, same_row + west, same_row + east,
         up + west, up + east, down + west, down + east]
    )
    tracer_next, power = call(
        last_kernel,
        [field, ((CRM_LEV, devices * capacity), F32)],
        [("s", around)] + v(base, heat, got, jnp.asarray(up_map, F32)),
        [((levels, col_count), F32)] * 5,
    )
    return (tracer_next, final, power)


def solution(mesh):
    return jax.shard_map(
        shards,
        mesh=mesh,
        in_specs=(
            P(None, "gcm", "crm"),
            P(None, "gcm", "crm"),
            P(None, "gcm", "crm"),
            P(("gcm", "crm"), None, None),
            P(("gcm", "crm"), None),
            P(("gcm", "crm")),
            P(),
            P(),
        ),
        out_specs=(P(None, "gcm", "crm"), P(("gcm", "crm"), None, None), P(None, ("gcm", "crm"))),
        check_vma=False,
    )
```

```python
import functools

import jax
import jax.numpy as jnp
import numpy as np
from jax import lax
from jax.experimental import pallas as pl
from jax.experimental.pallas import tpu as pltpu
from jax.sharding import PartitionSpec as P

CRM_X = 16
CRM_LEV = 16
DYN_STEPS = 2

DT_DYN = 0.04
DT_CRM = 0.05
DT_PHYS = 0.5
HIGH = lax.Precision.HIGHEST
F32 = jnp.float32
BF16 = jnp.bfloat16
GROUP = 8
CHUNK = 8
MIB = 1024 * 1024


def gll_tables():
    inv_root = 1.0 / np.sqrt(5.0)
    gll_nodes = np.array([-1.0, -inv_root, inv_root, 1.0])
    weights = np.array([1.0, 5.0, 5.0, 1.0]) / 6.0
    legendre = (5.0 * gll_nodes**3 - 3.0 * gll_nodes) / 2.0
    derivative = np.zeros((4, 4))
    for i in range(4):
        for j in range(4):
            if i != j:
                derivative[i, j] = legendre[i] / (legendre[j] * (gll_nodes[i] - gll_nodes[j]))
    derivative[0, 0] = -3.0
    derivative[3, 3] = 3.0
    return (2.0 * derivative, weights)


def level_tables(levels, crm_levels):
    spacing = levels / crm_levels
    centres = (np.arange(crm_levels) + 0.5) * spacing - 0.5
    hats = np.maximum(0.0, 1.0 - np.abs(np.arange(levels)[None, :] - centres[:, None]) / spacing)
    down_map = hats / hats.sum(axis=1, keepdims=True)
    up_map = hats.T / hats.T.sum(axis=1, keepdims=True)
    return (down_map, up_map)


DERIV, WEIGHTS = gll_tables()


def iota(shape, axis):
    return lax.broadcasted_iota(jnp.int32, shape, axis)


def derivative_terms(shape, axis):
    phase = iota(shape, axis) % 4
    terms = []
    for shift in range(-3, 4):
        value = jnp.zeros(shape, F32)
        for i in range(4):
            if 0 <= i + shift < 4:
                value = jnp.where(phase == i, F32(DERIV[i, i + shift]), value)
        terms.append((shift, value))
    return terms


def along(x, terms, axis):
    size = x.shape[axis]
    total = None
    for shift, value in terms:
        moved = x if shift == 0 else pltpu.roll(x, (-shift) % size, axis)
        part = value[None] * moved
        total = part if total is None else total + part
    return total


def tendency(x, u, v, row_terms, col_terms):
    halves = []
    for h in range(x.shape[2] // 128):
        cut = slice(128 * h, 128 * h + 128)
        q = x[:, :, cut]
        grad_x = along(q, row_terms, 1)
        grad_y = along(q, col_terms, 2)
        halves.append(-(u[:, :, cut] * grad_x + v[:, :, cut] * grad_y))
    return jnp.concatenate(halves, axis=2)


def pack_kernel(q_hbm, u_hbm, v_hbm, right_ref, left_ref, q_ref, u_ref, v_ref, sems):
    copies = []
    for i, (src, dst) in enumerate(((q_hbm, q_ref), (u_hbm, u_ref), (v_hbm, v_ref))):
        copies.append(pltpu.make_async_copy(src, dst, sems.at[i]))
    for copy in copies:
        copy.start()
    for copy in copies:
        copy.wait()
    lane = iota((8, 128), 1)

    def body(group, carry):
        right = jnp.zeros((8, 128), F32)
        left = jnp.zeros((8, 128), F32)
        for j in range(4):
            for f, ref in enumerate((q_ref, u_ref, v_ref)):
                start = 32 * j + 8 * f
                here = (lane >= start) & (lane < start + 8)
                x = ref[group * 4 + j]
                right = jnp.where(here, pltpu.roll(x[:, 128:256], (start - 120) % 128, 1), right)
                first = x[:, 0:128]
                if start:
                    first = pltpu.roll(first, start, 1)
                left = jnp.where(here, first, left)
        right_ref[group] = right
        left_ref[group] = left
        return carry

    lax.fori_loop(0, right_ref.shape[0], body, 0)


def put_rows(x, levels, top_ref, bot_ref, i):
    top_ref[i, levels, :] = x[:, 0, :]
    bot_ref[i, levels, :] = x[:, 7, :]


def first_kernel(q_ref, u_ref, v_ref, tend_ref, top_ref, bot_ref):
    row_terms = derivative_terms((8, 128), 0)
    col_terms = derivative_terms((8, 128), 1)

    def body(chunk, carry):
        levels = pl.ds(pl.multiple_of(chunk * CHUNK, CHUNK), CHUNK)
        q = q_ref[levels]
        tend = tendency(q, u_ref[levels], v_ref[levels], row_terms, col_terms)
        tend_ref[levels] = tend
        put_rows(tend, levels, top_ref, bot_ref, 0)
        put_rows(q, levels, top_ref, bot_ref, 1)
        return carry

    lax.fori_loop(0, q_ref.shape[0] // CHUNK, body, 0)


def strip_kernel(
    left_ref, right_ref, top_main, bot_main,
    q_ref, u_ref, v_ref, tend_ref, top_ref, bot_ref,
):
    row_terms = derivative_terms((8, 128), 0)
    col_terms = derivative_terms((8, 128), 1)
    lane = iota((8, 128), 1)
    top_ref[:, :, 0:256] = top_main[...]
    bot_ref[:, :, 0:256] = bot_main[...]

    def body(chunk, carry):
        tiles = [[], [], []]
        for half in range(CHUNK // 4):
            west = left_ref[chunk * (CHUNK // 4) + half]
            east = right_ref[chunk * (CHUNK // 4) + half]
            for j in range(4):
                for f in range(3):
                    start = 32 * j + 8 * f
                    a = pltpu.roll(east, 128 - start, 1) if start else east
                    b = pltpu.roll(west, (120 - start) % 128, 1)
                    tiles[f].append(jnp.where(lane < 8, a, jnp.where(lane >= 120, b, 0.0)))
        q, u, v = [jnp.stack(tile, axis=0) for tile in tiles]
        levels = pl.ds(pl.multiple_of(chunk * CHUNK, CHUNK), CHUNK)
        q_ref[levels] = q
        u_ref[levels] = u
        v_ref[levels] = v
        tend = tendency(q, u, v, row_terms, col_terms)
        tend_ref[levels] = tend
        for i, x in enumerate((tend, q)):
            top_ref[i, levels, 256:384] = x[:, 0, :]
            bot_ref[i, levels, 256:384] = x[:, 7, :]
        return carry

    lax.fori_loop(0, q_ref.shape[0] // CHUNK, body, 0)


def assemble_chunk(x, up, down):
    shape = x.shape
    row = iota(shape, 1)
    partner = jnp.where(
        row == 0,
        jnp.broadcast_to(up[:, None, :], shape),
        jnp.where(
            row == 7,
            jnp.broadcast_to(down[:, None, :], shape),
            jnp.where(row == 3, pltpu.roll(x, 7, 1), pltpu.roll(x, 1, 1)),
        ),
    )
    x = jnp.where((row % 4 == 0) | (row % 4 == 3), 0.5 * (x + partner), x)
    col = iota(shape, 2)
    partner = jnp.where(
        col % 4 == 3, pltpu.roll(x, shape[2] - 1, 2), pltpu.roll(x, 1, 2)
    )
    return jnp.where((col % 4 == 0) | (col % 4 == 3), 0.5 * (x + partner), x)


def join(main, strip):
    return jnp.concatenate([main, strip], axis=2)


def second_kernel(
    q_ref, u_ref, v_ref, tend_ref, q_strip, u_strip, v_strip, tend_strip, up_ref, down_ref,
    state_ref, smooth_ref, next_ref, top_ref, bot_ref,
):
    row_terms = derivative_terms((8, 128), 0)
    col_terms = derivative_terms((8, 128), 1)

    def body(chunk, carry):
        levels = pl.ds(pl.multiple_of(chunk * CHUNK, CHUNK), CHUNK)
        q = join(q_ref[levels], q_strip[levels])
        change = assemble_chunk(
            join(tend_ref[levels], tend_strip[levels]), up_ref[0, levels, :], down_ref[0, levels, :]
        )
        smooth = assemble_chunk(q, up_ref[1, levels, :], down_ref[1, levels, :])
        smooth_ref[levels] = smooth[:, :, 0:256]
        state = q + DT_DYN * change
        state_ref[levels] = state[:, :, 0:256]
        tend = tendency(
            state, join(u_ref[levels], u_strip[levels]), join(v_ref[levels], v_strip[levels]),
            row_terms, col_terms,
        )
        next_ref[levels] = tend
        put_rows(tend, levels, top_ref, bot_ref, 0)
        return carry

    lax.fori_loop(0, q_ref.shape[0] // CHUNK, body, 0)


def third_kernel(
    q_ref, state_ref, smooth_ref, tend_ref, up_ref, down_ref, down_map_ref,
    base_ref, cell_ref, near_ref, far_ref,
):
    cols = cell_ref.shape[0]
    half = cols // 2
    phase = iota((8, 256), 0) % 4
    row_weight = jnp.where((phase == 0) | (phase == 3), F32(WEIGHTS[0]), F32(WEIGHTS[1]))
    near_rows = jnp.where(iota((8, 256), 0) < 4, row_weight, 0.0)
    far_rows = row_weight - near_rows

    def body(chunk, carry):
        levels = pl.ds(pl.multiple_of(chunk * CHUNK, CHUNK), CHUNK)
        change = assemble_chunk(tend_ref[levels], up_ref[0, levels, :], down_ref[0, levels, :])
        moved = (state_ref[levels] + DT_DYN * change[:, :, 0:256]) - q_ref[levels]
        base_ref[levels] = smooth_ref[levels] + moved
        near_ref[levels, :] = jnp.sum(moved * near_rows[None], axis=1)
        far_ref[levels, :] = jnp.sum(moved * far_rows[None], axis=1)
        return carry

    lax.fori_loop(0, q_ref.shape[0] // CHUNK, body, 0)
    point = iota((256, cols), 0)
    element = iota((256, cols), 1)
    weight = jnp.where(
        (point % 4 == 0) | (point % 4 == 3), F32(WEIGHTS[0]), F32(WEIGHTS[1])
    ) * F32(0.25 / (DYN_STEPS * DT_DYN))
    near_cols = jnp.where(point // 4 == element, weight, 0.0)
    far_cols = jnp.where(point // 4 + half == element, weight, 0.0)
    means = jnp.dot(near_ref[...], near_cols, precision=HIGH, preferred_element_type=F32)
    means += jnp.dot(far_ref[...], far_cols, precision=HIGH, preferred_element_type=F32)
    forcing = jnp.dot(down_map_ref[...], means, precision=HIGH, preferred_element_type=F32)
    forcing = forcing.T.astype(BF16)
    cells = cell_ref.shape[1]
    spread = (iota((CRM_LEV, cells), 1) // CRM_X == iota((CRM_LEV, cells), 0)).astype(BF16)
    cell_ref[...] = DT_CRM * jnp.dot(forcing, spread, preferred_element_type=F32)


def crm_kernel(
    order_ref, count_ref, place_ref, drops_ref, cell_ref, slot_ref, coef_ref, growth_ref,
    final_ref, heat_ref, send_ref, state_ref, pair_ref, twice_ref, heat_cell_ref, echo_cell_ref,
):
    bins = drops_ref.shape[1]
    cells = drops_ref.shape[2]
    cols = drops_ref.shape[0]
    coef = coef_ref[...]
    growth = growth_ref[...]
    state_ref[...] = jnp.zeros(state_ref.shape, F32)
    mass = (iota((40, cells), 0) + 1).astype(F32) / F32(bins)

    def grow(k, which, zero):
        grown = state_ref[k] + growth * cell_ref[pl.ds(which, 1), :]
        for h in range(cells // 128):
            cut = slice(128 * h, 128 * h + 128)
            g = grown[0:32, cut]
            last = grown[32:40, cut]
            twice_ref[2 * k + h, 0:32, :] = g
            twice_ref[2 * k + h, 32:48, :] = g[0:16]
            for d in range(16):
                other = g if d % 8 == 0 else twice_ref[2 * k + h, pl.ds(zero + d, 32), :]
                if d == 8:
                    other = jnp.concatenate([g[8:], g[:8]], axis=0)
                pair_ref[k, 32 * d : 32 * d + 32, cut] = (g * other).astype(BF16)
            pair_ref[k, 512:528, cut] = (g[0:16] * g[16:32]).astype(BF16)
            pair_ref[k, 528:560, cut] = (g * last[0:1]).astype(BF16)
            tail = jnp.concatenate([last * last, jnp.zeros((8, 128), F32)], axis=0)
            pair_ref[k, 560:576, cut] = tail.astype(BF16)
        return grown

    def group(index, carry):
        base = index * GROUP
        which = [order_ref[base + k] for k in range(GROUP)]
        count = [count_ref[base + k] for k in range(GROUP)]
        for k in range(GROUP):
            state_ref[k, 0:bins, :] = drops_ref[which[k]].astype(F32)

        def step(s, c):
            for k in range(GROUP):
                grown = grow(k, which[k], place_ref[3])
                change = jnp.dot(coef, pair_ref[k], preferred_element_type=F32)
                moved = grown + DT_CRM * change[0:40]
                state_ref[k] = jnp.where(s < count[k], moved, state_ref[k])
            return c

        lax.fori_loop(0, count[0], step, 0)
        for k in range(GROUP):
            final = state_ref[k, 0:bins, :]
            initial = drops_ref[which[k]].astype(F32)
            final_ref[which[k]] = final.astype(BF16)
            weighted = mass[0:bins] * final
            heat = jnp.sum(mass[0:bins] * (final - initial), axis=0, keepdims=True)
            echo = jnp.sum(weighted * weighted, axis=0, keepdims=True)
            heat_cell_ref[pl.ds(which[k], 1), :] = heat
            echo_cell_ref[pl.ds(which[k], 1), :] = echo
        return carry

    lax.fori_loop(0, cols // GROUP, group, 0)
    means = jnp.where(
        iota((CRM_LEV, cells), 1) // CRM_X == iota((CRM_LEV, cells), 0), F32(1.0 / CRM_X), 0.0
    )
    contract = (((1,), (1,)), ((), ()))
    heat = lax.dot_general(
        means, heat_cell_ref[...], contract, precision=HIGH, preferred_element_type=F32
    )
    heat = heat.astype(BF16).astype(F32)
    heat_ref[...] = heat
    echo = lax.dot_general(
        means, echo_cell_ref[...], contract, precision=HIGH, preferred_element_type=F32
    )
    echo = jnp.log(1.0 + echo)

    devices = send_ref.shape[0]
    slots = 2 * cols
    capacity = slots // devices
    onehot = (slot_ref[...] == iota((slots, cols), 0)).astype(F32)
    packed = lax.dot_general(echo, onehot, contract, precision=HIGH, preferred_element_type=F32)
    coarse = packed.astype(BF16).astype(F32)
    rest = packed - coarse
    middle = rest.astype(BF16).astype(F32)
    pieces = (coarse, middle, rest - middle)
    lane = iota((CRM_LEV, 128), 1)
    near = heat
    far = pltpu.roll(heat, 64, 1)
    sides = jnp.where(
        lane == 1, pltpu.roll(heat, 65, 1), jnp.where(lane == 62, pltpu.roll(heat, 63, 1), heat)
    )
    n_gcm = place_ref[1]
    n_crm = place_ref[2]
    for d in range(devices):
        away = d // n_crm - place_ref[0]
        below = (away == 1) | (away == 1 - n_gcm)
        above = (away == -1) | (away == n_gcm - 1)
        block = jnp.where(below, far, jnp.where(above, near, sides))
        tile, offset = divmod(d * capacity, 128)
        for i, piece in enumerate(pieces):
            moved = pltpu.roll(
                piece[:, 128 * tile : 128 * tile + 128], (64 + i * capacity - offset) % 128, 1
            )
            start = 64 + i * capacity
            block = jnp.where((lane >= start) & (lane < start + capacity), moved, block)
        send_ref[d] = block.astype(BF16)


def last_kernel(around_ref, base_ref, own_ref, got_ref, up_map_ref, out_ref, power_ref, *back_refs):
    cols = own_ref.shape[1]
    half = cols // 2
    element = iota((cols, 256), 0)
    col = iota((cols, 256), 1)
    phase = col % 4
    edge = (phase == 0) | (phase == 3)
    other = jnp.where(phase == 0, col // 4 - 1, col // 4 + 1)

    def spread(centre, start, west, west_lane, east, east_lane):
        inside = jnp.where(element == col // 4 + start, jnp.where(edge, 0.5, 1.0), 0.0)
        beside = edge & (element == other + start) & (other >= 0) & (other < half)
        middle = jnp.where(beside, 0.5, inside).astype(BF16)
        from_west = jnp.where((col == 0) & (element == west_lane), 0.5, 0.0).astype(BF16)
        from_east = jnp.where((col == 255) & (element == east_lane), 0.5, 0.0).astype(BF16)
        total = jnp.dot(centre, middle, preferred_element_type=F32)
        total += jnp.dot(west, from_west, preferred_element_type=F32)
        total += jnp.dot(east, from_east, preferred_element_type=F32)
        return total

    own = own_ref[...].astype(BF16)
    up, down, left, right, up_left, up_right, down_left, down_right = [
        got_ref[around_ref[i]] for i in range(8)
    ]
    above = spread(up, 0, up_left, half - 1, up_right, 0)
    near = spread(own, 0, left, half - 1, right, 0)
    far = spread(own, half, left, half - 2, right, 1)
    below = spread(down, 0, down_left, half - 1, down_right, 0)
    parts = (
        0.5 * (above + near), near, 0.5 * (near + far), far, 0.5 * (far + below),
    )
    up_map = up_map_ref[...]
    for part, ref in zip(parts, back_refs):
        ref[...] = DT_PHYS * jnp.dot(up_map, part, precision=HIGH, preferred_element_type=F32)

    devices = got_ref.shape[0]
    slots = power_ref.shape[1]
    capacity = slots // devices
    lane = iota((CRM_LEV, 128), 1)
    tiles = [jnp.zeros((CRM_LEV, 128), F32) for _ in range(slots // 128)]
    for d in range(devices):
        block = got_ref[d].astype(F32)
        fine = pltpu.roll(block, 128 - 2 * capacity, 1) + pltpu.roll(block, 128 - capacity, 1)
        tile, offset = divmod(d * capacity, 128)
        moved = pltpu.roll(block + fine, (offset - 64) % 128, 1)
        tiles[tile] = jnp.where((lane >= offset) & (lane < offset + capacity), moved, tiles[tile])
    power_ref[...] = jnp.concatenate(tiles, axis=1)

    def body(chunk, carry):
        levels = pl.ds(pl.multiple_of(chunk * CHUNK, CHUNK), CHUNK)
        shape = (CHUNK, 8, 256)
        row = iota(shape, 1)
        wide = [jnp.broadcast_to(ref[levels, :][:, None, :], shape) for ref in back_refs]
        back = jnp.where(
            row == 0,
            wide[0],
            jnp.where(
                row < 3,
                wide[1],
                jnp.where(row < 5, wide[2], jnp.where(row < 7, wide[3], wide[4])),
            ),
        )
        out_ref[levels] = base_ref[levels] + back
        return carry

    lax.fori_loop(0, base_ref.shape[0] // CHUNK, body, 0)


def call(kernel, outs, args, scratch=(), sems=(), flops=10_000_000):
    spaces = {
        "s": pl.BlockSpec(memory_space=pltpu.SMEM),
        "v": pl.BlockSpec(memory_space=pltpu.VMEM),
        "h": pl.BlockSpec(memory_space=pl.ANY),
    }
    return pl.pallas_call(
        kernel,
        out_shape=[jax.ShapeDtypeStruct(s, t) for s, t in outs],
        in_specs=[spaces[kind] for kind, _ in args],
        out_specs=[spaces["v"]] * len(outs),
        scratch_shapes=[pltpu.VMEM(s, t) for s, t in scratch] + list(sems),
        compiler_params=pltpu.CompilerParams(vmem_limit_bytes=40 * MIB),
        cost_estimate=pl.CostEstimate(flops=flops, bytes_accessed=4_000_000, transcendentals=0),
    )(*[value for _, value in args])


def v(*values):
    return [("v", value) for value in values]


def shift(value, rows, cols):
    n_gcm = lax.axis_size("gcm")
    n_crm = lax.axis_size("crm")
    pairs = []
    for g in range(n_gcm):
        for c in range(n_crm):
            target = ((g + rows) % n_gcm) * n_crm + (c + cols) % n_crm
            pairs.append((g * n_crm + c, target))
    return lax.ppermute(value, ("gcm", "crm"), pairs)


def pair_table(bins):
    table = np.zeros((bins * bins, 576), np.float32)

    def put(column, i, j):
        table[i * bins + j, column] = 1.0
        table[j * bins + i, column] = 1.0

    for d in range(16):
        for b in range(32):
            put(32 * d + b, b, (b + d) % 32)
    for b in range(16):
        put(512 + b, b, b + 16)
    for b in range(32):
        put(528 + b, b, 32)
    put(560, 32, 32)
    return table


def rank_order(counts):
    total = counts.shape[0]
    index = jnp.arange(total, dtype=jnp.int32)
    ahead = (counts[None, :] > counts[:, None]) | (
        (counts[None, :] == counts[:, None]) & (index[None, :] < index[:, None])
    )
    rank = jnp.sum(ahead.astype(jnp.int32), axis=1)
    match = rank[None, :] == index[:, None]
    order = jnp.sum(jnp.where(match, index[None, :], 0), axis=1)
    ordered = jnp.sum(jnp.where(match, counts[None, :], 0), axis=1)
    return order, ordered


def shards(tracer, wind_x, wind_y, drops, owner, counts, collision, growth):
    devices = lax.axis_size("gcm") * lax.axis_size("crm")
    levels, row_count, col_count = tracer.shape
    col_total, bins, cells = drops.shape
    field = (tracer.shape, F32)
    strip = ((levels, row_count, 128), F32)
    rows = ((2, levels, col_count), F32)
    wide = col_count + 128
    down_map, up_map = level_tables(levels, CRM_LEV)

    to_right, to_left = call(
        pack_kernel,
        [((levels // 4, 8, 128), F32)] * 2,
        [("h", tracer), ("h", wind_x), ("h", wind_y)],
        [field] * 3,
        [pltpu.SemaphoreType.DMA((3,))],
    )
    from_left = shift(to_right, 0, 1)
    from_right = shift(to_left, 0, -1)
    tend, top, bot = call(first_kernel, [field, rows, rows], v(tracer, wind_x, wind_y))
    q_strip, u_strip, v_strip, tend_strip, top, bot = call(
        strip_kernel,
        [strip] * 4 + [((2, levels, wide), F32)] * 2,
        v(from_left, from_right, top, bot),
    )
    state, smooth, tend, top, bot = call(
        second_kernel,
        [field, field, ((levels, row_count, wide), F32)] + [((1, levels, wide), F32)] * 2,
        v(tracer, wind_x, wind_y, tend, q_strip, u_strip, v_strip, tend_strip)
        + v(shift(bot, 1, 0), shift(top, -1, 0)),
    )
    base, cell_forcing = call(
        third_kernel,
        [field, ((col_total, cells), F32)],
        v(tracer, state, smooth, tend, shift(bot, 1, 0), shift(top, -1, 0))
        + v(jnp.asarray(down_map, F32)),
        [((levels, col_count), F32), ((levels, col_count), F32)],
    )

    capacity = 2 * col_total // devices
    owners = owner[:, 0]
    index = jnp.arange(col_total, dtype=jnp.int32)
    same = (owners[:, None] == owners[None, :]) & (index[:, None] < index[None, :])
    slot_of = owners * capacity + jnp.sum(same.astype(jnp.int32), axis=0)
    order, ordered = rank_order(counts)
    table = jnp.asarray(pair_table(bins), BF16)
    coef = jnp.dot(collision, table, preferred_element_type=F32)
    coef = jnp.pad(coef.astype(BF16), ((0, 48 - bins), (0, 0)))
    growth_rows = jnp.broadcast_to(jnp.pad(growth, (0, 40 - bins))[:, None], (40, cells))
    n_gcm = lax.axis_size("gcm")
    n_crm = lax.axis_size("crm")
    g = lax.axis_index("gcm").astype(jnp.int32)
    c = lax.axis_index("crm").astype(jnp.int32)
    place = jnp.stack([g, jnp.int32(n_gcm), jnp.int32(n_crm), jnp.int32(0)])

    final, heat, send = call(
        crm_kernel,
        [((col_total, bins, cells), BF16), ((CRM_LEV, col_total), F32),
         ((devices, CRM_LEV, 128), BF16)],
        [("s", order), ("s", ordered), ("s", place)]
        + v(drops, cell_forcing, slot_of[None, :], coef, growth_rows),
        [((GROUP, 40, cells), F32), ((GROUP, 576, cells), BF16),
         ((2 * GROUP, 48, 128), F32),
         ((col_total, cells), F32), ((col_total, cells), F32)],
        flops=10_000_000_000,
    )
    got = lax.all_to_all(send, ("gcm", "crm"), split_axis=0, concat_axis=0, tiled=True)
    up = (g + n_gcm - 1) % n_gcm * n_crm
    same_row = g * n_crm
    down = (g + 1) % n_gcm * n_crm
    west = (c + n_crm - 1) % n_crm
    east = (c + 1) % n_crm
    around = jnp.stack(
        [up + c, down + c, same_row + west, same_row + east,
         up + west, up + east, down + west, down + east]
    )
    tracer_next, power = call(
        last_kernel,
        [field, ((CRM_LEV, devices * capacity), F32)],
        [("s", around)] + v(base, heat, got, jnp.asarray(up_map, F32)),
        [((levels, col_count), F32)] * 5,
    )
    return (tracer_next, final, power)


def solution(mesh):
    return jax.shard_map(
        shards,
        mesh=mesh,
        in_specs=(
            P(None, "gcm", "crm"),
            P(None, "gcm", "crm"),
            P(None, "gcm", "crm"),
            P(("gcm", "crm"), None, None),
            P(("gcm", "crm"), None),
            P(("gcm", "crm")),
            P(),
            P(),
        ),
        out_specs=(P(None, "gcm", "crm"), P(("gcm", "crm"), None, None), P(None, ("gcm", "crm"))),
        check_vma=False,
    )
```

```python
import functools

import jax
import jax.numpy as jnp
import numpy as np
from jax import lax
from jax.experimental import pallas as pl
from jax.experimental.pallas import tpu as pltpu
from jax.sharding import PartitionSpec as P

CRM_X = 16
CRM_LEV = 16
DYN_STEPS = 2

DT_DYN = 0.04
DT_CRM = 0.05
DT_PHYS = 0.5
HIGH = lax.Precision.HIGHEST
F32 = jnp.float32
BF16 = jnp.bfloat16
GROUP = 16
CHUNK = 8
MIB = 1024 * 1024


def gll_tables():
    inv_root = 1.0 / np.sqrt(5.0)
    gll_nodes = np.array([-1.0, -inv_root, inv_root, 1.0])
    weights = np.array([1.0, 5.0, 5.0, 1.0]) / 6.0
    legendre = (5.0 * gll_nodes**3 - 3.0 * gll_nodes) / 2.0
    derivative = np.zeros((4, 4))
    for i in range(4):
        for j in range(4):
            if i != j:
                derivative[i, j] = legendre[i] / (legendre[j] * (gll_nodes[i] - gll_nodes[j]))
    derivative[0, 0] = -3.0
    derivative[3, 3] = 3.0
    return (2.0 * derivative, weights)


def level_tables(levels, crm_levels):
    spacing = levels / crm_levels
    centres = (np.arange(crm_levels) + 0.5) * spacing - 0.5
    hats = np.maximum(0.0, 1.0 - np.abs(np.arange(levels)[None, :] - centres[:, None]) / spacing)
    down_map = hats / hats.sum(axis=1, keepdims=True)
    up_map = hats.T / hats.T.sum(axis=1, keepdims=True)
    return (down_map, up_map)


DERIV, WEIGHTS = gll_tables()


def iota(shape, axis):
    return lax.broadcasted_iota(jnp.int32, shape, axis)


def derivative_terms(shape, axis):
    phase = iota(shape, axis) % 4
    terms = []
    for shift in range(-3, 4):
        value = jnp.zeros(shape, F32)
        for i in range(4):
            if 0 <= i + shift < 4:
                value = jnp.where(phase == i, F32(DERIV[i, i + shift]), value)
        terms.append((shift, value))
    return terms


def along(x, terms, axis):
    size = x.shape[axis]
    total = None
    for shift, value in terms:
        moved = x if shift == 0 else pltpu.roll(x, (-shift) % size, axis)
        part = value[None] * moved
        total = part if total is None else total + part
    return total


def tendency(x, u, v, row_terms, col_terms):
    halves = []
    for h in range(x.shape[2] // 128):
        cut = slice(128 * h, 128 * h + 128)
        q = x[:, :, cut]
        grad_x = along(q, row_terms, 1)
        grad_y = along(q, col_terms, 2)
        halves.append(-(u[:, :, cut] * grad_x + v[:, :, cut] * grad_y))
    return jnp.concatenate(halves, axis=2)


def pack_kernel(q_hbm, u_hbm, v_hbm, right_ref, left_ref, q_ref, u_ref, v_ref, sems):
    copies = []
    for i, (src, dst) in enumerate(((q_hbm, q_ref), (u_hbm, u_ref), (v_hbm, v_ref))):
        copies.append(pltpu.make_async_copy(src, dst, sems.at[i]))
    for copy in copies:
        copy.start()
    for copy in copies:
        copy.wait()
    lane = iota((8, 128), 1)

    def body(group, carry):
        right = jnp.zeros((8, 128), F32)
        left = jnp.zeros((8, 128), F32)
        for j in range(4):
            for f, ref in enumerate((q_ref, u_ref, v_ref)):
                start = 32 * j + 8 * f
                here = (lane >= start) & (lane < start + 8)
                x = ref[group * 4 + j]
                right = jnp.where(here, pltpu.roll(x[:, 128:256], (start - 120) % 128, 1), right)
                first = x[:, 0:128]
                if start:
                    first = pltpu.roll(first, start, 1)
                left = jnp.where(here, first, left)
        right_ref[group] = right
        left_ref[group] = left
        return carry

    lax.fori_loop(0, right_ref.shape[0], body, 0)


def put_rows(x, levels, top_ref, bot_ref, i):
    top_ref[i, levels, :] = x[:, 0, :]
    bot_ref[i, levels, :] = x[:, 7, :]


def first_kernel(q_ref, u_ref, v_ref, tend_ref, top_ref, bot_ref):
    row_terms = derivative_terms((8, 128), 0)
    col_terms = derivative_terms((8, 128), 1)

    def body(chunk, carry):
        levels = pl.ds(pl.multiple_of(chunk * CHUNK, CHUNK), CHUNK)
        q = q_ref[levels]
        tend = tendency(q, u_ref[levels], v_ref[levels], row_terms, col_terms)
        tend_ref[levels] = tend
        put_rows(tend, levels, top_ref, bot_ref, 0)
        put_rows(q, levels, top_ref, bot_ref, 1)
        return carry

    lax.fori_loop(0, q_ref.shape[0] // CHUNK, body, 0)


def strip_kernel(
    left_ref, right_ref, top_main, bot_main,
    q_ref, u_ref, v_ref, tend_ref, top_ref, bot_ref,
):
    row_terms = derivative_terms((8, 128), 0)
    col_terms = derivative_terms((8, 128), 1)
    lane = iota((8, 128), 1)
    top_ref[:, :, 0:256] = top_main[...]
    bot_ref[:, :, 0:256] = bot_main[...]

    def body(chunk, carry):
        tiles = [[], [], []]
        for half in range(CHUNK // 4):
            west = left_ref[chunk * (CHUNK // 4) + half]
            east = right_ref[chunk * (CHUNK // 4) + half]
            for j in range(4):
                for f in range(3):
                    start = 32 * j + 8 * f
                    a = pltpu.roll(east, 128 - start, 1) if start else east
                    b = pltpu.roll(west, (120 - start) % 128, 1)
                    tiles[f].append(jnp.where(lane < 8, a, jnp.where(lane >= 120, b, 0.0)))
        q, u, v = [jnp.stack(tile, axis=0) for tile in tiles]
        levels = pl.ds(pl.multiple_of(chunk * CHUNK, CHUNK), CHUNK)
        q_ref[levels] = q
        u_ref[levels] = u
        v_ref[levels] = v
        tend = tendency(q, u, v, row_terms, col_terms)
        tend_ref[levels] = tend
        for i, x in enumerate((tend, q)):
            top_ref[i, levels, 256:384] = x[:, 0, :]
            bot_ref[i, levels, 256:384] = x[:, 7, :]
        return carry

    lax.fori_loop(0, q_ref.shape[0] // CHUNK, body, 0)


def assemble_chunk(x, up, down):
    shape = x.shape
    row = iota(shape, 1)
    partner = jnp.where(
        row == 0,
        jnp.broadcast_to(up[:, None, :], shape),
        jnp.where(
            row == 7,
            jnp.broadcast_to(down[:, None, :], shape),
            jnp.where(row == 3, pltpu.roll(x, 7, 1), pltpu.roll(x, 1, 1)),
        ),
    )
    x = jnp.where((row % 4 == 0) | (row % 4 == 3), 0.5 * (x + partner), x)
    col = iota(shape, 2)
    partner = jnp.where(
        col % 4 == 3, pltpu.roll(x, shape[2] - 1, 2), pltpu.roll(x, 1, 2)
    )
    return jnp.where((col % 4 == 0) | (col % 4 == 3), 0.5 * (x + partner), x)


def join(main, strip):
    return jnp.concatenate([main, strip], axis=2)


def second_kernel(
    q_ref, u_ref, v_ref, tend_ref, q_strip, u_strip, v_strip, tend_strip, up_ref, down_ref,
    state_ref, smooth_ref, next_ref, top_ref, bot_ref,
):
    row_terms = derivative_terms((8, 128), 0)
    col_terms = derivative_terms((8, 128), 1)

    def body(chunk, carry):
        levels = pl.ds(pl.multiple_of(chunk * CHUNK, CHUNK), CHUNK)
        q = join(q_ref[levels], q_strip[levels])
        change = assemble_chunk(
            join(tend_ref[levels], tend_strip[levels]), up_ref[0, levels, :], down_ref[0, levels, :]
        )
        smooth = assemble_chunk(q, up_ref[1, levels, :], down_ref[1, levels, :])
        smooth_ref[levels] = smooth[:, :, 0:256]
        state = q + DT_DYN * change
        state_ref[levels] = state[:, :, 0:256]
        tend = tendency(
            state, join(u_ref[levels], u_strip[levels]), join(v_ref[levels], v_strip[levels]),
            row_terms, col_terms,
        )
        next_ref[levels] = tend
        put_rows(tend, levels, top_ref, bot_ref, 0)
        return carry

    lax.fori_loop(0, q_ref.shape[0] // CHUNK, body, 0)


def third_kernel(
    q_ref, state_ref, smooth_ref, tend_ref, up_ref, down_ref, down_map_ref,
    base_ref, cell_ref, near_ref, far_ref,
):
    cols = cell_ref.shape[0]
    half = cols // 2
    phase = iota((8, 256), 0) % 4
    row_weight = jnp.where((phase == 0) | (phase == 3), F32(WEIGHTS[0]), F32(WEIGHTS[1]))
    near_rows = jnp.where(iota((8, 256), 0) < 4, row_weight, 0.0)
    far_rows = row_weight - near_rows

    def body(chunk, carry):
        levels = pl.ds(pl.multiple_of(chunk * CHUNK, CHUNK), CHUNK)
        change = assemble_chunk(tend_ref[levels], up_ref[0, levels, :], down_ref[0, levels, :])
        moved = (state_ref[levels] + DT_DYN * change[:, :, 0:256]) - q_ref[levels]
        base_ref[levels] = smooth_ref[levels] + moved
        near_ref[levels, :] = jnp.sum(moved * near_rows[None], axis=1)
        far_ref[levels, :] = jnp.sum(moved * far_rows[None], axis=1)
        return carry

    lax.fori_loop(0, q_ref.shape[0] // CHUNK, body, 0)
    point = iota((256, cols), 0)
    element = iota((256, cols), 1)
    weight = jnp.where(
        (point % 4 == 0) | (point % 4 == 3), F32(WEIGHTS[0]), F32(WEIGHTS[1])
    ) * F32(0.25 / (DYN_STEPS * DT_DYN))
    near_cols = jnp.where(point // 4 == element, weight, 0.0)
    far_cols = jnp.where(point // 4 + half == element, weight, 0.0)
    means = jnp.dot(near_ref[...], near_cols, precision=HIGH, preferred_element_type=F32)
    means += jnp.dot(far_ref[...], far_cols, precision=HIGH, preferred_element_type=F32)
    forcing = jnp.dot(down_map_ref[...], means, precision=HIGH, preferred_element_type=F32)
    forcing = forcing.T.astype(BF16)
    cells = cell_ref.shape[1]
    spread = (iota((CRM_LEV, cells), 1) // CRM_X == iota((CRM_LEV, cells), 0)).astype(BF16)
    cell_ref[...] = DT_CRM * jnp.dot(forcing, spread, preferred_element_type=F32)


def crm_kernel(
    order_ref, count_ref, place_ref, drops_ref, cell_ref, slot_ref, coef_ref, tail_coef_ref,
    growth_ref,
    final_ref, heat_ref, send_ref, state_ref, pair_ref, tail_ref, twice_ref,
    heat_cell_ref, echo_cell_ref,
):
    bins = drops_ref.shape[1]
    cells = drops_ref.shape[2]
    cols = drops_ref.shape[0]
    coef = coef_ref[...]
    tail_coef = tail_coef_ref[...]
    growth = growth_ref[...]
    state_ref[...] = jnp.zeros(state_ref.shape, F32)
    mass = (iota((40, cells), 0) + 1).astype(F32) / F32(bins)

    def grow(k, which, zero):
        grown = state_ref[k] + growth * cell_ref[pl.ds(which, 1), :]
        for h in range(cells // 128):
            cut = slice(128 * h, 128 * h + 128)
            g = grown[0:32, cut]
            last = grown[32:40, cut]
            twice_ref[2 * k + h, 0:32, :] = g
            twice_ref[2 * k + h, 32:48, :] = g[0:16]
            for d in range(16):
                other = g if d % 8 == 0 else twice_ref[2 * k + h, pl.ds(zero + d, 32), :]
                if d == 8:
                    other = jnp.concatenate([g[8:], g[:8]], axis=0)
                pair_ref[k, 32 * d : 32 * d + 32, cut] = (g * other).astype(BF16)
            at = 64 * (k % 4)
            tail_ref[k // 4, at : at + 16, cut] = (g[0:16] * g[16:32]).astype(BF16)
            tail_ref[k // 4, at + 16 : at + 48, cut] = (g * last[0:1]).astype(BF16)
            tail = jnp.concatenate([last * last, jnp.zeros((8, 128), F32)], axis=0)
            tail_ref[k // 4, at + 48 : at + 64, cut] = tail.astype(BF16)
        return grown

    def group(index, carry):
        base = index * GROUP
        which = [order_ref[base + k] for k in range(GROUP)]
        count = [count_ref[base + k] for k in range(GROUP)]
        for k in range(GROUP):
            state_ref[k, 0:bins, :] = drops_ref[which[k]].astype(F32)

        def step(s, c):
            for q in range(GROUP // 4):
                grown = [grow(4 * q + k, which[4 * q + k], place_ref[3]) for k in range(4)]
                tails = jnp.dot(tail_coef, tail_ref[q], preferred_element_type=F32)
                for k in range(4):
                    slot = 4 * q + k
                    change = jnp.dot(coef, pair_ref[slot], preferred_element_type=F32)
                    change = change + tails[80 * k : 80 * k + 80]
                    moved = grown[k] + (change[0:40] + change[40:80])
                    state_ref[slot] = jnp.where(s < count[slot], moved, state_ref[slot])
            return c

        lax.fori_loop(0, count[0], step, 0)
        for k in range(GROUP):
            final = state_ref[k, 0:bins, :]
            initial = drops_ref[which[k]].astype(F32)
            final_ref[which[k]] = final.astype(BF16)
            weighted = mass[0:bins] * final
            heat = jnp.sum(mass[0:bins] * (final - initial), axis=0, keepdims=True)
            echo = jnp.sum(weighted * weighted, axis=0, keepdims=True)
            heat_cell_ref[pl.ds(which[k], 1), :] = heat
            echo_cell_ref[pl.ds(which[k], 1), :] = echo
        return carry

    lax.fori_loop(0, cols // GROUP, group, 0)
    means = jnp.where(
        iota((CRM_LEV, cells), 1) // CRM_X == iota((CRM_LEV, cells), 0), F32(1.0 / CRM_X), 0.0
    )
    contract = (((1,), (1,)), ((), ()))
    heat = lax.dot_general(
        means, heat_cell_ref[...], contract, precision=HIGH, preferred_element_type=F32
    )
    heat = heat.astype(BF16).astype(F32)
    heat_ref[...] = heat
    echo = lax.dot_general(
        means, echo_cell_ref[...], contract, precision=HIGH, preferred_element_type=F32
    )
    echo = jnp.log(1.0 + echo)

    devices = send_ref.shape[0]
    slots = 2 * cols
    capacity = slots // devices
    onehot = (slot_ref[...] == iota((slots, cols), 0)).astype(F32)
    packed = lax.dot_general(echo, onehot, contract, precision=HIGH, preferred_element_type=F32)
    coarse = packed.astype(BF16).astype(F32)
    rest = packed - coarse
    middle = rest.astype(BF16).astype(F32)
    pieces = (coarse, middle, rest - middle)
    lane = iota((CRM_LEV, 128), 1)
    near = heat
    far = pltpu.roll(heat, 64, 1)
    sides = jnp.where(
        lane == 1, pltpu.roll(heat, 65, 1), jnp.where(lane == 62, pltpu.roll(heat, 63, 1), heat)
    )
    n_gcm = place_ref[1]
    n_crm = place_ref[2]
    for d in range(devices):
        away = d // n_crm - place_ref[0]
        below = (away == 1) | (away == 1 - n_gcm)
        above = (away == -1) | (away == n_gcm - 1)
        block = jnp.where(below, far, jnp.where(above, near, sides))
        tile, offset = divmod(d * capacity, 128)
        for i, piece in enumerate(pieces):
            moved = pltpu.roll(
                piece[:, 128 * tile : 128 * tile + 128], (64 + i * capacity - offset) % 128, 1
            )
            start = 64 + i * capacity
            block = jnp.where((lane >= start) & (lane < start + capacity), moved, block)
        send_ref[d] = block.astype(BF16)


def last_kernel(around_ref, base_ref, own_ref, got_ref, up_map_ref, out_ref, power_ref, *back_refs):
    cols = own_ref.shape[1]
    half = cols // 2
    element = iota((cols, 256), 0)
    col = iota((cols, 256), 1)
    phase = col % 4
    edge = (phase == 0) | (phase == 3)
    other = jnp.where(phase == 0, col // 4 - 1, col // 4 + 1)

    def spread(centre, start, west, west_lane, east, east_lane):
        inside = jnp.where(element == col // 4 + start, jnp.where(edge, 0.5, 1.0), 0.0)
        beside = edge & (element == other + start) & (other >= 0) & (other < half)
        middle = jnp.where(beside, 0.5, inside).astype(BF16)
        from_west = jnp.where((col == 0) & (element == west_lane), 0.5, 0.0).astype(BF16)
        from_east = jnp.where((col == 255) & (element == east_lane), 0.5, 0.0).astype(BF16)
        total = jnp.dot(centre, middle, preferred_element_type=F32)
        total += jnp.dot(west, from_west, preferred_element_type=F32)
        total += jnp.dot(east, from_east, preferred_element_type=F32)
        return total

    own = own_ref[...].astype(BF16)
    up, down, left, right, up_left, up_right, down_left, down_right = [
        got_ref[around_ref[i]] for i in range(8)
    ]
    above = spread(up, 0, up_left, half - 1, up_right, 0)
    near = spread(own, 0, left, half - 1, right, 0)
    far = spread(own, half, left, half - 2, right, 1)
    below = spread(down, 0, down_left, half - 1, down_right, 0)
    parts = (
        0.5 * (above + near), near, 0.5 * (near + far), far, 0.5 * (far + below),
    )
    up_map = up_map_ref[...]
    for part, ref in zip(parts, back_refs):
        ref[...] = DT_PHYS * jnp.dot(up_map, part, precision=HIGH, preferred_element_type=F32)

    devices = got_ref.shape[0]
    slots = power_ref.shape[1]
    capacity = slots // devices
    lane = iota((CRM_LEV, 128), 1)
    tiles = [jnp.zeros((CRM_LEV, 128), F32) for _ in range(slots // 128)]
    for d in range(devices):
        block = got_ref[d].astype(F32)
        fine = pltpu.roll(block, 128 - 2 * capacity, 1) + pltpu.roll(block, 128 - capacity, 1)
        tile, offset = divmod(d * capacity, 128)
        moved = pltpu.roll(block + fine, (offset - 64) % 128, 1)
        tiles[tile] = jnp.where((lane >= offset) & (lane < offset + capacity), moved, tiles[tile])
    power_ref[...] = jnp.concatenate(tiles, axis=1)

    def body(chunk, carry):
        levels = pl.ds(pl.multiple_of(chunk * CHUNK, CHUNK), CHUNK)
        shape = (CHUNK, 8, 256)
        row = iota(shape, 1)
        wide = [jnp.broadcast_to(ref[levels, :][:, None, :], shape) for ref in back_refs]
        back = jnp.where(
            row == 0,
            wide[0],
            jnp.where(
                row < 3,
                wide[1],
                jnp.where(row < 5, wide[2], jnp.where(row < 7, wide[3], wide[4])),
            ),
        )
        out_ref[levels] = base_ref[levels] + back
        return carry

    lax.fori_loop(0, base_ref.shape[0] // CHUNK, body, 0)


def call(kernel, outs, args, scratch=(), sems=(), flops=10_000_000):
    spaces = {
        "s": pl.BlockSpec(memory_space=pltpu.SMEM),
        "v": pl.BlockSpec(memory_space=pltpu.VMEM),
        "h": pl.BlockSpec(memory_space=pl.ANY),
    }
    return pl.pallas_call(
        kernel,
        out_shape=[jax.ShapeDtypeStruct(s, t) for s, t in outs],
        in_specs=[spaces[kind] for kind, _ in args],
        out_specs=[spaces["v"]] * len(outs),
        scratch_shapes=[pltpu.VMEM(s, t) for s, t in scratch] + list(sems),
        compiler_params=pltpu.CompilerParams(vmem_limit_bytes=40 * MIB),
        cost_estimate=pl.CostEstimate(flops=flops, bytes_accessed=4_000_000, transcendentals=0),
    )(*[value for _, value in args])


def v(*values):
    return [("v", value) for value in values]


def shift(value, rows, cols):
    n_gcm = lax.axis_size("gcm")
    n_crm = lax.axis_size("crm")
    pairs = []
    for g in range(n_gcm):
        for c in range(n_crm):
            target = ((g + rows) % n_gcm) * n_crm + (c + cols) % n_crm
            pairs.append((g * n_crm + c, target))
    return lax.ppermute(value, ("gcm", "crm"), pairs)


def pair_table(bins):
    table = np.zeros((bins * bins, 576), np.float32)

    def put(column, i, j):
        table[i * bins + j, column] = 1.0
        table[j * bins + i, column] = 1.0

    for d in range(16):
        for b in range(32):
            put(32 * d + b, b, (b + d) % 32)
    for b in range(16):
        put(512 + b, b, b + 16)
    for b in range(32):
        put(528 + b, b, 32)
    put(560, 32, 32)
    return table


def rank_order(counts):
    total = counts.shape[0]
    index = jnp.arange(total, dtype=jnp.int32)
    ahead = (counts[None, :] > counts[:, None]) | (
        (counts[None, :] == counts[:, None]) & (index[None, :] < index[:, None])
    )
    rank = jnp.sum(ahead.astype(jnp.int32), axis=1)
    match = rank[None, :] == index[:, None]
    order = jnp.sum(jnp.where(match, index[None, :], 0), axis=1)
    ordered = jnp.sum(jnp.where(match, counts[None, :], 0), axis=1)
    return order, ordered


def shards(tracer, wind_x, wind_y, drops, owner, counts, collision, growth):
    devices = lax.axis_size("gcm") * lax.axis_size("crm")
    levels, row_count, col_count = tracer.shape
    col_total, bins, cells = drops.shape
    field = (tracer.shape, F32)
    strip = ((levels, row_count, 128), F32)
    rows = ((2, levels, col_count), F32)
    wide = col_count + 128
    down_map, up_map = level_tables(levels, CRM_LEV)

    to_right, to_left = call(
        pack_kernel,
        [((levels // 4, 8, 128), F32)] * 2,
        [("h", tracer), ("h", wind_x), ("h", wind_y)],
        [field] * 3,
        [pltpu.SemaphoreType.DMA((3,))],
    )
    from_left = shift(to_right, 0, 1)
    from_right = shift(to_left, 0, -1)
    tend, top, bot = call(first_kernel, [field, rows, rows], v(tracer, wind_x, wind_y))
    q_strip, u_strip, v_strip, tend_strip, top, bot = call(
        strip_kernel,
        [strip] * 4 + [((2, levels, wide), F32)] * 2,
        v(from_left, from_right, top, bot),
    )
    state, smooth, tend, top, bot = call(
        second_kernel,
        [field, field, ((levels, row_count, wide), F32)] + [((1, levels, wide), F32)] * 2,
        v(tracer, wind_x, wind_y, tend, q_strip, u_strip, v_strip, tend_strip)
        + v(shift(bot, 1, 0), shift(top, -1, 0)),
    )
    base, cell_forcing = call(
        third_kernel,
        [field, ((col_total, cells), F32)],
        v(tracer, state, smooth, tend, shift(bot, 1, 0), shift(top, -1, 0))
        + v(jnp.asarray(down_map, F32)),
        [((levels, col_count), F32), ((levels, col_count), F32)],
    )

    capacity = 2 * col_total // devices
    owners = owner[:, 0]
    index = jnp.arange(col_total, dtype=jnp.int32)
    same = (owners[:, None] == owners[None, :]) & (index[:, None] < index[None, :])
    slot_of = owners * capacity + jnp.sum(same.astype(jnp.int32), axis=0)
    order, ordered = rank_order(counts)
    table = jnp.asarray(pair_table(bins), BF16)
    coef = DT_CRM * jnp.dot(collision, table, preferred_element_type=F32)
    coarse = lax.reduce_precision(coef, 8, 7)
    fine = coef - coarse
    pad = ((0, 40 - bins), (0, 0))
    coef = jnp.concatenate([jnp.pad(coarse, pad), jnp.pad(fine, pad)], axis=0).astype(BF16)
    tail = coef[:, 512:]
    tail_coef = jnp.concatenate(
        [jnp.pad(tail, ((0, 0), (64 * k, 192 - 64 * k))) for k in range(4)], axis=0
    )
    growth_rows = jnp.broadcast_to(jnp.pad(growth, (0, 40 - bins))[:, None], (40, cells))
    n_gcm = lax.axis_size("gcm")
    n_crm = lax.axis_size("crm")
    g = lax.axis_index("gcm").astype(jnp.int32)
    c = lax.axis_index("crm").astype(jnp.int32)
    place = jnp.stack([g, jnp.int32(n_gcm), jnp.int32(n_crm), jnp.int32(0)])

    final, heat, send = call(
        crm_kernel,
        [((col_total, bins, cells), BF16), ((CRM_LEV, col_total), F32),
         ((devices, CRM_LEV, 128), BF16)],
        [("s", order), ("s", ordered), ("s", place)]
        + v(drops, cell_forcing, slot_of[None, :], coef[:, :512], tail_coef, growth_rows),
        [((GROUP, 40, cells), F32), ((GROUP, 512, cells), BF16),
         ((GROUP // 4, 256, cells), BF16),
         ((2 * GROUP, 48, 128), F32),
         ((col_total, cells), F32), ((col_total, cells), F32)],
        flops=10_000_000_000,
    )
    got = lax.all_to_all(send, ("gcm", "crm"), split_axis=0, concat_axis=0, tiled=True)
    up = (g + n_gcm - 1) % n_gcm * n_crm
    same_row = g * n_crm
    down = (g + 1) % n_gcm * n_crm
    west = (c + n_crm - 1) % n_crm
    east = (c + 1) % n_crm
    around = jnp.stack(
        [up + c, down + c, same_row + west, same_row + east,
         up + west, up + east, down + west, down + east]
    )
    tracer_next, power = call(
        last_kernel,
        [field, ((CRM_LEV, devices * capacity), F32)],
        [("s", around)] + v(base, heat, got, jnp.asarray(up_map, F32)),
        [((levels, col_count), F32)] * 5,
    )
    return (tracer_next, final, power)


def solution(mesh):
    return jax.shard_map(
        shards,
        mesh=mesh,
        in_specs=(
            P(None, "gcm", "crm"),
            P(None, "gcm", "crm"),
            P(None, "gcm", "crm"),
            P(("gcm", "crm"), None, None),
            P(("gcm", "crm"), None),
            P(("gcm", "crm")),
            P(),
            P(),
        ),
        out_specs=(P(None, "gcm", "crm"), P(("gcm", "crm"), None, None), P(None, ("gcm", "crm"))),
        check_vma=False,
    )
```

```python
import functools

import jax
import jax.numpy as jnp
import numpy as np
from jax import lax
from jax.experimental import pallas as pl
from jax.experimental.pallas import tpu as pltpu
from jax.sharding import PartitionSpec as P

CRM_X = 16
CRM_LEV = 16
DYN_STEPS = 2

DT_DYN = 0.04
DT_CRM = 0.05
DT_PHYS = 0.5
HIGH = lax.Precision.HIGHEST
F32 = jnp.float32
BF16 = jnp.bfloat16
GROUP = 8
CHUNK = 8
MIB = 1024 * 1024


def gll_tables():
    inv_root = 1.0 / np.sqrt(5.0)
    gll_nodes = np.array([-1.0, -inv_root, inv_root, 1.0])
    weights = np.array([1.0, 5.0, 5.0, 1.0]) / 6.0
    legendre = (5.0 * gll_nodes**3 - 3.0 * gll_nodes) / 2.0
    derivative = np.zeros((4, 4))
    for i in range(4):
        for j in range(4):
            if i != j:
                derivative[i, j] = legendre[i] / (legendre[j] * (gll_nodes[i] - gll_nodes[j]))
    derivative[0, 0] = -3.0
    derivative[3, 3] = 3.0
    return (2.0 * derivative, weights)


def level_tables(levels, crm_levels):
    spacing = levels / crm_levels
    centres = (np.arange(crm_levels) + 0.5) * spacing - 0.5
    hats = np.maximum(0.0, 1.0 - np.abs(np.arange(levels)[None, :] - centres[:, None]) / spacing)
    down_map = hats / hats.sum(axis=1, keepdims=True)
    up_map = hats.T / hats.T.sum(axis=1, keepdims=True)
    return (down_map, up_map)


DERIV, WEIGHTS = gll_tables()


def iota(shape, axis):
    return lax.broadcasted_iota(jnp.int32, shape, axis)


def derivative_terms(shape, axis):
    phase = iota(shape, axis) % 4
    terms = []
    for shift in range(-3, 4):
        value = jnp.zeros(shape, F32)
        for i in range(4):
            if 0 <= i + shift < 4:
                value = jnp.where(phase == i, F32(DERIV[i, i + shift]), value)
        terms.append((shift, value))
    return terms


def along(x, terms, axis):
    size = x.shape[axis]
    total = None
    for shift, value in terms:
        moved = x if shift == 0 else pltpu.roll(x, (-shift) % size, axis)
        part = value[None] * moved
        total = part if total is None else total + part
    return total


def tendency(x, u, v, row_terms, col_terms):
    halves = []
    for h in range(x.shape[2] // 128):
        cut = slice(128 * h, 128 * h + 128)
        q = x[:, :, cut]
        grad_x = along(q, row_terms, 1)
        grad_y = along(q, col_terms, 2)
        halves.append(-(u[:, :, cut] * grad_x + v[:, :, cut] * grad_y))
    return jnp.concatenate(halves, axis=2)


def pack_kernel(q_hbm, u_hbm, v_hbm, right_ref, left_ref, q_ref, u_ref, v_ref, sems):
    copies = []
    for i, (src, dst) in enumerate(((q_hbm, q_ref), (u_hbm, u_ref), (v_hbm, v_ref))):
        copies.append(pltpu.make_async_copy(src, dst, sems.at[i]))
    for copy in copies:
        copy.start()
    for copy in copies:
        copy.wait()
    lane = iota((8, 128), 1)

    def body(group, carry):
        right = jnp.zeros((8, 128), F32)
        left = jnp.zeros((8, 128), F32)
        for j in range(4):
            for f, ref in enumerate((q_ref, u_ref, v_ref)):
                start = 32 * j + 8 * f
                here = (lane >= start) & (lane < start + 8)
                x = ref[group * 4 + j]
                right = jnp.where(here, pltpu.roll(x[:, 128:256], (start - 120) % 128, 1), right)
                first = x[:, 0:128]
                if start:
                    first = pltpu.roll(first, start, 1)
                left = jnp.where(here, first, left)
        right_ref[group] = right
        left_ref[group] = left
        return carry

    lax.fori_loop(0, right_ref.shape[0], body, 0)


def put_rows(x, levels, top_ref, bot_ref, i):
    top_ref[i, levels, :] = x[:, 0, :]
    bot_ref[i, levels, :] = x[:, 7, :]


def first_kernel(q_ref, u_ref, v_ref, tend_ref, top_ref, bot_ref):
    row_terms = derivative_terms((8, 128), 0)
    col_terms = derivative_terms((8, 128), 1)

    def body(chunk, carry):
        levels = pl.ds(pl.multiple_of(chunk * CHUNK, CHUNK), CHUNK)
        q = q_ref[levels]
        tend = tendency(q, u_ref[levels], v_ref[levels], row_terms, col_terms)
        tend_ref[levels] = tend
        put_rows(tend, levels, top_ref, bot_ref, 0)
        put_rows(q, levels, top_ref, bot_ref, 1)
        return carry

    lax.fori_loop(0, q_ref.shape[0] // CHUNK, body, 0)


def strip_kernel(
    left_ref, right_ref, top_main, bot_main,
    q_ref, u_ref, v_ref, tend_ref, top_ref, bot_ref,
):
    row_terms = derivative_terms((8, 128), 0)
    col_terms = derivative_terms((8, 128), 1)
    lane = iota((8, 128), 1)
    top_ref[:, :, 0:256] = top_main[...]
    bot_ref[:, :, 0:256] = bot_main[...]

    def body(chunk, carry):
        tiles = [[], [], []]
        for half in range(CHUNK // 4):
            west = left_ref[chunk * (CHUNK // 4) + half]
            east = right_ref[chunk * (CHUNK // 4) + half]
            for j in range(4):
                for f in range(3):
                    start = 32 * j + 8 * f
                    a = pltpu.roll(east, 128 - start, 1) if start else east
                    b = pltpu.roll(west, (120 - start) % 128, 1)
                    tiles[f].append(jnp.where(lane < 8, a, jnp.where(lane >= 120, b, 0.0)))
        q, u, v = [jnp.stack(tile, axis=0) for tile in tiles]
        levels = pl.ds(pl.multiple_of(chunk * CHUNK, CHUNK), CHUNK)
        q_ref[levels] = q
        u_ref[levels] = u
        v_ref[levels] = v
        tend = tendency(q, u, v, row_terms, col_terms)
        tend_ref[levels] = tend
        for i, x in enumerate((tend, q)):
            top_ref[i, levels, 256:384] = x[:, 0, :]
            bot_ref[i, levels, 256:384] = x[:, 7, :]
        return carry

    lax.fori_loop(0, q_ref.shape[0] // CHUNK, body, 0)


def assemble_chunk(x, up, down):
    shape = x.shape
    row = iota(shape, 1)
    partner = jnp.where(
        row == 0,
        jnp.broadcast_to(up[:, None, :], shape),
        jnp.where(
            row == 7,
            jnp.broadcast_to(down[:, None, :], shape),
            jnp.where(row == 3, pltpu.roll(x, 7, 1), pltpu.roll(x, 1, 1)),
        ),
    )
    x = jnp.where((row % 4 == 0) | (row % 4 == 3), 0.5 * (x + partner), x)
    col = iota(shape, 2)
    partner = jnp.where(
        col % 4 == 3, pltpu.roll(x, shape[2] - 1, 2), pltpu.roll(x, 1, 2)
    )
    return jnp.where((col % 4 == 0) | (col % 4 == 3), 0.5 * (x + partner), x)


def join(main, strip):
    return jnp.concatenate([main, strip], axis=2)


def second_kernel(
    q_ref, u_ref, v_ref, tend_ref, q_strip, u_strip, v_strip, tend_strip, up_ref, down_ref,
    state_ref, smooth_ref, next_ref, top_ref, bot_ref,
):
    row_terms = derivative_terms((8, 128), 0)
    col_terms = derivative_terms((8, 128), 1)

    def body(chunk, carry):
        levels = pl.ds(pl.multiple_of(chunk * CHUNK, CHUNK), CHUNK)
        q = join(q_ref[levels], q_strip[levels])
        change = assemble_chunk(
            join(tend_ref[levels], tend_strip[levels]), up_ref[0, levels, :], down_ref[0, levels, :]
        )
        smooth = assemble_chunk(q, up_ref[1, levels, :], down_ref[1, levels, :])
        smooth_ref[levels] = smooth[:, :, 0:256]
        state = q + DT_DYN * change
        state_ref[levels] = state[:, :, 0:256]
        tend = tendency(
            state, join(u_ref[levels], u_strip[levels]), join(v_ref[levels], v_strip[levels]),
            row_terms, col_terms,
        )
        next_ref[levels] = tend
        put_rows(tend, levels, top_ref, bot_ref, 0)
        return carry

    lax.fori_loop(0, q_ref.shape[0] // CHUNK, body, 0)


def third_kernel(
    q_ref, state_ref, smooth_ref, tend_ref, up_ref, down_ref, down_map_ref,
    base_ref, cell_ref, near_ref, far_ref,
):
    cols = cell_ref.shape[0]
    half = cols // 2
    phase = iota((8, 256), 0) % 4
    row_weight = jnp.where((phase == 0) | (phase == 3), F32(WEIGHTS[0]), F32(WEIGHTS[1]))
    near_rows = jnp.where(iota((8, 256), 0) < 4, row_weight, 0.0)
    far_rows = row_weight - near_rows

    def body(chunk, carry):
        levels = pl.ds(pl.multiple_of(chunk * CHUNK, CHUNK), CHUNK)
        change = assemble_chunk(tend_ref[levels], up_ref[0, levels, :], down_ref[0, levels, :])
        moved = (state_ref[levels] + DT_DYN * change[:, :, 0:256]) - q_ref[levels]
        base_ref[levels] = smooth_ref[levels] + moved
        near_ref[levels, :] = jnp.sum(moved * near_rows[None], axis=1)
        far_ref[levels, :] = jnp.sum(moved * far_rows[None], axis=1)
        return carry

    lax.fori_loop(0, q_ref.shape[0] // CHUNK, body, 0)
    point = iota((256, cols), 0)
    element = iota((256, cols), 1)
    weight = jnp.where(
        (point % 4 == 0) | (point % 4 == 3), F32(WEIGHTS[0]), F32(WEIGHTS[1])
    ) * F32(0.25 / (DYN_STEPS * DT_DYN))
    near_cols = jnp.where(point // 4 == element, weight, 0.0)
    far_cols = jnp.where(point // 4 + half == element, weight, 0.0)
    means = jnp.dot(near_ref[...], near_cols, precision=HIGH, preferred_element_type=F32)
    means += jnp.dot(far_ref[...], far_cols, precision=HIGH, preferred_element_type=F32)
    forcing = jnp.dot(down_map_ref[...], means, precision=HIGH, preferred_element_type=F32)
    forcing = forcing.T.astype(BF16)
    cells = cell_ref.shape[1]
    spread = (iota((CRM_LEV, cells), 1) // CRM_X == iota((CRM_LEV, cells), 0)).astype(BF16)
    cell_ref[...] = DT_CRM * jnp.dot(forcing, spread, preferred_element_type=F32)


def crm_kernel(
    order_ref, count_ref, place_ref, drops_ref, cell_ref, slot_ref, coef_ref, growth_ref,
    final_ref, heat_ref, send_ref, state_ref, heat_cell_ref, echo_cell_ref, *twice_refs,
):
    bins = drops_ref.shape[1]
    cells = drops_ref.shape[2]
    cols = drops_ref.shape[0]
    coef = coef_ref[...]
    growth = growth_ref[...]
    state_ref[...] = jnp.zeros(state_ref.shape, F32)
    mass = (iota((40, cells), 0) + 1).astype(F32) / F32(bins)

    def grow(k, which, zero):
        grown = state_ref[k] + growth * cell_ref[pl.ds(which, 1), :]
        halves = []
        for h in range(cells // 128):
            cut = slice(128 * h, 128 * h + 128)
            g = grown[0:32, cut]
            last = grown[32:40, cut]
            twice_ref = twice_refs[k]
            twice_ref[h, 0:32, :] = g
            twice_ref[h, 32:48, :] = g[0:16]
            rows = []
            for d in range(16):
                other = g if d == 0 else twice_ref[h, pl.ds(zero + d, 32), :]
                if d == 8:
                    other = jnp.concatenate([g[8:], g[:8]], axis=0)
                rows.append((g * other).astype(BF16))
            rows.append((g[0:16] * g[16:32]).astype(BF16))
            rows.append((g * last[0:1]).astype(BF16))
            tail = jnp.concatenate([last * last, jnp.zeros((8, 128), F32)], axis=0)
            rows.append(tail.astype(BF16))
            halves.append(jnp.concatenate(rows, axis=0))
        return grown, jnp.concatenate(halves, axis=1)

    def group(index, carry):
        base = index * GROUP
        which = [order_ref[base + k] for k in range(GROUP)]
        count = [count_ref[base + k] for k in range(GROUP)]
        for k in range(GROUP):
            state_ref[k, 0:bins, :] = drops_ref[which[k]].astype(F32)

        def step(s, c):
            for k in range(GROUP):
                grown, pairs = grow(k, which[k], place_ref[3])
                change = jnp.dot(coef, pairs, preferred_element_type=F32)
                moved = grown + (change[0:40] + change[40:80])
                state_ref[k] = jnp.where(s < count[k], moved, state_ref[k])
            return c

        lax.fori_loop(0, count[0], step, 0)
        for k in range(GROUP):
            final = state_ref[k, 0:bins, :]
            initial = drops_ref[which[k]].astype(F32)
            final_ref[which[k]] = final.astype(BF16)
            weighted = mass[0:bins] * final
            heat = jnp.sum(mass[0:bins] * (final - initial), axis=0, keepdims=True)
            echo = jnp.sum(weighted * weighted, axis=0, keepdims=True)
            heat_cell_ref[pl.ds(which[k], 1), :] = heat
            echo_cell_ref[pl.ds(which[k], 1), :] = echo
        return carry

    lax.fori_loop(0, cols // GROUP, group, 0)
    means = jnp.where(
        iota((CRM_LEV, cells), 1) // CRM_X == iota((CRM_LEV, cells), 0), F32(1.0 / CRM_X), 0.0
    )
    contract = (((1,), (1,)), ((), ()))
    heat = lax.dot_general(
        means, heat_cell_ref[...], contract, precision=HIGH, preferred_element_type=F32
    )
    heat = heat.astype(BF16).astype(F32)
    heat_ref[...] = heat
    echo = lax.dot_general(
        means, echo_cell_ref[...], contract, precision=HIGH, preferred_element_type=F32
    )
    echo = jnp.log(1.0 + echo)

    devices = send_ref.shape[0]
    slots = 2 * cols
    capacity = slots // devices
    onehot = (slot_ref[...] == iota((slots, cols), 0)).astype(F32)
    packed = lax.dot_general(echo, onehot, contract, precision=HIGH, preferred_element_type=F32)
    coarse = packed.astype(BF16).astype(F32)
    rest = packed - coarse
    middle = rest.astype(BF16).astype(F32)
    pieces = (coarse, middle, rest - middle)
    lane = iota((CRM_LEV, 128), 1)
    near = heat
    far = pltpu.roll(heat, 64, 1)
    sides = jnp.where(
        lane == 1, pltpu.roll(heat, 65, 1), jnp.where(lane == 62, pltpu.roll(heat, 63, 1), heat)
    )
    n_gcm = place_ref[1]
    n_crm = place_ref[2]
    for d in range(devices):
        away = d // n_crm - place_ref[0]
        below = (away == 1) | (away == 1 - n_gcm)
        above = (away == -1) | (away == n_gcm - 1)
        block = jnp.where(below, far, jnp.where(above, near, sides))
        tile, offset = divmod(d * capacity, 128)
        for i, piece in enumerate(pieces):
            moved = pltpu.roll(
                piece[:, 128 * tile : 128 * tile + 128], (64 + i * capacity - offset) % 128, 1
            )
            start = 64 + i * capacity
            block = jnp.where((lane >= start) & (lane < start + capacity), moved, block)
        send_ref[d] = block.astype(BF16)


def last_kernel(around_ref, base_ref, own_ref, got_ref, up_map_ref, out_ref, power_ref, *back_refs):
    cols = own_ref.shape[1]
    half = cols // 2
    element = iota((cols, 256), 0)
    col = iota((cols, 256), 1)
    phase = col % 4
    edge = (phase == 0) | (phase == 3)
    other = jnp.where(phase == 0, col // 4 - 1, col // 4 + 1)

    def spread(centre, start, west, west_lane, east, east_lane):
        inside = jnp.where(element == col // 4 + start, jnp.where(edge, 0.5, 1.0), 0.0)
        beside = edge & (element == other + start) & (other >= 0) & (other < half)
        middle = jnp.where(beside, 0.5, inside).astype(BF16)
        from_west = jnp.where((col == 0) & (element == west_lane), 0.5, 0.0).astype(BF16)
        from_east = jnp.where((col == 255) & (element == east_lane), 0.5, 0.0).astype(BF16)
        total = jnp.dot(centre, middle, preferred_element_type=F32)
        total += jnp.dot(west, from_west, preferred_element_type=F32)
        total += jnp.dot(east, from_east, preferred_element_type=F32)
        return total

    own = own_ref[...].astype(BF16)
    up, down, left, right, up_left, up_right, down_left, down_right = [
        got_ref[around_ref[i]] for i in range(8)
    ]
    above = spread(up, 0, up_left, half - 1, up_right, 0)
    near = spread(own, 0, left, half - 1, right, 0)
    far = spread(own, half, left, half - 2, right, 1)
    below = spread(down, 0, down_left, half - 1, down_right, 0)
    parts = (
        0.5 * (above + near), near, 0.5 * (near + far), far, 0.5 * (far + below),
    )
    up_map = up_map_ref[...]
    for part, ref in zip(parts, back_refs):
        ref[...] = DT_PHYS * jnp.dot(up_map, part, precision=HIGH, preferred_element_type=F32)

    devices = got_ref.shape[0]
    slots = power_ref.shape[1]
    capacity = slots // devices
    lane = iota((CRM_LEV, 128), 1)
    tiles = [jnp.zeros((CRM_LEV, 128), F32) for _ in range(slots // 128)]
    for d in range(devices):
        block = got_ref[d].astype(F32)
        fine = pltpu.roll(block, 128 - 2 * capacity, 1) + pltpu.roll(block, 128 - capacity, 1)
        tile, offset = divmod(d * capacity, 128)
        moved = pltpu.roll(block + fine, (offset - 64) % 128, 1)
        tiles[tile] = jnp.where((lane >= offset) & (lane < offset + capacity), moved, tiles[tile])
    power_ref[...] = jnp.concatenate(tiles, axis=1)

    def body(chunk, carry):
        levels = pl.ds(pl.multiple_of(chunk * CHUNK, CHUNK), CHUNK)
        shape = (CHUNK, 8, 256)
        row = iota(shape, 1)
        wide = [jnp.broadcast_to(ref[levels, :][:, None, :], shape) for ref in back_refs]
        back = jnp.where(
            row == 0,
            wide[0],
            jnp.where(
                row < 3,
                wide[1],
                jnp.where(row < 5, wide[2], jnp.where(row < 7, wide[3], wide[4])),
            ),
        )
        out_ref[levels] = base_ref[levels] + back
        return carry

    lax.fori_loop(0, base_ref.shape[0] // CHUNK, body, 0)


def call(kernel, outs, args, scratch=(), sems=(), flops=10_000_000):
    spaces = {
        "s": pl.BlockSpec(memory_space=pltpu.SMEM),
        "v": pl.BlockSpec(memory_space=pltpu.VMEM),
        "h": pl.BlockSpec(memory_space=pl.ANY),
    }
    return pl.pallas_call(
        kernel,
        out_shape=[jax.ShapeDtypeStruct(s, t) for s, t in outs],
        in_specs=[spaces[kind] for kind, _ in args],
        out_specs=[spaces["v"]] * len(outs),
        scratch_shapes=[pltpu.VMEM(s, t) for s, t in scratch] + list(sems),
        compiler_params=pltpu.CompilerParams(vmem_limit_bytes=40 * MIB),
        cost_estimate=pl.CostEstimate(flops=flops, bytes_accessed=4_000_000, transcendentals=0),
    )(*[value for _, value in args])


def v(*values):
    return [("v", value) for value in values]


def shift(value, rows, cols):
    n_gcm = lax.axis_size("gcm")
    n_crm = lax.axis_size("crm")
    pairs = []
    for g in range(n_gcm):
        for c in range(n_crm):
            target = ((g + rows) % n_gcm) * n_crm + (c + cols) % n_crm
            pairs.append((g * n_crm + c, target))
    return lax.ppermute(value, ("gcm", "crm"), pairs)


def pair_table(bins):
    table = np.zeros((bins * bins, 576), np.float32)

    def put(column, i, j):
        table[i * bins + j, column] = 1.0
        table[j * bins + i, column] = 1.0

    for d in range(16):
        for b in range(32):
            put(32 * d + b, b, (b + d) % 32)
    for b in range(16):
        put(512 + b, b, b + 16)
    for b in range(32):
        put(528 + b, b, 32)
    put(560, 32, 32)
    return table


def rank_order(counts):
    total = counts.shape[0]
    index = jnp.arange(total, dtype=jnp.int32)
    ahead = (counts[None, :] > counts[:, None]) | (
        (counts[None, :] == counts[:, None]) & (index[None, :] < index[:, None])
    )
    rank = jnp.sum(ahead.astype(jnp.int32), axis=1)
    match = rank[None, :] == index[:, None]
    order = jnp.sum(jnp.where(match, index[None, :], 0), axis=1)
    ordered = jnp.sum(jnp.where(match, counts[None, :], 0), axis=1)
    return order, ordered


def shards(tracer, wind_x, wind_y, drops, owner, counts, collision, growth):
    devices = lax.axis_size("gcm") * lax.axis_size("crm")
    levels, row_count, col_count = tracer.shape
    col_total, bins, cells = drops.shape
    field = (tracer.shape, F32)
    strip = ((levels, row_count, 128), F32)
    rows = ((2, levels, col_count), F32)
    wide = col_count + 128
    down_map, up_map = level_tables(levels, CRM_LEV)

    to_right, to_left = call(
        pack_kernel,
        [((levels // 4, 8, 128), F32)] * 2,
        [("h", tracer), ("h", wind_x), ("h", wind_y)],
        [field] * 3,
        [pltpu.SemaphoreType.DMA((3,))],
    )
    from_left = shift(to_right, 0, 1)
    from_right = shift(to_left, 0, -1)
    tend, top, bot = call(first_kernel, [field, rows, rows], v(tracer, wind_x, wind_y))
    q_strip, u_strip, v_strip, tend_strip, top, bot = call(
        strip_kernel,
        [strip] * 4 + [((2, levels, wide), F32)] * 2,
        v(from_left, from_right, top, bot),
    )
    state, smooth, tend, top, bot = call(
        second_kernel,
        [field, field, ((levels, row_count, wide), F32)] + [((1, levels, wide), F32)] * 2,
        v(tracer, wind_x, wind_y, tend, q_strip, u_strip, v_strip, tend_strip)
        + v(shift(bot, 1, 0), shift(top, -1, 0)),
    )
    base, cell_forcing = call(
        third_kernel,
        [field, ((col_total, cells), F32)],
        v(tracer, state, smooth, tend, shift(bot, 1, 0), shift(top, -1, 0))
        + v(jnp.asarray(down_map, F32)),
        [((levels, col_count), F32), ((levels, col_count), F32)],
    )

    capacity = 2 * col_total // devices
    owners = owner[:, 0]
    index = jnp.arange(col_total, dtype=jnp.int32)
    same = (owners[:, None] == owners[None, :]) & (index[:, None] < index[None, :])
    slot_of = owners * capacity + jnp.sum(same.astype(jnp.int32), axis=0)
    order, ordered = rank_order(counts)
    table = jnp.asarray(pair_table(bins), BF16)
    coef = DT_CRM * jnp.dot(collision, table, preferred_element_type=F32)
    coarse = lax.reduce_precision(coef, 8, 7)
    fine = coef - coarse
    pad = ((0, 40 - bins), (0, 0))
    coef = jnp.concatenate([jnp.pad(coarse, pad), jnp.pad(fine, pad)], axis=0).astype(BF16)
    growth_rows = jnp.broadcast_to(jnp.pad(growth, (0, 40 - bins))[:, None], (40, cells))
    n_gcm = lax.axis_size("gcm")
    n_crm = lax.axis_size("crm")
    g = lax.axis_index("gcm").astype(jnp.int32)
    c = lax.axis_index("crm").astype(jnp.int32)
    place = jnp.stack([g, jnp.int32(n_gcm), jnp.int32(n_crm), jnp.int32(0)])

    final, heat, send = call(
        crm_kernel,
        [((col_total, bins, cells), BF16), ((CRM_LEV, col_total), F32),
         ((devices, CRM_LEV, 128), BF16)],
        [("s", order), ("s", ordered), ("s", place)]
        + v(drops, cell_forcing, slot_of[None, :], coef, growth_rows),
        [((GROUP, 40, cells), F32), ((col_total, cells), F32),
         ((col_total, cells), F32)] + [((2, 48, 128), F32)] * GROUP,
        flops=10_000_000_000,
    )
    got = lax.all_to_all(send, ("gcm", "crm"), split_axis=0, concat_axis=0, tiled=True)
    up = (g + n_gcm - 1) % n_gcm * n_crm
    same_row = g * n_crm
    down = (g + 1) % n_gcm * n_crm
    west = (c + n_crm - 1) % n_crm
    east = (c + 1) % n_crm
    around = jnp.stack(
        [up + c, down + c, same_row + west, same_row + east,
         up + west, up + east, down + west, down + east]
    )
    tracer_next, power = call(
        last_kernel,
        [field, ((CRM_LEV, devices * capacity), F32)],
        [("s", around)] + v(base, heat, got, jnp.asarray(up_map, F32)),
        [((levels, col_count), F32)] * 5,
    )
    return (tracer_next, final, power)


def solution(mesh):
    return jax.shard_map(
        shards,
        mesh=mesh,
        in_specs=(
            P(None, "gcm", "crm"),
            P(None, "gcm", "crm"),
            P(None, "gcm", "crm"),
            P(("gcm", "crm"), None, None),
            P(("gcm", "crm"), None),
            P(("gcm", "crm")),
            P(),
            P(),
        ),
        out_specs=(P(None, "gcm", "crm"), P(("gcm", "crm"), None, None), P(None, ("gcm", "crm"))),
        check_vma=False,
    )
```

```python
import functools

import jax
import jax.numpy as jnp
import numpy as np
from jax import lax
from jax.experimental import pallas as pl
from jax.experimental.pallas import tpu as pltpu
from jax.sharding import PartitionSpec as P

CRM_X = 16
CRM_LEV = 16
DYN_STEPS = 2

DT_DYN = 0.04
DT_CRM = 0.05
DT_PHYS = 0.5
HIGH = lax.Precision.HIGHEST
F32 = jnp.float32
BF16 = jnp.bfloat16
GROUP = 8
CHUNK = 8
MIB = 1024 * 1024


def gll_tables():
    inv_root = 1.0 / np.sqrt(5.0)
    gll_nodes = np.array([-1.0, -inv_root, inv_root, 1.0])
    weights = np.array([1.0, 5.0, 5.0, 1.0]) / 6.0
    legendre = (5.0 * gll_nodes**3 - 3.0 * gll_nodes) / 2.0
    derivative = np.zeros((4, 4))
    for i in range(4):
        for j in range(4):
            if i != j:
                derivative[i, j] = legendre[i] / (legendre[j] * (gll_nodes[i] - gll_nodes[j]))
    derivative[0, 0] = -3.0
    derivative[3, 3] = 3.0
    return (2.0 * derivative, weights)


def level_tables(levels, crm_levels):
    spacing = levels / crm_levels
    centres = (np.arange(crm_levels) + 0.5) * spacing - 0.5
    hats = np.maximum(0.0, 1.0 - np.abs(np.arange(levels)[None, :] - centres[:, None]) / spacing)
    down_map = hats / hats.sum(axis=1, keepdims=True)
    up_map = hats.T / hats.T.sum(axis=1, keepdims=True)
    return (down_map, up_map)


DERIV, WEIGHTS = gll_tables()


def iota(shape, axis):
    return lax.broadcasted_iota(jnp.int32, shape, axis)


def derivative_terms(shape, axis):
    phase = iota(shape, axis) % 4
    terms = []
    for shift in range(-3, 4):
        value = jnp.zeros(shape, F32)
        for i in range(4):
            if 0 <= i + shift < 4:
                value = jnp.where(phase == i, F32(DERIV[i, i + shift]), value)
        terms.append((shift, value))
    return terms


def along(x, terms, axis):
    size = x.shape[axis]
    total = None
    for shift, value in terms:
        moved = x if shift == 0 else pltpu.roll(x, (-shift) % size, axis)
        part = value[None] * moved
        total = part if total is None else total + part
    return total


def tendency(x, u, v, row_terms, col_terms):
    halves = []
    for h in range(x.shape[2] // 128):
        cut = slice(128 * h, 128 * h + 128)
        q = x[:, :, cut]
        grad_x = along(q, row_terms, 1)
        grad_y = along(q, col_terms, 2)
        halves.append(-(u[:, :, cut] * grad_x + v[:, :, cut] * grad_y))
    return jnp.concatenate(halves, axis=2)


def put_rows(x, levels, top_ref, bot_ref, i):
    top_ref[i, levels, :] = x[:, 0, :]
    bot_ref[i, levels, :] = x[:, 7, :]


def first_kernel(
    q_hbm, u_hbm, v_hbm, tend_ref, top_ref, bot_ref, right_ref, left_ref, q_ref, u_ref, v_ref, sems
):
    row_terms = derivative_terms((8, 128), 0)
    col_terms = derivative_terms((8, 128), 1)
    lane = iota((8, 128), 1)
    chunks = q_ref.shape[0] // CHUNK

    def copies(chunk):
        levels = pl.ds(pl.multiple_of(chunk * CHUNK, CHUNK), CHUNK)
        return [
            pltpu.make_async_copy(src.at[levels], dst.at[levels], sems.at[i, chunk])
            for i, (src, dst) in enumerate(((q_hbm, q_ref), (u_hbm, u_ref), (v_hbm, v_ref)))
        ]

    for chunk in range(chunks):
        for copy in copies(chunk):
            copy.start()

    def body(chunk, carry):
        for copy in copies(chunk):
            copy.wait()
        for half in range(CHUNK // 4):
            right = jnp.zeros((8, 128), F32)
            left = jnp.zeros((8, 128), F32)
            for j in range(4):
                for f, ref in enumerate((q_ref, u_ref, v_ref)):
                    start = 32 * j + 8 * f
                    here = (lane >= start) & (lane < start + 8)
                    x = ref[chunk * CHUNK + half * 4 + j]
                    moved = pltpu.roll(x[:, 128:256], (start - 120) % 128, 1)
                    right = jnp.where(here, moved, right)
                    first = x[:, 0:128]
                    if start:
                        first = pltpu.roll(first, start, 1)
                    left = jnp.where(here, first, left)
            right_ref[chunk * (CHUNK // 4) + half] = right
            left_ref[chunk * (CHUNK // 4) + half] = left
        levels = pl.ds(pl.multiple_of(chunk * CHUNK, CHUNK), CHUNK)
        q = q_ref[levels]
        tend = tendency(q, u_ref[levels], v_ref[levels], row_terms, col_terms)
        tend_ref[levels] = tend
        put_rows(tend, levels, top_ref, bot_ref, 0)
        put_rows(q, levels, top_ref, bot_ref, 1)
        return carry

    lax.fori_loop(0, chunks, body, 0)


def strip_kernel(
    left_ref, right_ref, top_main, bot_main,
    q_ref, u_ref, v_ref, tend_ref, top_ref, bot_ref,
):
    row_terms = derivative_terms((8, 128), 0)
    col_terms = derivative_terms((8, 128), 1)
    lane = iota((8, 128), 1)
    top_ref[:, :, 0:256] = top_main[...]
    bot_ref[:, :, 0:256] = bot_main[...]

    def body(chunk, carry):
        tiles = [[], [], []]
        for half in range(CHUNK // 4):
            west = left_ref[chunk * (CHUNK // 4) + half]
            east = right_ref[chunk * (CHUNK // 4) + half]
            for j in range(4):
                for f in range(3):
                    start = 32 * j + 8 * f
                    a = pltpu.roll(east, 128 - start, 1) if start else east
                    b = pltpu.roll(west, (120 - start) % 128, 1)
                    tiles[f].append(jnp.where(lane < 8, a, jnp.where(lane >= 120, b, 0.0)))
        q, u, v = [jnp.stack(tile, axis=0) for tile in tiles]
        levels = pl.ds(pl.multiple_of(chunk * CHUNK, CHUNK), CHUNK)
        q_ref[levels] = q
        u_ref[levels] = u
        v_ref[levels] = v
        tend = tendency(q, u, v, row_terms, col_terms)
        tend_ref[levels] = tend
        for i, x in enumerate((tend, q)):
            top_ref[i, levels, 256:384] = x[:, 0, :]
            bot_ref[i, levels, 256:384] = x[:, 7, :]
        return carry

    lax.fori_loop(0, q_ref.shape[0] // CHUNK, body, 0)


def assemble_chunk(x, up, down):
    shape = x.shape
    row = iota(shape, 1)
    partner = jnp.where(
        row == 0,
        jnp.broadcast_to(up[:, None, :], shape),
        jnp.where(
            row == 7,
            jnp.broadcast_to(down[:, None, :], shape),
            jnp.where(row == 3, pltpu.roll(x, 7, 1), pltpu.roll(x, 1, 1)),
        ),
    )
    x = jnp.where((row % 4 == 0) | (row % 4 == 3), 0.5 * (x + partner), x)
    col = iota(shape, 2)
    partner = jnp.where(
        col % 4 == 3, pltpu.roll(x, shape[2] - 1, 2), pltpu.roll(x, 1, 2)
    )
    return jnp.where((col % 4 == 0) | (col % 4 == 3), 0.5 * (x + partner), x)


def join(main, strip):
    return jnp.concatenate([main, strip], axis=2)


def second_kernel(
    q_ref, u_ref, v_ref, tend_ref, q_strip, u_strip, v_strip, tend_strip, up_ref, down_ref,
    state_ref, smooth_ref, next_ref, top_ref, bot_ref,
):
    row_terms = derivative_terms((8, 128), 0)
    col_terms = derivative_terms((8, 128), 1)

    def body(chunk, carry):
        levels = pl.ds(pl.multiple_of(chunk * CHUNK, CHUNK), CHUNK)
        q = join(q_ref[levels], q_strip[levels])
        change = assemble_chunk(
            join(tend_ref[levels], tend_strip[levels]), up_ref[0, levels, :], down_ref[0, levels, :]
        )
        smooth = assemble_chunk(q, up_ref[1, levels, :], down_ref[1, levels, :])
        smooth_ref[levels] = smooth[:, :, 0:256]
        state = q + DT_DYN * change
        state_ref[levels] = state[:, :, 0:256]
        tend = tendency(
            state, join(u_ref[levels], u_strip[levels]), join(v_ref[levels], v_strip[levels]),
            row_terms, col_terms,
        )
        next_ref[levels] = tend
        put_rows(tend, levels, top_ref, bot_ref, 0)
        return carry

    lax.fori_loop(0, q_ref.shape[0] // CHUNK, body, 0)


def third_kernel(
    q_ref, state_ref, smooth_ref, tend_ref, up_ref, down_ref, down_map_ref,
    base_ref, cell_ref, near_ref, far_ref,
):
    cols = cell_ref.shape[0]
    half = cols // 2
    phase = iota((8, 256), 0) % 4
    row_weight = jnp.where((phase == 0) | (phase == 3), F32(WEIGHTS[0]), F32(WEIGHTS[1]))
    near_rows = jnp.where(iota((8, 256), 0) < 4, row_weight, 0.0)
    far_rows = row_weight - near_rows

    def body(chunk, carry):
        levels = pl.ds(pl.multiple_of(chunk * CHUNK, CHUNK), CHUNK)
        change = assemble_chunk(tend_ref[levels], up_ref[0, levels, :], down_ref[0, levels, :])
        moved = (state_ref[levels] + DT_DYN * change[:, :, 0:256]) - q_ref[levels]
        base_ref[levels] = smooth_ref[levels] + moved
        near_ref[levels, :] = jnp.sum(moved * near_rows[None], axis=1)
        far_ref[levels, :] = jnp.sum(moved * far_rows[None], axis=1)
        return carry

    lax.fori_loop(0, q_ref.shape[0] // CHUNK, body, 0)
    point = iota((256, cols), 0)
    element = iota((256, cols), 1)
    weight = jnp.where(
        (point % 4 == 0) | (point % 4 == 3), F32(WEIGHTS[0]), F32(WEIGHTS[1])
    ) * F32(0.25 / (DYN_STEPS * DT_DYN))
    near_cols = jnp.where(point // 4 == element, weight, 0.0)
    far_cols = jnp.where(point // 4 + half == element, weight, 0.0)
    means = jnp.dot(near_ref[...], near_cols, precision=HIGH, preferred_element_type=F32)
    means += jnp.dot(far_ref[...], far_cols, precision=HIGH, preferred_element_type=F32)
    forcing = jnp.dot(down_map_ref[...], means, precision=HIGH, preferred_element_type=F32)
    forcing = forcing.T.astype(BF16)
    cells = cell_ref.shape[1]
    spread = (iota((CRM_LEV, cells), 1) // CRM_X == iota((CRM_LEV, cells), 0)).astype(BF16)
    cell_ref[...] = DT_CRM * jnp.dot(forcing, spread, preferred_element_type=F32)


def coef_kernel(collision_ref, table_ref, after_ref, coef_ref):
    total = jnp.dot(collision_ref[...], table_ref[...], preferred_element_type=F32) * DT_CRM
    coarse = total.astype(BF16)
    fine = total - coarse.astype(F32)
    coef_ref[...] = jnp.concatenate([coarse.astype(F32), fine], axis=0).astype(BF16)


def crm_kernel(
    order_ref, count_ref, place_ref, drops_ref, cell_ref, slot_ref, coef_ref, growth_ref,
    final_ref, heat_ref, send_ref, state_ref, pair_ref, twice_ref, heat_cell_ref, echo_cell_ref,
):
    bins = drops_ref.shape[1]
    cells = drops_ref.shape[2]
    cols = drops_ref.shape[0]
    coef = coef_ref[...]
    growth = growth_ref[...]
    state_ref[...] = jnp.zeros(state_ref.shape, F32)
    mass = (iota((40, cells), 0) + 1).astype(F32) / F32(bins)

    def grow(k, which, zero):
        grown = state_ref[k] + growth * cell_ref[pl.ds(which, 1), :]
        for h in range(cells // 128):
            cut = slice(128 * h, 128 * h + 128)
            g = grown[0:32, cut]
            last = grown[32:40, cut]
            twice_ref[2 * k + h, 0:32, :] = g
            twice_ref[2 * k + h, 32:48, :] = g[0:16]
            for d in range(16):
                other = g if d % 8 == 0 else twice_ref[2 * k + h, pl.ds(zero + d, 32), :]
                if d == 8:
                    other = jnp.concatenate([g[8:], g[:8]], axis=0)
                pair_ref[k, 32 * d : 32 * d + 32, cut] = (g * other).astype(BF16)
            pair_ref[k, 512:528, cut] = (g[0:16] * g[16:32]).astype(BF16)
            pair_ref[k, 528:560, cut] = (g * last[0:1]).astype(BF16)
            tail = jnp.concatenate([last * last, jnp.zeros((8, 128), F32)], axis=0)
            pair_ref[k, 560:576, cut] = tail.astype(BF16)
        return grown

    def group(index, carry):
        base = index * GROUP
        which = [order_ref[base + k] for k in range(GROUP)]
        count = [count_ref[base + k] for k in range(GROUP)]
        for k in range(GROUP):
            state_ref[k, 0:bins, :] = drops_ref[which[k]].astype(F32)

        def step(s, c):
            for k in range(GROUP):
                grown = grow(k, which[k], place_ref[3])
                change = jnp.dot(coef, pair_ref[k], preferred_element_type=F32)
                moved = grown + (change[0:40] + change[40:80])
                state_ref[k] = jnp.where(s < count[k], moved, state_ref[k])
            return c

        lax.fori_loop(0, count[0], step, 0)
        for k in range(GROUP):
            final = state_ref[k, 0:bins, :]
            initial = drops_ref[which[k]].astype(F32)
            final_ref[which[k]] = final.astype(BF16)
            weighted = mass[0:bins] * final
            heat = jnp.sum(mass[0:bins] * (final - initial), axis=0, keepdims=True)
            echo = jnp.sum(weighted * weighted, axis=0, keepdims=True)
            heat_cell_ref[pl.ds(which[k], 1), :] = heat
            echo_cell_ref[pl.ds(which[k], 1), :] = echo
        return carry

    lax.fori_loop(0, cols // GROUP, group, 0)
    means = jnp.where(
        iota((CRM_LEV, cells), 1) // CRM_X == iota((CRM_LEV, cells), 0), F32(1.0 / CRM_X), 0.0
    )
    contract = (((1,), (1,)), ((), ()))
    heat = lax.dot_general(
        means, heat_cell_ref[...], contract, precision=HIGH, preferred_element_type=F32
    )
    heat = heat.astype(BF16).astype(F32)
    heat_ref[...] = heat
    echo = lax.dot_general(
        means, echo_cell_ref[...], contract, precision=HIGH, preferred_element_type=F32
    )
    echo = jnp.log(1.0 + echo)

    devices = send_ref.shape[0]
    slots = 2 * cols
    capacity = slots // devices
    onehot = (slot_ref[...] == iota((slots, cols), 0)).astype(F32)
    packed = lax.dot_general(echo, onehot, contract, precision=HIGH, preferred_element_type=F32)
    coarse = packed.astype(BF16).astype(F32)
    rest = packed - coarse
    middle = rest.astype(BF16).astype(F32)
    pieces = (coarse, middle, rest - middle)
    lane = iota((CRM_LEV, 128), 1)
    near = heat
    far = pltpu.roll(heat, 64, 1)
    sides = jnp.where(
        lane == 1, pltpu.roll(heat, 65, 1), jnp.where(lane == 62, pltpu.roll(heat, 63, 1), heat)
    )
    n_gcm = place_ref[1]
    n_crm = place_ref[2]
    for d in range(devices):
        away = d // n_crm - place_ref[0]
        below = (away == 1) | (away == 1 - n_gcm)
        above = (away == -1) | (away == n_gcm - 1)
        block = jnp.where(below, far, jnp.where(above, near, sides))
        tile, offset = divmod(d * capacity, 128)
        for i, piece in enumerate(pieces):
            moved = pltpu.roll(
                piece[:, 128 * tile : 128 * tile + 128], (64 + i * capacity - offset) % 128, 1
            )
            start = 64 + i * capacity
            block = jnp.where((lane >= start) & (lane < start + capacity), moved, block)
        send_ref[d] = block.astype(BF16)


def last_kernel(around_ref, base_ref, own_ref, got_ref, up_map_ref, out_ref, power_ref, *back_refs):
    cols = own_ref.shape[1]
    half = cols // 2
    element = iota((cols, 256), 0)
    col = iota((cols, 256), 1)
    phase = col % 4
    edge = (phase == 0) | (phase == 3)
    other = jnp.where(phase == 0, col // 4 - 1, col // 4 + 1)

    def spread(centre, start, west, west_lane, east, east_lane):
        inside = jnp.where(element == col // 4 + start, jnp.where(edge, 0.5, 1.0), 0.0)
        beside = edge & (element == other + start) & (other >= 0) & (other < half)
        middle = jnp.where(beside, 0.5, inside).astype(BF16)
        from_west = jnp.where((col == 0) & (element == west_lane), 0.5, 0.0).astype(BF16)
        from_east = jnp.where((col == 255) & (element == east_lane), 0.5, 0.0).astype(BF16)
        total = jnp.dot(centre, middle, preferred_element_type=F32)
        total += jnp.dot(west, from_west, preferred_element_type=F32)
        total += jnp.dot(east, from_east, preferred_element_type=F32)
        return total

    own = own_ref[...].astype(BF16)
    up, down, left, right, up_left, up_right, down_left, down_right = [
        got_ref[around_ref[i]] for i in range(8)
    ]
    above = spread(up, 0, up_left, half - 1, up_right, 0)
    near = spread(own, 0, left, half - 1, right, 0)
    far = spread(own, half, left, half - 2, right, 1)
    below = spread(down, 0, down_left, half - 1, down_right, 0)
    parts = (
        0.5 * (above + near), near, 0.5 * (near + far), far, 0.5 * (far + below),
    )
    up_map = up_map_ref[...]
    for part, ref in zip(parts, back_refs):
        ref[...] = DT_PHYS * jnp.dot(up_map, part, precision=HIGH, preferred_element_type=F32)

    devices = got_ref.shape[0]
    slots = power_ref.shape[1]
    capacity = slots // devices
    lane = iota((CRM_LEV, 128), 1)
    tiles = [jnp.zeros((CRM_LEV, 128), F32) for _ in range(slots // 128)]
    for d in range(devices):
        block = got_ref[d].astype(F32)
        fine = pltpu.roll(block, 128 - 2 * capacity, 1) + pltpu.roll(block, 128 - capacity, 1)
        tile, offset = divmod(d * capacity, 128)
        moved = pltpu.roll(block + fine, (offset - 64) % 128, 1)
        tiles[tile] = jnp.where((lane >= offset) & (lane < offset + capacity), moved, tiles[tile])
    power_ref[...] = jnp.concatenate(tiles, axis=1)

    def body(chunk, carry):
        levels = pl.ds(pl.multiple_of(chunk * CHUNK, CHUNK), CHUNK)
        shape = (CHUNK, 8, 256)
        row = iota(shape, 1)
        wide = [jnp.broadcast_to(ref[levels, :][:, None, :], shape) for ref in back_refs]
        back = jnp.where(
            row == 0,
            wide[0],
            jnp.where(
                row < 3,
                wide[1],
                jnp.where(row < 5, wide[2], jnp.where(row < 7, wide[3], wide[4])),
            ),
        )
        out_ref[levels] = base_ref[levels] + back
        return carry

    lax.fori_loop(0, base_ref.shape[0] // CHUNK, body, 0)


def call(kernel, outs, args, scratch=(), sems=(), flops=10_000_000):
    spaces = {
        "s": pl.BlockSpec(memory_space=pltpu.SMEM),
        "v": pl.BlockSpec(memory_space=pltpu.VMEM),
        "h": pl.BlockSpec(memory_space=pl.ANY),
    }
    return pl.pallas_call(
        kernel,
        out_shape=[jax.ShapeDtypeStruct(s, t) for s, t in outs],
        in_specs=[spaces[kind] for kind, _ in args],
        out_specs=[spaces["v"]] * len(outs),
        scratch_shapes=[pltpu.VMEM(s, t) for s, t in scratch] + list(sems),
        compiler_params=pltpu.CompilerParams(vmem_limit_bytes=40 * MIB),
        cost_estimate=pl.CostEstimate(flops=flops, bytes_accessed=4_000_000, transcendentals=0),
    )(*[value for _, value in args])


def v(*values):
    return [("v", value) for value in values]


def shift(value, rows, cols):
    n_gcm = lax.axis_size("gcm")
    n_crm = lax.axis_size("crm")
    pairs = []
    for g in range(n_gcm):
        for c in range(n_crm):
            target = ((g + rows) % n_gcm) * n_crm + (c + cols) % n_crm
            pairs.append((g * n_crm + c, target))
    return lax.ppermute(value, ("gcm", "crm"), pairs)


def pair_table(bins):
    table = np.zeros((bins * bins, 576), np.float32)

    def put(column, i, j):
        table[i * bins + j, column] = 1.0
        table[j * bins + i, column] = 1.0

    for d in range(16):
        for b in range(32):
            put(32 * d + b, b, (b + d) % 32)
    for b in range(16):
        put(512 + b, b, b + 16)
    for b in range(32):
        put(528 + b, b, 32)
    put(560, 32, 32)
    return table


def rank_order(counts):
    total = counts.shape[0]
    index = jnp.arange(total, dtype=jnp.int32)
    ahead = (counts[None, :] > counts[:, None]) | (
        (counts[None, :] == counts[:, None]) & (index[None, :] < index[:, None])
    )
    rank = jnp.sum(ahead.astype(jnp.int32), axis=1)
    match = rank[None, :] == index[:, None]
    order = jnp.sum(jnp.where(match, index[None, :], 0), axis=1)
    ordered = jnp.sum(jnp.where(match, counts[None, :], 0), axis=1)
    return order, ordered


def shards(tracer, wind_x, wind_y, drops, owner, counts, collision, growth):
    devices = lax.axis_size("gcm") * lax.axis_size("crm")
    levels, row_count, col_count = tracer.shape
    col_total, bins, cells = drops.shape
    field = (tracer.shape, F32)
    strip = ((levels, row_count, 128), F32)
    rows = ((2, levels, col_count), F32)
    wide = col_count + 128
    down_map, up_map = level_tables(levels, CRM_LEV)

    tend, top, bot, to_right, to_left = call(
        first_kernel,
        [field, rows, rows] + [((levels // 4, 8, 128), F32)] * 2,
        [("h", tracer), ("h", wind_x), ("h", wind_y)],
        [field] * 3,
        [pltpu.SemaphoreType.DMA((3, levels // CHUNK))],
    )
    from_left = shift(to_right, 0, 1)
    from_right = shift(to_left, 0, -1)
    q_strip, u_strip, v_strip, tend_strip, top, bot = call(
        strip_kernel,
        [strip] * 4 + [((2, levels, wide), F32)] * 2,
        v(from_left, from_right, top, bot),
    )
    (coef,) = call(
        coef_kernel,
        [((80, 576), BF16)],
        v(jnp.pad(collision, ((0, 40 - bins), (0, 0))), jnp.asarray(pair_table(bins), BF16))
        + [("h", top)],
    )
    state, smooth, tend, top, bot = call(
        second_kernel,
        [field, field, ((levels, row_count, wide), F32)] + [((1, levels, wide), F32)] * 2,
        v(tracer, wind_x, wind_y, tend, q_strip, u_strip, v_strip, tend_strip)
        + v(shift(bot, 1, 0), shift(top, -1, 0)),
    )
    base, cell_forcing = call(
        third_kernel,
        [field, ((col_total, cells), F32)],
        v(tracer, state, smooth, tend, shift(bot, 1, 0), shift(top, -1, 0))
        + v(jnp.asarray(down_map, F32)),
        [((levels, col_count), F32), ((levels, col_count), F32)],
    )

    capacity = 2 * col_total // devices
    owners = owner[:, 0]
    index = jnp.arange(col_total, dtype=jnp.int32)
    same = (owners[:, None] == owners[None, :]) & (index[:, None] < index[None, :])
    slot_of = owners * capacity + jnp.sum(same.astype(jnp.int32), axis=0)
    order, ordered = rank_order(counts)
    growth_rows = jnp.broadcast_to(jnp.pad(growth, (0, 40 - bins))[:, None], (40, cells))
    n_gcm = lax.axis_size("gcm")
    n_crm = lax.axis_size("crm")
    g = lax.axis_index("gcm").astype(jnp.int32)
    c = lax.axis_index("crm").astype(jnp.int32)
    place = jnp.stack([g, jnp.int32(n_gcm), jnp.int32(n_crm), jnp.int32(0)])

    final, heat, send = call(
        crm_kernel,
        [((col_total, bins, cells), BF16), ((CRM_LEV, col_total), F32),
         ((devices, CRM_LEV, 128), BF16)],
        [("s", order), ("s", ordered), ("s", place)]
        + v(drops, cell_forcing, slot_of[None, :], coef, growth_rows),
        [((GROUP, 40, cells), F32), ((GROUP, 576, cells), BF16),
         ((2 * GROUP, 48, 128), F32),
         ((col_total, cells), F32), ((col_total, cells), F32)],
        flops=10_000_000_000,
    )
    got = lax.all_to_all(send, ("gcm", "crm"), split_axis=0, concat_axis=0, tiled=True)
    up = (g + n_gcm - 1) % n_gcm * n_crm
    same_row = g * n_crm
    down = (g + 1) % n_gcm * n_crm
    west = (c + n_crm - 1) % n_crm
    east = (c + 1) % n_crm
    around = jnp.stack(
        [up + c, down + c, same_row + west, same_row + east,
         up + west, up + east, down + west, down + east]
    )
    tracer_next, power = call(
        last_kernel,
        [field, ((CRM_LEV, devices * capacity), F32)],
        [("s", around)] + v(base, heat, got, jnp.asarray(up_map, F32)),
        [((levels, col_count), F32)] * 5,
    )
    return (tracer_next, final, power)


def solution(mesh):
    return jax.shard_map(
        shards,
        mesh=mesh,
        in_specs=(
            P(None, "gcm", "crm"),
            P(None, "gcm", "crm"),
            P(None, "gcm", "crm"),
            P(("gcm", "crm"), None, None),
            P(("gcm", "crm"), None),
            P(("gcm", "crm")),
            P(),
            P(),
        ),
        out_specs=(P(None, "gcm", "crm"), P(("gcm", "crm"), None, None), P(None, ("gcm", "crm"))),
        check_vma=False,
    )
```

```python
import functools

import jax
import jax.numpy as jnp
import numpy as np
from jax import lax
from jax.experimental import pallas as pl
from jax.experimental.pallas import tpu as pltpu
from jax.sharding import PartitionSpec as P

CRM_X = 16
CRM_LEV = 16
DYN_STEPS = 2

DT_DYN = 0.04
DT_CRM = 0.05
DT_PHYS = 0.5
HIGH = lax.Precision.HIGHEST
F32 = jnp.float32
BF16 = jnp.bfloat16
GROUP = 8
CHUNK = 8
MIB = 1024 * 1024


def gll_tables():
    inv_root = 1.0 / np.sqrt(5.0)
    gll_nodes = np.array([-1.0, -inv_root, inv_root, 1.0])
    weights = np.array([1.0, 5.0, 5.0, 1.0]) / 6.0
    legendre = (5.0 * gll_nodes**3 - 3.0 * gll_nodes) / 2.0
    derivative = np.zeros((4, 4))
    for i in range(4):
        for j in range(4):
            if i != j:
                derivative[i, j] = legendre[i] / (legendre[j] * (gll_nodes[i] - gll_nodes[j]))
    derivative[0, 0] = -3.0
    derivative[3, 3] = 3.0
    return (2.0 * derivative, weights)


def level_tables(levels, crm_levels):
    spacing = levels / crm_levels
    centres = (np.arange(crm_levels) + 0.5) * spacing - 0.5
    hats = np.maximum(0.0, 1.0 - np.abs(np.arange(levels)[None, :] - centres[:, None]) / spacing)
    down_map = hats / hats.sum(axis=1, keepdims=True)
    up_map = hats.T / hats.T.sum(axis=1, keepdims=True)
    return (down_map, up_map)


DERIV, WEIGHTS = gll_tables()


def iota(shape, axis):
    return lax.broadcasted_iota(jnp.int32, shape, axis)


def derivative_terms(shape, axis):
    phase = iota(shape, axis) % 4
    terms = []
    for shift in range(-3, 4):
        value = jnp.zeros(shape, F32)
        for i in range(4):
            if 0 <= i + shift < 4:
                value = jnp.where(phase == i, F32(DERIV[i, i + shift]), value)
        terms.append((shift, value))
    return terms


def along(x, terms, axis):
    size = x.shape[axis]
    total = None
    for shift, value in terms:
        moved = x if shift == 0 else pltpu.roll(x, (-shift) % size, axis)
        part = value[None] * moved
        total = part if total is None else total + part
    return total


def tendency(x, u, v, row_terms, col_terms):
    halves = []
    for h in range(x.shape[2] // 128):
        cut = slice(128 * h, 128 * h + 128)
        q = x[:, :, cut]
        grad_x = along(q, row_terms, 1)
        grad_y = along(q, col_terms, 2)
        halves.append(-(u[:, :, cut] * grad_x + v[:, :, cut] * grad_y))
    return jnp.concatenate(halves, axis=2)


def put_rows(x, levels, top_ref, bot_ref, i):
    top_ref[i, levels, :] = x[:, 0, :]
    bot_ref[i, levels, :] = x[:, 7, :]


def first_kernel(
    q_hbm, u_hbm, v_hbm, tend_ref, top_ref, bot_ref, right_ref, left_ref, q_ref, u_ref, v_ref, sems
):
    row_terms = derivative_terms((8, 128), 0)
    col_terms = derivative_terms((8, 128), 1)
    lane = iota((8, 128), 1)
    chunks = q_ref.shape[0] // CHUNK

    def copies(chunk):
        levels = pl.ds(pl.multiple_of(chunk * CHUNK, CHUNK), CHUNK)
        return [
            pltpu.make_async_copy(src.at[levels], dst.at[levels], sems.at[i, chunk])
            for i, (src, dst) in enumerate(((q_hbm, q_ref), (u_hbm, u_ref), (v_hbm, v_ref)))
        ]

    for chunk in range(chunks):
        for copy in copies(chunk):
            copy.start()

    def body(chunk, carry):
        for copy in copies(chunk):
            copy.wait()
        for half in range(CHUNK // 4):
            right = jnp.zeros((8, 128), F32)
            left = jnp.zeros((8, 128), F32)
            for j in range(4):
                for f, ref in enumerate((q_ref, u_ref, v_ref)):
                    start = 32 * j + 8 * f
                    here = (lane >= start) & (lane < start + 8)
                    x = ref[chunk * CHUNK + half * 4 + j]
                    moved = pltpu.roll(x[:, 128:256], (start - 120) % 128, 1)
                    right = jnp.where(here, moved, right)
                    first = x[:, 0:128]
                    if start:
                        first = pltpu.roll(first, start, 1)
                    left = jnp.where(here, first, left)
            right_ref[chunk * (CHUNK // 4) + half] = right
            left_ref[chunk * (CHUNK // 4) + half] = left
        levels = pl.ds(pl.multiple_of(chunk * CHUNK, CHUNK), CHUNK)
        q = q_ref[levels]
        tend = tendency(q, u_ref[levels], v_ref[levels], row_terms, col_terms)
        tend_ref[levels] = tend
        put_rows(tend, levels, top_ref, bot_ref, 0)
        put_rows(q, levels, top_ref, bot_ref, 1)
        return carry

    lax.fori_loop(0, chunks, body, 0)


def strip_kernel(
    left_ref, right_ref, top_main, bot_main,
    q_ref, u_ref, v_ref, tend_ref, top_ref, bot_ref,
):
    row_terms = derivative_terms((8, 128), 0)
    col_terms = derivative_terms((8, 128), 1)
    lane = iota((8, 128), 1)
    top_ref[:, :, 0:256] = top_main[...]
    bot_ref[:, :, 0:256] = bot_main[...]

    def body(chunk, carry):
        tiles = [[], [], []]
        for half in range(CHUNK // 4):
            west = left_ref[chunk * (CHUNK // 4) + half]
            east = right_ref[chunk * (CHUNK // 4) + half]
            for j in range(4):
                for f in range(3):
                    start = 32 * j + 8 * f
                    a = pltpu.roll(east, 128 - start, 1) if start else east
                    b = pltpu.roll(west, (120 - start) % 128, 1)
                    tiles[f].append(jnp.where(lane < 8, a, jnp.where(lane >= 120, b, 0.0)))
        q, u, v = [jnp.stack(tile, axis=0) for tile in tiles]
        levels = pl.ds(pl.multiple_of(chunk * CHUNK, CHUNK), CHUNK)
        q_ref[levels] = q
        u_ref[levels] = u
        v_ref[levels] = v
        tend = tendency(q, u, v, row_terms, col_terms)
        tend_ref[levels] = tend
        for i, x in enumerate((tend, q)):
            top_ref[i, levels, 256:384] = x[:, 0, :]
            bot_ref[i, levels, 256:384] = x[:, 7, :]
        return carry

    lax.fori_loop(0, q_ref.shape[0] // CHUNK, body, 0)


def assemble_chunk(x, up, down):
    shape = x.shape
    row = iota(shape, 1)
    partner = jnp.where(
        row == 0,
        jnp.broadcast_to(up[:, None, :], shape),
        jnp.where(
            row == 7,
            jnp.broadcast_to(down[:, None, :], shape),
            jnp.where(row == 3, pltpu.roll(x, 7, 1), pltpu.roll(x, 1, 1)),
        ),
    )
    x = jnp.where((row % 4 == 0) | (row % 4 == 3), 0.5 * (x + partner), x)
    col = iota(shape, 2)
    partner = jnp.where(
        col % 4 == 3, pltpu.roll(x, shape[2] - 1, 2), pltpu.roll(x, 1, 2)
    )
    return jnp.where((col % 4 == 0) | (col % 4 == 3), 0.5 * (x + partner), x)


def join(main, strip):
    return jnp.concatenate([main, strip], axis=2)


def second_kernel(
    q_ref, u_ref, v_ref, tend_ref, q_strip, u_strip, v_strip, tend_strip, up_ref, down_ref,
    state_ref, smooth_ref, next_ref, top_ref, bot_ref,
):
    row_terms = derivative_terms((8, 128), 0)
    col_terms = derivative_terms((8, 128), 1)

    def body(chunk, carry):
        levels = pl.ds(pl.multiple_of(chunk * CHUNK, CHUNK), CHUNK)
        q = join(q_ref[levels], q_strip[levels])
        change = assemble_chunk(
            join(tend_ref[levels], tend_strip[levels]), up_ref[0, levels, :], down_ref[0, levels, :]
        )
        smooth = assemble_chunk(q, up_ref[1, levels, :], down_ref[1, levels, :])
        smooth_ref[levels] = smooth[:, :, 0:256]
        state = q + DT_DYN * change
        state_ref[levels] = state[:, :, 0:256]
        tend = tendency(
            state, join(u_ref[levels], u_strip[levels]), join(v_ref[levels], v_strip[levels]),
            row_terms, col_terms,
        )
        next_ref[levels] = tend
        put_rows(tend, levels, top_ref, bot_ref, 0)
        return carry

    lax.fori_loop(0, q_ref.shape[0] // CHUNK, body, 0)


def third_kernel(
    q_ref, state_ref, smooth_ref, tend_ref, up_ref, down_ref, down_map_ref,
    base_ref, cell_ref, near_ref, far_ref,
):
    cols = cell_ref.shape[0]
    half = cols // 2
    phase = iota((8, 256), 0) % 4
    row_weight = jnp.where((phase == 0) | (phase == 3), F32(WEIGHTS[0]), F32(WEIGHTS[1]))
    near_rows = jnp.where(iota((8, 256), 0) < 4, row_weight, 0.0)
    far_rows = row_weight - near_rows

    def body(chunk, carry):
        levels = pl.ds(pl.multiple_of(chunk * CHUNK, CHUNK), CHUNK)
        change = assemble_chunk(tend_ref[levels], up_ref[0, levels, :], down_ref[0, levels, :])
        moved = (state_ref[levels] + DT_DYN * change[:, :, 0:256]) - q_ref[levels]
        base_ref[levels] = smooth_ref[levels] + moved
        near_ref[levels, :] = jnp.sum(moved * near_rows[None], axis=1)
        far_ref[levels, :] = jnp.sum(moved * far_rows[None], axis=1)
        return carry

    lax.fori_loop(0, q_ref.shape[0] // CHUNK, body, 0)
    point = iota((256, cols), 0)
    element = iota((256, cols), 1)
    weight = jnp.where(
        (point % 4 == 0) | (point % 4 == 3), F32(WEIGHTS[0]), F32(WEIGHTS[1])
    ) * F32(0.25 / (DYN_STEPS * DT_DYN))
    near_cols = jnp.where(point // 4 == element, weight, 0.0)
    far_cols = jnp.where(point // 4 + half == element, weight, 0.0)
    means = jnp.dot(near_ref[...], near_cols, precision=HIGH, preferred_element_type=F32)
    means += jnp.dot(far_ref[...], far_cols, precision=HIGH, preferred_element_type=F32)
    forcing = jnp.dot(down_map_ref[...], means, precision=HIGH, preferred_element_type=F32)
    forcing = forcing.T.astype(BF16)
    cells = cell_ref.shape[1]
    spread = (iota((CRM_LEV, cells), 1) // CRM_X == iota((CRM_LEV, cells), 0)).astype(BF16)
    cell_ref[...] = DT_CRM * jnp.dot(forcing, spread, preferred_element_type=F32)


def coef_kernel(collision_ref, table_ref, after_ref, coef_ref):
    total = jnp.dot(collision_ref[...], table_ref[...], preferred_element_type=F32) * DT_CRM
    coarse = total.astype(BF16)
    fine = total - coarse.astype(F32)
    coef_ref[...] = jnp.concatenate([coarse.astype(F32), fine], axis=0).astype(BF16)


def crm_kernel(
    order_ref, count_ref, place_ref, drops_ref, cell_ref, slot_ref, coef_ref, growth_ref,
    final_ref, heat_ref, send_ref, state_ref, pair_ref, twice_ref, heat_cell_ref, echo_cell_ref,
):
    bins = drops_ref.shape[1]
    cells = drops_ref.shape[2]
    cols = drops_ref.shape[0]
    coef = coef_ref[...]
    growth = growth_ref[...]
    state_ref[...] = jnp.zeros(state_ref.shape, F32)
    mass = (iota((40, cells), 0) + 1).astype(F32) / F32(bins)

    def grow(k, which, zero):
        grown = state_ref[k] + growth * cell_ref[pl.ds(which, 1), :]
        for h in range(cells // 128):
            cut = slice(128 * h, 128 * h + 128)
            g = grown[0:32, cut]
            last = grown[32:40, cut]
            twice_ref[2 * k + h, 0:32, :] = g
            twice_ref[2 * k + h, 32:48, :] = g[0:16]
            for d in range(16):
                other = g if d % 8 == 0 else twice_ref[2 * k + h, pl.ds(zero + d, 32), :]
                if d == 8:
                    other = jnp.concatenate([g[8:], g[:8]], axis=0)
                pair_ref[k, 32 * d : 32 * d + 32, cut] = (g * other).astype(BF16)
            pair_ref[k, 512:528, cut] = (g[0:16] * g[16:32]).astype(BF16)
            pair_ref[k, 528:560, cut] = (g * last[0:1]).astype(BF16)
            tail = jnp.concatenate([last * last, jnp.zeros((8, 128), F32)], axis=0)
            pair_ref[k, 560:576, cut] = tail.astype(BF16)
        return grown

    def group(index, carry):
        base = index * GROUP
        which = [order_ref[base + k] for k in range(GROUP)]
        count = [count_ref[base + k] for k in range(GROUP)]
        for k in range(GROUP):
            state_ref[k, 0:bins, :] = drops_ref[which[k]].astype(F32)

        def step(s, c):
            for k in range(GROUP):
                grown = grow(k, which[k], place_ref[3])
                change = jnp.dot(coef, pair_ref[k], preferred_element_type=F32)
                moved = grown + (change[0:40] + change[40:80])
                state_ref[k] = jnp.where(s < count[k], moved, state_ref[k])
            return c

        lax.fori_loop(0, count[0], step, 0)
        for k in range(GROUP):
            final = state_ref[k, 0:bins, :]
            initial = drops_ref[which[k]].astype(F32)
            final_ref[which[k]] = final.astype(BF16)
            weighted = mass[0:bins] * final
            heat = jnp.sum(mass[0:bins] * (final - initial), axis=0, keepdims=True)
            echo = jnp.sum(weighted * weighted, axis=0, keepdims=True)
            heat_cell_ref[pl.ds(which[k], 1), :] = heat
            echo_cell_ref[pl.ds(which[k], 1), :] = echo
        return carry

    lax.fori_loop(0, cols // GROUP, group, 0)
    means = jnp.where(
        iota((CRM_LEV, cells), 1) // CRM_X == iota((CRM_LEV, cells), 0), F32(1.0 / CRM_X), 0.0
    )
    contract = (((1,), (1,)), ((), ()))
    heat = lax.dot_general(
        means, heat_cell_ref[...], contract, precision=HIGH, preferred_element_type=F32
    )
    heat = heat.astype(BF16).astype(F32)
    heat_ref[...] = heat
    echo = lax.dot_general(
        means, echo_cell_ref[...], contract, precision=HIGH, preferred_element_type=F32
    )
    echo = jnp.log(1.0 + echo)

    devices = send_ref.shape[0]
    slots = 2 * cols
    capacity = slots // devices
    onehot = (slot_ref[...] == iota((slots, cols), 0)).astype(F32)
    packed = lax.dot_general(echo, onehot, contract, precision=HIGH, preferred_element_type=F32)
    coarse = packed.astype(BF16).astype(F32)
    rest = packed - coarse
    middle = rest.astype(BF16).astype(F32)
    pieces = (coarse, middle, rest - middle)
    lane = iota((CRM_LEV, 128), 1)
    near = heat
    far = pltpu.roll(heat, 64, 1)
    sides = jnp.where(
        lane == 1, pltpu.roll(heat, 65, 1), jnp.where(lane == 62, pltpu.roll(heat, 63, 1), heat)
    )
    n_gcm = place_ref[1]
    n_crm = place_ref[2]
    for d in range(devices):
        away = d // n_crm - place_ref[0]
        below = (away == 1) | (away == 1 - n_gcm)
        above = (away == -1) | (away == n_gcm - 1)
        block = jnp.where(below, far, jnp.where(above, near, sides))
        tile, offset = divmod(d * capacity, 128)
        for i, piece in enumerate(pieces):
            moved = pltpu.roll(
                piece[:, 128 * tile : 128 * tile + 128], (64 + i * capacity - offset) % 128, 1
            )
            start = 64 + i * capacity
            block = jnp.where((lane >= start) & (lane < start + capacity), moved, block)
        send_ref[d] = block.astype(BF16)


def last_kernel(around_ref, base_ref, own_ref, got_ref, up_map_ref, out_ref, power_ref, *back_refs):
    cols = own_ref.shape[1]
    half = cols // 2
    element = iota((cols, 256), 0)
    col = iota((cols, 256), 1)
    phase = col % 4
    edge = (phase == 0) | (phase == 3)
    other = jnp.where(phase == 0, col // 4 - 1, col // 4 + 1)

    def spread(centre, start, west, west_lane, east, east_lane):
        inside = jnp.where(element == col // 4 + start, jnp.where(edge, 0.5, 1.0), 0.0)
        beside = edge & (element == other + start) & (other >= 0) & (other < half)
        middle = jnp.where(beside, 0.5, inside).astype(BF16)
        from_west = jnp.where((col == 0) & (element == west_lane), 0.5, 0.0).astype(BF16)
        from_east = jnp.where((col == 255) & (element == east_lane), 0.5, 0.0).astype(BF16)
        total = jnp.dot(centre, middle, preferred_element_type=F32)
        total += jnp.dot(west, from_west, preferred_element_type=F32)
        total += jnp.dot(east, from_east, preferred_element_type=F32)
        return total

    own = own_ref[...].astype(BF16)
    up, down, left, right, up_left, up_right, down_left, down_right = [
        got_ref[around_ref[i]] for i in range(8)
    ]
    above = spread(up, 0, up_left, half - 1, up_right, 0)
    near = spread(own, 0, left, half - 1, right, 0)
    far = spread(own, half, left, half - 2, right, 1)
    below = spread(down, 0, down_left, half - 1, down_right, 0)
    parts = (
        0.5 * (above + near), near, 0.5 * (near + far), far, 0.5 * (far + below),
    )
    up_map = up_map_ref[...]
    for part, ref in zip(parts, back_refs):
        ref[...] = DT_PHYS * jnp.dot(up_map, part, precision=HIGH, preferred_element_type=F32)

    devices = got_ref.shape[0]
    slots = power_ref.shape[1]
    capacity = slots // devices
    lane = iota((CRM_LEV, 128), 1)
    tiles = [jnp.zeros((CRM_LEV, 128), F32) for _ in range(slots // 128)]
    for d in range(devices):
        block = got_ref[d].astype(F32)
        fine = pltpu.roll(block, 128 - 2 * capacity, 1) + pltpu.roll(block, 128 - capacity, 1)
        tile, offset = divmod(d * capacity, 128)
        moved = pltpu.roll(block + fine, (offset - 64) % 128, 1)
        tiles[tile] = jnp.where((lane >= offset) & (lane < offset + capacity), moved, tiles[tile])
    power_ref[...] = jnp.concatenate(tiles, axis=1)

    def body(chunk, carry):
        levels = pl.ds(pl.multiple_of(chunk * CHUNK, CHUNK), CHUNK)
        shape = (CHUNK, 8, 256)
        row = iota(shape, 1)
        wide = [jnp.broadcast_to(ref[levels, :][:, None, :], shape) for ref in back_refs]
        back = jnp.where(
            row == 0,
            wide[0],
            jnp.where(
                row < 3,
                wide[1],
                jnp.where(row < 5, wide[2], jnp.where(row < 7, wide[3], wide[4])),
            ),
        )
        out_ref[levels] = base_ref[levels] + back
        return carry

    lax.fori_loop(0, base_ref.shape[0] // CHUNK, body, 0)


def call(kernel, outs, args, scratch=(), sems=(), flops=10_000_000, limit=40):
    spaces = {
        "s": pl.BlockSpec(memory_space=pltpu.SMEM),
        "v": pl.BlockSpec(memory_space=pltpu.VMEM),
        "h": pl.BlockSpec(memory_space=pl.ANY),
    }
    return pl.pallas_call(
        kernel,
        out_shape=[jax.ShapeDtypeStruct(s, t) for s, t in outs],
        in_specs=[spaces[kind] for kind, _ in args],
        out_specs=[spaces["v"]] * len(outs),
        scratch_shapes=[pltpu.VMEM(s, t) for s, t in scratch] + list(sems),
        compiler_params=pltpu.CompilerParams(vmem_limit_bytes=limit * MIB),
        cost_estimate=pl.CostEstimate(flops=flops, bytes_accessed=4_000_000, transcendentals=0),
    )(*[value for _, value in args])


def v(*values):
    return [("v", value) for value in values]


def shift(value, rows, cols):
    n_gcm = lax.axis_size("gcm")
    n_crm = lax.axis_size("crm")
    pairs = []
    for g in range(n_gcm):
        for c in range(n_crm):
            target = ((g + rows) % n_gcm) * n_crm + (c + cols) % n_crm
            pairs.append((g * n_crm + c, target))
    return lax.ppermute(value, ("gcm", "crm"), pairs)


def pair_table(bins):
    table = np.zeros((bins * bins, 576), np.float32)

    def put(column, i, j):
        table[i * bins + j, column] = 1.0
        table[j * bins + i, column] = 1.0

    for d in range(16):
        for b in range(32):
            put(32 * d + b, b, (b + d) % 32)
    for b in range(16):
        put(512 + b, b, b + 16)
    for b in range(32):
        put(528 + b, b, 32)
    put(560, 32, 32)
    return table


def rank_order(counts):
    total = counts.shape[0]
    index = jnp.arange(total, dtype=jnp.int32)
    ahead = (counts[None, :] > counts[:, None]) | (
        (counts[None, :] == counts[:, None]) & (index[None, :] < index[:, None])
    )
    rank = jnp.sum(ahead.astype(jnp.int32), axis=1)
    match = rank[None, :] == index[:, None]
    order = jnp.sum(jnp.where(match, index[None, :], 0), axis=1)
    ordered = jnp.sum(jnp.where(match, counts[None, :], 0), axis=1)
    return order, ordered


def shards(tracer, wind_x, wind_y, drops, owner, counts, collision, growth):
    devices = lax.axis_size("gcm") * lax.axis_size("crm")
    levels, row_count, col_count = tracer.shape
    col_total, bins, cells = drops.shape
    field = (tracer.shape, F32)
    strip = ((levels, row_count, 128), F32)
    rows = ((2, levels, col_count), F32)
    wide = col_count + 128
    down_map, up_map = level_tables(levels, CRM_LEV)

    tend, top, bot, to_right, to_left = call(
        first_kernel,
        [field, rows, rows] + [((levels // 4, 8, 128), F32)] * 2,
        [("h", tracer), ("h", wind_x), ("h", wind_y)],
        [field] * 3,
        [pltpu.SemaphoreType.DMA((3, levels // CHUNK))],
        limit=62,
    )
    from_left = shift(to_right, 0, 1)
    from_right = shift(to_left, 0, -1)
    q_strip, u_strip, v_strip, tend_strip, top, bot = call(
        strip_kernel,
        [strip] * 4 + [((2, levels, wide), F32)] * 2,
        v(from_left, from_right, top, bot),
    )
    (coef,) = call(
        coef_kernel,
        [((80, 576), BF16)],
        v(jnp.pad(collision, ((0, 40 - bins), (0, 0))), jnp.asarray(pair_table(bins), BF16))
        + [("h", top)],
    )
    state, smooth, tend, top, bot = call(
        second_kernel,
        [field, field, ((levels, row_count, wide), F32)] + [((1, levels, wide), F32)] * 2,
        v(tracer, wind_x, wind_y, tend, q_strip, u_strip, v_strip, tend_strip)
        + v(shift(bot, 1, 0), shift(top, -1, 0)),
    )
    base, cell_forcing = call(
        third_kernel,
        [field, ((col_total, cells), F32)],
        v(tracer, state, smooth, tend, shift(bot, 1, 0), shift(top, -1, 0))
        + v(jnp.asarray(down_map, F32)),
        [((levels, col_count), F32), ((levels, col_count), F32)],
    )

    capacity = 2 * col_total // devices
    owners = owner[:, 0]
    index = jnp.arange(col_total, dtype=jnp.int32)
    same = (owners[:, None] == owners[None, :]) & (index[:, None] < index[None, :])
    slot_of = owners * capacity + jnp.sum(same.astype(jnp.int32), axis=0)
    order, ordered = rank_order(counts)
    growth_rows = jnp.broadcast_to(jnp.pad(growth, (0, 40 - bins))[:, None], (40, cells))
    n_gcm = lax.axis_size("gcm")
    n_crm = lax.axis_size("crm")
    g = lax.axis_index("gcm").astype(jnp.int32)
    c = lax.axis_index("crm").astype(jnp.int32)
    place = jnp.stack([g, jnp.int32(n_gcm), jnp.int32(n_crm), jnp.int32(0)])

    final, heat, send = call(
        crm_kernel,
        [((col_total, bins, cells), BF16), ((CRM_LEV, col_total), F32),
         ((devices, CRM_LEV, 128), BF16)],
        [("s", order), ("s", ordered), ("s", place)]
        + v(drops, cell_forcing, slot_of[None, :], coef, growth_rows),
        [((GROUP, 40, cells), F32), ((GROUP, 576, cells), BF16),
         ((2 * GROUP, 48, 128), F32),
         ((col_total, cells), F32), ((col_total, cells), F32)],
        flops=10_000_000_000,
    )
    got = lax.all_to_all(send, ("gcm", "crm"), split_axis=0, concat_axis=0, tiled=True)
    up = (g + n_gcm - 1) % n_gcm * n_crm
    same_row = g * n_crm
    down = (g + 1) % n_gcm * n_crm
    west = (c + n_crm - 1) % n_crm
    east = (c + 1) % n_crm
    around = jnp.stack(
        [up + c, down + c, same_row + west, same_row + east,
         up + west, up + east, down + west, down + east]
    )
    tracer_next, power = call(
        last_kernel,
        [field, ((CRM_LEV, devices * capacity), F32)],
        [("s", around)] + v(base, heat, got, jnp.asarray(up_map, F32)),
        [((levels, col_count), F32)] * 5,
    )
    return (tracer_next, final, power)


def solution(mesh):
    return jax.shard_map(
        shards,
        mesh=mesh,
        in_specs=(
            P(None, "gcm", "crm"),
            P(None, "gcm", "crm"),
            P(None, "gcm", "crm"),
            P(("gcm", "crm"), None, None),
            P(("gcm", "crm"), None),
            P(("gcm", "crm")),
            P(),
            P(),
        ),
        out_specs=(P(None, "gcm", "crm"), P(("gcm", "crm"), None, None), P(None, ("gcm", "crm"))),
        check_vma=False,
    )
```

```python
import functools

import jax
import jax.numpy as jnp
import numpy as np
from jax import lax
from jax.experimental import pallas as pl
from jax.experimental.pallas import tpu as pltpu
from jax.sharding import PartitionSpec as P

CRM_X = 16
CRM_LEV = 16
DYN_STEPS = 2

DT_DYN = 0.04
DT_CRM = 0.05
DT_PHYS = 0.5
HIGH = lax.Precision.HIGHEST
F32 = jnp.float32
BF16 = jnp.bfloat16
GROUP = 8
CHUNK = 8
MIB = 1024 * 1024


def gll_tables():
    inv_root = 1.0 / np.sqrt(5.0)
    gll_nodes = np.array([-1.0, -inv_root, inv_root, 1.0])
    weights = np.array([1.0, 5.0, 5.0, 1.0]) / 6.0
    legendre = (5.0 * gll_nodes**3 - 3.0 * gll_nodes) / 2.0
    derivative = np.zeros((4, 4))
    for i in range(4):
        for j in range(4):
            if i != j:
                derivative[i, j] = legendre[i] / (legendre[j] * (gll_nodes[i] - gll_nodes[j]))
    derivative[0, 0] = -3.0
    derivative[3, 3] = 3.0
    return (2.0 * derivative, weights)


def level_tables(levels, crm_levels):
    spacing = levels / crm_levels
    centres = (np.arange(crm_levels) + 0.5) * spacing - 0.5
    hats = np.maximum(0.0, 1.0 - np.abs(np.arange(levels)[None, :] - centres[:, None]) / spacing)
    down_map = hats / hats.sum(axis=1, keepdims=True)
    up_map = hats.T / hats.T.sum(axis=1, keepdims=True)
    return (down_map, up_map)


DERIV, WEIGHTS = gll_tables()


def iota(shape, axis):
    return lax.broadcasted_iota(jnp.int32, shape, axis)


def derivative_terms(shape, axis):
    phase = iota(shape, axis) % 4
    terms = []
    for shift in range(-3, 4):
        value = jnp.zeros(shape, F32)
        for i in range(4):
            if 0 <= i + shift < 4:
                value = jnp.where(phase == i, F32(DERIV[i, i + shift]), value)
        terms.append((shift, value))
    return terms


def along(x, terms, axis):
    size = x.shape[axis]
    total = None
    for shift, value in terms:
        moved = x if shift == 0 else pltpu.roll(x, (-shift) % size, axis)
        part = value[None] * moved
        total = part if total is None else total + part
    return total


def tendency(x, u, v, row_terms, col_terms):
    halves = []
    for h in range(x.shape[2] // 128):
        cut = slice(128 * h, 128 * h + 128)
        q = x[:, :, cut]
        grad_x = along(q, row_terms, 1)
        grad_y = along(q, col_terms, 2)
        halves.append(-(u[:, :, cut] * grad_x + v[:, :, cut] * grad_y))
    return jnp.concatenate(halves, axis=2)


def put_rows(x, levels, top_ref, bot_ref, i):
    top_ref[i, levels, :] = x[:, 0, :]
    bot_ref[i, levels, :] = x[:, 7, :]


def first_kernel(
    q_hbm, u_hbm, v_hbm, tend_ref, top_ref, bot_ref, right_ref, left_ref, q_ref, u_ref, v_ref, sems
):
    row_terms = derivative_terms((8, 128), 0)
    col_terms = derivative_terms((8, 128), 1)
    lane = iota((8, 128), 1)
    chunks = q_ref.shape[0] // CHUNK

    def copies(chunk):
        levels = pl.ds(pl.multiple_of(chunk * CHUNK, CHUNK), CHUNK)
        return [
            pltpu.make_async_copy(src.at[levels], dst.at[levels], sems.at[i, chunk])
            for i, (src, dst) in enumerate(((q_hbm, q_ref), (u_hbm, u_ref), (v_hbm, v_ref)))
        ]

    for chunk in range(chunks):
        for copy in copies(chunk):
            copy.start()

    def body(chunk, carry):
        for copy in copies(chunk):
            copy.wait()
        for half in range(CHUNK // 4):
            right = jnp.zeros((8, 128), F32)
            left = jnp.zeros((8, 128), F32)
            for j in range(4):
                for f, ref in enumerate((q_ref, u_ref, v_ref)):
                    start = 32 * j + 8 * f
                    here = (lane >= start) & (lane < start + 8)
                    x = ref[chunk * CHUNK + half * 4 + j]
                    moved = pltpu.roll(x[:, 128:256], (start - 120) % 128, 1)
                    right = jnp.where(here, moved, right)
                    first = x[:, 0:128]
                    if start:
                        first = pltpu.roll(first, start, 1)
                    left = jnp.where(here, first, left)
            right_ref[chunk * (CHUNK // 4) + half] = right
            left_ref[chunk * (CHUNK // 4) + half] = left
        levels = pl.ds(pl.multiple_of(chunk * CHUNK, CHUNK), CHUNK)
        q = q_ref[levels]
        tend = tendency(q, u_ref[levels], v_ref[levels], row_terms, col_terms)
        tend_ref[levels] = tend
        put_rows(tend, levels, top_ref, bot_ref, 0)
        put_rows(q, levels, top_ref, bot_ref, 1)
        return carry

    lax.fori_loop(0, chunks, body, 0)


def strip_kernel(
    left_ref, right_ref, top_main, bot_main,
    q_ref, u_ref, v_ref, tend_ref, top_ref, bot_ref,
):
    row_terms = derivative_terms((8, 128), 0)
    col_terms = derivative_terms((8, 128), 1)
    lane = iota((8, 128), 1)
    top_ref[:, :, 0:256] = top_main[...]
    bot_ref[:, :, 0:256] = bot_main[...]

    def body(chunk, carry):
        tiles = [[], [], []]
        for half in range(CHUNK // 4):
            west = left_ref[chunk * (CHUNK // 4) + half]
            east = right_ref[chunk * (CHUNK // 4) + half]
            for j in range(4):
                for f in range(3):
                    start = 32 * j + 8 * f
                    a = pltpu.roll(east, 128 - start, 1) if start else east
                    b = pltpu.roll(west, (120 - start) % 128, 1)
                    tiles[f].append(jnp.where(lane < 8, a, jnp.where(lane >= 120, b, 0.0)))
        q, u, v = [jnp.stack(tile, axis=0) for tile in tiles]
        levels = pl.ds(pl.multiple_of(chunk * CHUNK, CHUNK), CHUNK)
        q_ref[levels] = q
        u_ref[levels] = u
        v_ref[levels] = v
        tend = tendency(q, u, v, row_terms, col_terms)
        tend_ref[levels] = tend
        for i, x in enumerate((tend, q)):
            top_ref[i, levels, 256:384] = x[:, 0, :]
            bot_ref[i, levels, 256:384] = x[:, 7, :]
        return carry

    lax.fori_loop(0, q_ref.shape[0] // CHUNK, body, 0)


def assemble_chunk(x, up, down):
    shape = x.shape
    row = iota(shape, 1)
    partner = jnp.where(
        row == 0,
        jnp.broadcast_to(up[:, None, :], shape),
        jnp.where(
            row == 7,
            jnp.broadcast_to(down[:, None, :], shape),
            jnp.where(row == 3, pltpu.roll(x, 7, 1), pltpu.roll(x, 1, 1)),
        ),
    )
    x = jnp.where((row % 4 == 0) | (row % 4 == 3), 0.5 * (x + partner), x)
    col = iota(shape, 2)
    partner = jnp.where(
        col % 4 == 3, pltpu.roll(x, shape[2] - 1, 2), pltpu.roll(x, 1, 2)
    )
    return jnp.where((col % 4 == 0) | (col % 4 == 3), 0.5 * (x + partner), x)


def join(main, strip):
    return jnp.concatenate([main, strip], axis=2)


def second_kernel(
    q_ref, u_ref, v_ref, tend_ref, q_strip, u_strip, v_strip, tend_strip, up_ref, down_ref,
    state_ref, smooth_ref, next_ref, top_ref, bot_ref,
):
    row_terms = derivative_terms((8, 128), 0)
    col_terms = derivative_terms((8, 128), 1)

    def body(chunk, carry):
        levels = pl.ds(pl.multiple_of(chunk * CHUNK, CHUNK), CHUNK)
        q = join(q_ref[levels], q_strip[levels])
        change = assemble_chunk(
            join(tend_ref[levels], tend_strip[levels]), up_ref[0, levels, :], down_ref[0, levels, :]
        )
        smooth = assemble_chunk(q, up_ref[1, levels, :], down_ref[1, levels, :])
        smooth_ref[levels] = smooth[:, :, 0:256]
        state = q + DT_DYN * change
        state_ref[levels] = state[:, :, 0:256]
        tend = tendency(
            state, join(u_ref[levels], u_strip[levels]), join(v_ref[levels], v_strip[levels]),
            row_terms, col_terms,
        )
        next_ref[levels] = tend
        put_rows(tend, levels, top_ref, bot_ref, 0)
        return carry

    lax.fori_loop(0, q_ref.shape[0] // CHUNK, body, 0)


def third_kernel(
    q_ref, state_ref, smooth_ref, tend_ref, up_ref, down_ref, down_map_ref,
    base_ref, forcing_ref, near_ref, far_ref,
):
    cols = forcing_ref.shape[1]
    half = cols // 2
    phase = iota((8, 256), 0) % 4
    row_weight = jnp.where((phase == 0) | (phase == 3), F32(WEIGHTS[0]), F32(WEIGHTS[1]))
    near_rows = jnp.where(iota((8, 256), 0) < 4, row_weight, 0.0)
    far_rows = row_weight - near_rows

    def body(chunk, carry):
        levels = pl.ds(pl.multiple_of(chunk * CHUNK, CHUNK), CHUNK)
        change = assemble_chunk(tend_ref[levels], up_ref[0, levels, :], down_ref[0, levels, :])
        moved = (state_ref[levels] + DT_DYN * change[:, :, 0:256]) - q_ref[levels]
        base_ref[levels] = smooth_ref[levels] + moved
        near_ref[levels, :] = jnp.sum(moved * near_rows[None], axis=1)
        far_ref[levels, :] = jnp.sum(moved * far_rows[None], axis=1)
        return carry

    lax.fori_loop(0, q_ref.shape[0] // CHUNK, body, 0)
    point = iota((256, cols), 0)
    element = iota((256, cols), 1)
    weight = jnp.where(
        (point % 4 == 0) | (point % 4 == 3), F32(WEIGHTS[0]), F32(WEIGHTS[1])
    ) * F32(0.25 / (DYN_STEPS * DT_DYN))
    near_cols = jnp.where(point // 4 == element, weight, 0.0)
    far_cols = jnp.where(point // 4 + half == element, weight, 0.0)
    means = jnp.dot(near_ref[...], near_cols, precision=HIGH, preferred_element_type=F32)
    means += jnp.dot(far_ref[...], far_cols, precision=HIGH, preferred_element_type=F32)
    forcing = jnp.dot(down_map_ref[...], means, precision=HIGH, preferred_element_type=F32)
    forcing_ref[...] = forcing.astype(BF16).astype(F32)


def coef_kernel(collision_ref, table_ref, after_ref, coef_ref):
    total = jnp.dot(collision_ref[...], table_ref[...], preferred_element_type=F32) * DT_CRM
    coarse = total.astype(BF16)
    fine = total - coarse.astype(F32)
    coef_ref[...] = jnp.concatenate([coarse.astype(F32), fine], axis=0).astype(BF16)


def rank_row(values):
    total = values.shape[1]
    across = jnp.broadcast_to(values, (total, total))
    down = across.T
    earlier = iota((total, total), 0) < iota((total, total), 1)
    ahead = (down > across) | ((down == across) & earlier)
    return jnp.sum(ahead.astype(F32), axis=0, keepdims=True)


def plan_kernel(
    capacity, count_ref, other_ref, owner_ref,
    sent_ref, order_ref, force_ref, ordered_ref, rank_ref, slot_ref,
):
    cols = count_ref.shape[1]
    counts = count_ref[...].astype(F32)
    others = other_ref[...].astype(F32)
    rank = rank_row(counts)
    other_rank = rank_row(others)
    square = (cols, cols)
    index = iota(square, 0).astype(F32)
    odd = 2.0 * iota(square, 1).astype(F32) + 1.0
    down_rank = jnp.broadcast_to(rank, square).T
    sent = jnp.sum(jnp.where(down_rank == odd, index, 0.0), axis=0, keepdims=True)
    sent_ref[...] = sent.astype(jnp.int32)
    rank_ref[...] = rank.astype(jnp.int32)

    is_odd = rank.astype(jnp.int32) % 2 == 1
    other_odd = other_rank.astype(jnp.int32) % 2 == 1
    listed = jnp.concatenate(
        [jnp.where(is_odd, -1.0, counts), jnp.where(other_odd, others, -1.0)], axis=1
    )
    lane = iota((1, cols), 1).astype(F32)
    name = jnp.concatenate([lane, cols + 0.5 * (other_rank - 1.0)], axis=1)
    wide = (2 * cols, 2 * cols)
    place = jnp.broadcast_to(rank_row(listed), wide).T[:, 0:cols]
    here = place == iota((2 * cols, cols), 1).astype(F32)
    force = iota((2 * cols, cols), 0).astype(F32)
    name = jnp.broadcast_to(name, wide).T[:, 0:cols]
    value = jnp.broadcast_to(listed, wide).T[:, 0:cols]
    for what, ref in ((name, order_ref), (force, force_ref), (value, ordered_ref)):
        total = jnp.sum(jnp.where(here, what, 0.0), axis=0, keepdims=True)
        ref[...] = total.astype(jnp.int32)

    owners = jnp.broadcast_to(owner_ref[...].astype(F32), square)
    same = (owners.T == owners) & (iota(square, 0) < iota(square, 1))
    earlier = jnp.sum(same.astype(F32), axis=0, keepdims=True)
    slot_ref[...] = owner_ref[...] * capacity + earlier.astype(jnp.int32)


def gather_kernel(sent_ref, drops_ref, out_ref):
    def body(p, carry):
        out_ref[p] = drops_ref[sent_ref[0, p]]
        return carry

    lax.fori_loop(0, out_ref.shape[0], body, 0)


def merge_kernel(sent_ref, final_ref, back_ref, out_ref):
    out_ref[...] = final_ref[...]

    def body(p, carry):
        out_ref[sent_ref[0, p]] = back_ref[p]
        return carry

    lax.fori_loop(0, back_ref.shape[0], body, 0)


def crm_kernel(
    order_ref, force_ref, count_ref, place_ref,
    drops_ref, guest_ref, forcing_ref, other_ref, coef_ref, growth_ref,
    final_ref, back_ref, own_ref, away_ref,
    state_ref, start_ref, pair_ref, twice_ref, cell_ref, heat_cell_ref, echo_cell_ref,
):
    bins = drops_ref.shape[1]
    cells = drops_ref.shape[2]
    cols = drops_ref.shape[0]
    guests = guest_ref.shape[0]
    coef = coef_ref[...]
    growth = growth_ref[...]
    state_ref[...] = jnp.zeros(state_ref.shape, F32)
    heat_cell_ref[...] = jnp.zeros(heat_cell_ref.shape, F32)
    echo_cell_ref[...] = jnp.zeros(echo_cell_ref.shape, F32)
    mass = (iota((40, cells), 0) + 1).astype(F32) / F32(bins)
    spread = (iota((CRM_LEV, cells), 1) // CRM_X == iota((CRM_LEV, cells), 0)).astype(BF16)
    for i, ref in enumerate((forcing_ref, other_ref)):
        rows = jnp.dot(ref[...].T.astype(BF16), spread, preferred_element_type=F32)
        cell_ref[cols * i : cols * i + cols, :] = DT_CRM * rows

    def grow(k, which, zero):
        grown = state_ref[k] + growth * cell_ref[pl.ds(which, 1), :]
        for h in range(cells // 128):
            cut = slice(128 * h, 128 * h + 128)
            g = grown[0:32, cut]
            last = grown[32:40, cut]
            twice_ref[2 * k + h, 0:32, :] = g
            twice_ref[2 * k + h, 32:48, :] = g[0:16]
            for d in range(16):
                other = g if d % 8 == 0 else twice_ref[2 * k + h, pl.ds(zero + d, 32), :]
                if d == 8:
                    other = jnp.concatenate([g[8:], g[:8]], axis=0)
                pair_ref[k, 32 * d : 32 * d + 32, cut] = (g * other).astype(BF16)
            pair_ref[k, 512:528, cut] = (g[0:16] * g[16:32]).astype(BF16)
            pair_ref[k, 528:560, cut] = (g * last[0:1]).astype(BF16)
            tail = jnp.concatenate([last * last, jnp.zeros((8, 128), F32)], axis=0)
            pair_ref[k, 560:576, cut] = tail.astype(BF16)
        return grown

    def group(index, carry):
        base = index * GROUP
        which = [order_ref[0, base + k] for k in range(GROUP)]
        force = [force_ref[0, base + k] for k in range(GROUP)]
        count = [count_ref[0, base + k] for k in range(GROUP)]
        for k in range(GROUP):
            mine = drops_ref[jnp.minimum(which[k], cols - 1)].astype(F32)
            guest = guest_ref[jnp.clip(which[k] - cols, 0, guests - 1)].astype(F32)
            start = jnp.where(which[k] < cols, mine, guest)
            start_ref[k, 0:bins, :] = start
            state_ref[k, 0:bins, :] = start

        def step(s, c):
            for k in range(GROUP):
                grown = grow(k, force[k], place_ref[3])
                change = jnp.dot(coef, pair_ref[k], preferred_element_type=F32)
                moved = grown + (change[0:40] + change[40:80])
                state_ref[k] = jnp.where(s < count[k], moved, state_ref[k])
            return c

        lax.fori_loop(0, count[0], step, 0)
        for k in range(GROUP):
            final = state_ref[k, 0:bins, :]
            weighted = mass[0:bins] * final
            heat = jnp.sum(mass[0:bins] * (final - start_ref[k, 0:bins, :]), axis=0, keepdims=True)
            echo = jnp.sum(weighted * weighted, axis=0, keepdims=True)
            heat_cell_ref[pl.ds(which[k], 1), :] = heat
            echo_cell_ref[pl.ds(which[k], 1), :] = echo

            @pl.when(which[k] < cols)
            def _():
                final_ref[jnp.minimum(which[k], cols - 1)] = state_ref[k, 0:bins, :].astype(BF16)

            @pl.when(which[k] >= cols)
            def _():
                row = jnp.clip(which[k] - cols, 0, guests - 1)
                back_ref[row] = state_ref[k, 0:bins, :].astype(BF16)

        return carry

    lax.fori_loop(0, cols // GROUP, group, 0)
    means = jnp.where(
        iota((CRM_LEV, cells), 1) // CRM_X == iota((CRM_LEV, cells), 0), F32(1.0 / CRM_X), 0.0
    )
    contract = (((1,), (1,)), ((), ()))
    heat = lax.dot_general(
        means, heat_cell_ref[...], contract, precision=HIGH, preferred_element_type=F32
    )
    heat = heat.astype(BF16).astype(F32)
    echo = lax.dot_general(
        means, echo_cell_ref[...], contract, precision=HIGH, preferred_element_type=F32
    )
    both = jnp.concatenate([heat, jnp.log(1.0 + echo)], axis=0)
    own_ref[...] = both[:, 0:cols]
    away_ref[...] = both[:, cols : 2 * cols]


def block_kernel(place_ref, own_ref, back_ref, rank_ref, slot_ref, heat_ref, send_ref):
    cols = own_ref.shape[1]
    odd = 2 * iota((cols, cols), 0) + 1
    home = (rank_ref[...] == odd).astype(F32)
    both = own_ref[...] + jnp.dot(
        back_ref[...], home, precision=HIGH, preferred_element_type=F32
    )
    heat = both[0:CRM_LEV]
    echo = both[CRM_LEV:]
    heat_ref[...] = heat
    contract = (((1,), (1,)), ((), ()))
    devices = send_ref.shape[0]
    slots = 2 * cols
    capacity = slots // devices
    onehot = (slot_ref[...] == iota((slots, cols), 0)).astype(F32)
    packed = lax.dot_general(echo, onehot, contract, precision=HIGH, preferred_element_type=F32)
    coarse = packed.astype(BF16).astype(F32)
    rest = packed - coarse
    middle = rest.astype(BF16).astype(F32)
    pieces = (coarse, middle, rest - middle)
    lane = iota((CRM_LEV, 128), 1)
    near = heat
    far = pltpu.roll(heat, 64, 1)
    sides = jnp.where(
        lane == 1, pltpu.roll(heat, 65, 1), jnp.where(lane == 62, pltpu.roll(heat, 63, 1), heat)
    )
    n_gcm = place_ref[1]
    n_crm = place_ref[2]
    for d in range(devices):
        away = d // n_crm - place_ref[0]
        below = (away == 1) | (away == 1 - n_gcm)
        above = (away == -1) | (away == n_gcm - 1)
        block = jnp.where(below, far, jnp.where(above, near, sides))
        tile, offset = divmod(d * capacity, 128)
        for i, piece in enumerate(pieces):
            moved = pltpu.roll(
                piece[:, 128 * tile : 128 * tile + 128], (64 + i * capacity - offset) % 128, 1
            )
            start = 64 + i * capacity
            block = jnp.where((lane >= start) & (lane < start + capacity), moved, block)
        send_ref[d] = block.astype(BF16)


def last_kernel(around_ref, base_ref, own_ref, got_ref, up_map_ref, out_ref, power_ref, *back_refs):
    cols = own_ref.shape[1]
    half = cols // 2
    element = iota((cols, 256), 0)
    col = iota((cols, 256), 1)
    phase = col % 4
    edge = (phase == 0) | (phase == 3)
    other = jnp.where(phase == 0, col // 4 - 1, col // 4 + 1)

    def spread(centre, start, west, west_lane, east, east_lane):
        inside = jnp.where(element == col // 4 + start, jnp.where(edge, 0.5, 1.0), 0.0)
        beside = edge & (element == other + start) & (other >= 0) & (other < half)
        middle = jnp.where(beside, 0.5, inside).astype(BF16)
        from_west = jnp.where((col == 0) & (element == west_lane), 0.5, 0.0).astype(BF16)
        from_east = jnp.where((col == 255) & (element == east_lane), 0.5, 0.0).astype(BF16)
        total = jnp.dot(centre, middle, preferred_element_type=F32)
        total += jnp.dot(west, from_west, preferred_element_type=F32)
        total += jnp.dot(east, from_east, preferred_element_type=F32)
        return total

    own = own_ref[...].astype(BF16)
    up, down, left, right, up_left, up_right, down_left, down_right = [
        got_ref[around_ref[i]] for i in range(8)
    ]
    above = spread(up, 0, up_left, half - 1, up_right, 0)
    near = spread(own, 0, left, half - 1, right, 0)
    far = spread(own, half, left, half - 2, right, 1)
    below = spread(down, 0, down_left, half - 1, down_right, 0)
    parts = (
        0.5 * (above + near), near, 0.5 * (near + far), far, 0.5 * (far + below),
    )
    up_map = up_map_ref[...]
    for part, ref in zip(parts, back_refs):
        ref[...] = DT_PHYS * jnp.dot(up_map, part, precision=HIGH, preferred_element_type=F32)

    devices = got_ref.shape[0]
    slots = power_ref.shape[1]
    capacity = slots // devices
    lane = iota((CRM_LEV, 128), 1)
    tiles = [jnp.zeros((CRM_LEV, 128), F32) for _ in range(slots // 128)]
    for d in range(devices):
        block = got_ref[d].astype(F32)
        fine = pltpu.roll(block, 128 - 2 * capacity, 1) + pltpu.roll(block, 128 - capacity, 1)
        tile, offset = divmod(d * capacity, 128)
        moved = pltpu.roll(block + fine, (offset - 64) % 128, 1)
        tiles[tile] = jnp.where((lane >= offset) & (lane < offset + capacity), moved, tiles[tile])
    power_ref[...] = jnp.concatenate(tiles, axis=1)

    def body(chunk, carry):
        levels = pl.ds(pl.multiple_of(chunk * CHUNK, CHUNK), CHUNK)
        shape = (CHUNK, 8, 256)
        row = iota(shape, 1)
        wide = [jnp.broadcast_to(ref[levels, :][:, None, :], shape) for ref in back_refs]
        back = jnp.where(
            row == 0,
            wide[0],
            jnp.where(
                row < 3,
                wide[1],
                jnp.where(row < 5, wide[2], jnp.where(row < 7, wide[3], wide[4])),
            ),
        )
        out_ref[levels] = base_ref[levels] + back
        return carry

    lax.fori_loop(0, base_ref.shape[0] // CHUNK, body, 0)


def call(kernel, outs, args, scratch=(), sems=(), flops=10_000_000, limit=40):
    spaces = {
        "s": pl.BlockSpec(memory_space=pltpu.SMEM),
        "v": pl.BlockSpec(memory_space=pltpu.VMEM),
        "h": pl.BlockSpec(memory_space=pl.ANY),
    }
    return pl.pallas_call(
        kernel,
        out_shape=[jax.ShapeDtypeStruct(s, t) for s, t in outs],
        in_specs=[spaces[kind] for kind, _ in args],
        out_specs=[spaces["v"]] * len(outs),
        scratch_shapes=[pltpu.VMEM(s, t) for s, t in scratch] + list(sems),
        compiler_params=pltpu.CompilerParams(vmem_limit_bytes=limit * MIB),
        cost_estimate=pl.CostEstimate(flops=flops, bytes_accessed=4_000_000, transcendentals=0),
    )(*[value for _, value in args])


def v(*values):
    return [("v", value) for value in values]


def shift(value, rows, cols):
    n_gcm = lax.axis_size("gcm")
    n_crm = lax.axis_size("crm")
    pairs = []
    for g in range(n_gcm):
        for c in range(n_crm):
            target = ((g + rows) % n_gcm) * n_crm + (c + cols) % n_crm
            pairs.append((g * n_crm + c, target))
    return lax.ppermute(value, ("gcm", "crm"), pairs)


def pair_table(bins):
    table = np.zeros((bins * bins, 576), np.float32)

    def put(column, i, j):
        table[i * bins + j, column] = 1.0
        table[j * bins + i, column] = 1.0

    for d in range(16):
        for b in range(32):
            put(32 * d + b, b, (b + d) % 32)
    for b in range(16):
        put(512 + b, b, b + 16)
    for b in range(32):
        put(528 + b, b, 32)
    put(560, 32, 32)
    return table


def to_partner(value):
    n_gcm = lax.axis_size("gcm")
    n_crm = lax.axis_size("crm")
    pairs = []
    for g in range(n_gcm):
        for c in range(n_crm):
            pairs.append((g * n_crm + c, (g ^ 1) * n_crm + c))
    return lax.ppermute(value, ("gcm", "crm"), pairs)


def shards(tracer, wind_x, wind_y, drops, owner, counts, collision, growth):
    devices = lax.axis_size("gcm") * lax.axis_size("crm")
    levels, row_count, col_count = tracer.shape
    col_total, bins, cells = drops.shape
    field = (tracer.shape, F32)
    strip = ((levels, row_count, 128), F32)
    rows = ((2, levels, col_count), F32)
    wide = col_count + 128
    down_map, up_map = level_tables(levels, CRM_LEV)

    row = ((1, col_total), jnp.int32)
    capacity = 2 * col_total // devices
    guests = col_total // 2
    count_row = counts[None, :]
    other_counts = to_partner(count_row)
    tend, top, bot, to_right, to_left = call(
        first_kernel,
        [field, rows, rows] + [((levels // 4, 8, 128), F32)] * 2,
        [("h", tracer), ("h", wind_x), ("h", wind_y)],
        [field] * 3,
        [pltpu.SemaphoreType.DMA((3, levels // CHUNK))],
        limit=62,
    )
    from_left = shift(to_right, 0, 1)
    from_right = shift(to_left, 0, -1)
    sent, order, force, ordered, rank, slot = call(
        functools.partial(plan_kernel, capacity),
        [row] * 6,
        v(count_row, other_counts, owner.T),
    )
    (leaving,) = call(
        gather_kernel,
        [((guests, bins, cells), BF16)],
        [("s", sent)] + v(drops),
    )
    guest_drops = to_partner(leaving)
    q_strip, u_strip, v_strip, tend_strip, top, bot = call(
        strip_kernel,
        [strip] * 4 + [((2, levels, wide), F32)] * 2,
        v(from_left, from_right, top, bot),
    )
    (coef,) = call(
        coef_kernel,
        [((80, 576), BF16)],
        v(jnp.pad(collision, ((0, 40 - bins), (0, 0))), jnp.asarray(pair_table(bins), BF16))
        + [("h", top)],
    )
    state, smooth, tend, top, bot = call(
        second_kernel,
        [field, field, ((levels, row_count, wide), F32)] + [((1, levels, wide), F32)] * 2,
        v(tracer, wind_x, wind_y, tend, q_strip, u_strip, v_strip, tend_strip)
        + v(shift(bot, 1, 0), shift(top, -1, 0)),
    )
    base, forcing = call(
        third_kernel,
        [field, ((CRM_LEV, col_total), F32)],
        v(tracer, state, smooth, tend, shift(bot, 1, 0), shift(top, -1, 0))
        + v(jnp.asarray(down_map, F32)),
        [((levels, col_count), F32), ((levels, col_count), F32)],
    )

    other_forcing = to_partner(forcing)
    growth_rows = jnp.broadcast_to(jnp.pad(growth, (0, 40 - bins))[:, None], (40, cells))
    n_gcm = lax.axis_size("gcm")
    n_crm = lax.axis_size("crm")
    g = lax.axis_index("gcm").astype(jnp.int32)
    c = lax.axis_index("crm").astype(jnp.int32)
    place = jnp.stack([g, jnp.int32(n_gcm), jnp.int32(n_crm), jnp.int32(0)])

    pairs = ((2 * CRM_LEV, col_total), F32)
    final, back, own, away = call(
        crm_kernel,
        [((col_total, bins, cells), BF16), ((guests, bins, cells), BF16), pairs, pairs],
        [("s", order), ("s", force), ("s", ordered), ("s", place)]
        + v(drops, guest_drops, forcing, other_forcing, coef, growth_rows),
        [((GROUP, 40, cells), F32), ((GROUP, 40, cells), F32), ((GROUP, 576, cells), BF16),
         ((2 * GROUP, 48, 128), F32), ((2 * col_total, cells), F32),
         ((2 * col_total, cells), F32), ((2 * col_total, cells), F32)],
        flops=10_000_000_000,
    )
    returned = to_partner(away)
    returned_drops = to_partner(back)
    heat, send = call(
        block_kernel,
        [((CRM_LEV, col_total), F32), ((devices, CRM_LEV, 128), BF16)],
        [("s", place)] + v(own, returned, rank, slot),
    )
    got = lax.all_to_all(send, ("gcm", "crm"), split_axis=0, concat_axis=0, tiled=True)
    (drops_next,) = call(
        merge_kernel,
        [((col_total, bins, cells), BF16)],
        [("s", sent)] + v(final, returned_drops),
    )
    up = (g + n_gcm - 1) % n_gcm * n_crm
    same_row = g * n_crm
    down = (g + 1) % n_gcm * n_crm
    west = (c + n_crm - 1) % n_crm
    east = (c + 1) % n_crm
    around = jnp.stack(
        [up + c, down + c, same_row + west, same_row + east,
         up + west, up + east, down + west, down + east]
    )
    tracer_next, power = call(
        last_kernel,
        [field, ((CRM_LEV, devices * capacity), F32)],
        [("s", around)] + v(base, heat, got, jnp.asarray(up_map, F32)),
        [((levels, col_count), F32)] * 5,
    )
    return (tracer_next, drops_next, power)


def solution(mesh):
    return jax.shard_map(
        shards,
        mesh=mesh,
        in_specs=(
            P(None, "gcm", "crm"),
            P(None, "gcm", "crm"),
            P(None, "gcm", "crm"),
            P(("gcm", "crm"), None, None),
            P(("gcm", "crm"), None),
            P(("gcm", "crm")),
            P(),
            P(),
        ),
        out_specs=(P(None, "gcm", "crm"), P(("gcm", "crm"), None, None), P(None, ("gcm", "crm"))),
        check_vma=False,
    )
```

```python
import functools

import jax
import jax.numpy as jnp
import numpy as np
from jax import lax
from jax.experimental import pallas as pl
from jax.experimental.pallas import tpu as pltpu
from jax.sharding import PartitionSpec as P

CRM_X = 16
CRM_LEV = 16
DYN_STEPS = 2

DT_DYN = 0.04
DT_CRM = 0.05
DT_PHYS = 0.5
HIGH = lax.Precision.HIGHEST
F32 = jnp.float32
BF16 = jnp.bfloat16
GROUP = 8
CHUNK = 8
MIB = 1024 * 1024


def gll_tables():
    inv_root = 1.0 / np.sqrt(5.0)
    gll_nodes = np.array([-1.0, -inv_root, inv_root, 1.0])
    weights = np.array([1.0, 5.0, 5.0, 1.0]) / 6.0
    legendre = (5.0 * gll_nodes**3 - 3.0 * gll_nodes) / 2.0
    derivative = np.zeros((4, 4))
    for i in range(4):
        for j in range(4):
            if i != j:
                derivative[i, j] = legendre[i] / (legendre[j] * (gll_nodes[i] - gll_nodes[j]))
    derivative[0, 0] = -3.0
    derivative[3, 3] = 3.0
    return (2.0 * derivative, weights)


def level_tables(levels, crm_levels):
    spacing = levels / crm_levels
    centres = (np.arange(crm_levels) + 0.5) * spacing - 0.5
    hats = np.maximum(0.0, 1.0 - np.abs(np.arange(levels)[None, :] - centres[:, None]) / spacing)
    down_map = hats / hats.sum(axis=1, keepdims=True)
    up_map = hats.T / hats.T.sum(axis=1, keepdims=True)
    return (down_map, up_map)


DERIV, WEIGHTS = gll_tables()


def iota(shape, axis):
    return lax.broadcasted_iota(jnp.int32, shape, axis)


def derivative_terms(shape, axis):
    phase = iota(shape, axis) % 4
    terms = []
    for shift in range(-3, 4):
        value = jnp.zeros(shape, F32)
        for i in range(4):
            if 0 <= i + shift < 4:
                value = jnp.where(phase == i, F32(DERIV[i, i + shift]), value)
        terms.append((shift, value))
    return terms


def along(x, terms, axis):
    size = x.shape[axis]
    total = None
    for shift, value in terms:
        moved = x if shift == 0 else pltpu.roll(x, (-shift) % size, axis)
        part = value[None] * moved
        total = part if total is None else total + part
    return total


def tendency(x, u, v, row_terms, col_terms):
    halves = []
    for h in range(x.shape[2] // 128):
        cut = slice(128 * h, 128 * h + 128)
        q = x[:, :, cut]
        grad_x = along(q, row_terms, 1)
        grad_y = along(q, col_terms, 2)
        halves.append(-(u[:, :, cut] * grad_x + v[:, :, cut] * grad_y))
    return jnp.concatenate(halves, axis=2)


def put_rows(x, levels, top_ref, bot_ref, i):
    top_ref[i, levels, :] = x[:, 0, :]
    bot_ref[i, levels, :] = x[:, 7, :]


def first_kernel(
    q_hbm, u_hbm, v_hbm, count_ref,
    tend_ref, top_ref, bot_ref, right_ref, left_ref, count_out_ref, q_ref, u_ref, v_ref, sems,
):
    row_terms = derivative_terms((8, 128), 0)
    col_terms = derivative_terms((8, 128), 1)
    lane = iota((8, 128), 1)
    count_out_ref[...] = count_ref[...]
    chunks = q_ref.shape[0] // CHUNK

    def copies(chunk):
        levels = pl.ds(pl.multiple_of(chunk * CHUNK, CHUNK), CHUNK)
        return [
            pltpu.make_async_copy(src.at[levels], dst.at[levels], sems.at[i, chunk])
            for i, (src, dst) in enumerate(((q_hbm, q_ref), (u_hbm, u_ref), (v_hbm, v_ref)))
        ]

    for chunk in range(chunks):
        for copy in copies(chunk):
            copy.start()

    def body(chunk, carry):
        for copy in copies(chunk):
            copy.wait()
        for half in range(CHUNK // 4):
            right = jnp.zeros((8, 128), F32)
            left = jnp.zeros((8, 128), F32)
            for j in range(4):
                for f, ref in enumerate((q_ref, u_ref, v_ref)):
                    start = 32 * j + 8 * f
                    here = (lane >= start) & (lane < start + 8)
                    x = ref[chunk * CHUNK + half * 4 + j]
                    moved = pltpu.roll(x[:, 128:256], (start - 120) % 128, 1)
                    right = jnp.where(here, moved, right)
                    first = x[:, 0:128]
                    if start:
                        first = pltpu.roll(first, start, 1)
                    left = jnp.where(here, first, left)
            right_ref[chunk * (CHUNK // 4) + half] = right
            left_ref[chunk * (CHUNK // 4) + half] = left
        levels = pl.ds(pl.multiple_of(chunk * CHUNK, CHUNK), CHUNK)
        q = q_ref[levels]
        tend = tendency(q, u_ref[levels], v_ref[levels], row_terms, col_terms)
        tend_ref[levels] = tend
        put_rows(tend, levels, top_ref, bot_ref, 0)
        put_rows(q, levels, top_ref, bot_ref, 1)
        return carry

    lax.fori_loop(0, chunks, body, 0)


def strip_kernel(
    left_ref, right_ref, top_main, bot_main,
    q_ref, u_ref, v_ref, tend_ref, top_ref, bot_ref,
):
    row_terms = derivative_terms((8, 128), 0)
    col_terms = derivative_terms((8, 128), 1)
    lane = iota((8, 128), 1)
    top_ref[:, :, 0:256] = top_main[...]
    bot_ref[:, :, 0:256] = bot_main[...]

    def body(chunk, carry):
        tiles = [[], [], []]
        for half in range(CHUNK // 4):
            west = left_ref[chunk * (CHUNK // 4) + half]
            east = right_ref[chunk * (CHUNK // 4) + half]
            for j in range(4):
                for f in range(3):
                    start = 32 * j + 8 * f
                    a = pltpu.roll(east, 128 - start, 1) if start else east
                    b = pltpu.roll(west, (120 - start) % 128, 1)
                    tiles[f].append(jnp.where(lane < 8, a, jnp.where(lane >= 120, b, 0.0)))
        q, u, v = [jnp.stack(tile, axis=0) for tile in tiles]
        levels = pl.ds(pl.multiple_of(chunk * CHUNK, CHUNK), CHUNK)
        q_ref[levels] = q
        u_ref[levels] = u
        v_ref[levels] = v
        tend = tendency(q, u, v, row_terms, col_terms)
        tend_ref[levels] = tend
        for i, x in enumerate((tend, q)):
            top_ref[i, levels, 256:384] = x[:, 0, :]
            bot_ref[i, levels, 256:384] = x[:, 7, :]
        return carry

    lax.fori_loop(0, q_ref.shape[0] // CHUNK, body, 0)


def assemble_chunk(x, up, down):
    shape = x.shape
    row = iota(shape, 1)
    partner = jnp.where(
        row == 0,
        jnp.broadcast_to(up[:, None, :], shape),
        jnp.where(
            row == 7,
            jnp.broadcast_to(down[:, None, :], shape),
            jnp.where(row == 3, pltpu.roll(x, 7, 1), pltpu.roll(x, 1, 1)),
        ),
    )
    x = jnp.where((row % 4 == 0) | (row % 4 == 3), 0.5 * (x + partner), x)
    col = iota(shape, 2)
    partner = jnp.where(
        col % 4 == 3, pltpu.roll(x, shape[2] - 1, 2), pltpu.roll(x, 1, 2)
    )
    return jnp.where((col % 4 == 0) | (col % 4 == 3), 0.5 * (x + partner), x)


def join(main, strip):
    return jnp.concatenate([main, strip], axis=2)


def second_kernel(
    q_ref, u_ref, v_ref, tend_ref, q_strip, u_strip, v_strip, tend_strip, up_ref, down_ref,
    state_ref, smooth_ref, next_ref, top_ref, bot_ref,
):
    row_terms = derivative_terms((8, 128), 0)
    col_terms = derivative_terms((8, 128), 1)

    def body(chunk, carry):
        levels = pl.ds(pl.multiple_of(chunk * CHUNK, CHUNK), CHUNK)
        q = join(q_ref[levels], q_strip[levels])
        change = assemble_chunk(
            join(tend_ref[levels], tend_strip[levels]), up_ref[0, levels, :], down_ref[0, levels, :]
        )
        smooth = assemble_chunk(q, up_ref[1, levels, :], down_ref[1, levels, :])
        smooth_ref[levels] = smooth[:, :, 0:256]
        state = q + DT_DYN * change
        state_ref[levels] = state[:, :, 0:256]
        tend = tendency(
            state, join(u_ref[levels], u_strip[levels]), join(v_ref[levels], v_strip[levels]),
            row_terms, col_terms,
        )
        next_ref[levels] = tend
        put_rows(tend, levels, top_ref, bot_ref, 0)
        return carry

    lax.fori_loop(0, q_ref.shape[0] // CHUNK, body, 0)


def third_kernel(
    q_ref, state_ref, smooth_ref, tend_ref, up_ref, down_ref, down_map_ref,
    base_ref, forcing_ref, near_ref, far_ref,
):
    cols = forcing_ref.shape[1]
    half = cols // 2
    phase = iota((8, 256), 0) % 4
    row_weight = jnp.where((phase == 0) | (phase == 3), F32(WEIGHTS[0]), F32(WEIGHTS[1]))
    near_rows = jnp.where(iota((8, 256), 0) < 4, row_weight, 0.0)
    far_rows = row_weight - near_rows

    def body(chunk, carry):
        levels = pl.ds(pl.multiple_of(chunk * CHUNK, CHUNK), CHUNK)
        change = assemble_chunk(tend_ref[levels], up_ref[0, levels, :], down_ref[0, levels, :])
        moved = (state_ref[levels] + DT_DYN * change[:, :, 0:256]) - q_ref[levels]
        base_ref[levels] = smooth_ref[levels] + moved
        near_ref[levels, :] = jnp.sum(moved * near_rows[None], axis=1)
        far_ref[levels, :] = jnp.sum(moved * far_rows[None], axis=1)
        return carry

    lax.fori_loop(0, q_ref.shape[0] // CHUNK, body, 0)
    point = iota((256, cols), 0)
    element = iota((256, cols), 1)
    weight = jnp.where(
        (point % 4 == 0) | (point % 4 == 3), F32(WEIGHTS[0]), F32(WEIGHTS[1])
    ) * F32(0.25 / (DYN_STEPS * DT_DYN))
    near_cols = jnp.where(point // 4 == element, weight, 0.0)
    far_cols = jnp.where(point // 4 + half == element, weight, 0.0)
    means = jnp.dot(near_ref[...], near_cols, precision=HIGH, preferred_element_type=F32)
    means += jnp.dot(far_ref[...], far_cols, precision=HIGH, preferred_element_type=F32)
    forcing = jnp.dot(down_map_ref[...], means, precision=HIGH, preferred_element_type=F32)
    forcing_ref[...] = forcing.astype(BF16).astype(F32)


def coef_kernel(collision_ref, table_ref, after_ref, coef_ref):
    total = jnp.dot(collision_ref[...], table_ref[...], preferred_element_type=F32) * DT_CRM
    coarse = total.astype(BF16)
    fine = total - coarse.astype(F32)
    coef_ref[...] = jnp.concatenate([coarse.astype(F32), fine], axis=0).astype(BF16)


def rank_row(values):
    total = values.shape[1]
    across = jnp.broadcast_to(values, (total, total))
    down = across.T
    earlier = iota((total, total), 0) < iota((total, total), 1)
    ahead = (down > across) | ((down == across) & earlier)
    return jnp.sum(ahead.astype(F32), axis=0, keepdims=True)


def plan_kernel(
    capacity, count_ref, other_ref, owner_ref, after_ref,
    sent_ref, order_ref, force_ref, ordered_ref, rank_ref, slot_ref,
):
    cols = count_ref.shape[1]
    counts = count_ref[...].astype(F32)
    others = other_ref[...].astype(F32)
    rank = rank_row(counts)
    other_rank = rank_row(others)
    square = (cols, cols)
    index = iota(square, 0).astype(F32)
    odd = 2.0 * iota(square, 1).astype(F32) + 1.0
    down_rank = jnp.broadcast_to(rank, square).T
    sent = jnp.sum(jnp.where(down_rank == odd, index, 0.0), axis=0, keepdims=True)
    sent_ref[...] = sent.astype(jnp.int32)
    rank_ref[...] = rank.astype(jnp.int32)

    is_odd = rank.astype(jnp.int32) % 2 == 1
    other_odd = other_rank.astype(jnp.int32) % 2 == 1
    listed = jnp.concatenate(
        [jnp.where(is_odd, -1.0, counts), jnp.where(other_odd, others, -1.0)], axis=1
    )
    lane = iota((1, cols), 1).astype(F32)
    name = jnp.concatenate([lane, cols + 0.5 * (other_rank - 1.0)], axis=1)
    wide = (2 * cols, 2 * cols)
    place = jnp.broadcast_to(rank_row(listed), wide).T[:, 0:cols]
    here = place == iota((2 * cols, cols), 1).astype(F32)
    force = iota((2 * cols, cols), 0).astype(F32)
    name = jnp.broadcast_to(name, wide).T[:, 0:cols]
    value = jnp.broadcast_to(listed, wide).T[:, 0:cols]
    for what, ref in ((name, order_ref), (force, force_ref), (value, ordered_ref)):
        total = jnp.sum(jnp.where(here, what, 0.0), axis=0, keepdims=True)
        ref[...] = total.astype(jnp.int32)

    owners = jnp.broadcast_to(owner_ref[...].astype(F32), square)
    same = (owners.T == owners) & (iota(square, 0) < iota(square, 1))
    earlier = jnp.sum(same.astype(F32), axis=0, keepdims=True)
    slot_ref[...] = owner_ref[...] * capacity + earlier.astype(jnp.int32)


def gather_kernel(sent_ref, drops_ref, out_ref, wide_ref):
    bins = drops_ref.shape[1]
    wide_ref[...] = jnp.zeros(wide_ref.shape, F32)

    def body(p, carry):
        for k in range(2):
            wide_ref[k, 0:bins, :] = drops_ref[sent_ref[0, 2 * p + k]].astype(F32)
            out_ref[2 * p + k] = wide_ref[k].astype(BF16)
        return carry

    lax.fori_loop(0, out_ref.shape[0] // 2, body, 0)


def merge_kernel(sent_ref, final_ref, back_ref, out_ref):
    out_ref[...] = final_ref[...]

    def body(p, carry):
        out_ref[sent_ref[0, p]] = back_ref[p, 0 : out_ref.shape[1], :]
        return carry

    lax.fori_loop(0, back_ref.shape[0], body, 0)


def crm_kernel(
    order_ref, force_ref, count_ref, place_ref,
    drops_ref, guest_ref, forcing_ref, other_ref, coef_ref, growth_ref,
    final_ref, back_ref, own_ref, away_ref,
    state_ref, start_ref, pair_ref, twice_ref, cell_ref, heat_cell_ref, echo_cell_ref,
):
    bins = drops_ref.shape[1]
    cells = drops_ref.shape[2]
    cols = drops_ref.shape[0]
    guests = guest_ref.shape[0]
    coef = coef_ref[...]
    growth = growth_ref[...]
    state_ref[...] = jnp.zeros(state_ref.shape, F32)
    heat_cell_ref[...] = jnp.zeros(heat_cell_ref.shape, F32)
    echo_cell_ref[...] = jnp.zeros(echo_cell_ref.shape, F32)
    mass = (iota((40, cells), 0) + 1).astype(F32) / F32(bins)
    spread = (iota((CRM_LEV, cells), 1) // CRM_X == iota((CRM_LEV, cells), 0)).astype(BF16)
    for i, ref in enumerate((forcing_ref, other_ref)):
        rows = jnp.dot(ref[...].T.astype(BF16), spread, preferred_element_type=F32)
        cell_ref[cols * i : cols * i + cols, :] = DT_CRM * rows

    def grow(k, which, zero):
        grown = state_ref[k] + growth * cell_ref[pl.ds(which, 1), :]
        for h in range(cells // 128):
            cut = slice(128 * h, 128 * h + 128)
            g = grown[0:32, cut]
            last = grown[32:40, cut]
            twice_ref[2 * k + h, 0:32, :] = g
            twice_ref[2 * k + h, 32:48, :] = g[0:16]
            for d in range(16):
                other = g if d % 8 == 0 else twice_ref[2 * k + h, pl.ds(zero + d, 32), :]
                if d == 8:
                    other = jnp.concatenate([g[8:], g[:8]], axis=0)
                pair_ref[k, 32 * d : 32 * d + 32, cut] = (g * other).astype(BF16)
            pair_ref[k, 512:528, cut] = (g[0:16] * g[16:32]).astype(BF16)
            pair_ref[k, 528:560, cut] = (g * last[0:1]).astype(BF16)
            tail = jnp.concatenate([last * last, jnp.zeros((8, 128), F32)], axis=0)
            pair_ref[k, 560:576, cut] = tail.astype(BF16)
        return grown

    def group(index, carry):
        base = index * GROUP
        which = [order_ref[0, base + k] for k in range(GROUP)]
        force = [force_ref[0, base + k] for k in range(GROUP)]
        count = [count_ref[0, base + k] for k in range(GROUP)]
        for k in range(GROUP):
            mine = drops_ref[jnp.minimum(which[k], cols - 1)].astype(F32)
            guest = guest_ref[jnp.clip(which[k] - cols, 0, guests - 1)].astype(F32)
            start = jnp.where(which[k] < cols, mine, guest[0:bins])
            start_ref[k, 0:bins, :] = start
            state_ref[k, 0:bins, :] = start

        def step(s, c):
            for k in range(GROUP):
                grown = grow(k, force[k], place_ref[3])
                change = jnp.dot(coef, pair_ref[k], preferred_element_type=F32)
                moved = grown + (change[0:40] + change[40:80])
                state_ref[k] = jnp.where(s < count[k], moved, state_ref[k])
            return c

        lax.fori_loop(0, count[0], step, 0)
        for k in range(GROUP):
            final = state_ref[k, 0:bins, :]
            weighted = mass[0:bins] * final
            heat = jnp.sum(mass[0:bins] * (final - start_ref[k, 0:bins, :]), axis=0, keepdims=True)
            echo = jnp.sum(weighted * weighted, axis=0, keepdims=True)
            heat_cell_ref[pl.ds(which[k], 1), :] = heat
            echo_cell_ref[pl.ds(which[k], 1), :] = echo

            @pl.when(which[k] < cols)
            def _():
                final_ref[jnp.minimum(which[k], cols - 1)] = state_ref[k, 0:bins, :].astype(BF16)

            @pl.when(which[k] >= cols)
            def _():
                row = jnp.clip(which[k] - cols, 0, guests - 1)
                back_ref[row] = state_ref[k].astype(BF16)

        return carry

    lax.fori_loop(0, cols // GROUP, group, 0)
    means = jnp.where(
        iota((CRM_LEV, cells), 1) // CRM_X == iota((CRM_LEV, cells), 0), F32(1.0 / CRM_X), 0.0
    )
    contract = (((1,), (1,)), ((), ()))
    heat = lax.dot_general(
        means, heat_cell_ref[...], contract, precision=HIGH, preferred_element_type=F32
    )
    heat = heat.astype(BF16).astype(F32)
    echo = lax.dot_general(
        means, echo_cell_ref[...], contract, precision=HIGH, preferred_element_type=F32
    )
    both = jnp.concatenate([heat, jnp.log(1.0 + echo)], axis=0)
    own_ref[...] = both[:, 0:cols]
    away_ref[...] = both[:, cols : 2 * cols]


def block_kernel(place_ref, own_ref, back_ref, rank_ref, slot_ref, heat_ref, send_ref):
    cols = own_ref.shape[1]
    odd = 2 * iota((cols, cols), 0) + 1
    home = (rank_ref[...] == odd).astype(F32)
    both = own_ref[...] + jnp.dot(
        back_ref[...], home, precision=HIGH, preferred_element_type=F32
    )
    heat = both[0:CRM_LEV]
    echo = both[CRM_LEV:]
    heat_ref[...] = heat
    contract = (((1,), (1,)), ((), ()))
    devices = send_ref.shape[0]
    slots = 2 * cols
    capacity = slots // devices
    onehot = (slot_ref[...] == iota((slots, cols), 0)).astype(F32)
    packed = lax.dot_general(echo, onehot, contract, precision=HIGH, preferred_element_type=F32)
    coarse = packed.astype(BF16).astype(F32)
    rest = packed - coarse
    middle = rest.astype(BF16).astype(F32)
    pieces = (coarse, middle, rest - middle)
    lane = iota((CRM_LEV, 128), 1)
    near = heat
    far = pltpu.roll(heat, 64, 1)
    sides = jnp.where(
        lane == 1, pltpu.roll(heat, 65, 1), jnp.where(lane == 62, pltpu.roll(heat, 63, 1), heat)
    )
    n_gcm = place_ref[1]
    n_crm = place_ref[2]
    for d in range(devices):
        away = d // n_crm - place_ref[0]
        below = (away == 1) | (away == 1 - n_gcm)
        above = (away == -1) | (away == n_gcm - 1)
        block = jnp.where(below, far, jnp.where(above, near, sides))
        tile, offset = divmod(d * capacity, 128)
        for i, piece in enumerate(pieces):
            moved = pltpu.roll(
                piece[:, 128 * tile : 128 * tile + 128], (64 + i * capacity - offset) % 128, 1
            )
            start = 64 + i * capacity
            block = jnp.where((lane >= start) & (lane < start + capacity), moved, block)
        send_ref[d] = block.astype(BF16)


def last_kernel(
    around_ref, base_ref, own_ref, got_ref, up_map_ref, drops_in, out_ref, power_ref, drops_out,
    *back_refs,
):
    cols = own_ref.shape[1]
    half = cols // 2
    element = iota((cols, 256), 0)
    col = iota((cols, 256), 1)
    phase = col % 4
    edge = (phase == 0) | (phase == 3)
    other = jnp.where(phase == 0, col // 4 - 1, col // 4 + 1)

    def spread(centre, start, west, west_lane, east, east_lane):
        inside = jnp.where(element == col // 4 + start, jnp.where(edge, 0.5, 1.0), 0.0)
        beside = edge & (element == other + start) & (other >= 0) & (other < half)
        middle = jnp.where(beside, 0.5, inside).astype(BF16)
        from_west = jnp.where((col == 0) & (element == west_lane), 0.5, 0.0).astype(BF16)
        from_east = jnp.where((col == 255) & (element == east_lane), 0.5, 0.0).astype(BF16)
        total = jnp.dot(centre, middle, preferred_element_type=F32)
        total += jnp.dot(west, from_west, preferred_element_type=F32)
        total += jnp.dot(east, from_east, preferred_element_type=F32)
        return total

    own = own_ref[...].astype(BF16)
    up, down, left, right, up_left, up_right, down_left, down_right = [
        got_ref[around_ref[i]] for i in range(8)
    ]
    above = spread(up, 0, up_left, half - 1, up_right, 0)
    near = spread(own, 0, left, half - 1, right, 0)
    far = spread(own, half, left, half - 2, right, 1)
    below = spread(down, 0, down_left, half - 1, down_right, 0)
    parts = (
        0.5 * (above + near), near, 0.5 * (near + far), far, 0.5 * (far + below),
    )
    up_map = up_map_ref[...]
    for part, ref in zip(parts, back_refs):
        ref[...] = DT_PHYS * jnp.dot(up_map, part, precision=HIGH, preferred_element_type=F32)

    devices = got_ref.shape[0]
    slots = power_ref.shape[1]
    capacity = slots // devices
    lane = iota((CRM_LEV, 128), 1)
    tiles = [jnp.zeros((CRM_LEV, 128), F32) for _ in range(slots // 128)]
    for d in range(devices):
        block = got_ref[d].astype(F32)
        fine = pltpu.roll(block, 128 - 2 * capacity, 1) + pltpu.roll(block, 128 - capacity, 1)
        tile, offset = divmod(d * capacity, 128)
        moved = pltpu.roll(block + fine, (offset - 64) % 128, 1)
        tiles[tile] = jnp.where((lane >= offset) & (lane < offset + capacity), moved, tiles[tile])
    power_ref[...] = jnp.concatenate(tiles, axis=1)

    def body(chunk, carry):
        levels = pl.ds(pl.multiple_of(chunk * CHUNK, CHUNK), CHUNK)
        shape = (CHUNK, 8, 256)
        row = iota(shape, 1)
        wide = [jnp.broadcast_to(ref[levels, :][:, None, :], shape) for ref in back_refs]
        back = jnp.where(
            row == 0,
            wide[0],
            jnp.where(
                row < 3,
                wide[1],
                jnp.where(row < 5, wide[2], jnp.where(row < 7, wide[3], wide[4])),
            ),
        )
        out_ref[levels] = base_ref[levels] + back
        return carry

    lax.fori_loop(0, base_ref.shape[0] // CHUNK, body, 0)


def call(kernel, outs, args, scratch=(), sems=(), flops=10_000_000, limit=16, through=()):
    spaces = {
        "s": pl.BlockSpec(memory_space=pltpu.SMEM),
        "v": pl.BlockSpec(memory_space=pltpu.VMEM),
        "h": pl.BlockSpec(memory_space=pl.ANY),
    }
    return pl.pallas_call(
        kernel,
        out_shape=[jax.ShapeDtypeStruct(s, t) for s, t in outs]
        + [jax.ShapeDtypeStruct(args[i][1].shape, args[i][1].dtype) for i in through],
        in_specs=[spaces[kind] for kind, _ in args],
        out_specs=[spaces["v"]] * len(outs) + [spaces["h"]] * len(through),
        input_output_aliases={i: len(outs) + n for n, i in enumerate(through)},
        scratch_shapes=[pltpu.VMEM(s, t) for s, t in scratch] + list(sems),
        compiler_params=pltpu.CompilerParams(vmem_limit_bytes=limit * MIB),
        cost_estimate=pl.CostEstimate(flops=flops, bytes_accessed=4_000_000, transcendentals=0),
    )(*[value for _, value in args])


def v(*values):
    return [("v", value) for value in values]


def shift(value, rows, cols):
    n_gcm = lax.axis_size("gcm")
    n_crm = lax.axis_size("crm")
    pairs = []
    for g in range(n_gcm):
        for c in range(n_crm):
            target = ((g + rows) % n_gcm) * n_crm + (c + cols) % n_crm
            pairs.append((g * n_crm + c, target))
    return lax.ppermute(value, ("gcm", "crm"), pairs)


def pair_table(bins):
    table = np.zeros((bins * bins, 576), np.float32)

    def put(column, i, j):
        table[i * bins + j, column] = 1.0
        table[j * bins + i, column] = 1.0

    for d in range(16):
        for b in range(32):
            put(32 * d + b, b, (b + d) % 32)
    for b in range(16):
        put(512 + b, b, b + 16)
    for b in range(32):
        put(528 + b, b, 32)
    put(560, 32, 32)
    return table


def to_partner(value):
    n_gcm = lax.axis_size("gcm")
    n_crm = lax.axis_size("crm")
    pairs = []
    for g in range(n_gcm):
        for c in range(n_crm):
            pairs.append((g * n_crm + c, (g ^ 1) * n_crm + c))
    return lax.ppermute(value, ("gcm", "crm"), pairs)


def shards(tracer, wind_x, wind_y, drops, owner, counts, collision, growth):
    devices = lax.axis_size("gcm") * lax.axis_size("crm")
    levels, row_count, col_count = tracer.shape
    col_total, bins, cells = drops.shape
    field = (tracer.shape, F32)
    strip = ((levels, row_count, 128), F32)
    rows = ((2, levels, col_count), F32)
    wide = col_count + 128
    down_map, up_map = level_tables(levels, CRM_LEV)

    row = ((1, col_total), jnp.int32)
    capacity = 2 * col_total // devices
    guests = col_total // 2
    tend, top, bot, to_right, to_left, count_row = call(
        first_kernel,
        [field, rows, rows] + [((levels // 4, 8, 128), F32)] * 2 + [row],
        [("h", tracer), ("h", wind_x), ("h", wind_y)] + v(counts[None, :]),
        [field] * 3,
        [pltpu.SemaphoreType.DMA((3, levels // CHUNK))],
        limit=62,
    )
    from_left = shift(to_right, 0, 1)
    from_right = shift(to_left, 0, -1)
    other_counts = to_partner(count_row)
    q_strip, u_strip, v_strip, tend_strip, top, bot = call(
        strip_kernel,
        [strip] * 4 + [((2, levels, wide), F32)] * 2,
        v(from_left, from_right, top, bot),
    )
    sent, order, force, ordered, rank, slot = call(
        functools.partial(plan_kernel, capacity),
        [row] * 6,
        v(count_row, other_counts, owner.T) + [("h", top)],
    )
    (leaving,) = call(
        gather_kernel,
        [((guests, 40, cells), BF16)],
        [("s", sent)] + v(drops),
        [((2, 40, cells), F32)],
    )
    guest_drops = to_partner(leaving)
    (coef,) = call(
        coef_kernel,
        [((80, 576), BF16)],
        v(jnp.pad(collision, ((0, 40 - bins), (0, 0))), jnp.asarray(pair_table(bins), BF16))
        + [("h", top)],
    )
    state, smooth, tend, top, bot = call(
        second_kernel,
        [field, field, ((levels, row_count, wide), F32)] + [((1, levels, wide), F32)] * 2,
        v(tracer, wind_x, wind_y, tend, q_strip, u_strip, v_strip, tend_strip)
        + v(shift(bot, 1, 0), shift(top, -1, 0)),
    )
    base, forcing = call(
        third_kernel,
        [field, ((CRM_LEV, col_total), F32)],
        v(tracer, state, smooth, tend, shift(bot, 1, 0), shift(top, -1, 0))
        + v(jnp.asarray(down_map, F32)),
        [((levels, col_count), F32), ((levels, col_count), F32)],
    )

    other_forcing = to_partner(forcing)
    growth_rows = jnp.broadcast_to(jnp.pad(growth, (0, 40 - bins))[:, None], (40, cells))
    n_gcm = lax.axis_size("gcm")
    n_crm = lax.axis_size("crm")
    g = lax.axis_index("gcm").astype(jnp.int32)
    c = lax.axis_index("crm").astype(jnp.int32)
    place = jnp.stack([g, jnp.int32(n_gcm), jnp.int32(n_crm), jnp.int32(0)])

    pairs = ((2 * CRM_LEV, col_total), F32)
    final, back, own, away = call(
        crm_kernel,
        [((col_total, bins, cells), BF16), ((guests, 40, cells), BF16), pairs, pairs],
        [("s", order), ("s", force), ("s", ordered), ("s", place)]
        + v(drops, guest_drops, forcing, other_forcing, coef, growth_rows),
        [((GROUP, 40, cells), F32), ((GROUP, 40, cells), F32), ((GROUP, 576, cells), BF16),
         ((2 * GROUP, 48, 128), F32), ((2 * col_total, cells), F32),
         ((2 * col_total, cells), F32), ((2 * col_total, cells), F32)],
        flops=10_000_000_000,
        limit=24,
    )
    returned = to_partner(away)
    returned_drops = to_partner(back)
    heat, send = call(
        block_kernel,
        [((CRM_LEV, col_total), F32), ((devices, CRM_LEV, 128), BF16)],
        [("s", place)] + v(own, returned, rank, slot),
    )
    got = lax.all_to_all(send, ("gcm", "crm"), split_axis=0, concat_axis=0, tiled=True)
    (drops_next,) = call(
        merge_kernel,
        [((col_total, bins, cells), BF16)],
        [("s", sent)] + v(final, returned_drops),
    )
    up = (g + n_gcm - 1) % n_gcm * n_crm
    same_row = g * n_crm
    down = (g + 1) % n_gcm * n_crm
    west = (c + n_crm - 1) % n_crm
    east = (c + 1) % n_crm
    around = jnp.stack(
        [up + c, down + c, same_row + west, same_row + east,
         up + west, up + east, down + west, down + east]
    )
    tracer_next, power, by_bin = call(
        last_kernel,
        [field, ((CRM_LEV, devices * capacity), F32)],
        [("s", around)] + v(base, heat, got, jnp.asarray(up_map, F32))
        + [("h", drops_next.transpose(1, 0, 2))],
        [((levels, col_count), F32)] * 5,
        through=(5,),
    )
    drops_next = by_bin.transpose(1, 0, 2)
    return (tracer_next, drops_next, power)


def solution(mesh):
    return jax.shard_map(
        shards,
        mesh=mesh,
        in_specs=(
            P(None, "gcm", "crm"),
            P(None, "gcm", "crm"),
            P(None, "gcm", "crm"),
            P(("gcm", "crm"), None, None),
            P(("gcm", "crm"), None),
            P(("gcm", "crm")),
            P(),
            P(),
        ),
        out_specs=(P(None, "gcm", "crm"), P(("gcm", "crm"), None, None), P(None, ("gcm", "crm"))),
        check_vma=False,
    )
```

```python
import functools

import jax
import jax.numpy as jnp
import numpy as np
from jax import lax
from jax.experimental import pallas as pl
from jax.experimental.pallas import tpu as pltpu
from jax.sharding import PartitionSpec as P

CRM_X = 16
CRM_LEV = 16
DYN_STEPS = 2

DT_DYN = 0.04
DT_CRM = 0.05
DT_PHYS = 0.5
HIGH = lax.Precision.HIGHEST
F32 = jnp.float32
BF16 = jnp.bfloat16
GROUP = 8
CHUNK = 8
MIB = 1024 * 1024


def gll_tables():
    inv_root = 1.0 / np.sqrt(5.0)
    gll_nodes = np.array([-1.0, -inv_root, inv_root, 1.0])
    weights = np.array([1.0, 5.0, 5.0, 1.0]) / 6.0
    legendre = (5.0 * gll_nodes**3 - 3.0 * gll_nodes) / 2.0
    derivative = np.zeros((4, 4))
    for i in range(4):
        for j in range(4):
            if i != j:
                derivative[i, j] = legendre[i] / (legendre[j] * (gll_nodes[i] - gll_nodes[j]))
    derivative[0, 0] = -3.0
    derivative[3, 3] = 3.0
    return (2.0 * derivative, weights)


def level_tables(levels, crm_levels):
    spacing = levels / crm_levels
    centres = (np.arange(crm_levels) + 0.5) * spacing - 0.5
    hats = np.maximum(0.0, 1.0 - np.abs(np.arange(levels)[None, :] - centres[:, None]) / spacing)
    down_map = hats / hats.sum(axis=1, keepdims=True)
    up_map = hats.T / hats.T.sum(axis=1, keepdims=True)
    return (down_map, up_map)


DERIV, WEIGHTS = gll_tables()


def iota(shape, axis):
    return lax.broadcasted_iota(jnp.int32, shape, axis)


def derivative_terms(shape, axis):
    phase = iota(shape, axis) % 4
    terms = []
    for shift in range(-3, 4):
        value = jnp.zeros(shape, F32)
        for i in range(4):
            if 0 <= i + shift < 4:
                value = jnp.where(phase == i, F32(DERIV[i, i + shift]), value)
        terms.append((shift, value))
    return terms


def along(x, terms, axis):
    size = x.shape[axis]
    total = None
    for shift, value in terms:
        moved = x if shift == 0 else pltpu.roll(x, (-shift) % size, axis)
        part = value[None] * moved
        total = part if total is None else total + part
    return total


def tendency(x, u, v, row_terms, col_terms):
    halves = []
    for h in range(x.shape[2] // 128):
        cut = slice(128 * h, 128 * h + 128)
        q = x[:, :, cut]
        grad_x = along(q, row_terms, 1)
        grad_y = along(q, col_terms, 2)
        halves.append(-(u[:, :, cut] * grad_x + v[:, :, cut] * grad_y))
    return jnp.concatenate(halves, axis=2)


def put_rows(x, levels, top_ref, bot_ref, i):
    top_ref[i, levels, :] = x[:, 0, :]
    bot_ref[i, levels, :] = x[:, 7, :]


def first_kernel(
    q_hbm, u_hbm, v_hbm, count_ref,
    tend_ref, top_ref, bot_ref, right_ref, left_ref, count_out_ref, q_ref, u_ref, v_ref, sems,
):
    row_terms = derivative_terms((8, 128), 0)
    col_terms = derivative_terms((8, 128), 1)
    lane = iota((8, 128), 1)
    count_out_ref[...] = count_ref[...]
    chunks = q_ref.shape[0] // CHUNK

    def copies(chunk):
        levels = pl.ds(pl.multiple_of(chunk * CHUNK, CHUNK), CHUNK)
        return [
            pltpu.make_async_copy(src.at[levels], dst.at[levels], sems.at[i, chunk])
            for i, (src, dst) in enumerate(((q_hbm, q_ref), (u_hbm, u_ref), (v_hbm, v_ref)))
        ]

    for chunk in range(chunks):
        for copy in copies(chunk):
            copy.start()

    def body(chunk, carry):
        for copy in copies(chunk):
            copy.wait()
        for half in range(CHUNK // 4):
            right = jnp.zeros((8, 128), F32)
            left = jnp.zeros((8, 128), F32)
            for j in range(4):
                for f, ref in enumerate((q_ref, u_ref, v_ref)):
                    start = 32 * j + 8 * f
                    here = (lane >= start) & (lane < start + 8)
                    x = ref[chunk * CHUNK + half * 4 + j]
                    moved = pltpu.roll(x[:, 128:256], (start - 120) % 128, 1)
                    right = jnp.where(here, moved, right)
                    first = x[:, 0:128]
                    if start:
                        first = pltpu.roll(first, start, 1)
                    left = jnp.where(here, first, left)
            right_ref[chunk * (CHUNK // 4) + half] = right
            left_ref[chunk * (CHUNK // 4) + half] = left
        levels = pl.ds(pl.multiple_of(chunk * CHUNK, CHUNK), CHUNK)
        q = q_ref[levels]
        tend = tendency(q, u_ref[levels], v_ref[levels], row_terms, col_terms)
        tend_ref[levels] = tend
        put_rows(tend, levels, top_ref, bot_ref, 0)
        put_rows(q, levels, top_ref, bot_ref, 1)
        return carry

    lax.fori_loop(0, chunks, body, 0)


def strip_kernel(
    left_ref, right_ref, top_main, bot_main,
    q_ref, u_ref, v_ref, tend_ref, top_ref, bot_ref,
):
    row_terms = derivative_terms((8, 128), 0)
    col_terms = derivative_terms((8, 128), 1)
    lane = iota((8, 128), 1)
    top_ref[:, :, 0:256] = top_main[...]
    bot_ref[:, :, 0:256] = bot_main[...]

    def body(chunk, carry):
        tiles = [[], [], []]
        for half in range(CHUNK // 4):
            west = left_ref[chunk * (CHUNK // 4) + half]
            east = right_ref[chunk * (CHUNK // 4) + half]
            for j in range(4):
                for f in range(3):
                    start = 32 * j + 8 * f
                    a = pltpu.roll(east, 128 - start, 1) if start else east
                    b = pltpu.roll(west, (120 - start) % 128, 1)
                    tiles[f].append(jnp.where(lane < 8, a, jnp.where(lane >= 120, b, 0.0)))
        q, u, v = [jnp.stack(tile, axis=0) for tile in tiles]
        levels = pl.ds(pl.multiple_of(chunk * CHUNK, CHUNK), CHUNK)
        q_ref[levels] = q
        u_ref[levels] = u
        v_ref[levels] = v
        tend = tendency(q, u, v, row_terms, col_terms)
        tend_ref[levels] = tend
        for i, x in enumerate((tend, q)):
            top_ref[i, levels, 256:384] = x[:, 0, :]
            bot_ref[i, levels, 256:384] = x[:, 7, :]
        return carry

    lax.fori_loop(0, q_ref.shape[0] // CHUNK, body, 0)


def assemble_chunk(x, up, down):
    shape = x.shape
    row = iota(shape, 1)
    partner = jnp.where(
        row == 0,
        jnp.broadcast_to(up[:, None, :], shape),
        jnp.where(
            row == 7,
            jnp.broadcast_to(down[:, None, :], shape),
            jnp.where(row == 3, pltpu.roll(x, 7, 1), pltpu.roll(x, 1, 1)),
        ),
    )
    x = jnp.where((row % 4 == 0) | (row % 4 == 3), 0.5 * (x + partner), x)
    col = iota(shape, 2)
    partner = jnp.where(
        col % 4 == 3, pltpu.roll(x, shape[2] - 1, 2), pltpu.roll(x, 1, 2)
    )
    return jnp.where((col % 4 == 0) | (col % 4 == 3), 0.5 * (x + partner), x)


def join(main, strip):
    return jnp.concatenate([main, strip], axis=2)


def second_kernel(
    q_ref, u_ref, v_ref, tend_ref, q_strip, u_strip, v_strip, tend_strip, up_ref, down_ref,
    state_ref, smooth_ref, next_ref, top_ref, bot_ref,
):
    row_terms = derivative_terms((8, 128), 0)
    col_terms = derivative_terms((8, 128), 1)

    def body(chunk, carry):
        levels = pl.ds(pl.multiple_of(chunk * CHUNK, CHUNK), CHUNK)
        q = join(q_ref[levels], q_strip[levels])
        change = assemble_chunk(
            join(tend_ref[levels], tend_strip[levels]), up_ref[0, levels, :], down_ref[0, levels, :]
        )
        smooth = assemble_chunk(q, up_ref[1, levels, :], down_ref[1, levels, :])
        smooth_ref[levels] = smooth[:, :, 0:256]
        state = q + DT_DYN * change
        state_ref[levels] = state[:, :, 0:256]
        tend = tendency(
            state, join(u_ref[levels], u_strip[levels]), join(v_ref[levels], v_strip[levels]),
            row_terms, col_terms,
        )
        next_ref[levels] = tend
        put_rows(tend, levels, top_ref, bot_ref, 0)
        return carry

    lax.fori_loop(0, q_ref.shape[0] // CHUNK, body, 0)


def third_kernel(
    q_ref, state_ref, smooth_ref, tend_ref, up_ref, down_ref, down_map_ref, coef_ref, growth_ref,
    base_ref, forcing_ref, near_ref, far_ref,
):
    cols = forcing_ref.shape[1]
    half = cols // 2
    phase = iota((8, 256), 0) % 4
    row_weight = jnp.where((phase == 0) | (phase == 3), F32(WEIGHTS[0]), F32(WEIGHTS[1]))
    near_rows = jnp.where(iota((8, 256), 0) < 4, row_weight, 0.0)
    far_rows = row_weight - near_rows

    def body(chunk, carry):
        levels = pl.ds(pl.multiple_of(chunk * CHUNK, CHUNK), CHUNK)
        change = assemble_chunk(tend_ref[levels], up_ref[0, levels, :], down_ref[0, levels, :])
        moved = (state_ref[levels] + DT_DYN * change[:, :, 0:256]) - q_ref[levels]
        base_ref[levels] = smooth_ref[levels] + moved
        near_ref[levels, :] = jnp.sum(moved * near_rows[None], axis=1)
        far_ref[levels, :] = jnp.sum(moved * far_rows[None], axis=1)
        return carry

    lax.fori_loop(0, q_ref.shape[0] // CHUNK, body, 0)
    point = iota((256, cols), 0)
    element = iota((256, cols), 1)
    weight = jnp.where(
        (point % 4 == 0) | (point % 4 == 3), F32(WEIGHTS[0]), F32(WEIGHTS[1])
    ) * F32(0.25 / (DYN_STEPS * DT_DYN))
    near_cols = jnp.where(point // 4 == element, weight, 0.0)
    far_cols = jnp.where(point // 4 + half == element, weight, 0.0)
    means = jnp.dot(near_ref[...], near_cols, precision=HIGH, preferred_element_type=F32)
    means += jnp.dot(far_ref[...], far_cols, precision=HIGH, preferred_element_type=F32)
    forcing = jnp.dot(down_map_ref[...], means, precision=HIGH, preferred_element_type=F32)
    forcing_ref[...] = forcing.astype(BF16).astype(F32)


def coef_kernel(
    collision_ref, table_ref, growth_ref, after_ref, coef_ref, growth_out_ref, wide_ref, line_ref
):
    bins = collision_ref.shape[0]
    total = jnp.dot(collision_ref[...], table_ref[...], preferred_element_type=F32) * DT_CRM
    coarse = total.astype(BF16).astype(F32)
    wide_ref[...] = jnp.zeros(wide_ref.shape, F32)
    wide_ref[0:bins, :] = coarse
    wide_ref[40 : 40 + bins, :] = total - coarse
    coef_ref[...] = wide_ref[...].astype(BF16)
    line_ref[...] = jnp.zeros(line_ref.shape, F32)
    line_ref[0:1, 0:bins] = growth_ref[...]
    rows = jnp.broadcast_to(line_ref[0:1, :], (128, 128)).T[0:40]
    for h in range(growth_out_ref.shape[1] // 128):
        growth_out_ref[:, 128 * h : 128 * h + 128] = rows


def rank_row(values):
    total = values.shape[1]
    across = jnp.broadcast_to(values, (total, total))
    down = across.T
    earlier = iota((total, total), 0) < iota((total, total), 1)
    ahead = (down > across) | ((down == across) & earlier)
    return jnp.sum(ahead.astype(F32), axis=0, keepdims=True)


def plan_kernel(
    capacity, count_ref, other_ref, owner_ref, after_ref,
    sent_ref, order_ref, force_ref, ordered_ref, rank_ref, slot_ref,
):
    cols = count_ref.shape[1]
    counts = count_ref[...].astype(F32)
    others = other_ref[...].astype(F32)
    rank = rank_row(counts)
    other_rank = rank_row(others)
    square = (cols, cols)
    index = iota(square, 0).astype(F32)
    odd = 2.0 * iota(square, 1).astype(F32) + 1.0
    down_rank = jnp.broadcast_to(rank, square).T
    sent = jnp.sum(jnp.where(down_rank == odd, index, 0.0), axis=0, keepdims=True)
    sent_ref[...] = sent.astype(jnp.int32)
    rank_ref[...] = rank.astype(jnp.int32)

    is_odd = rank.astype(jnp.int32) % 2 == 1
    other_odd = other_rank.astype(jnp.int32) % 2 == 1
    listed = jnp.concatenate(
        [jnp.where(is_odd, -1.0, counts), jnp.where(other_odd, others, -1.0)], axis=1
    )
    lane = iota((1, cols), 1).astype(F32)
    name = jnp.concatenate([lane, cols + 0.5 * (other_rank - 1.0)], axis=1)
    wide = (2 * cols, 2 * cols)
    place = jnp.broadcast_to(rank_row(listed), wide).T[:, 0:cols]
    here = place == iota((2 * cols, cols), 1).astype(F32)
    force = iota((2 * cols, cols), 0).astype(F32)
    name = jnp.broadcast_to(name, wide).T[:, 0:cols]
    value = jnp.broadcast_to(listed, wide).T[:, 0:cols]
    for what, ref in ((name, order_ref), (force, force_ref), (value, ordered_ref)):
        total = jnp.sum(jnp.where(here, what, 0.0), axis=0, keepdims=True)
        ref[...] = total.astype(jnp.int32)

    owners = jnp.broadcast_to(owner_ref[...].astype(F32), square)
    same = (owners.T == owners) & (iota(square, 0) < iota(square, 1))
    earlier = jnp.sum(same.astype(F32), axis=0, keepdims=True)
    slot_ref[...] = owner_ref[...] * capacity + earlier.astype(jnp.int32)


def gather_kernel(sent_ref, drops_ref, out_ref, wide_ref):
    bins = drops_ref.shape[1]
    wide_ref[...] = jnp.zeros(wide_ref.shape, F32)

    def body(p, carry):
        for k in range(8):
            wide_ref[k, 0:bins, :] = drops_ref[sent_ref[0, 8 * p + k]].astype(F32)
        for k in range(8):
            out_ref[8 * p + k] = wide_ref[k].astype(BF16)
        return carry

    lax.fori_loop(0, out_ref.shape[0] // 8, body, 0)


def merge_kernel(sent_ref, final_ref, back_ref, out_ref):
    out_ref[...] = final_ref[...]

    def body(p, carry):
        row = back_ref[p].astype(F32)[0 : out_ref.shape[1]]
        out_ref[sent_ref[0, p]] = row.astype(BF16)
        return carry

    lax.fori_loop(0, back_ref.shape[0], body, 0)


def crm_kernel(
    order_ref, force_ref, count_ref,
    drops_ref, guest_ref, forcing_ref, other_ref, coef_ref, growth_ref,
    final_ref, back_ref, own_ref, away_ref,
    state_ref, start_ref, pair_ref, twice_ref, cell_ref, heat_cell_ref, echo_cell_ref,
):
    bins = drops_ref.shape[1]
    cells = drops_ref.shape[2]
    cols = drops_ref.shape[0]
    guests = guest_ref.shape[0]
    coef = coef_ref[...]
    growth = growth_ref[...]
    state_ref[...] = jnp.zeros(state_ref.shape, F32)
    heat_cell_ref[...] = jnp.zeros(heat_cell_ref.shape, F32)
    echo_cell_ref[...] = jnp.zeros(echo_cell_ref.shape, F32)
    mass = (iota((40, cells), 0) + 1).astype(F32) / F32(bins)
    spread = (iota((CRM_LEV, cells), 1) // CRM_X == iota((CRM_LEV, cells), 0)).astype(BF16)
    for i, ref in enumerate((forcing_ref, other_ref)):
        rows = jnp.dot(ref[...].T.astype(BF16), spread, preferred_element_type=F32)
        cell_ref[cols * i : cols * i + cols, :] = DT_CRM * rows

    def grow(k, which, zero):
        grown = state_ref[k] + growth * cell_ref[pl.ds(which, 1), :]
        for h in range(cells // 128):
            cut = slice(128 * h, 128 * h + 128)
            g = grown[0:32, cut]
            last = grown[32:40, cut]
            twice_ref[2 * k + h, 0:32, :] = g
            twice_ref[2 * k + h, 32:48, :] = g[0:16]
            for d in range(16):
                other = g if d % 8 == 0 else twice_ref[2 * k + h, pl.ds(zero + d, 32), :]
                if d == 8:
                    other = jnp.concatenate([g[8:], g[:8]], axis=0)
                pair_ref[k, 32 * d : 32 * d + 32, cut] = (g * other).astype(BF16)
            pair_ref[k, 512:528, cut] = (g[0:16] * g[16:32]).astype(BF16)
            pair_ref[k, 528:560, cut] = (g * last[0:1]).astype(BF16)
            tail = jnp.concatenate([last * last, jnp.zeros((8, 128), F32)], axis=0)
            pair_ref[k, 560:576, cut] = tail.astype(BF16)
        return grown

    def group(index, carry):
        base = index * GROUP
        which = [order_ref[0, base + k] for k in range(GROUP)]
        force = [force_ref[0, base + k] for k in range(GROUP)]
        count = [count_ref[0, base + k] for k in range(GROUP)]
        for k in range(GROUP):
            mine = drops_ref[jnp.minimum(which[k], cols - 1)].astype(F32)
            guest = guest_ref[jnp.clip(which[k] - cols, 0, guests - 1)].astype(F32)
            start = jnp.where(which[k] < cols, mine, guest[0:bins])
            start_ref[k, 0:bins, :] = start
            state_ref[k, 0:bins, :] = start

        zero = jnp.minimum(which[0], 0)

        def step(s, c):
            for k in range(GROUP):
                grown = grow(k, force[k], zero)
                change = jnp.dot(coef, pair_ref[k], preferred_element_type=F32)
                moved = grown + (change[0:40] + change[40:80])
                state_ref[k] = jnp.where(s < count[k], moved, state_ref[k])
            return c

        lax.fori_loop(0, count[0], step, 0)
        for k in range(GROUP):
            final = state_ref[k, 0:bins, :]
            weighted = mass[0:bins] * final
            heat = jnp.sum(mass[0:bins] * (final - start_ref[k, 0:bins, :]), axis=0, keepdims=True)
            echo = jnp.sum(weighted * weighted, axis=0, keepdims=True)
            heat_cell_ref[pl.ds(which[k], 1), :] = heat
            echo_cell_ref[pl.ds(which[k], 1), :] = echo

            @pl.when(which[k] < cols)
            def _():
                final_ref[jnp.minimum(which[k], cols - 1)] = state_ref[k, 0:bins, :].astype(BF16)

            @pl.when(which[k] >= cols)
            def _():
                row = jnp.clip(which[k] - cols, 0, guests - 1)
                back_ref[row] = state_ref[k].astype(BF16)

        return carry

    lax.fori_loop(0, cols // GROUP, group, 0)
    means = jnp.where(
        iota((CRM_LEV, cells), 1) // CRM_X == iota((CRM_LEV, cells), 0), F32(1.0 / CRM_X), 0.0
    )
    contract = (((1,), (1,)), ((), ()))
    heat = lax.dot_general(
        means, heat_cell_ref[...], contract, precision=HIGH, preferred_element_type=F32
    )
    heat = heat.astype(BF16).astype(F32)
    echo = lax.dot_general(
        means, echo_cell_ref[...], contract, precision=HIGH, preferred_element_type=F32
    )
    both = jnp.concatenate([heat, jnp.log(1.0 + echo)], axis=0)
    own_ref[...] = both[:, 0:cols]
    away_ref[...] = both[:, cols : 2 * cols]


def block_kernel(n_gcm, n_crm, own_ref, back_ref, rank_ref, slot_ref, heat_ref, send_ref):
    cols = own_ref.shape[1]
    odd = 2 * iota((cols, cols), 0) + 1
    home = (rank_ref[...] == odd).astype(F32)
    both = own_ref[...] + jnp.dot(
        back_ref[...], home, precision=HIGH, preferred_element_type=F32
    )
    heat = both[0:CRM_LEV]
    echo = both[CRM_LEV:]
    heat_ref[...] = heat
    contract = (((1,), (1,)), ((), ()))
    devices = send_ref.shape[0]
    slots = 2 * cols
    capacity = slots // devices
    onehot = (slot_ref[...] == iota((slots, cols), 0)).astype(F32)
    packed = lax.dot_general(echo, onehot, contract, precision=HIGH, preferred_element_type=F32)
    coarse = packed.astype(BF16).astype(F32)
    rest = packed - coarse
    middle = rest.astype(BF16).astype(F32)
    pieces = (coarse, middle, rest - middle)
    lane = iota((CRM_LEV, 128), 1)
    near = heat
    far = pltpu.roll(heat, 64, 1)
    sides = jnp.where(
        lane == 1, pltpu.roll(heat, 65, 1), jnp.where(lane == 62, pltpu.roll(heat, 63, 1), heat)
    )
    g = lax.axis_index("gcm")
    for d in range(devices):
        away = d // n_crm - g
        below = (away == 1) | (away == 1 - n_gcm)
        above = (away == -1) | (away == n_gcm - 1)
        block = jnp.where(below, far, jnp.where(above, near, sides))
        tile, offset = divmod(d * capacity, 128)
        for i, piece in enumerate(pieces):
            moved = pltpu.roll(
                piece[:, 128 * tile : 128 * tile + 128], (64 + i * capacity - offset) % 128, 1
            )
            start = 64 + i * capacity
            block = jnp.where((lane >= start) & (lane < start + capacity), moved, block)
        send_ref[d] = block.astype(BF16)


def last_kernel(
    n_gcm, n_crm, base_ref, own_ref, got_ref, up_map_ref, drops_in, out_ref, power_ref, drops_out,
    *back_refs,
):
    cols = own_ref.shape[1]
    half = cols // 2
    element = iota((cols, 256), 0)
    col = iota((cols, 256), 1)
    phase = col % 4
    edge = (phase == 0) | (phase == 3)
    other = jnp.where(phase == 0, col // 4 - 1, col // 4 + 1)

    def spread(centre, start, west, west_lane, east, east_lane):
        inside = jnp.where(element == col // 4 + start, jnp.where(edge, 0.5, 1.0), 0.0)
        beside = edge & (element == other + start) & (other >= 0) & (other < half)
        middle = jnp.where(beside, 0.5, inside).astype(BF16)
        from_west = jnp.where((col == 0) & (element == west_lane), 0.5, 0.0).astype(BF16)
        from_east = jnp.where((col == 255) & (element == east_lane), 0.5, 0.0).astype(BF16)
        total = jnp.dot(centre, middle, preferred_element_type=F32)
        total += jnp.dot(west, from_west, preferred_element_type=F32)
        total += jnp.dot(east, from_east, preferred_element_type=F32)
        return total

    own = own_ref[...].astype(BF16)
    g = lax.axis_index("gcm")
    c = lax.axis_index("crm")
    north = jnp.where(g == 0, n_gcm - 1, g - 1) * n_crm
    south = jnp.where(g == n_gcm - 1, 0, g + 1) * n_crm
    west = jnp.where(c == 0, n_crm - 1, c - 1)
    east = jnp.where(c == n_crm - 1, 0, c + 1)
    up, down = got_ref[north + c], got_ref[south + c]
    left, right = got_ref[g * n_crm + west], got_ref[g * n_crm + east]
    up_left, up_right = got_ref[north + west], got_ref[north + east]
    down_left, down_right = got_ref[south + west], got_ref[south + east]
    above = spread(up, 0, up_left, half - 1, up_right, 0)
    near = spread(own, 0, left, half - 1, right, 0)
    far = spread(own, half, left, half - 2, right, 1)
    below = spread(down, 0, down_left, half - 1, down_right, 0)
    parts = (
        0.5 * (above + near), near, 0.5 * (near + far), far, 0.5 * (far + below),
    )
    up_map = up_map_ref[...]
    for part, ref in zip(parts, back_refs):
        ref[...] = DT_PHYS * jnp.dot(up_map, part, precision=HIGH, preferred_element_type=F32)

    devices = got_ref.shape[0]
    slots = power_ref.shape[1]
    capacity = slots // devices
    lane = iota((CRM_LEV, 128), 1)
    tiles = [jnp.zeros((CRM_LEV, 128), F32) for _ in range(slots // 128)]
    for d in range(devices):
        block = got_ref[d].astype(F32)
        fine = pltpu.roll(block, 128 - 2 * capacity, 1) + pltpu.roll(block, 128 - capacity, 1)
        tile, offset = divmod(d * capacity, 128)
        moved = pltpu.roll(block + fine, (offset - 64) % 128, 1)
        tiles[tile] = jnp.where((lane >= offset) & (lane < offset + capacity), moved, tiles[tile])
    power_ref[...] = jnp.concatenate(tiles, axis=1)

    def body(chunk, carry):
        levels = pl.ds(pl.multiple_of(chunk * CHUNK, CHUNK), CHUNK)
        shape = (CHUNK, 8, 256)
        row = iota(shape, 1)
        wide = [jnp.broadcast_to(ref[levels, :][:, None, :], shape) for ref in back_refs]
        back = jnp.where(
            row == 0,
            wide[0],
            jnp.where(
                row < 3,
                wide[1],
                jnp.where(row < 5, wide[2], jnp.where(row < 7, wide[3], wide[4])),
            ),
        )
        out_ref[levels] = base_ref[levels] + back
        return carry

    lax.fori_loop(0, base_ref.shape[0] // CHUNK, body, 0)


def call(kernel, outs, args, scratch=(), sems=(), flops=10_000_000, limit=16, through=()):
    spaces = {
        "s": pl.BlockSpec(memory_space=pltpu.SMEM),
        "v": pl.BlockSpec(memory_space=pltpu.VMEM),
        "h": pl.BlockSpec(memory_space=pl.ANY),
    }
    return pl.pallas_call(
        kernel,
        out_shape=[jax.ShapeDtypeStruct(s, t) for s, t in outs]
        + [jax.ShapeDtypeStruct(args[i][1].shape, args[i][1].dtype) for i in through],
        in_specs=[spaces[kind] for kind, _ in args],
        out_specs=[spaces["v"]] * len(outs) + [spaces["h"]] * len(through),
        input_output_aliases={i: len(outs) + n for n, i in enumerate(through)},
        scratch_shapes=[pltpu.VMEM(s, t) for s, t in scratch] + list(sems),
        compiler_params=pltpu.CompilerParams(vmem_limit_bytes=limit * MIB),
        cost_estimate=pl.CostEstimate(flops=flops, bytes_accessed=4_000_000, transcendentals=0),
    )(*[value for _, value in args])


def v(*values):
    return [("v", value) for value in values]


def shift(value, rows, cols):
    n_gcm = lax.axis_size("gcm")
    n_crm = lax.axis_size("crm")
    pairs = []
    for g in range(n_gcm):
        for c in range(n_crm):
            target = ((g + rows) % n_gcm) * n_crm + (c + cols) % n_crm
            pairs.append((g * n_crm + c, target))
    return lax.ppermute(value, ("gcm", "crm"), pairs)


def pair_table(bins):
    table = np.zeros((bins * bins, 576), np.float32)

    def put(column, i, j):
        table[i * bins + j, column] = 1.0
        table[j * bins + i, column] = 1.0

    for d in range(16):
        for b in range(32):
            put(32 * d + b, b, (b + d) % 32)
    for b in range(16):
        put(512 + b, b, b + 16)
    for b in range(32):
        put(528 + b, b, 32)
    put(560, 32, 32)
    return table


def to_partner(value):
    n_gcm = lax.axis_size("gcm")
    n_crm = lax.axis_size("crm")
    pairs = []
    for g in range(n_gcm):
        for c in range(n_crm):
            pairs.append((g * n_crm + c, (g ^ 1) * n_crm + c))
    return lax.ppermute(value, ("gcm", "crm"), pairs)


def shards(tracer, wind_x, wind_y, drops, owner, counts, collision, growth):
    devices = lax.axis_size("gcm") * lax.axis_size("crm")
    levels, row_count, col_count = tracer.shape
    col_total, bins, cells = drops.shape
    field = (tracer.shape, F32)
    strip = ((levels, row_count, 128), F32)
    rows = ((2, levels, col_count), F32)
    wide = col_count + 128
    down_map, up_map = level_tables(levels, CRM_LEV)

    row = ((1, col_total), jnp.int32)
    capacity = 2 * col_total // devices
    guests = col_total // 2
    tend, top, bot, to_right, to_left, count_row = call(
        first_kernel,
        [field, rows, rows] + [((levels // 4, 8, 128), F32)] * 2 + [row],
        [("h", tracer), ("h", wind_x), ("h", wind_y)] + v(counts[None, :]),
        [field] * 3,
        [pltpu.SemaphoreType.DMA((3, levels // CHUNK))],
        limit=62,
    )
    from_left = shift(to_right, 0, 1)
    from_right = shift(to_left, 0, -1)
    other_counts = to_partner(count_row)
    q_strip, u_strip, v_strip, tend_strip, top, bot = call(
        strip_kernel,
        [strip] * 4 + [((2, levels, wide), F32)] * 2,
        v(from_left, from_right, top, bot),
    )
    sent, order, force, ordered, rank, slot = call(
        functools.partial(plan_kernel, capacity),
        [row] * 6,
        v(count_row, other_counts, owner.T) + [("h", top)],
    )
    (leaving,) = call(
        gather_kernel,
        [((guests, 40, cells), BF16)],
        [("s", sent)] + v(drops),
        [((8, 40, cells), F32)],
    )
    guest_drops = to_partner(leaving)
    coef, growth_rows = call(
        coef_kernel,
        [((80, 576), BF16), ((40, cells), F32)],
        v(collision, jnp.asarray(pair_table(bins), BF16), growth[None, :]) + [("h", top)],
        [((80, 576), F32), ((8, 128), F32)],
    )
    state, smooth, tend, top, bot = call(
        second_kernel,
        [field, field, ((levels, row_count, wide), F32)] + [((1, levels, wide), F32)] * 2,
        v(tracer, wind_x, wind_y, tend, q_strip, u_strip, v_strip, tend_strip)
        + v(shift(bot, 1, 0), shift(top, -1, 0)),
    )
    base, forcing = call(
        third_kernel,
        [field, ((CRM_LEV, col_total), F32)],
        v(tracer, state, smooth, tend, shift(bot, 1, 0), shift(top, -1, 0))
        + v(jnp.asarray(down_map, F32)) + [("h", coef), ("h", growth_rows)],
        [((levels, col_count), F32), ((levels, col_count), F32)],
    )

    other_forcing = to_partner(forcing)
    n_gcm = lax.axis_size("gcm")
    n_crm = lax.axis_size("crm")

    pairs = ((2 * CRM_LEV, col_total), F32)
    final, back, own, away = call(
        crm_kernel,
        [((col_total, bins, cells), BF16), ((guests, 40, cells), BF16), pairs, pairs],
        [("s", order), ("s", force), ("s", ordered)]
        + v(drops, guest_drops, forcing, other_forcing, coef, growth_rows),
        [((GROUP, 40, cells), F32), ((GROUP, 40, cells), F32), ((GROUP, 576, cells), BF16),
         ((2 * GROUP, 48, 128), F32), ((2 * col_total, cells), F32),
         ((2 * col_total, cells), F32), ((2 * col_total, cells), F32)],
        flops=10_000_000_000,
        limit=24,
    )
    returned = to_partner(away)
    returned_drops = to_partner(back)
    heat, send = call(
        functools.partial(block_kernel, n_gcm, n_crm),
        [((CRM_LEV, col_total), F32), ((devices, CRM_LEV, 128), BF16)],
        v(own, returned, rank, slot),
    )
    got = lax.all_to_all(send, ("gcm", "crm"), split_axis=0, concat_axis=0, tiled=True)
    (drops_next,) = call(
        merge_kernel,
        [((col_total, bins, cells), BF16)],
        [("s", sent)] + v(final, returned_drops),
    )
    tracer_next, power, by_bin = call(
        functools.partial(last_kernel, n_gcm, n_crm),
        [field, ((CRM_LEV, devices * capacity), F32)],
        v(base, heat, got, jnp.asarray(up_map, F32))
        + [("h", drops_next.transpose(1, 0, 2))],
        [((levels, col_count), F32)] * 5,
        through=(4,),
    )
    drops_next = by_bin.transpose(1, 0, 2)
    return (tracer_next, drops_next, power)


def solution(mesh):
    return jax.shard_map(
        shards,
        mesh=mesh,
        in_specs=(
            P(None, "gcm", "crm"),
            P(None, "gcm", "crm"),
            P(None, "gcm", "crm"),
            P(("gcm", "crm"), None, None),
            P(("gcm", "crm"), None),
            P(("gcm", "crm")),
            P(),
            P(),
        ),
        out_specs=(P(None, "gcm", "crm"), P(("gcm", "crm"), None, None), P(None, ("gcm", "crm"))),
        check_vma=False,
    )
```

```python
import functools

import jax
import jax.numpy as jnp
import numpy as np
from jax import lax
from jax.experimental import pallas as pl
from jax.experimental.pallas import tpu as pltpu
from jax.sharding import PartitionSpec as P

CRM_X = 16
CRM_LEV = 16
DYN_STEPS = 2

DT_DYN = 0.04
DT_CRM = 0.05
DT_PHYS = 0.5
HIGH = lax.Precision.HIGHEST
F32 = jnp.float32
BF16 = jnp.bfloat16
GROUP = 8
CHUNK = 8
MIB = 1024 * 1024


def gll_tables():
    inv_root = 1.0 / np.sqrt(5.0)
    gll_nodes = np.array([-1.0, -inv_root, inv_root, 1.0])
    weights = np.array([1.0, 5.0, 5.0, 1.0]) / 6.0
    legendre = (5.0 * gll_nodes**3 - 3.0 * gll_nodes) / 2.0
    derivative = np.zeros((4, 4))
    for i in range(4):
        for j in range(4):
            if i != j:
                derivative[i, j] = legendre[i] / (legendre[j] * (gll_nodes[i] - gll_nodes[j]))
    derivative[0, 0] = -3.0
    derivative[3, 3] = 3.0
    return (2.0 * derivative, weights)


def level_tables(levels, crm_levels):
    spacing = levels / crm_levels
    centres = (np.arange(crm_levels) + 0.5) * spacing - 0.5
    hats = np.maximum(0.0, 1.0 - np.abs(np.arange(levels)[None, :] - centres[:, None]) / spacing)
    down_map = hats / hats.sum(axis=1, keepdims=True)
    up_map = hats.T / hats.T.sum(axis=1, keepdims=True)
    return (down_map, up_map)


DERIV, WEIGHTS = gll_tables()


def iota(shape, axis):
    return lax.broadcasted_iota(jnp.int32, shape, axis)


def derivative_terms(shape, axis):
    phase = iota(shape, axis) % 4
    terms = []
    for shift in range(-3, 4):
        value = jnp.zeros(shape, F32)
        for i in range(4):
            if 0 <= i + shift < 4:
                value = jnp.where(phase == i, F32(DERIV[i, i + shift]), value)
        terms.append((shift, value))
    return terms


def along(x, terms, axis):
    size = x.shape[axis]
    total = None
    for shift, value in terms:
        moved = x if shift == 0 else pltpu.roll(x, (-shift) % size, axis)
        part = value[None] * moved
        total = part if total is None else total + part
    return total


def tendency(x, u, v, row_terms, col_terms):
    halves = []
    for h in range(x.shape[2] // 128):
        cut = slice(128 * h, 128 * h + 128)
        q = x[:, :, cut]
        grad_x = along(q, row_terms, 1)
        grad_y = along(q, col_terms, 2)
        halves.append(-(u[:, :, cut] * grad_x + v[:, :, cut] * grad_y))
    return jnp.concatenate(halves, axis=2)


def put_rows(x, levels, top_ref, bot_ref, i):
    top_ref[i, levels, :] = x[:, 0, :]
    bot_ref[i, levels, :] = x[:, 7, :]


def first_kernel(
    q_hbm, u_hbm, v_hbm, count_ref,
    tend_ref, top_ref, bot_ref, right_ref, left_ref, count_out_ref, q_ref, u_ref, v_ref, sems,
):
    row_terms = derivative_terms((8, 128), 0)
    col_terms = derivative_terms((8, 128), 1)
    lane = iota((8, 128), 1)
    count_out_ref[...] = count_ref[...]
    chunks = q_ref.shape[0] // CHUNK

    def copies(chunk):
        levels = pl.ds(pl.multiple_of(chunk * CHUNK, CHUNK), CHUNK)
        return [
            pltpu.make_async_copy(src.at[levels], dst.at[levels], sems.at[i, chunk])
            for i, (src, dst) in enumerate(((q_hbm, q_ref), (u_hbm, u_ref), (v_hbm, v_ref)))
        ]

    for chunk in range(chunks):
        for copy in copies(chunk):
            copy.start()

    def body(chunk, carry):
        for copy in copies(chunk):
            copy.wait()
        for half in range(CHUNK // 4):
            right = jnp.zeros((8, 128), F32)
            left = jnp.zeros((8, 128), F32)
            for j in range(4):
                for f, ref in enumerate((q_ref, u_ref, v_ref)):
                    start = 32 * j + 8 * f
                    here = (lane >= start) & (lane < start + 8)
                    x = ref[chunk * CHUNK + half * 4 + j]
                    moved = pltpu.roll(x[:, 128:256], (start - 120) % 128, 1)
                    right = jnp.where(here, moved, right)
                    first = x[:, 0:128]
                    if start:
                        first = pltpu.roll(first, start, 1)
                    left = jnp.where(here, first, left)
            right_ref[chunk * (CHUNK // 4) + half] = right
            left_ref[chunk * (CHUNK // 4) + half] = left
        levels = pl.ds(pl.multiple_of(chunk * CHUNK, CHUNK), CHUNK)
        q = q_ref[levels]
        tend = tendency(q, u_ref[levels], v_ref[levels], row_terms, col_terms)
        tend_ref[levels] = tend
        put_rows(tend, levels, top_ref, bot_ref, 0)
        put_rows(q, levels, top_ref, bot_ref, 1)
        return carry

    lax.fori_loop(0, chunks, body, 0)


def strip_kernel(
    left_ref, right_ref, top_main, bot_main,
    q_ref, u_ref, v_ref, tend_ref, top_ref, bot_ref,
):
    row_terms = derivative_terms((8, 128), 0)
    col_terms = derivative_terms((8, 128), 1)
    lane = iota((8, 128), 1)
    for out, main in ((top_ref, top_main), (bot_ref, bot_main)):
        out[:, 0:256] = main[0]
        out[:, 256:512] = main[1]

    def body(chunk, carry):
        tiles = [[], [], []]
        for half in range(CHUNK // 4):
            west = left_ref[chunk * (CHUNK // 4) + half]
            east = right_ref[chunk * (CHUNK // 4) + half]
            for j in range(4):
                for f in range(3):
                    start = 32 * j + 8 * f
                    a = pltpu.roll(east, 128 - start, 1) if start else east
                    b = pltpu.roll(west, (120 - start) % 128, 1)
                    tiles[f].append(jnp.where(lane < 8, a, jnp.where(lane >= 120, b, 0.0)))
        q, u, v = [jnp.stack(tile, axis=0) for tile in tiles]
        levels = pl.ds(pl.multiple_of(chunk * CHUNK, CHUNK), CHUNK)
        q_ref[levels] = q
        u_ref[levels] = u
        v_ref[levels] = v
        tend = tendency(q, u, v, row_terms, col_terms)
        tend_ref[levels] = tend
        shared = jnp.where((lane >= 8) & (lane < 24), pltpu.roll(q, 16, 2), tend)
        top_ref[levels, 512:640] = shared[:, 0, :]
        bot_ref[levels, 512:640] = shared[:, 7, :]
        return carry

    lax.fori_loop(0, q_ref.shape[0] // CHUNK, body, 0)


def assemble_chunk(x, up, down):
    shape = x.shape
    row = iota(shape, 1)
    partner = jnp.where(
        row == 0,
        jnp.broadcast_to(up[:, None, :], shape),
        jnp.where(
            row == 7,
            jnp.broadcast_to(down[:, None, :], shape),
            jnp.where(row == 3, pltpu.roll(x, 7, 1), pltpu.roll(x, 1, 1)),
        ),
    )
    x = jnp.where((row % 4 == 0) | (row % 4 == 3), 0.5 * (x + partner), x)
    col = iota(shape, 2)
    partner = jnp.where(
        col % 4 == 3, pltpu.roll(x, shape[2] - 1, 2), pltpu.roll(x, 1, 2)
    )
    return jnp.where((col % 4 == 0) | (col % 4 == 3), 0.5 * (x + partner), x)


def join(main, strip):
    return jnp.concatenate([main, strip], axis=2)


def second_kernel(
    q_ref, u_ref, v_ref, tend_ref, q_strip, u_strip, v_strip, tend_strip, up_ref, down_ref,
    state_ref, smooth_ref, next_ref, top_ref, bot_ref,
):
    row_terms = derivative_terms((8, 128), 0)
    col_terms = derivative_terms((8, 128), 1)

    def body(chunk, carry):
        levels = pl.ds(pl.multiple_of(chunk * CHUNK, CHUNK), CHUNK)
        q = join(q_ref[levels], q_strip[levels])
        rows = []
        for ref in (up_ref, down_ref):
            shared = ref[levels, 512:640]
            rows.append(jnp.concatenate([ref[levels, 0:256], shared], axis=1))
            rows.append(jnp.concatenate([ref[levels, 256:512], pltpu.roll(shared, 112, 1)], axis=1))
        change = assemble_chunk(join(tend_ref[levels], tend_strip[levels]), rows[0], rows[2])
        smooth = assemble_chunk(q, rows[1], rows[3])
        smooth_ref[levels] = smooth[:, :, 0:256]
        state = q + DT_DYN * change
        state_ref[levels] = state[:, :, 0:256]
        tend = tendency(
            state, join(u_ref[levels], u_strip[levels]), join(v_ref[levels], v_strip[levels]),
            row_terms, col_terms,
        )
        next_ref[levels] = tend
        put_rows(tend, levels, top_ref, bot_ref, 0)
        return carry

    lax.fori_loop(0, q_ref.shape[0] // CHUNK, body, 0)


def third_kernel(
    q_ref, state_ref, smooth_ref, tend_ref, up_ref, down_ref, down_map_ref, coef_ref, growth_ref,
    base_ref, forcing_ref, near_ref, far_ref,
):
    cols = forcing_ref.shape[1]
    half = cols // 2
    phase = iota((8, 256), 0) % 4
    row_weight = jnp.where((phase == 0) | (phase == 3), F32(WEIGHTS[0]), F32(WEIGHTS[1]))
    near_rows = jnp.where(iota((8, 256), 0) < 4, row_weight, 0.0)
    far_rows = row_weight - near_rows

    def body(chunk, carry):
        levels = pl.ds(pl.multiple_of(chunk * CHUNK, CHUNK), CHUNK)
        change = assemble_chunk(tend_ref[levels], up_ref[0, levels, :], down_ref[0, levels, :])
        moved = (state_ref[levels] + DT_DYN * change[:, :, 0:256]) - q_ref[levels]
        base_ref[levels] = smooth_ref[levels] + moved
        near_ref[levels, :] = jnp.sum(moved * near_rows[None], axis=1)
        far_ref[levels, :] = jnp.sum(moved * far_rows[None], axis=1)
        return carry

    lax.fori_loop(0, q_ref.shape[0] // CHUNK, body, 0)
    point = iota((256, cols), 0)
    element = iota((256, cols), 1)
    weight = jnp.where(
        (point % 4 == 0) | (point % 4 == 3), F32(WEIGHTS[0]), F32(WEIGHTS[1])
    ) * F32(0.25 / (DYN_STEPS * DT_DYN))
    near_cols = jnp.where(point // 4 == element, weight, 0.0)
    far_cols = jnp.where(point // 4 + half == element, weight, 0.0)
    means = jnp.dot(near_ref[...], near_cols, precision=HIGH, preferred_element_type=F32)
    means += jnp.dot(far_ref[...], far_cols, precision=HIGH, preferred_element_type=F32)
    forcing = jnp.dot(down_map_ref[...], means, precision=HIGH, preferred_element_type=F32)
    forcing_ref[...] = forcing.astype(BF16).astype(F32)


def coef_kernel(
    collision_ref, table_ref, growth_ref, after_ref, coef_ref, growth_out_ref, wide_ref, line_ref
):
    bins = collision_ref.shape[0]
    total = jnp.dot(collision_ref[...], table_ref[...], preferred_element_type=F32) * DT_CRM
    coarse = total.astype(BF16).astype(F32)
    wide_ref[...] = jnp.zeros(wide_ref.shape, F32)
    wide_ref[0:bins, :] = coarse
    wide_ref[40 : 40 + bins, :] = total - coarse
    coef_ref[...] = wide_ref[...].astype(BF16)
    line_ref[...] = jnp.zeros(line_ref.shape, F32)
    line_ref[0:1, 0:bins] = growth_ref[...]
    rows = jnp.broadcast_to(line_ref[0:1, :], (128, 128)).T[0:40]
    for h in range(growth_out_ref.shape[1] // 128):
        growth_out_ref[:, 128 * h : 128 * h + 128] = rows


def rank_row(values):
    total = values.shape[1]
    across = jnp.broadcast_to(values, (total, total))
    down = across.T
    earlier = iota((total, total), 0) < iota((total, total), 1)
    ahead = (down > across) | ((down == across) & earlier)
    return jnp.sum(ahead.astype(F32), axis=0, keepdims=True)


def plan_kernel(
    capacity, count_ref, other_ref, owner_ref, after_ref,
    sent_ref, order_ref, force_ref, ordered_ref, rank_ref, slot_ref,
):
    cols = count_ref.shape[1]
    counts = count_ref[...].astype(F32)
    others = other_ref[...].astype(F32)
    rank = rank_row(counts)
    other_rank = rank_row(others)
    square = (cols, cols)
    index = iota(square, 0).astype(F32)
    odd = 2.0 * iota(square, 1).astype(F32) + 1.0
    down_rank = jnp.broadcast_to(rank, square).T
    sent = jnp.sum(jnp.where(down_rank == odd, index, 0.0), axis=0, keepdims=True)
    sent_ref[...] = sent.astype(jnp.int32)
    rank_ref[...] = rank.astype(jnp.int32)

    is_odd = rank.astype(jnp.int32) % 2 == 1
    other_odd = other_rank.astype(jnp.int32) % 2 == 1
    listed = jnp.concatenate(
        [jnp.where(is_odd, -1.0, counts), jnp.where(other_odd, others, -1.0)], axis=1
    )
    lane = iota((1, cols), 1).astype(F32)
    name = jnp.concatenate([lane, cols + 0.5 * (other_rank - 1.0)], axis=1)
    wide = (2 * cols, 2 * cols)
    place = jnp.broadcast_to(rank_row(listed), wide).T[:, 0:cols]
    here = place == iota((2 * cols, cols), 1).astype(F32)
    force = iota((2 * cols, cols), 0).astype(F32)
    name = jnp.broadcast_to(name, wide).T[:, 0:cols]
    value = jnp.broadcast_to(listed, wide).T[:, 0:cols]
    for what, ref in ((name, order_ref), (force, force_ref), (value, ordered_ref)):
        total = jnp.sum(jnp.where(here, what, 0.0), axis=0, keepdims=True)
        ref[...] = total.astype(jnp.int32)

    owners = jnp.broadcast_to(owner_ref[...].astype(F32), square)
    same = (owners.T == owners) & (iota(square, 0) < iota(square, 1))
    earlier = jnp.sum(same.astype(F32), axis=0, keepdims=True)
    slot_ref[...] = owner_ref[...] * capacity + earlier.astype(jnp.int32)


def gather_kernel(sent_ref, drops_ref, out_ref, wide_ref):
    bins = drops_ref.shape[1]
    wide_ref[...] = jnp.zeros(wide_ref.shape, F32)

    def body(p, carry):
        for k in range(8):
            wide_ref[k, 0:bins, :] = drops_ref[sent_ref[0, 8 * p + k]].astype(F32)
        for k in range(8):
            out_ref[8 * p + k] = wide_ref[k].astype(BF16)
        return carry

    lax.fori_loop(0, out_ref.shape[0] // 8, body, 0)


def merge_kernel(sent_ref, final_ref, back_ref, out_ref):
    out_ref[...] = final_ref[...]

    def body(p, carry):
        row = back_ref[p].astype(F32)[0 : out_ref.shape[1]]
        out_ref[sent_ref[0, p]] = row.astype(BF16)
        return carry

    lax.fori_loop(0, back_ref.shape[0] - 1, body, 0)


def crm_kernel(
    order_ref, force_ref, count_ref, sent_ref,
    drops_ref, guest_ref, forcing_ref, other_ref, coef_ref, growth_ref,
    final_ref, back_ref, own_ref, away_ref,
    state_ref, start_ref, pair_ref, twice_ref, cell_ref, heat_cell_ref, echo_cell_ref,
):
    bins = drops_ref.shape[1]
    cells = drops_ref.shape[2]
    cols = drops_ref.shape[0]
    guests = guest_ref.shape[0]
    coef = coef_ref[...]
    growth = growth_ref[...]
    state_ref[...] = jnp.zeros(state_ref.shape, F32)
    heat_cell_ref[...] = jnp.zeros(heat_cell_ref.shape, F32)
    echo_cell_ref[...] = jnp.zeros(echo_cell_ref.shape, F32)
    mass = (iota((40, cells), 0) + 1).astype(F32) / F32(bins)
    spread = (iota((CRM_LEV, cells), 1) // CRM_X == iota((CRM_LEV, cells), 0)).astype(BF16)
    for i, ref in enumerate((forcing_ref, other_ref)):
        rows = jnp.dot(ref[...].T.astype(BF16), spread, preferred_element_type=F32)
        cell_ref[cols * i : cols * i + cols, :] = DT_CRM * rows

    def grow(k, which, zero):
        grown = state_ref[k] + growth * cell_ref[pl.ds(which, 1), :]
        for h in range(cells // 128):
            cut = slice(128 * h, 128 * h + 128)
            g = grown[0:32, cut]
            last = grown[32:40, cut]
            twice_ref[2 * k + h, 0:32, :] = g
            twice_ref[2 * k + h, 32:48, :] = g[0:16]
            for d in range(16):
                other = g if d % 8 == 0 else twice_ref[2 * k + h, pl.ds(zero + d, 32), :]
                if d == 8:
                    other = jnp.concatenate([g[8:], g[:8]], axis=0)
                pair_ref[k, 32 * d : 32 * d + 32, cut] = (g * other).astype(BF16)
            pair_ref[k, 512:528, cut] = (g[0:16] * g[16:32]).astype(BF16)
            pair_ref[k, 528:560, cut] = (g * last[0:1]).astype(BF16)
            tail = jnp.concatenate([last * last, jnp.zeros((8, 128), F32)], axis=0)
            pair_ref[k, 560:576, cut] = tail.astype(BF16)
        return grown

    def group(index, carry):
        base = index * GROUP
        which = [order_ref[0, base + k] for k in range(GROUP)]
        force = [force_ref[0, base + k] for k in range(GROUP)]
        count = [count_ref[0, base + k] for k in range(GROUP)]
        for k in range(GROUP):
            mine = drops_ref[jnp.minimum(which[k], cols - 1)].astype(F32)
            guest = guest_ref[jnp.clip(which[k] - cols, 0, guests - 1)].astype(F32)
            start = jnp.where(which[k] < cols, mine, guest[0:bins])
            start_ref[k, 0:bins, :] = start
            state_ref[k, 0:bins, :] = start

        zero = jnp.minimum(which[0], 0)

        def step(s, c):
            for k in range(GROUP):
                grown = grow(k, force[k], zero)
                change = jnp.dot(coef, pair_ref[k], preferred_element_type=F32)
                moved = grown + (change[0:40] + change[40:80])
                state_ref[k] = jnp.where(s < count[k], moved, state_ref[k])
            return c

        lax.fori_loop(0, count[0], step, 0)
        for k in range(GROUP):
            final = state_ref[k, 0:bins, :]
            weighted = mass[0:bins] * final
            heat = jnp.sum(mass[0:bins] * (final - start_ref[k, 0:bins, :]), axis=0, keepdims=True)
            echo = jnp.sum(weighted * weighted, axis=0, keepdims=True)
            heat_cell_ref[pl.ds(which[k], 1), :] = heat
            echo_cell_ref[pl.ds(which[k], 1), :] = echo

            result = state_ref[k].astype(BF16)
            guest = jnp.clip(which[k] - cols, 0, guests - 1)
            mine = which[k] < cols
            final_ref[jnp.where(mine, which[k], sent_ref[0, guest])] = final.astype(BF16)
            back_ref[jnp.where(mine, guests, guest)] = result
        return carry

    lax.fori_loop(0, cols // GROUP, group, 0)
    means = jnp.where(
        iota((CRM_LEV, cells), 1) // CRM_X == iota((CRM_LEV, cells), 0), F32(1.0 / CRM_X), 0.0
    )
    contract = (((1,), (1,)), ((), ()))
    heat = lax.dot_general(
        means, heat_cell_ref[...], contract, precision=HIGH, preferred_element_type=F32
    )
    heat = heat.astype(BF16).astype(F32)
    echo = lax.dot_general(
        means, echo_cell_ref[...], contract, precision=HIGH, preferred_element_type=F32
    )
    both = jnp.concatenate([heat, jnp.log(1.0 + echo)], axis=0)
    own_ref[...] = both[:, 0:cols]
    away_ref[...] = both[:, cols : 2 * cols]


def block_kernel(n_gcm, n_crm, own_ref, back_ref, rank_ref, slot_ref, heat_ref, send_ref):
    cols = own_ref.shape[1]
    odd = 2 * iota((cols, cols), 0) + 1
    home = (rank_ref[...] == odd).astype(F32)
    both = own_ref[...] + jnp.dot(
        back_ref[...], home, precision=HIGH, preferred_element_type=F32
    )
    heat = both[0:CRM_LEV]
    echo = both[CRM_LEV:]
    heat_ref[...] = heat
    contract = (((1,), (1,)), ((), ()))
    devices = send_ref.shape[0]
    slots = 2 * cols
    capacity = slots // devices
    onehot = (slot_ref[...] == iota((slots, cols), 0)).astype(F32)
    packed = lax.dot_general(echo, onehot, contract, precision=HIGH, preferred_element_type=F32)
    coarse = packed.astype(BF16).astype(F32)
    rest = packed - coarse
    middle = rest.astype(BF16).astype(F32)
    pieces = (coarse, middle, rest - middle)
    lane = iota((CRM_LEV, 128), 1)
    near = heat
    far = pltpu.roll(heat, 64, 1)
    sides = jnp.where(
        lane == 1, pltpu.roll(heat, 65, 1), jnp.where(lane == 62, pltpu.roll(heat, 63, 1), heat)
    )
    g = lax.axis_index("gcm")
    for d in range(devices):
        away = d // n_crm - g
        below = (away == 1) | (away == 1 - n_gcm)
        above = (away == -1) | (away == n_gcm - 1)
        block = jnp.where(below, far, jnp.where(above, near, sides))
        tile, offset = divmod(d * capacity, 128)
        for i, piece in enumerate(pieces):
            moved = pltpu.roll(
                piece[:, 128 * tile : 128 * tile + 128], (64 + i * capacity - offset) % 128, 1
            )
            start = 64 + i * capacity
            block = jnp.where((lane >= start) & (lane < start + capacity), moved, block)
        send_ref[d] = block.astype(BF16)


def last_kernel(
    n_gcm, n_crm, base_ref, own_ref, got_ref, up_map_ref, drops_in, out_ref, power_ref, drops_out,
    *back_refs,
):
    cols = own_ref.shape[1]
    half = cols // 2
    element = iota((cols, 256), 0)
    col = iota((cols, 256), 1)
    phase = col % 4
    edge = (phase == 0) | (phase == 3)
    other = jnp.where(phase == 0, col // 4 - 1, col // 4 + 1)

    def spread(centre, start, west, west_lane, east, east_lane):
        inside = jnp.where(element == col // 4 + start, jnp.where(edge, 0.5, 1.0), 0.0)
        beside = edge & (element == other + start) & (other >= 0) & (other < half)
        middle = jnp.where(beside, 0.5, inside).astype(BF16)
        from_west = jnp.where((col == 0) & (element == west_lane), 0.5, 0.0).astype(BF16)
        from_east = jnp.where((col == 255) & (element == east_lane), 0.5, 0.0).astype(BF16)
        total = jnp.dot(centre, middle, preferred_element_type=F32)
        total += jnp.dot(west, from_west, preferred_element_type=F32)
        total += jnp.dot(east, from_east, preferred_element_type=F32)
        return total

    own = own_ref[...].astype(BF16)
    g = lax.axis_index("gcm")
    c = lax.axis_index("crm")
    north = jnp.where(g == 0, n_gcm - 1, g - 1) * n_crm
    south = jnp.where(g == n_gcm - 1, 0, g + 1) * n_crm
    west = jnp.where(c == 0, n_crm - 1, c - 1)
    east = jnp.where(c == n_crm - 1, 0, c + 1)
    up, down = got_ref[north + c], got_ref[south + c]
    left, right = got_ref[g * n_crm + west], got_ref[g * n_crm + east]
    up_left, up_right = got_ref[north + west], got_ref[north + east]
    down_left, down_right = got_ref[south + west], got_ref[south + east]
    above = spread(up, 0, up_left, half - 1, up_right, 0)
    near = spread(own, 0, left, half - 1, right, 0)
    far = spread(own, half, left, half - 2, right, 1)
    below = spread(down, 0, down_left, half - 1, down_right, 0)
    parts = (
        0.5 * (above + near), near, 0.5 * (near + far), far, 0.5 * (far + below),
    )
    up_map = up_map_ref[...]
    for part, ref in zip(parts, back_refs):
        ref[...] = DT_PHYS * jnp.dot(up_map, part, precision=HIGH, preferred_element_type=F32)

    devices = got_ref.shape[0]
    slots = power_ref.shape[1]
    capacity = slots // devices
    lane = iota((CRM_LEV, 128), 1)
    tiles = [jnp.zeros((CRM_LEV, 128), F32) for _ in range(slots // 128)]
    for d in range(devices):
        block = got_ref[d].astype(F32)
        fine = pltpu.roll(block, 128 - 2 * capacity, 1) + pltpu.roll(block, 128 - capacity, 1)
        tile, offset = divmod(d * capacity, 128)
        moved = pltpu.roll(block + fine, (offset - 64) % 128, 1)
        tiles[tile] = jnp.where((lane >= offset) & (lane < offset + capacity), moved, tiles[tile])
    power_ref[...] = jnp.concatenate(tiles, axis=1)

    def body(chunk, carry):
        levels = pl.ds(pl.multiple_of(chunk * CHUNK, CHUNK), CHUNK)
        shape = (CHUNK, 8, 256)
        row = iota(shape, 1)
        wide = [jnp.broadcast_to(ref[levels, :][:, None, :], shape) for ref in back_refs]
        back = jnp.where(
            row == 0,
            wide[0],
            jnp.where(
                row < 3,
                wide[1],
                jnp.where(row < 5, wide[2], jnp.where(row < 7, wide[3], wide[4])),
            ),
        )
        out_ref[levels] = base_ref[levels] + back
        return carry

    lax.fori_loop(0, base_ref.shape[0] // CHUNK, body, 0)


def call(kernel, outs, args, scratch=(), sems=(), flops=10_000_000, limit=16, through=()):
    spaces = {
        "s": pl.BlockSpec(memory_space=pltpu.SMEM),
        "v": pl.BlockSpec(memory_space=pltpu.VMEM),
        "h": pl.BlockSpec(memory_space=pl.ANY),
    }
    return pl.pallas_call(
        kernel,
        out_shape=[jax.ShapeDtypeStruct(s, t) for s, t in outs]
        + [jax.ShapeDtypeStruct(args[i][1].shape, args[i][1].dtype) for i in through],
        in_specs=[spaces[kind] for kind, _ in args],
        out_specs=[spaces["v"]] * len(outs) + [spaces["h"]] * len(through),
        input_output_aliases={i: len(outs) + n for n, i in enumerate(through)},
        scratch_shapes=[pltpu.VMEM(s, t) for s, t in scratch] + list(sems),
        compiler_params=pltpu.CompilerParams(vmem_limit_bytes=limit * MIB),
        cost_estimate=pl.CostEstimate(flops=flops, bytes_accessed=4_000_000, transcendentals=0),
    )(*[value for _, value in args])


def v(*values):
    return [("v", value) for value in values]


def shift(value, rows, cols):
    n_gcm = lax.axis_size("gcm")
    n_crm = lax.axis_size("crm")
    pairs = []
    for g in range(n_gcm):
        for c in range(n_crm):
            target = ((g + rows) % n_gcm) * n_crm + (c + cols) % n_crm
            pairs.append((g * n_crm + c, target))
    return lax.ppermute(value, ("gcm", "crm"), pairs)


def pair_table(bins):
    table = np.zeros((bins * bins, 576), np.float32)

    def put(column, i, j):
        table[i * bins + j, column] = 1.0
        table[j * bins + i, column] = 1.0

    for d in range(16):
        for b in range(32):
            put(32 * d + b, b, (b + d) % 32)
    for b in range(16):
        put(512 + b, b, b + 16)
    for b in range(32):
        put(528 + b, b, 32)
    put(560, 32, 32)
    return table


def to_partner(value):
    n_gcm = lax.axis_size("gcm")
    n_crm = lax.axis_size("crm")
    pairs = []
    for g in range(n_gcm):
        for c in range(n_crm):
            pairs.append((g * n_crm + c, (g ^ 1) * n_crm + c))
    return lax.ppermute(value, ("gcm", "crm"), pairs)


def shards(tracer, wind_x, wind_y, drops, owner, counts, collision, growth):
    devices = lax.axis_size("gcm") * lax.axis_size("crm")
    levels, row_count, col_count = tracer.shape
    col_total, bins, cells = drops.shape
    field = (tracer.shape, F32)
    strip = ((levels, row_count, 128), F32)
    rows = ((2, levels, col_count), F32)
    wide = col_count + 128
    down_map, up_map = level_tables(levels, CRM_LEV)

    row = ((1, col_total), jnp.int32)
    capacity = 2 * col_total // devices
    guests = col_total // 2
    tend, top, bot, to_right, to_left, count_row = call(
        first_kernel,
        [field, rows, rows] + [((levels // 4, 8, 128), F32)] * 2 + [row],
        [("h", tracer), ("h", wind_x), ("h", wind_y)] + v(counts[None, :]),
        [field] * 3,
        [pltpu.SemaphoreType.DMA((3, levels // CHUNK))],
        limit=62,
    )
    from_left = shift(to_right, 0, 1)
    from_right = shift(to_left, 0, -1)
    other_counts = to_partner(count_row)
    q_strip, u_strip, v_strip, tend_strip, top, bot = call(
        strip_kernel,
        [strip] * 4 + [((levels, wide + col_count), F32)] * 2,
        v(from_left, from_right, top, bot),
    )
    sent, order, force, ordered, rank, slot = call(
        functools.partial(plan_kernel, capacity),
        [row] * 6,
        v(count_row, other_counts, owner.T) + [("h", top)],
    )
    (leaving,) = call(
        gather_kernel,
        [((guests, 40, cells), BF16)],
        [("s", sent)] + v(drops),
        [((8, 40, cells), F32)],
    )
    guest_drops = to_partner(leaving)
    coef, growth_rows = call(
        coef_kernel,
        [((80, 576), BF16), ((40, cells), F32)],
        v(collision, jnp.asarray(pair_table(bins), BF16), growth[None, :]) + [("h", top)],
        [((80, 576), F32), ((8, 128), F32)],
    )
    state, smooth, tend, top, bot = call(
        second_kernel,
        [field, field, ((levels, row_count, wide), F32)] + [((1, levels, wide), F32)] * 2,
        v(tracer, wind_x, wind_y, tend, q_strip, u_strip, v_strip, tend_strip)
        + v(shift(bot, 1, 0), shift(top, -1, 0)),
    )
    base, forcing = call(
        third_kernel,
        [field, ((CRM_LEV, col_total), F32)],
        v(tracer, state, smooth, tend, shift(bot, 1, 0), shift(top, -1, 0))
        + v(jnp.asarray(down_map, F32)) + [("h", coef), ("h", growth_rows)],
        [((levels, col_count), F32), ((levels, col_count), F32)],
    )

    other_forcing = to_partner(forcing)
    n_gcm = lax.axis_size("gcm")
    n_crm = lax.axis_size("crm")

    pairs = ((2 * CRM_LEV, col_total), F32)
    final, back, own, away = call(
        crm_kernel,
        [((col_total, bins, cells), BF16), ((guests + 1, 40, cells), BF16), pairs, pairs],
        [("s", order), ("s", force), ("s", ordered), ("s", sent)]
        + v(drops, guest_drops, forcing, other_forcing, coef, growth_rows),
        [((GROUP, 40, cells), F32), ((GROUP, 40, cells), F32), ((GROUP, 576, cells), BF16),
         ((2 * GROUP, 48, 128), F32), ((2 * col_total, cells), F32),
         ((2 * col_total, cells), F32), ((2 * col_total, cells), F32)],
        flops=10_000_000_000,
        limit=24,
    )
    returned = to_partner(away)
    returned_drops = to_partner(back)
    heat, send = call(
        functools.partial(block_kernel, n_gcm, n_crm),
        [((CRM_LEV, col_total), F32), ((devices, CRM_LEV, 128), BF16)],
        v(own, returned, rank, slot),
    )
    got = lax.all_to_all(send, ("gcm", "crm"), split_axis=0, concat_axis=0, tiled=True)
    (drops_next,) = call(
        merge_kernel,
        [((col_total, bins, cells), BF16)],
        [("s", sent)] + v(final, returned_drops),
    )
    tracer_next, power, by_bin = call(
        functools.partial(last_kernel, n_gcm, n_crm),
        [field, ((CRM_LEV, devices * capacity), F32)],
        v(base, heat, got, jnp.asarray(up_map, F32))
        + [("h", drops_next.transpose(1, 0, 2))],
        [((levels, col_count), F32)] * 5,
        through=(4,),
    )
    drops_next = by_bin.transpose(1, 0, 2)
    return (tracer_next, drops_next, power)


def solution(mesh):
    return jax.shard_map(
        shards,
        mesh=mesh,
        in_specs=(
            P(None, "gcm", "crm"),
            P(None, "gcm", "crm"),
            P(None, "gcm", "crm"),
            P(("gcm", "crm"), None, None),
            P(("gcm", "crm"), None),
            P(("gcm", "crm")),
            P(),
            P(),
        ),
        out_specs=(P(None, "gcm", "crm"), P(("gcm", "crm"), None, None), P(None, ("gcm", "crm"))),
        check_vma=False,
    )
```

```python
import functools

import jax
import jax.numpy as jnp
import numpy as np
from jax import lax
from jax.experimental import pallas as pl
from jax.experimental.pallas import tpu as pltpu
from jax.sharding import PartitionSpec as P

CRM_X = 16
CRM_LEV = 16
DYN_STEPS = 2

DT_DYN = 0.04
DT_CRM = 0.05
DT_PHYS = 0.5
HIGH = lax.Precision.HIGHEST
F32 = jnp.float32
BF16 = jnp.bfloat16
GROUP = 8
CHUNK = 8
MIB = 1024 * 1024


def gll_tables():
    inv_root = 1.0 / np.sqrt(5.0)
    gll_nodes = np.array([-1.0, -inv_root, inv_root, 1.0])
    weights = np.array([1.0, 5.0, 5.0, 1.0]) / 6.0
    legendre = (5.0 * gll_nodes**3 - 3.0 * gll_nodes) / 2.0
    derivative = np.zeros((4, 4))
    for i in range(4):
        for j in range(4):
            if i != j:
                derivative[i, j] = legendre[i] / (legendre[j] * (gll_nodes[i] - gll_nodes[j]))
    derivative[0, 0] = -3.0
    derivative[3, 3] = 3.0
    return (2.0 * derivative, weights)


def level_tables(levels, crm_levels):
    spacing = levels / crm_levels
    centres = (np.arange(crm_levels) + 0.5) * spacing - 0.5
    hats = np.maximum(0.0, 1.0 - np.abs(np.arange(levels)[None, :] - centres[:, None]) / spacing)
    down_map = hats / hats.sum(axis=1, keepdims=True)
    up_map = hats.T / hats.T.sum(axis=1, keepdims=True)
    return (down_map, up_map)


DERIV, WEIGHTS = gll_tables()


def iota(shape, axis):
    return lax.broadcasted_iota(jnp.int32, shape, axis)


def derivative_terms(shape, axis):
    phase = iota(shape, axis) % 4
    terms = []
    for shift in range(-3, 4):
        value = jnp.zeros(shape, F32)
        for i in range(4):
            if 0 <= i + shift < 4:
                value = jnp.where(phase == i, F32(DERIV[i, i + shift]), value)
        terms.append((shift, value))
    return terms


def along(x, terms, axis):
    size = x.shape[axis]
    total = None
    for shift, value in terms:
        moved = x if shift == 0 else pltpu.roll(x, (-shift) % size, axis)
        part = value[None] * moved
        total = part if total is None else total + part
    return total


def tendency(x, u, v, row_terms, col_terms):
    halves = []
    for h in range(x.shape[2] // 128):
        cut = slice(128 * h, 128 * h + 128)
        q = x[:, :, cut]
        grad_x = along(q, row_terms, 1)
        grad_y = along(q, col_terms, 2)
        halves.append(-(u[:, :, cut] * grad_x + v[:, :, cut] * grad_y))
    return jnp.concatenate(halves, axis=2)


def put_rows(x, levels, top_ref, bot_ref, i):
    top_ref[i, levels, :] = x[:, 0, :]
    bot_ref[i, levels, :] = x[:, 7, :]


def first_kernel(
    q_hbm, u_hbm, v_hbm, count_ref,
    tend_ref, top_ref, bot_ref, right_ref, left_ref, count_out_ref, q_ref, u_ref, v_ref, sems,
):
    row_terms = derivative_terms((8, 128), 0)
    col_terms = derivative_terms((8, 128), 1)
    lane = iota((8, 128), 1)
    count_out_ref[...] = count_ref[...]
    chunks = q_ref.shape[0] // CHUNK

    def copies(chunk):
        levels = pl.ds(pl.multiple_of(chunk * CHUNK, CHUNK), CHUNK)
        return [
            pltpu.make_async_copy(src.at[levels], dst.at[levels], sems.at[i, chunk])
            for i, (src, dst) in enumerate(((q_hbm, q_ref), (u_hbm, u_ref), (v_hbm, v_ref)))
        ]

    for chunk in range(chunks):
        for copy in copies(chunk):
            copy.start()

    def body(chunk, carry):
        for copy in copies(chunk):
            copy.wait()
        for half in range(CHUNK // 4):
            right = jnp.zeros((8, 128), F32)
            left = jnp.zeros((8, 128), F32)
            for j in range(4):
                for f, ref in enumerate((q_ref, u_ref, v_ref)):
                    start = 32 * j + 8 * f
                    here = (lane >= start) & (lane < start + 8)
                    x = ref[chunk * CHUNK + half * 4 + j]
                    moved = pltpu.roll(x[:, 128:256], (start - 120) % 128, 1)
                    right = jnp.where(here, moved, right)
                    first = x[:, 0:128]
                    if start:
                        first = pltpu.roll(first, start, 1)
                    left = jnp.where(here, first, left)
            right_ref[chunk * (CHUNK // 4) + half] = right
            left_ref[chunk * (CHUNK // 4) + half] = left
        levels = pl.ds(pl.multiple_of(chunk * CHUNK, CHUNK), CHUNK)
        q = q_ref[levels]
        tend = tendency(q, u_ref[levels], v_ref[levels], row_terms, col_terms)
        tend_ref[levels] = tend
        put_rows(tend, levels, top_ref, bot_ref, 0)
        put_rows(q, levels, top_ref, bot_ref, 1)
        return carry

    lax.fori_loop(0, chunks, body, 0)


def strip_kernel(
    left_ref, right_ref, top_main, bot_main,
    q_ref, u_ref, v_ref, tend_ref, top_ref, bot_ref,
):
    row_terms = derivative_terms((8, 128), 0)
    col_terms = derivative_terms((8, 128), 1)
    lane = iota((8, 128), 1)
    for out, main in ((top_ref, top_main), (bot_ref, bot_main)):
        out[:, 0:256] = main[0]
        out[:, 256:512] = main[1]

    def body(chunk, carry):
        tiles = [[], [], []]
        for half in range(CHUNK // 4):
            west = left_ref[chunk * (CHUNK // 4) + half]
            east = right_ref[chunk * (CHUNK // 4) + half]
            for j in range(4):
                for f in range(3):
                    start = 32 * j + 8 * f
                    a = pltpu.roll(east, 128 - start, 1) if start else east
                    b = pltpu.roll(west, (120 - start) % 128, 1)
                    tiles[f].append(jnp.where(lane < 8, a, jnp.where(lane >= 120, b, 0.0)))
        q, u, v = [jnp.stack(tile, axis=0) for tile in tiles]
        levels = pl.ds(pl.multiple_of(chunk * CHUNK, CHUNK), CHUNK)
        q_ref[levels] = q
        u_ref[levels] = u
        v_ref[levels] = v
        tend = tendency(q, u, v, row_terms, col_terms)
        tend_ref[levels] = tend
        shared = jnp.where((lane >= 8) & (lane < 24), pltpu.roll(q, 16, 2), tend)
        top_ref[levels, 512:640] = shared[:, 0, :]
        bot_ref[levels, 512:640] = shared[:, 7, :]
        return carry

    lax.fori_loop(0, q_ref.shape[0] // CHUNK, body, 0)


def assemble_chunk(x, up, down):
    shape = x.shape
    row = iota(shape, 1)
    partner = jnp.where(
        row == 0,
        jnp.broadcast_to(up[:, None, :], shape),
        jnp.where(
            row == 7,
            jnp.broadcast_to(down[:, None, :], shape),
            jnp.where(row == 3, pltpu.roll(x, 7, 1), pltpu.roll(x, 1, 1)),
        ),
    )
    x = jnp.where((row % 4 == 0) | (row % 4 == 3), 0.5 * (x + partner), x)
    col = iota(shape, 2)
    partner = jnp.where(
        col % 4 == 3, pltpu.roll(x, shape[2] - 1, 2), pltpu.roll(x, 1, 2)
    )
    return jnp.where((col % 4 == 0) | (col % 4 == 3), 0.5 * (x + partner), x)


def join(main, strip):
    return jnp.concatenate([main, strip], axis=2)


def second_kernel(
    q_ref, u_ref, v_ref, tend_ref, q_strip, u_strip, v_strip, tend_strip, up_ref, down_ref,
    state_ref, smooth_ref, next_ref, top_ref, bot_ref,
):
    row_terms = derivative_terms((8, 128), 0)
    col_terms = derivative_terms((8, 128), 1)

    def body(chunk, carry):
        levels = pl.ds(pl.multiple_of(chunk * CHUNK, CHUNK), CHUNK)
        q = join(q_ref[levels], q_strip[levels])
        rows = []
        for ref in (up_ref, down_ref):
            shared = ref[levels, 512:640]
            rows.append(jnp.concatenate([ref[levels, 0:256], shared], axis=1))
            rows.append(jnp.concatenate([ref[levels, 256:512], pltpu.roll(shared, 112, 1)], axis=1))
        change = assemble_chunk(join(tend_ref[levels], tend_strip[levels]), rows[0], rows[2])
        smooth = assemble_chunk(q, rows[1], rows[3])
        smooth_ref[levels] = smooth[:, :, 0:256]
        state = q + DT_DYN * change
        state_ref[levels] = state[:, :, 0:256]
        tend = tendency(
            state, join(u_ref[levels], u_strip[levels]), join(v_ref[levels], v_strip[levels]),
            row_terms, col_terms,
        )
        next_ref[levels] = tend
        put_rows(tend, levels, top_ref, bot_ref, 0)
        return carry

    lax.fori_loop(0, q_ref.shape[0] // CHUNK, body, 0)


def third_kernel(
    q_ref, state_ref, smooth_ref, tend_ref, up_ref, down_ref, down_map_ref, coef_ref, growth_ref,
    base_ref, forcing_ref, near_ref, far_ref,
):
    cols = forcing_ref.shape[1]
    half = cols // 2
    phase = iota((8, 256), 0) % 4
    row_weight = jnp.where((phase == 0) | (phase == 3), F32(WEIGHTS[0]), F32(WEIGHTS[1]))
    near_rows = jnp.where(iota((8, 256), 0) < 4, row_weight, 0.0)
    far_rows = row_weight - near_rows

    def body(chunk, carry):
        levels = pl.ds(pl.multiple_of(chunk * CHUNK, CHUNK), CHUNK)
        change = assemble_chunk(tend_ref[levels], up_ref[0, levels, :], down_ref[0, levels, :])
        moved = (state_ref[levels] + DT_DYN * change[:, :, 0:256]) - q_ref[levels]
        base_ref[levels] = smooth_ref[levels] + moved
        near_ref[levels, :] = jnp.sum(moved * near_rows[None], axis=1)
        far_ref[levels, :] = jnp.sum(moved * far_rows[None], axis=1)
        return carry

    lax.fori_loop(0, q_ref.shape[0] // CHUNK, body, 0)
    point = iota((256, cols), 0)
    element = iota((256, cols), 1)
    weight = jnp.where(
        (point % 4 == 0) | (point % 4 == 3), F32(WEIGHTS[0]), F32(WEIGHTS[1])
    ) * F32(0.25 / (DYN_STEPS * DT_DYN))
    near_cols = jnp.where(point // 4 == element, weight, 0.0)
    far_cols = jnp.where(point // 4 + half == element, weight, 0.0)
    means = jnp.dot(near_ref[...], near_cols, precision=HIGH, preferred_element_type=F32)
    means += jnp.dot(far_ref[...], far_cols, precision=HIGH, preferred_element_type=F32)
    forcing = jnp.dot(down_map_ref[...], means, precision=HIGH, preferred_element_type=F32)
    forcing_ref[...] = forcing.astype(BF16).astype(F32)


def coef_kernel(
    collision_ref, table_ref, growth_ref, after_ref, coef_ref, growth_out_ref, wide_ref, line_ref
):
    bins = collision_ref.shape[0]
    total = jnp.dot(collision_ref[...], table_ref[...], preferred_element_type=F32) * DT_CRM
    coarse = total.astype(BF16).astype(F32)
    wide_ref[...] = jnp.zeros(wide_ref.shape, F32)
    wide_ref[0:bins, :] = coarse
    wide_ref[40 : 40 + bins, :] = total - coarse
    coef_ref[...] = wide_ref[...].astype(BF16)
    line_ref[...] = jnp.zeros(line_ref.shape, F32)
    line_ref[0:1, 0:bins] = growth_ref[...]
    rows = jnp.broadcast_to(line_ref[0:1, :], (128, 128)).T[0:40]
    for h in range(growth_out_ref.shape[1] // 128):
        growth_out_ref[:, 128 * h : 128 * h + 128] = rows


def rank_row(values):
    total = values.shape[1]
    across = jnp.broadcast_to(values, (total, total))
    down = across.T
    earlier = iota((total, total), 0) < iota((total, total), 1)
    ahead = (down > across) | ((down == across) & earlier)
    return jnp.sum(ahead.astype(F32), axis=0, keepdims=True)


def plan_kernel(
    capacity, count_ref, other_ref, owner_ref, after_ref,
    sent_ref, order_ref, force_ref, ordered_ref, rank_ref, slot_ref,
):
    cols = count_ref.shape[1]
    counts = count_ref[...].astype(F32)
    others = other_ref[...].astype(F32)
    rank = rank_row(counts)
    other_rank = rank_row(others)
    square = (cols, cols)
    index = iota(square, 0).astype(F32)
    odd = 2.0 * iota(square, 1).astype(F32) + 1.0
    down_rank = jnp.broadcast_to(rank, square).T
    sent = jnp.sum(jnp.where(down_rank == odd, index, 0.0), axis=0, keepdims=True)
    sent_ref[...] = sent.astype(jnp.int32)
    rank_ref[...] = rank.astype(jnp.int32)

    is_odd = rank.astype(jnp.int32) % 2 == 1
    other_odd = other_rank.astype(jnp.int32) % 2 == 1
    listed = jnp.concatenate(
        [jnp.where(is_odd, -1.0, counts), jnp.where(other_odd, others, -1.0)], axis=1
    )
    lane = iota((1, cols), 1).astype(F32)
    name = jnp.concatenate([lane, cols + 0.5 * (other_rank - 1.0)], axis=1)
    wide = (2 * cols, 2 * cols)
    place = jnp.broadcast_to(rank_row(listed), wide).T[:, 0:cols]
    here = place == iota((2 * cols, cols), 1).astype(F32)
    force = iota((2 * cols, cols), 0).astype(F32)
    name = jnp.broadcast_to(name, wide).T[:, 0:cols]
    value = jnp.broadcast_to(listed, wide).T[:, 0:cols]
    for what, ref in ((name, order_ref), (force, force_ref), (value, ordered_ref)):
        total = jnp.sum(jnp.where(here, what, 0.0), axis=0, keepdims=True)
        ref[...] = total.astype(jnp.int32)

    owners = jnp.broadcast_to(owner_ref[...].astype(F32), square)
    same = (owners.T == owners) & (iota(square, 0) < iota(square, 1))
    earlier = jnp.sum(same.astype(F32), axis=0, keepdims=True)
    slot_ref[...] = owner_ref[...] * capacity + earlier.astype(jnp.int32)


def gather_kernel(sent_ref, drops_ref, above_ref, below_ref, out_ref, wide_ref):
    bins = drops_ref.shape[1]
    wide_ref[...] = jnp.zeros(wide_ref.shape, F32)

    def body(p, carry):
        for k in range(8):
            wide_ref[k, 0:bins, :] = drops_ref[sent_ref[0, 8 * p + k]].astype(F32)
        for k in range(8):
            out_ref[8 * p + k] = wide_ref[k].astype(BF16)
        return carry

    lax.fori_loop(0, out_ref.shape[0] // 8, body, 0)


def merge_kernel(sent_ref, final_ref, back_ref, out_ref):
    out_ref[...] = final_ref[...]

    def body(p, carry):
        row = back_ref[p].astype(F32)[0 : out_ref.shape[1]]
        out_ref[sent_ref[0, p]] = row.astype(BF16)
        return carry

    lax.fori_loop(0, back_ref.shape[0] - 1, body, 0)


def crm_kernel(
    order_ref, force_ref, count_ref, sent_ref,
    drops_ref, guest_ref, forcing_ref, other_ref, coef_ref, growth_ref,
    final_ref, back_ref, own_ref, away_ref,
    state_ref, start_ref, pair_ref, twice_ref, cell_ref, heat_cell_ref, echo_cell_ref,
):
    bins = drops_ref.shape[1]
    cells = drops_ref.shape[2]
    cols = drops_ref.shape[0]
    guests = guest_ref.shape[0]
    coef = coef_ref[...]
    growth = growth_ref[...]
    state_ref[...] = jnp.zeros(state_ref.shape, F32)
    heat_cell_ref[...] = jnp.zeros(heat_cell_ref.shape, F32)
    echo_cell_ref[...] = jnp.zeros(echo_cell_ref.shape, F32)
    mass = (iota((40, cells), 0) + 1).astype(F32) / F32(bins)
    spread = (iota((CRM_LEV, cells), 1) // CRM_X == iota((CRM_LEV, cells), 0)).astype(BF16)
    for i, ref in enumerate((forcing_ref, other_ref)):
        rows = jnp.dot(ref[...].T.astype(BF16), spread, preferred_element_type=F32)
        cell_ref[cols * i : cols * i + cols, :] = DT_CRM * rows

    def grow(k, which, zero):
        grown = state_ref[k] + growth * cell_ref[pl.ds(which, 1), :]
        for h in range(cells // 128):
            cut = slice(128 * h, 128 * h + 128)
            g = grown[0:32, cut]
            last = grown[32:40, cut]
            twice_ref[2 * k + h, 0:32, :] = g
            twice_ref[2 * k + h, 32:48, :] = g[0:16]
            for d in range(16):
                other = g if d % 8 == 0 else twice_ref[2 * k + h, pl.ds(zero + d, 32), :]
                if d == 8:
                    other = jnp.concatenate([g[8:], g[:8]], axis=0)
                pair_ref[k, 32 * d : 32 * d + 32, cut] = (g * other).astype(BF16)
            pair_ref[k, 512:528, cut] = (g[0:16] * g[16:32]).astype(BF16)
            pair_ref[k, 528:560, cut] = (g * last[0:1]).astype(BF16)
            tail = jnp.concatenate([last * last, jnp.zeros((8, 128), F32)], axis=0)
            pair_ref[k, 560:576, cut] = tail.astype(BF16)
        return grown

    def group(index, carry):
        base = index * GROUP
        which = [order_ref[0, base + k] for k in range(GROUP)]
        force = [force_ref[0, base + k] for k in range(GROUP)]
        count = [count_ref[0, base + k] for k in range(GROUP)]
        for k in range(GROUP):
            mine = drops_ref[jnp.minimum(which[k], cols - 1)].astype(F32)
            guest = guest_ref[jnp.clip(which[k] - cols, 0, guests - 1)].astype(F32)
            start = jnp.where(which[k] < cols, mine, guest[0:bins])
            start_ref[k, 0:bins, :] = start
            state_ref[k, 0:bins, :] = start

        zero = jnp.minimum(which[0], 0)

        def step(s, c):
            for k in range(GROUP):
                grown = grow(k, force[k], zero)
                change = jnp.dot(coef, pair_ref[k], preferred_element_type=F32)
                moved = grown + (change[0:40] + change[40:80])
                state_ref[k] = jnp.where(s < count[k], moved, state_ref[k])
            return c

        lax.fori_loop(0, count[0], step, 0)
        for k in range(GROUP):
            final = state_ref[k, 0:bins, :]
            weighted = mass[0:bins] * final
            heat = jnp.sum(mass[0:bins] * (final - start_ref[k, 0:bins, :]), axis=0, keepdims=True)
            echo = jnp.sum(weighted * weighted, axis=0, keepdims=True)
            heat_cell_ref[pl.ds(which[k], 1), :] = heat
            echo_cell_ref[pl.ds(which[k], 1), :] = echo

            result = state_ref[k].astype(BF16)
            guest = jnp.clip(which[k] - cols, 0, guests - 1)
            mine = which[k] < cols
            final_ref[jnp.where(mine, which[k], sent_ref[0, guest])] = final.astype(BF16)
            back_ref[jnp.where(mine, guests, guest)] = result
        return carry

    lax.fori_loop(0, cols // GROUP, group, 0)
    means = jnp.where(
        iota((CRM_LEV, cells), 1) // CRM_X == iota((CRM_LEV, cells), 0), F32(1.0 / CRM_X), 0.0
    )
    contract = (((1,), (1,)), ((), ()))
    heat = lax.dot_general(
        means, heat_cell_ref[...], contract, precision=HIGH, preferred_element_type=F32
    )
    heat = heat.astype(BF16).astype(F32)
    echo = lax.dot_general(
        means, echo_cell_ref[...], contract, precision=HIGH, preferred_element_type=F32
    )
    both = jnp.concatenate([heat, jnp.log(1.0 + echo)], axis=0)
    own_ref[...] = both[:, 0:cols]
    away_ref[...] = both[:, cols : 2 * cols]


def block_kernel(n_gcm, n_crm, own_ref, back_ref, rank_ref, slot_ref, heat_ref, send_ref):
    cols = own_ref.shape[1]
    odd = 2 * iota((cols, cols), 0) + 1
    home = (rank_ref[...] == odd).astype(F32)
    both = own_ref[...] + jnp.dot(
        back_ref[...], home, precision=HIGH, preferred_element_type=F32
    )
    heat = both[0:CRM_LEV]
    echo = both[CRM_LEV:]
    heat_ref[...] = heat
    contract = (((1,), (1,)), ((), ()))
    devices = send_ref.shape[0]
    slots = 2 * cols
    capacity = slots // devices
    onehot = (slot_ref[...] == iota((slots, cols), 0)).astype(F32)
    packed = lax.dot_general(echo, onehot, contract, precision=HIGH, preferred_element_type=F32)
    coarse = packed.astype(BF16).astype(F32)
    rest = packed - coarse
    middle = rest.astype(BF16).astype(F32)
    pieces = (coarse, middle, rest - middle)
    lane = iota((CRM_LEV, 128), 1)
    near = heat
    far = pltpu.roll(heat, 64, 1)
    sides = jnp.where(
        lane == 1, pltpu.roll(heat, 65, 1), jnp.where(lane == 62, pltpu.roll(heat, 63, 1), heat)
    )
    g = lax.axis_index("gcm")
    for d in range(devices):
        away = d // n_crm - g
        below = (away == 1) | (away == 1 - n_gcm)
        above = (away == -1) | (away == n_gcm - 1)
        block = jnp.where(below, far, jnp.where(above, near, sides))
        tile, offset = divmod(d * capacity, 128)
        for i, piece in enumerate(pieces):
            moved = pltpu.roll(
                piece[:, 128 * tile : 128 * tile + 128], (64 + i * capacity - offset) % 128, 1
            )
            start = 64 + i * capacity
            block = jnp.where((lane >= start) & (lane < start + capacity), moved, block)
        send_ref[d] = block.astype(BF16)


def last_kernel(
    n_gcm, n_crm, base_ref, own_ref, got_ref, up_map_ref, drops_in, out_ref, power_ref, drops_out,
    *back_refs,
):
    cols = own_ref.shape[1]
    half = cols // 2
    element = iota((cols, 256), 0)
    col = iota((cols, 256), 1)
    phase = col % 4
    edge = (phase == 0) | (phase == 3)
    other = jnp.where(phase == 0, col // 4 - 1, col // 4 + 1)

    def spread(centre, start, west, west_lane, east, east_lane):
        inside = jnp.where(element == col // 4 + start, jnp.where(edge, 0.5, 1.0), 0.0)
        beside = edge & (element == other + start) & (other >= 0) & (other < half)
        middle = jnp.where(beside, 0.5, inside).astype(BF16)
        from_west = jnp.where((col == 0) & (element == west_lane), 0.5, 0.0).astype(BF16)
        from_east = jnp.where((col == 255) & (element == east_lane), 0.5, 0.0).astype(BF16)
        total = jnp.dot(centre, middle, preferred_element_type=F32)
        total += jnp.dot(west, from_west, preferred_element_type=F32)
        total += jnp.dot(east, from_east, preferred_element_type=F32)
        return total

    own = own_ref[...].astype(BF16)
    g = lax.axis_index("gcm")
    c = lax.axis_index("crm")
    north = jnp.where(g == 0, n_gcm - 1, g - 1) * n_crm
    south = jnp.where(g == n_gcm - 1, 0, g + 1) * n_crm
    west = jnp.where(c == 0, n_crm - 1, c - 1)
    east = jnp.where(c == n_crm - 1, 0, c + 1)
    up, down = got_ref[north + c], got_ref[south + c]
    left, right = got_ref[g * n_crm + west], got_ref[g * n_crm + east]
    up_left, up_right = got_ref[north + west], got_ref[north + east]
    down_left, down_right = got_ref[south + west], got_ref[south + east]
    above = spread(up, 0, up_left, half - 1, up_right, 0)
    near = spread(own, 0, left, half - 1, right, 0)
    far = spread(own, half, left, half - 2, right, 1)
    below = spread(down, 0, down_left, half - 1, down_right, 0)
    parts = (
        0.5 * (above + near), near, 0.5 * (near + far), far, 0.5 * (far + below),
    )
    up_map = up_map_ref[...]
    for part, ref in zip(parts, back_refs):
        ref[...] = DT_PHYS * jnp.dot(up_map, part, precision=HIGH, preferred_element_type=F32)

    devices = got_ref.shape[0]
    slots = power_ref.shape[1]
    capacity = slots // devices
    lane = iota((CRM_LEV, 128), 1)
    tiles = [jnp.zeros((CRM_LEV, 128), F32) for _ in range(slots // 128)]
    for d in range(devices):
        block = got_ref[d].astype(F32)
        fine = pltpu.roll(block, 128 - 2 * capacity, 1) + pltpu.roll(block, 128 - capacity, 1)
        tile, offset = divmod(d * capacity, 128)
        moved = pltpu.roll(block + fine, (offset - 64) % 128, 1)
        tiles[tile] = jnp.where((lane >= offset) & (lane < offset + capacity), moved, tiles[tile])
    power_ref[...] = jnp.concatenate(tiles, axis=1)

    def body(chunk, carry):
        levels = pl.ds(pl.multiple_of(chunk * CHUNK, CHUNK), CHUNK)
        shape = (CHUNK, 8, 256)
        row = iota(shape, 1)
        wide = [jnp.broadcast_to(ref[levels, :][:, None, :], shape) for ref in back_refs]
        back = jnp.where(
            row == 0,
            wide[0],
            jnp.where(
                row < 3,
                wide[1],
                jnp.where(row < 5, wide[2], jnp.where(row < 7, wide[3], wide[4])),
            ),
        )
        out_ref[levels] = base_ref[levels] + back
        return carry

    lax.fori_loop(0, base_ref.shape[0] // CHUNK, body, 0)


def call(kernel, outs, args, scratch=(), sems=(), flops=10_000_000, limit=16, through=()):
    spaces = {
        "s": pl.BlockSpec(memory_space=pltpu.SMEM),
        "v": pl.BlockSpec(memory_space=pltpu.VMEM),
        "h": pl.BlockSpec(memory_space=pl.ANY),
    }
    return pl.pallas_call(
        kernel,
        out_shape=[jax.ShapeDtypeStruct(s, t) for s, t in outs]
        + [jax.ShapeDtypeStruct(args[i][1].shape, args[i][1].dtype) for i in through],
        in_specs=[spaces[kind] for kind, _ in args],
        out_specs=[spaces["v"]] * len(outs) + [spaces["h"]] * len(through),
        input_output_aliases={i: len(outs) + n for n, i in enumerate(through)},
        scratch_shapes=[pltpu.VMEM(s, t) for s, t in scratch] + list(sems),
        compiler_params=pltpu.CompilerParams(vmem_limit_bytes=limit * MIB),
        cost_estimate=pl.CostEstimate(flops=flops, bytes_accessed=4_000_000, transcendentals=0),
    )(*[value for _, value in args])


def v(*values):
    return [("v", value) for value in values]


def shift(value, rows, cols):
    n_gcm = lax.axis_size("gcm")
    n_crm = lax.axis_size("crm")
    pairs = []
    for g in range(n_gcm):
        for c in range(n_crm):
            target = ((g + rows) % n_gcm) * n_crm + (c + cols) % n_crm
            pairs.append((g * n_crm + c, target))
    return lax.ppermute(value, ("gcm", "crm"), pairs)


def pair_table(bins):
    table = np.zeros((bins * bins, 576), np.float32)

    def put(column, i, j):
        table[i * bins + j, column] = 1.0
        table[j * bins + i, column] = 1.0

    for d in range(16):
        for b in range(32):
            put(32 * d + b, b, (b + d) % 32)
    for b in range(16):
        put(512 + b, b, b + 16)
    for b in range(32):
        put(528 + b, b, 32)
    put(560, 32, 32)
    return table


def to_partner(value):
    n_gcm = lax.axis_size("gcm")
    n_crm = lax.axis_size("crm")
    pairs = []
    for g in range(n_gcm):
        for c in range(n_crm):
            pairs.append((g * n_crm + c, (g ^ 1) * n_crm + c))
    return lax.ppermute(value, ("gcm", "crm"), pairs)


def shards(tracer, wind_x, wind_y, drops, owner, counts, collision, growth):
    devices = lax.axis_size("gcm") * lax.axis_size("crm")
    levels, row_count, col_count = tracer.shape
    col_total, bins, cells = drops.shape
    field = (tracer.shape, F32)
    strip = ((levels, row_count, 128), F32)
    rows = ((2, levels, col_count), F32)
    wide = col_count + 128
    down_map, up_map = level_tables(levels, CRM_LEV)

    row = ((1, col_total), jnp.int32)
    capacity = 2 * col_total // devices
    guests = col_total // 2
    tend, top, bot, to_right, to_left, count_row = call(
        first_kernel,
        [field, rows, rows] + [((levels // 4, 8, 128), F32)] * 2 + [row],
        [("h", tracer), ("h", wind_x), ("h", wind_y)] + v(counts[None, :]),
        [field] * 3,
        [pltpu.SemaphoreType.DMA((3, levels // CHUNK))],
        limit=62,
    )
    from_left = shift(to_right, 0, 1)
    from_right = shift(to_left, 0, -1)
    other_counts = to_partner(count_row)
    q_strip, u_strip, v_strip, tend_strip, top, bot = call(
        strip_kernel,
        [strip] * 4 + [((levels, wide + col_count), F32)] * 2,
        v(from_left, from_right, top, bot),
    )
    drops, _ = lax.optimization_barrier((drops, top))
    sent, order, force, ordered, rank, slot = call(
        functools.partial(plan_kernel, capacity),
        [row] * 6,
        v(count_row, other_counts, owner.T) + [("h", top)],
    )
    from_above = shift(bot, 1, 0)
    from_below = shift(top, -1, 0)
    (leaving,) = call(
        gather_kernel,
        [((guests, 40, cells), BF16)],
        [("s", sent)] + v(drops) + [("h", from_above), ("h", from_below)],
        [((8, 40, cells), F32)],
    )
    guest_drops = to_partner(leaving)
    coef, growth_rows = call(
        coef_kernel,
        [((80, 576), BF16), ((40, cells), F32)],
        v(collision, jnp.asarray(pair_table(bins), BF16), growth[None, :]) + [("h", top)],
        [((80, 576), F32), ((8, 128), F32)],
    )
    state, smooth, tend, top, bot = call(
        second_kernel,
        [field, field, ((levels, row_count, wide), F32)] + [((1, levels, wide), F32)] * 2,
        v(tracer, wind_x, wind_y, tend, q_strip, u_strip, v_strip, tend_strip)
        + v(from_above, from_below),
    )
    base, forcing = call(
        third_kernel,
        [field, ((CRM_LEV, col_total), F32)],
        v(tracer, state, smooth, tend, shift(bot, 1, 0), shift(top, -1, 0))
        + v(jnp.asarray(down_map, F32)) + [("h", coef), ("h", growth_rows)],
        [((levels, col_count), F32), ((levels, col_count), F32)],
    )

    other_forcing = to_partner(forcing)
    n_gcm = lax.axis_size("gcm")
    n_crm = lax.axis_size("crm")

    pairs = ((2 * CRM_LEV, col_total), F32)
    final, back, own, away = call(
        crm_kernel,
        [((col_total, bins, cells), BF16), ((guests + 1, 40, cells), BF16), pairs, pairs],
        [("s", order), ("s", force), ("s", ordered), ("s", sent)]
        + v(drops, guest_drops, forcing, other_forcing, coef, growth_rows),
        [((GROUP, 40, cells), F32), ((GROUP, 40, cells), F32), ((GROUP, 576, cells), BF16),
         ((2 * GROUP, 48, 128), F32), ((2 * col_total, cells), F32),
         ((2 * col_total, cells), F32), ((2 * col_total, cells), F32)],
        flops=10_000_000_000,
        limit=24,
    )
    returned = to_partner(away)
    returned_drops = to_partner(back)
    heat, send = call(
        functools.partial(block_kernel, n_gcm, n_crm),
        [((CRM_LEV, col_total), F32), ((devices, CRM_LEV, 128), BF16)],
        v(own, returned, rank, slot),
    )
    got = lax.all_to_all(send, ("gcm", "crm"), split_axis=0, concat_axis=0, tiled=True)
    (drops_next,) = call(
        merge_kernel,
        [((col_total, bins, cells), BF16)],
        [("s", sent)] + v(final, returned_drops),
    )
    tracer_next, power, by_bin = call(
        functools.partial(last_kernel, n_gcm, n_crm),
        [field, ((CRM_LEV, devices * capacity), F32)],
        v(base, heat, got, jnp.asarray(up_map, F32))
        + [("h", drops_next.transpose(1, 0, 2))],
        [((levels, col_count), F32)] * 5,
        through=(4,),
    )
    drops_next = by_bin.transpose(1, 0, 2)
    return (tracer_next, drops_next, power)


def solution(mesh):
    return jax.shard_map(
        shards,
        mesh=mesh,
        in_specs=(
            P(None, "gcm", "crm"),
            P(None, "gcm", "crm"),
            P(None, "gcm", "crm"),
            P(("gcm", "crm"), None, None),
            P(("gcm", "crm"), None),
            P(("gcm", "crm")),
            P(),
            P(),
        ),
        out_specs=(P(None, "gcm", "crm"), P(("gcm", "crm"), None, None), P(None, ("gcm", "crm"))),
        check_vma=False,
    )
```

```python
import functools

import jax
import jax.numpy as jnp
import numpy as np
from jax import lax
from jax.experimental import pallas as pl
from jax.experimental.pallas import tpu as pltpu
from jax.sharding import PartitionSpec as P

CRM_X = 16
CRM_LEV = 16
DYN_STEPS = 2

DT_DYN = 0.04
DT_CRM = 0.05
DT_PHYS = 0.5
HIGH = lax.Precision.HIGHEST
F32 = jnp.float32
BF16 = jnp.bfloat16
GROUP = 8
CHUNK = 8
MIB = 1024 * 1024


def gll_tables():
    inv_root = 1.0 / np.sqrt(5.0)
    gll_nodes = np.array([-1.0, -inv_root, inv_root, 1.0])
    weights = np.array([1.0, 5.0, 5.0, 1.0]) / 6.0
    legendre = (5.0 * gll_nodes**3 - 3.0 * gll_nodes) / 2.0
    derivative = np.zeros((4, 4))
    for i in range(4):
        for j in range(4):
            if i != j:
                derivative[i, j] = legendre[i] / (legendre[j] * (gll_nodes[i] - gll_nodes[j]))
    derivative[0, 0] = -3.0
    derivative[3, 3] = 3.0
    return (2.0 * derivative, weights)


def level_tables(levels, crm_levels):
    spacing = levels / crm_levels
    centres = (np.arange(crm_levels) + 0.5) * spacing - 0.5
    hats = np.maximum(0.0, 1.0 - np.abs(np.arange(levels)[None, :] - centres[:, None]) / spacing)
    down_map = hats / hats.sum(axis=1, keepdims=True)
    up_map = hats.T / hats.T.sum(axis=1, keepdims=True)
    return (down_map, up_map)


DERIV, WEIGHTS = gll_tables()


def iota(shape, axis):
    return lax.broadcasted_iota(jnp.int32, shape, axis)


def derivative_terms(shape, axis):
    phase = iota(shape, axis) % 4
    terms = []
    for shift in range(-3, 4):
        value = jnp.zeros(shape, F32)
        for i in range(4):
            if 0 <= i + shift < 4:
                value = jnp.where(phase == i, F32(DERIV[i, i + shift]), value)
        terms.append((shift, value))
    return terms


def along(x, terms, axis):
    size = x.shape[axis]
    total = None
    for shift, value in terms:
        moved = x if shift == 0 else pltpu.roll(x, (-shift) % size, axis)
        part = value[None] * moved
        total = part if total is None else total + part
    return total


def tendency(x, u, v, row_terms, col_terms):
    halves = []
    for h in range(x.shape[2] // 128):
        cut = slice(128 * h, 128 * h + 128)
        q = x[:, :, cut]
        grad_x = along(q, row_terms, 1)
        grad_y = along(q, col_terms, 2)
        halves.append(-(u[:, :, cut] * grad_x + v[:, :, cut] * grad_y))
    return jnp.concatenate(halves, axis=2)


def put_rows(x, levels, top_ref, bot_ref, i):
    top_ref[i, levels, :] = x[:, 0, :]
    bot_ref[i, levels, :] = x[:, 7, :]


def first_kernel(
    q_hbm, u_hbm, v_hbm, tend_ref, top_ref, bot_ref, right_ref, left_ref, q_ref, u_ref, v_ref, sems
):
    row_terms = derivative_terms((8, 128), 0)
    col_terms = derivative_terms((8, 128), 1)
    lane = iota((8, 128), 1)
    chunks = q_ref.shape[0] // CHUNK

    def copies(chunk):
        levels = pl.ds(pl.multiple_of(chunk * CHUNK, CHUNK), CHUNK)
        return [
            pltpu.make_async_copy(src.at[levels], dst.at[levels], sems.at[i, chunk])
            for i, (src, dst) in enumerate(((q_hbm, q_ref), (u_hbm, u_ref), (v_hbm, v_ref)))
        ]

    for chunk in range(chunks):
        for copy in copies(chunk):
            copy.start()

    def body(chunk, carry):
        for copy in copies(chunk):
            copy.wait()
        for half in range(CHUNK // 4):
            right = jnp.zeros((8, 128), F32)
            left = jnp.zeros((8, 128), F32)
            for j in range(4):
                for f, ref in enumerate((q_ref, u_ref, v_ref)):
                    start = 32 * j + 8 * f
                    here = (lane >= start) & (lane < start + 8)
                    x = ref[chunk * CHUNK + half * 4 + j]
                    moved = pltpu.roll(x[:, 128:256], (start - 120) % 128, 1)
                    right = jnp.where(here, moved, right)
                    first = x[:, 0:128]
                    if start:
                        first = pltpu.roll(first, start, 1)
                    left = jnp.where(here, first, left)
            right_ref[chunk * (CHUNK // 4) + half] = right
            left_ref[chunk * (CHUNK // 4) + half] = left
        levels = pl.ds(pl.multiple_of(chunk * CHUNK, CHUNK), CHUNK)
        q = q_ref[levels]
        tend = tendency(q, u_ref[levels], v_ref[levels], row_terms, col_terms)
        tend_ref[levels] = tend
        put_rows(tend, levels, top_ref, bot_ref, 0)
        put_rows(q, levels, top_ref, bot_ref, 1)
        return carry

    lax.fori_loop(0, chunks, body, 0)


def strip_kernel(
    left_ref, right_ref, top_main, bot_main, after_ref,
    q_ref, u_ref, v_ref, tend_ref, top_ref, bot_ref,
):
    row_terms = derivative_terms((8, 128), 0)
    col_terms = derivative_terms((8, 128), 1)
    lane = iota((8, 128), 1)
    for out, main in ((top_ref, top_main), (bot_ref, bot_main)):
        out[:, 0:256] = main[0]
        out[:, 256:512] = main[1]

    def body(chunk, carry):
        tiles = [[], [], []]
        for half in range(CHUNK // 4):
            west = left_ref[chunk * (CHUNK // 4) + half]
            east = right_ref[chunk * (CHUNK // 4) + half]
            for j in range(4):
                for f in range(3):
                    start = 32 * j + 8 * f
                    a = pltpu.roll(east, 128 - start, 1) if start else east
                    b = pltpu.roll(west, (120 - start) % 128, 1)
                    tiles[f].append(jnp.where(lane < 8, a, jnp.where(lane >= 120, b, 0.0)))
        q, u, v = [jnp.stack(tile, axis=0) for tile in tiles]
        levels = pl.ds(pl.multiple_of(chunk * CHUNK, CHUNK), CHUNK)
        q_ref[levels] = q
        u_ref[levels] = u
        v_ref[levels] = v
        tend = tendency(q, u, v, row_terms, col_terms)
        tend_ref[levels] = tend
        shared = jnp.where((lane >= 8) & (lane < 24), pltpu.roll(q, 16, 2), tend)
        top_ref[levels, 512:640] = shared[:, 0, :]
        bot_ref[levels, 512:640] = shared[:, 7, :]
        return carry

    lax.fori_loop(0, q_ref.shape[0] // CHUNK, body, 0)


def assemble_chunk(x, up, down):
    shape = x.shape
    row = iota(shape, 1)
    partner = jnp.where(
        row == 0,
        jnp.broadcast_to(up[:, None, :], shape),
        jnp.where(
            row == 7,
            jnp.broadcast_to(down[:, None, :], shape),
            jnp.where(row == 3, pltpu.roll(x, 7, 1), pltpu.roll(x, 1, 1)),
        ),
    )
    x = jnp.where((row % 4 == 0) | (row % 4 == 3), 0.5 * (x + partner), x)
    col = iota(shape, 2)
    partner = jnp.where(
        col % 4 == 3, pltpu.roll(x, shape[2] - 1, 2), pltpu.roll(x, 1, 2)
    )
    return jnp.where((col % 4 == 0) | (col % 4 == 3), 0.5 * (x + partner), x)


def join(main, strip):
    return jnp.concatenate([main, strip], axis=2)


def second_kernel(
    q_ref, u_ref, v_ref, tend_ref, q_strip, u_strip, v_strip, tend_strip, up_ref, down_ref,
    state_ref, smooth_ref, next_ref, top_ref, bot_ref,
):
    row_terms = derivative_terms((8, 128), 0)
    col_terms = derivative_terms((8, 128), 1)

    def body(chunk, carry):
        levels = pl.ds(pl.multiple_of(chunk * CHUNK, CHUNK), CHUNK)
        q = join(q_ref[levels], q_strip[levels])
        rows = []
        for ref in (up_ref, down_ref):
            shared = ref[levels, 512:640]
            rows.append(jnp.concatenate([ref[levels, 0:256], shared], axis=1))
            rows.append(jnp.concatenate([ref[levels, 256:512], pltpu.roll(shared, 112, 1)], axis=1))
        change = assemble_chunk(join(tend_ref[levels], tend_strip[levels]), rows[0], rows[2])
        smooth = assemble_chunk(q, rows[1], rows[3])
        smooth_ref[levels] = smooth[:, :, 0:256]
        state = q + DT_DYN * change
        state_ref[levels] = state[:, :, 0:256]
        tend = tendency(
            state, join(u_ref[levels], u_strip[levels]), join(v_ref[levels], v_strip[levels]),
            row_terms, col_terms,
        )
        next_ref[levels] = tend
        put_rows(tend, levels, top_ref, bot_ref, 0)
        return carry

    lax.fori_loop(0, q_ref.shape[0] // CHUNK, body, 0)


def third_kernel(
    q_ref, state_ref, smooth_ref, tend_ref, up_ref, down_ref, down_map_ref, coef_ref, growth_ref,
    base_ref, forcing_ref, near_ref, far_ref,
):
    cols = forcing_ref.shape[1]
    half = cols // 2
    phase = iota((8, 256), 0) % 4
    row_weight = jnp.where((phase == 0) | (phase == 3), F32(WEIGHTS[0]), F32(WEIGHTS[1]))
    near_rows = jnp.where(iota((8, 256), 0) < 4, row_weight, 0.0)
    far_rows = row_weight - near_rows

    def body(chunk, carry):
        levels = pl.ds(pl.multiple_of(chunk * CHUNK, CHUNK), CHUNK)
        change = assemble_chunk(tend_ref[levels], up_ref[0, levels, :], down_ref[0, levels, :])
        moved = (state_ref[levels] + DT_DYN * change[:, :, 0:256]) - q_ref[levels]
        base_ref[levels] = smooth_ref[levels] + moved
        near_ref[levels, :] = jnp.sum(moved * near_rows[None], axis=1)
        far_ref[levels, :] = jnp.sum(moved * far_rows[None], axis=1)
        return carry

    lax.fori_loop(0, q_ref.shape[0] // CHUNK, body, 0)
    point = iota((256, cols), 0)
    element = iota((256, cols), 1)
    weight = jnp.where(
        (point % 4 == 0) | (point % 4 == 3), F32(WEIGHTS[0]), F32(WEIGHTS[1])
    ) * F32(0.25 / (DYN_STEPS * DT_DYN))
    near_cols = jnp.where(point // 4 == element, weight, 0.0)
    far_cols = jnp.where(point // 4 + half == element, weight, 0.0)
    means = jnp.dot(near_ref[...], near_cols, precision=HIGH, preferred_element_type=F32)
    means += jnp.dot(far_ref[...], far_cols, precision=HIGH, preferred_element_type=F32)
    forcing = jnp.dot(down_map_ref[...], means, precision=HIGH, preferred_element_type=F32)
    forcing_ref[...] = forcing.astype(BF16).astype(F32)


def coef_kernel(
    collision_ref, table_ref, growth_ref, after_ref, coef_ref, growth_out_ref, wide_ref, line_ref
):
    bins = collision_ref.shape[0]
    total = jnp.dot(collision_ref[...], table_ref[...], preferred_element_type=F32) * DT_CRM
    coarse = total.astype(BF16).astype(F32)
    wide_ref[...] = jnp.zeros(wide_ref.shape, F32)
    wide_ref[0:bins, :] = coarse
    wide_ref[40 : 40 + bins, :] = total - coarse
    coef_ref[...] = wide_ref[...].astype(BF16)
    line_ref[...] = jnp.zeros(line_ref.shape, F32)
    line_ref[0:1, 0:bins] = growth_ref[...]
    rows = jnp.broadcast_to(line_ref[0:1, :], (128, 128)).T[0:40]
    for h in range(growth_out_ref.shape[1] // 128):
        growth_out_ref[:, 128 * h : 128 * h + 128] = rows


def rank_row(values):
    total = values.shape[1]
    across = jnp.broadcast_to(values, (total, total))
    down = across.T
    earlier = iota((total, total), 0) < iota((total, total), 1)
    ahead = (down > across) | ((down == across) & earlier)
    return jnp.sum(ahead.astype(F32), axis=0, keepdims=True)


def plan_kernel(
    capacity, count_ref, other_ref, owner_ref, after_ref,
    sent_ref, order_ref, force_ref, ordered_ref, rank_ref, slot_ref,
):
    cols = count_ref.shape[1]
    counts = count_ref[...].astype(F32)
    others = other_ref[...].astype(F32)
    rank = rank_row(counts)
    other_rank = rank_row(others)
    square = (cols, cols)
    index = iota(square, 0).astype(F32)
    odd = 2.0 * iota(square, 1).astype(F32) + 1.0
    down_rank = jnp.broadcast_to(rank, square).T
    sent = jnp.sum(jnp.where(down_rank == odd, index, 0.0), axis=0, keepdims=True)
    sent_ref[...] = sent.astype(jnp.int32)
    rank_ref[...] = rank.astype(jnp.int32)

    is_odd = rank.astype(jnp.int32) % 2 == 1
    other_odd = other_rank.astype(jnp.int32) % 2 == 1
    listed = jnp.concatenate(
        [jnp.where(is_odd, -1.0, counts), jnp.where(other_odd, others, -1.0)], axis=1
    )
    lane = iota((1, cols), 1).astype(F32)
    name = jnp.concatenate([lane, cols + 0.5 * (other_rank - 1.0)], axis=1)
    wide = (2 * cols, 2 * cols)
    place = jnp.broadcast_to(rank_row(listed), wide).T[:, 0:cols]
    here = place == iota((2 * cols, cols), 1).astype(F32)
    force = iota((2 * cols, cols), 0).astype(F32)
    name = jnp.broadcast_to(name, wide).T[:, 0:cols]
    value = jnp.broadcast_to(listed, wide).T[:, 0:cols]
    for what, ref in ((name, order_ref), (force, force_ref), (value, ordered_ref)):
        total = jnp.sum(jnp.where(here, what, 0.0), axis=0, keepdims=True)
        ref[...] = total.astype(jnp.int32)

    owners = jnp.broadcast_to(owner_ref[...].astype(F32), square)
    same = (owners.T == owners) & (iota(square, 0) < iota(square, 1))
    earlier = jnp.sum(same.astype(F32), axis=0, keepdims=True)
    slot_ref[...] = owner_ref[...] * capacity + earlier.astype(jnp.int32)


def gather_kernel(sent_ref, drops_ref, out_ref, wide_ref):
    bins = drops_ref.shape[1]
    wide_ref[...] = jnp.zeros(wide_ref.shape, F32)

    def body(p, carry):
        for k in range(8):
            wide_ref[k, 0:bins, :] = drops_ref[sent_ref[0, 8 * p + k]].astype(F32)
        for k in range(8):
            out_ref[8 * p + k] = wide_ref[k].astype(BF16)
        return carry

    lax.fori_loop(0, out_ref.shape[0] // 8, body, 0)


def merge_kernel(sent_ref, final_ref, back_ref, out_ref):
    out_ref[...] = final_ref[...]

    def body(p, carry):
        row = back_ref[p].astype(F32)[0 : out_ref.shape[1]]
        out_ref[sent_ref[0, p]] = row.astype(BF16)
        return carry

    lax.fori_loop(0, back_ref.shape[0] - 1, body, 0)


def crm_kernel(
    order_ref, force_ref, count_ref, sent_ref,
    drops_ref, guest_ref, forcing_ref, other_ref, coef_ref, growth_ref,
    final_ref, back_ref, own_ref, away_ref,
    state_ref, start_ref, pair_ref, twice_ref, cell_ref, heat_cell_ref, echo_cell_ref,
):
    bins = drops_ref.shape[1]
    cells = drops_ref.shape[2]
    cols = drops_ref.shape[0]
    guests = guest_ref.shape[0]
    coef = coef_ref[...]
    growth = growth_ref[...]
    state_ref[...] = jnp.zeros(state_ref.shape, F32)
    heat_cell_ref[...] = jnp.zeros(heat_cell_ref.shape, F32)
    echo_cell_ref[...] = jnp.zeros(echo_cell_ref.shape, F32)
    mass = (iota((40, cells), 0) + 1).astype(F32) / F32(bins)
    spread = (iota((CRM_LEV, cells), 1) // CRM_X == iota((CRM_LEV, cells), 0)).astype(BF16)
    for i, ref in enumerate((forcing_ref, other_ref)):
        rows = jnp.dot(ref[...].T.astype(BF16), spread, preferred_element_type=F32)
        cell_ref[cols * i : cols * i + cols, :] = DT_CRM * rows

    def grow(k, which, zero):
        grown = state_ref[k] + growth * cell_ref[pl.ds(which, 1), :]
        for h in range(cells // 128):
            cut = slice(128 * h, 128 * h + 128)
            g = grown[0:32, cut]
            last = grown[32:40, cut]
            twice_ref[2 * k + h, 0:32, :] = g
            twice_ref[2 * k + h, 32:48, :] = g[0:16]
            for d in range(16):
                other = g if d % 8 == 0 else twice_ref[2 * k + h, pl.ds(zero + d, 32), :]
                if d == 8:
                    other = jnp.concatenate([g[8:], g[:8]], axis=0)
                pair_ref[k, 32 * d : 32 * d + 32, cut] = (g * other).astype(BF16)
            pair_ref[k, 512:528, cut] = (g[0:16] * g[16:32]).astype(BF16)
            pair_ref[k, 528:560, cut] = (g * last[0:1]).astype(BF16)
            tail = jnp.concatenate([last * last, jnp.zeros((8, 128), F32)], axis=0)
            pair_ref[k, 560:576, cut] = tail.astype(BF16)
        return grown

    def group(index, carry):
        base = index * GROUP
        which = [order_ref[0, base + k] for k in range(GROUP)]
        force = [force_ref[0, base + k] for k in range(GROUP)]
        count = [count_ref[0, base + k] for k in range(GROUP)]
        for k in range(GROUP):
            mine = drops_ref[jnp.minimum(which[k], cols - 1)].astype(F32)
            guest = guest_ref[jnp.clip(which[k] - cols, 0, guests - 1)].astype(F32)
            start = jnp.where(which[k] < cols, mine, guest[0:bins])
            start_ref[k, 0:bins, :] = start
            state_ref[k, 0:bins, :] = start

        zero = jnp.minimum(which[0], 0)

        def step(s, c):
            for k in range(GROUP):
                grown = grow(k, force[k], zero)
                change = jnp.dot(coef, pair_ref[k], preferred_element_type=F32)
                moved = grown + (change[0:40] + change[40:80])
                state_ref[k] = jnp.where(s < count[k], moved, state_ref[k])
            return c

        lax.fori_loop(0, count[0], step, 0)
        for k in range(GROUP):
            final = state_ref[k, 0:bins, :]
            weighted = mass[0:bins] * final
            heat = jnp.sum(mass[0:bins] * (final - start_ref[k, 0:bins, :]), axis=0, keepdims=True)
            echo = jnp.sum(weighted * weighted, axis=0, keepdims=True)
            heat_cell_ref[pl.ds(which[k], 1), :] = heat
            echo_cell_ref[pl.ds(which[k], 1), :] = echo

            result = state_ref[k].astype(BF16)
            guest = jnp.clip(which[k] - cols, 0, guests - 1)
            mine = which[k] < cols
            final_ref[jnp.where(mine, which[k], sent_ref[0, guest])] = final.astype(BF16)
            back_ref[jnp.where(mine, guests, guest)] = result
        return carry

    lax.fori_loop(0, cols // GROUP, group, 0)
    means = jnp.where(
        iota((CRM_LEV, cells), 1) // CRM_X == iota((CRM_LEV, cells), 0), F32(1.0 / CRM_X), 0.0
    )
    contract = (((1,), (1,)), ((), ()))
    heat = lax.dot_general(
        means, heat_cell_ref[...], contract, precision=HIGH, preferred_element_type=F32
    )
    heat = heat.astype(BF16).astype(F32)
    echo = lax.dot_general(
        means, echo_cell_ref[...], contract, precision=HIGH, preferred_element_type=F32
    )
    both = jnp.concatenate([heat, jnp.log(1.0 + echo)], axis=0)
    own_ref[...] = both[:, 0:cols]
    away_ref[...] = both[:, cols : 2 * cols]


def block_kernel(n_gcm, n_crm, own_ref, back_ref, rank_ref, slot_ref, heat_ref, send_ref):
    cols = own_ref.shape[1]
    odd = 2 * iota((cols, cols), 0) + 1
    home = (rank_ref[...] == odd).astype(F32)
    both = own_ref[...] + jnp.dot(
        back_ref[...], home, precision=HIGH, preferred_element_type=F32
    )
    heat = both[0:CRM_LEV]
    echo = both[CRM_LEV:]
    heat_ref[...] = heat
    contract = (((1,), (1,)), ((), ()))
    devices = send_ref.shape[0]
    slots = 2 * cols
    capacity = slots // devices
    onehot = (slot_ref[...] == iota((slots, cols), 0)).astype(F32)
    packed = lax.dot_general(echo, onehot, contract, precision=HIGH, preferred_element_type=F32)
    coarse = packed.astype(BF16).astype(F32)
    rest = packed - coarse
    middle = rest.astype(BF16).astype(F32)
    pieces = (coarse, middle, rest - middle)
    lane = iota((CRM_LEV, 128), 1)
    near = heat
    far = pltpu.roll(heat, 64, 1)
    sides = jnp.where(
        lane == 1, pltpu.roll(heat, 65, 1), jnp.where(lane == 62, pltpu.roll(heat, 63, 1), heat)
    )
    g = lax.axis_index("gcm")
    for d in range(devices):
        away = d // n_crm - g
        below = (away == 1) | (away == 1 - n_gcm)
        above = (away == -1) | (away == n_gcm - 1)
        block = jnp.where(below, far, jnp.where(above, near, sides))
        tile, offset = divmod(d * capacity, 128)
        for i, piece in enumerate(pieces):
            moved = pltpu.roll(
                piece[:, 128 * tile : 128 * tile + 128], (64 + i * capacity - offset) % 128, 1
            )
            start = 64 + i * capacity
            block = jnp.where((lane >= start) & (lane < start + capacity), moved, block)
        send_ref[d] = block.astype(BF16)


def last_kernel(
    n_gcm, n_crm, base_ref, own_ref, got_ref, up_map_ref, drops_in, out_ref, power_ref, drops_out,
    *back_refs,
):
    cols = own_ref.shape[1]
    half = cols // 2
    element = iota((cols, 256), 0)
    col = iota((cols, 256), 1)
    phase = col % 4
    edge = (phase == 0) | (phase == 3)
    other = jnp.where(phase == 0, col // 4 - 1, col // 4 + 1)

    def spread(centre, start, west, west_lane, east, east_lane):
        inside = jnp.where(element == col // 4 + start, jnp.where(edge, 0.5, 1.0), 0.0)
        beside = edge & (element == other + start) & (other >= 0) & (other < half)
        middle = jnp.where(beside, 0.5, inside).astype(BF16)
        from_west = jnp.where((col == 0) & (element == west_lane), 0.5, 0.0).astype(BF16)
        from_east = jnp.where((col == 255) & (element == east_lane), 0.5, 0.0).astype(BF16)
        total = jnp.dot(centre, middle, preferred_element_type=F32)
        total += jnp.dot(west, from_west, preferred_element_type=F32)
        total += jnp.dot(east, from_east, preferred_element_type=F32)
        return total

    own = own_ref[...].astype(BF16)
    g = lax.axis_index("gcm")
    c = lax.axis_index("crm")
    north = jnp.where(g == 0, n_gcm - 1, g - 1) * n_crm
    south = jnp.where(g == n_gcm - 1, 0, g + 1) * n_crm
    west = jnp.where(c == 0, n_crm - 1, c - 1)
    east = jnp.where(c == n_crm - 1, 0, c + 1)
    up, down = got_ref[north + c], got_ref[south + c]
    left, right = got_ref[g * n_crm + west], got_ref[g * n_crm + east]
    up_left, up_right = got_ref[north + west], got_ref[north + east]
    down_left, down_right = got_ref[south + west], got_ref[south + east]
    above = spread(up, 0, up_left, half - 1, up_right, 0)
    near = spread(own, 0, left, half - 1, right, 0)
    far = spread(own, half, left, half - 2, right, 1)
    below = spread(down, 0, down_left, half - 1, down_right, 0)
    parts = (
        0.5 * (above + near), near, 0.5 * (near + far), far, 0.5 * (far + below),
    )
    up_map = up_map_ref[...]
    for part, ref in zip(parts, back_refs):
        ref[...] = DT_PHYS * jnp.dot(up_map, part, precision=HIGH, preferred_element_type=F32)

    devices = got_ref.shape[0]
    slots = power_ref.shape[1]
    capacity = slots // devices
    lane = iota((CRM_LEV, 128), 1)
    tiles = [jnp.zeros((CRM_LEV, 128), F32) for _ in range(slots // 128)]
    for d in range(devices):
        block = got_ref[d].astype(F32)
        fine = pltpu.roll(block, 128 - 2 * capacity, 1) + pltpu.roll(block, 128 - capacity, 1)
        tile, offset = divmod(d * capacity, 128)
        moved = pltpu.roll(block + fine, (offset - 64) % 128, 1)
        tiles[tile] = jnp.where((lane >= offset) & (lane < offset + capacity), moved, tiles[tile])
    power_ref[...] = jnp.concatenate(tiles, axis=1)

    def body(chunk, carry):
        levels = pl.ds(pl.multiple_of(chunk * CHUNK, CHUNK), CHUNK)
        shape = (CHUNK, 8, 256)
        row = iota(shape, 1)
        wide = [jnp.broadcast_to(ref[levels, :][:, None, :], shape) for ref in back_refs]
        back = jnp.where(
            row == 0,
            wide[0],
            jnp.where(
                row < 3,
                wide[1],
                jnp.where(row < 5, wide[2], jnp.where(row < 7, wide[3], wide[4])),
            ),
        )
        out_ref[levels] = base_ref[levels] + back
        return carry

    lax.fori_loop(0, base_ref.shape[0] // CHUNK, body, 0)


def call(kernel, outs, args, scratch=(), sems=(), flops=10_000_000, limit=16, through=()):
    spaces = {
        "s": pl.BlockSpec(memory_space=pltpu.SMEM),
        "v": pl.BlockSpec(memory_space=pltpu.VMEM),
        "h": pl.BlockSpec(memory_space=pl.ANY),
    }
    return pl.pallas_call(
        kernel,
        out_shape=[jax.ShapeDtypeStruct(s, t) for s, t in outs]
        + [jax.ShapeDtypeStruct(args[i][1].shape, args[i][1].dtype) for i in through],
        in_specs=[spaces[kind] for kind, _ in args],
        out_specs=[spaces["v"]] * len(outs) + [spaces["h"]] * len(through),
        input_output_aliases={i: len(outs) + n for n, i in enumerate(through)},
        scratch_shapes=[pltpu.VMEM(s, t) for s, t in scratch] + list(sems),
        compiler_params=pltpu.CompilerParams(vmem_limit_bytes=limit * MIB),
        cost_estimate=pl.CostEstimate(flops=flops, bytes_accessed=4_000_000, transcendentals=0),
    )(*[value for _, value in args])


def v(*values):
    return [("v", value) for value in values]


def shift(value, rows, cols):
    n_gcm = lax.axis_size("gcm")
    n_crm = lax.axis_size("crm")
    pairs = []
    for g in range(n_gcm):
        for c in range(n_crm):
            target = ((g + rows) % n_gcm) * n_crm + (c + cols) % n_crm
            pairs.append((g * n_crm + c, target))
    return lax.ppermute(value, ("gcm", "crm"), pairs)


def pair_table(bins):
    table = np.zeros((bins * bins, 576), np.float32)

    def put(column, i, j):
        table[i * bins + j, column] = 1.0
        table[j * bins + i, column] = 1.0

    for d in range(16):
        for b in range(32):
            put(32 * d + b, b, (b + d) % 32)
    for b in range(16):
        put(512 + b, b, b + 16)
    for b in range(32):
        put(528 + b, b, 32)
    put(560, 32, 32)
    return table


def to_partner(value):
    n_gcm = lax.axis_size("gcm")
    n_crm = lax.axis_size("crm")
    pairs = []
    for g in range(n_gcm):
        for c in range(n_crm):
            pairs.append((g * n_crm + c, (g ^ 1) * n_crm + c))
    return lax.ppermute(value, ("gcm", "crm"), pairs)


def shards(tracer, wind_x, wind_y, drops, owner, counts, collision, growth):
    devices = lax.axis_size("gcm") * lax.axis_size("crm")
    levels, row_count, col_count = tracer.shape
    col_total, bins, cells = drops.shape
    field = (tracer.shape, F32)
    strip = ((levels, row_count, 128), F32)
    rows = ((2, levels, col_count), F32)
    wide = col_count + 128
    down_map, up_map = level_tables(levels, CRM_LEV)

    row = ((1, col_total), jnp.int32)
    capacity = 2 * col_total // devices
    guests = col_total // 2
    tend, top, bot, to_right, to_left = call(
        first_kernel,
        [field, rows, rows] + [((levels // 4, 8, 128), F32)] * 2,
        [("h", tracer), ("h", wind_x), ("h", wind_y)],
        [field] * 3,
        [pltpu.SemaphoreType.DMA((3, levels // CHUNK))],
        limit=62,
    )
    from_left = shift(to_right, 0, 1)
    from_right = shift(to_left, 0, -1)
    count_row, _ = lax.optimization_barrier((counts[None, :], to_left))
    other_counts = to_partner(count_row)
    q_strip, u_strip, v_strip, tend_strip, top, bot = call(
        strip_kernel,
        [strip] * 4 + [((levels, wide + col_count), F32)] * 2,
        v(from_left, from_right, top, bot) + [("h", drops)],
    )
    sent, order, force, ordered, rank, slot = call(
        functools.partial(plan_kernel, capacity),
        [row] * 6,
        v(count_row, other_counts, owner.T) + [("h", top)],
    )
    (leaving,) = call(
        gather_kernel,
        [((guests, 40, cells), BF16)],
        [("s", sent)] + v(drops),
        [((8, 40, cells), F32)],
    )
    from_above = shift(bot, 1, 0)
    from_below = shift(top, -1, 0)
    leaving, from_above, from_below = lax.optimization_barrier((leaving, from_above, from_below))
    guest_drops = to_partner(leaving)
    coef, growth_rows = call(
        coef_kernel,
        [((80, 576), BF16), ((40, cells), F32)],
        v(collision, jnp.asarray(pair_table(bins), BF16), growth[None, :]) + [("h", top)],
        [((80, 576), F32), ((8, 128), F32)],
    )
    state, smooth, tend, top, bot = call(
        second_kernel,
        [field, field, ((levels, row_count, wide), F32)] + [((1, levels, wide), F32)] * 2,
        v(tracer, wind_x, wind_y, tend, q_strip, u_strip, v_strip, tend_strip)
        + v(from_above, from_below),
    )
    base, forcing = call(
        third_kernel,
        [field, ((CRM_LEV, col_total), F32)],
        v(tracer, state, smooth, tend, shift(bot, 1, 0), shift(top, -1, 0))
        + v(jnp.asarray(down_map, F32)) + [("h", coef), ("h", growth_rows)],
        [((levels, col_count), F32), ((levels, col_count), F32)],
    )

    other_forcing = to_partner(forcing)
    n_gcm = lax.axis_size("gcm")
    n_crm = lax.axis_size("crm")

    pairs = ((2 * CRM_LEV, col_total), F32)
    final, back, own, away = call(
        crm_kernel,
        [((col_total, bins, cells), BF16), ((guests + 1, 40, cells), BF16), pairs, pairs],
        [("s", order), ("s", force), ("s", ordered), ("s", sent)]
        + v(drops, guest_drops, forcing, other_forcing, coef, growth_rows),
        [((GROUP, 40, cells), F32), ((GROUP, 40, cells), F32), ((GROUP, 576, cells), BF16),
         ((2 * GROUP, 48, 128), F32), ((2 * col_total, cells), F32),
         ((2 * col_total, cells), F32), ((2 * col_total, cells), F32)],
        flops=10_000_000_000,
        limit=24,
    )
    returned = to_partner(away)
    returned, back = lax.optimization_barrier((returned, back))
    returned_drops = to_partner(back)
    heat, send = call(
        functools.partial(block_kernel, n_gcm, n_crm),
        [((CRM_LEV, col_total), F32), ((devices, CRM_LEV, 128), BF16)],
        v(own, returned, rank, slot),
    )
    got = lax.all_to_all(send, ("gcm", "crm"), split_axis=0, concat_axis=0, tiled=True)
    (drops_next,) = call(
        merge_kernel,
        [((col_total, bins, cells), BF16)],
        [("s", sent)] + v(final, returned_drops),
    )
    tracer_next, power, by_bin = call(
        functools.partial(last_kernel, n_gcm, n_crm),
        [field, ((CRM_LEV, devices * capacity), F32)],
        v(base, heat, got, jnp.asarray(up_map, F32))
        + [("h", drops_next.transpose(1, 0, 2))],
        [((levels, col_count), F32)] * 5,
        through=(4,),
    )
    drops_next = by_bin.transpose(1, 0, 2)
    return (tracer_next, drops_next, power)


def solution(mesh):
    return jax.shard_map(
        shards,
        mesh=mesh,
        in_specs=(
            P(None, "gcm", "crm"),
            P(None, "gcm", "crm"),
            P(None, "gcm", "crm"),
            P(("gcm", "crm"), None, None),
            P(("gcm", "crm"), None),
            P(("gcm", "crm")),
            P(),
            P(),
        ),
        out_specs=(P(None, "gcm", "crm"), P(("gcm", "crm"), None, None), P(None, ("gcm", "crm"))),
        check_vma=False,
    )
```

```python
import functools

import jax
import jax.numpy as jnp
import numpy as np
from jax import lax
from jax.experimental import pallas as pl
from jax.experimental.pallas import tpu as pltpu
from jax.sharding import PartitionSpec as P

CRM_X = 16
CRM_LEV = 16
DYN_STEPS = 2

DT_DYN = 0.04
DT_CRM = 0.05
DT_PHYS = 0.5
HIGH = lax.Precision.HIGHEST
F32 = jnp.float32
BF16 = jnp.bfloat16
GROUP = 16
CHUNK = 8
MIB = 1024 * 1024


def gll_tables():
    inv_root = 1.0 / np.sqrt(5.0)
    gll_nodes = np.array([-1.0, -inv_root, inv_root, 1.0])
    weights = np.array([1.0, 5.0, 5.0, 1.0]) / 6.0
    legendre = (5.0 * gll_nodes**3 - 3.0 * gll_nodes) / 2.0
    derivative = np.zeros((4, 4))
    for i in range(4):
        for j in range(4):
            if i != j:
                derivative[i, j] = legendre[i] / (legendre[j] * (gll_nodes[i] - gll_nodes[j]))
    derivative[0, 0] = -3.0
    derivative[3, 3] = 3.0
    return (2.0 * derivative, weights)


def level_tables(levels, crm_levels):
    spacing = levels / crm_levels
    centres = (np.arange(crm_levels) + 0.5) * spacing - 0.5
    hats = np.maximum(0.0, 1.0 - np.abs(np.arange(levels)[None, :] - centres[:, None]) / spacing)
    down_map = hats / hats.sum(axis=1, keepdims=True)
    up_map = hats.T / hats.T.sum(axis=1, keepdims=True)
    return (down_map, up_map)


DERIV, WEIGHTS = gll_tables()


def iota(shape, axis):
    return lax.broadcasted_iota(jnp.int32, shape, axis)


def derivative_terms(shape, axis):
    phase = iota(shape, axis) % 4
    terms = []
    for shift in range(-3, 4):
        value = jnp.zeros(shape, F32)
        for i in range(4):
            if 0 <= i + shift < 4:
                value = jnp.where(phase == i, F32(DERIV[i, i + shift]), value)
        terms.append((shift, value))
    return terms


def along(x, terms, axis):
    size = x.shape[axis]
    total = None
    for shift, value in terms:
        moved = x if shift == 0 else pltpu.roll(x, (-shift) % size, axis)
        part = value[None] * moved
        total = part if total is None else total + part
    return total


def tendency(x, u, v, row_terms, col_terms):
    halves = []
    for h in range(x.shape[2] // 128):
        cut = slice(128 * h, 128 * h + 128)
        q = x[:, :, cut]
        grad_x = along(q, row_terms, 1)
        grad_y = along(q, col_terms, 2)
        halves.append(-(u[:, :, cut] * grad_x + v[:, :, cut] * grad_y))
    return jnp.concatenate(halves, axis=2)


def put_rows(x, levels, top_ref, bot_ref, i):
    top_ref[i, levels, :] = x[:, 0, :]
    bot_ref[i, levels, :] = x[:, 7, :]


def first_kernel(
    q_hbm, u_hbm, v_hbm, tend_ref, top_ref, bot_ref, right_ref, left_ref, q_ref, u_ref, v_ref, sems
):
    row_terms = derivative_terms((8, 128), 0)
    col_terms = derivative_terms((8, 128), 1)
    lane = iota((8, 128), 1)
    chunks = q_ref.shape[0] // CHUNK

    def copies(chunk):
        levels = pl.ds(pl.multiple_of(chunk * CHUNK, CHUNK), CHUNK)
        return [
            pltpu.make_async_copy(src.at[levels], dst.at[levels], sems.at[i, chunk])
            for i, (src, dst) in enumerate(((q_hbm, q_ref), (u_hbm, u_ref), (v_hbm, v_ref)))
        ]

    for chunk in range(chunks):
        for copy in copies(chunk):
            copy.start()

    def body(chunk, carry):
        for copy in copies(chunk):
            copy.wait()
        for half in range(CHUNK // 4):
            right = jnp.zeros((8, 128), F32)
            left = jnp.zeros((8, 128), F32)
            for j in range(4):
                for f, ref in enumerate((q_ref, u_ref, v_ref)):
                    start = 32 * j + 8 * f
                    here = (lane >= start) & (lane < start + 8)
                    x = ref[chunk * CHUNK + half * 4 + j]
                    moved = pltpu.roll(x[:, 128:256], (start - 120) % 128, 1)
                    right = jnp.where(here, moved, right)
                    first = x[:, 0:128]
                    if start:
                        first = pltpu.roll(first, start, 1)
                    left = jnp.where(here, first, left)
            right_ref[chunk * (CHUNK // 4) + half] = right
            left_ref[chunk * (CHUNK // 4) + half] = left
        levels = pl.ds(pl.multiple_of(chunk * CHUNK, CHUNK), CHUNK)
        q = q_ref[levels]
        tend = tendency(q, u_ref[levels], v_ref[levels], row_terms, col_terms)
        tend_ref[levels] = tend
        put_rows(tend, levels, top_ref, bot_ref, 0)
        put_rows(q, levels, top_ref, bot_ref, 1)
        return carry

    lax.fori_loop(0, chunks, body, 0)


def strip_kernel(
    left_ref, right_ref, top_main, bot_main, after_ref,
    q_ref, u_ref, v_ref, tend_ref, top_ref, bot_ref,
):
    row_terms = derivative_terms((8, 128), 0)
    col_terms = derivative_terms((8, 128), 1)
    lane = iota((8, 128), 1)
    for out, main in ((top_ref, top_main), (bot_ref, bot_main)):
        out[:, 0:256] = main[0]
        out[:, 256:512] = main[1]

    def body(chunk, carry):
        tiles = [[], [], []]
        for half in range(CHUNK // 4):
            west = left_ref[chunk * (CHUNK // 4) + half]
            east = right_ref[chunk * (CHUNK // 4) + half]
            for j in range(4):
                for f in range(3):
                    start = 32 * j + 8 * f
                    a = pltpu.roll(east, 128 - start, 1) if start else east
                    b = pltpu.roll(west, (120 - start) % 128, 1)
                    tiles[f].append(jnp.where(lane < 8, a, jnp.where(lane >= 120, b, 0.0)))
        q, u, v = [jnp.stack(tile, axis=0) for tile in tiles]
        levels = pl.ds(pl.multiple_of(chunk * CHUNK, CHUNK), CHUNK)
        q_ref[levels] = q
        u_ref[levels] = u
        v_ref[levels] = v
        tend = tendency(q, u, v, row_terms, col_terms)
        tend_ref[levels] = tend
        shared = jnp.where((lane >= 8) & (lane < 24), pltpu.roll(q, 16, 2), tend)
        top_ref[levels, 512:640] = shared[:, 0, :]
        bot_ref[levels, 512:640] = shared[:, 7, :]
        return carry

    lax.fori_loop(0, q_ref.shape[0] // CHUNK, body, 0)


def assemble_chunk(x, up, down):
    shape = x.shape
    row = iota(shape, 1)
    partner = jnp.where(
        row == 0,
        jnp.broadcast_to(up[:, None, :], shape),
        jnp.where(
            row == 7,
            jnp.broadcast_to(down[:, None, :], shape),
            jnp.where(row == 3, pltpu.roll(x, 7, 1), pltpu.roll(x, 1, 1)),
        ),
    )
    x = jnp.where((row % 4 == 0) | (row % 4 == 3), 0.5 * (x + partner), x)
    col = iota(shape, 2)
    partner = jnp.where(
        col % 4 == 3, pltpu.roll(x, shape[2] - 1, 2), pltpu.roll(x, 1, 2)
    )
    return jnp.where((col % 4 == 0) | (col % 4 == 3), 0.5 * (x + partner), x)


def join(main, strip):
    return jnp.concatenate([main, strip], axis=2)


def second_kernel(
    q_ref, u_ref, v_ref, tend_ref, q_strip, u_strip, v_strip, tend_strip, up_ref, down_ref,
    state_ref, smooth_ref, next_ref, top_ref, bot_ref,
):
    row_terms = derivative_terms((8, 128), 0)
    col_terms = derivative_terms((8, 128), 1)

    def body(chunk, carry):
        levels = pl.ds(pl.multiple_of(chunk * CHUNK, CHUNK), CHUNK)
        q = join(q_ref[levels], q_strip[levels])
        rows = []
        for ref in (up_ref, down_ref):
            shared = ref[levels, 512:640]
            rows.append(jnp.concatenate([ref[levels, 0:256], shared], axis=1))
            rows.append(jnp.concatenate([ref[levels, 256:512], pltpu.roll(shared, 112, 1)], axis=1))
        change = assemble_chunk(join(tend_ref[levels], tend_strip[levels]), rows[0], rows[2])
        smooth = assemble_chunk(q, rows[1], rows[3])
        smooth_ref[levels] = smooth[:, :, 0:256]
        state = q + DT_DYN * change
        state_ref[levels] = state[:, :, 0:256]
        tend = tendency(
            state, join(u_ref[levels], u_strip[levels]), join(v_ref[levels], v_strip[levels]),
            row_terms, col_terms,
        )
        next_ref[levels] = tend
        put_rows(tend, levels, top_ref, bot_ref, 0)
        return carry

    lax.fori_loop(0, q_ref.shape[0] // CHUNK, body, 0)


def third_kernel(
    q_ref, state_ref, smooth_ref, tend_ref, up_ref, down_ref, down_map_ref, coef_ref, growth_ref,
    base_ref, forcing_ref, near_ref, far_ref,
):
    cols = forcing_ref.shape[1]
    half = cols // 2
    phase = iota((8, 256), 0) % 4
    row_weight = jnp.where((phase == 0) | (phase == 3), F32(WEIGHTS[0]), F32(WEIGHTS[1]))
    near_rows = jnp.where(iota((8, 256), 0) < 4, row_weight, 0.0)
    far_rows = row_weight - near_rows

    def body(chunk, carry):
        levels = pl.ds(pl.multiple_of(chunk * CHUNK, CHUNK), CHUNK)
        change = assemble_chunk(tend_ref[levels], up_ref[0, levels, :], down_ref[0, levels, :])
        moved = (state_ref[levels] + DT_DYN * change[:, :, 0:256]) - q_ref[levels]
        base_ref[levels] = smooth_ref[levels] + moved
        near_ref[levels, :] = jnp.sum(moved * near_rows[None], axis=1)
        far_ref[levels, :] = jnp.sum(moved * far_rows[None], axis=1)
        return carry

    lax.fori_loop(0, q_ref.shape[0] // CHUNK, body, 0)
    point = iota((256, cols), 0)
    element = iota((256, cols), 1)
    weight = jnp.where(
        (point % 4 == 0) | (point % 4 == 3), F32(WEIGHTS[0]), F32(WEIGHTS[1])
    ) * F32(0.25 / (DYN_STEPS * DT_DYN))
    near_cols = jnp.where(point // 4 == element, weight, 0.0)
    far_cols = jnp.where(point // 4 + half == element, weight, 0.0)
    means = jnp.dot(near_ref[...], near_cols, precision=HIGH, preferred_element_type=F32)
    means += jnp.dot(far_ref[...], far_cols, precision=HIGH, preferred_element_type=F32)
    forcing = jnp.dot(down_map_ref[...], means, precision=HIGH, preferred_element_type=F32)
    forcing_ref[...] = forcing.astype(BF16).astype(F32)


def coef_kernel(
    collision_ref, table_ref, growth_ref, after_ref, coef_ref, growth_out_ref, wide_ref, line_ref
):
    bins = collision_ref.shape[0]
    total = jnp.dot(collision_ref[...], table_ref[...], preferred_element_type=F32) * DT_CRM
    coarse = total.astype(BF16).astype(F32)
    wide_ref[...] = jnp.zeros(wide_ref.shape, F32)
    wide_ref[0:bins, :] = coarse
    wide_ref[40 : 40 + bins, :] = total - coarse
    coef_ref[...] = wide_ref[...].astype(BF16)
    line_ref[...] = jnp.zeros(line_ref.shape, F32)
    line_ref[0:1, 0:bins] = growth_ref[...]
    rows = jnp.broadcast_to(line_ref[0:1, :], (128, 128)).T[0:40]
    for h in range(growth_out_ref.shape[1] // 128):
        growth_out_ref[:, 128 * h : 128 * h + 128] = rows


def rank_row(values):
    total = values.shape[1]
    across = jnp.broadcast_to(values, (total, total))
    down = across.T
    earlier = iota((total, total), 0) < iota((total, total), 1)
    ahead = (down > across) | ((down == across) & earlier)
    return jnp.sum(ahead.astype(F32), axis=0, keepdims=True)


def plan_kernel(
    capacity, count_ref, other_ref, owner_ref, after_ref,
    sent_ref, order_ref, force_ref, ordered_ref, rank_ref, slot_ref,
):
    cols = count_ref.shape[1]
    counts = count_ref[...].astype(F32)
    others = other_ref[...].astype(F32)
    rank = rank_row(counts)
    other_rank = rank_row(others)
    square = (cols, cols)
    index = iota(square, 0).astype(F32)
    odd = 2.0 * iota(square, 1).astype(F32) + 1.0
    down_rank = jnp.broadcast_to(rank, square).T
    sent = jnp.sum(jnp.where(down_rank == odd, index, 0.0), axis=0, keepdims=True)
    sent_ref[...] = sent.astype(jnp.int32)
    rank_ref[...] = rank.astype(jnp.int32)

    is_odd = rank.astype(jnp.int32) % 2 == 1
    other_odd = other_rank.astype(jnp.int32) % 2 == 1
    listed = jnp.concatenate(
        [jnp.where(is_odd, -1.0, counts), jnp.where(other_odd, others, -1.0)], axis=1
    )
    lane = iota((1, cols), 1).astype(F32)
    name = jnp.concatenate([lane, cols + 0.5 * (other_rank - 1.0)], axis=1)
    wide = (2 * cols, 2 * cols)
    place = jnp.broadcast_to(rank_row(listed), wide).T[:, 0:cols]
    here = place == iota((2 * cols, cols), 1).astype(F32)
    force = iota((2 * cols, cols), 0).astype(F32)
    name = jnp.broadcast_to(name, wide).T[:, 0:cols]
    value = jnp.broadcast_to(listed, wide).T[:, 0:cols]
    for what, ref in ((name, order_ref), (force, force_ref), (value, ordered_ref)):
        total = jnp.sum(jnp.where(here, what, 0.0), axis=0, keepdims=True)
        ref[...] = total.astype(jnp.int32)

    owners = jnp.broadcast_to(owner_ref[...].astype(F32), square)
    same = (owners.T == owners) & (iota(square, 0) < iota(square, 1))
    earlier = jnp.sum(same.astype(F32), axis=0, keepdims=True)
    slot_ref[...] = owner_ref[...] * capacity + earlier.astype(jnp.int32)


def gather_kernel(sent_ref, drops_ref, out_ref, wide_ref):
    bins = drops_ref.shape[1]
    wide_ref[...] = jnp.zeros(wide_ref.shape, F32)

    def body(p, carry):
        for k in range(8):
            wide_ref[k, 0:bins, :] = drops_ref[sent_ref[0, 8 * p + k]].astype(F32)
        for k in range(8):
            out_ref[8 * p + k] = wide_ref[k].astype(BF16)
        return carry

    lax.fori_loop(0, out_ref.shape[0] // 8, body, 0)


def merge_kernel(sent_ref, final_ref, back_ref, out_ref):
    out_ref[...] = final_ref[...]

    def body(p, carry):
        row = back_ref[p].astype(F32)[0 : out_ref.shape[1]]
        out_ref[sent_ref[0, p]] = row.astype(BF16)
        return carry

    lax.fori_loop(0, back_ref.shape[0] - 1, body, 0)


def crm_kernel(
    order_ref, force_ref, count_ref, sent_ref,
    drops_ref, guest_ref, forcing_ref, other_ref, coef_ref, growth_ref,
    final_ref, back_ref, own_ref, away_ref,
    state_ref, start_ref, pair_ref, twice_ref, cell_ref, heat_cell_ref, echo_cell_ref,
):
    bins = drops_ref.shape[1]
    cells = drops_ref.shape[2]
    cols = drops_ref.shape[0]
    guests = guest_ref.shape[0]
    coef = coef_ref[...]
    growth = growth_ref[...]
    state_ref[...] = jnp.zeros(state_ref.shape, F32)
    heat_cell_ref[...] = jnp.zeros(heat_cell_ref.shape, F32)
    echo_cell_ref[...] = jnp.zeros(echo_cell_ref.shape, F32)
    mass = (iota((40, cells), 0) + 1).astype(F32) / F32(bins)
    spread = (iota((CRM_LEV, cells), 1) // CRM_X == iota((CRM_LEV, cells), 0)).astype(BF16)
    for i, ref in enumerate((forcing_ref, other_ref)):
        rows = jnp.dot(ref[...].T.astype(BF16), spread, preferred_element_type=F32)
        cell_ref[cols * i : cols * i + cols, :] = DT_CRM * rows

    def grow(k, which, zero):
        grown = state_ref[k] + growth * cell_ref[pl.ds(which, 1), :]
        for h in range(cells // 128):
            cut = slice(128 * h, 128 * h + 128)
            g = grown[0:32, cut]
            last = grown[32:40, cut]
            twice_ref[2 * k + h, 0:32, :] = g
            twice_ref[2 * k + h, 32:48, :] = g[0:16]
            for d in range(16):
                other = g if d % 8 == 0 else twice_ref[2 * k + h, pl.ds(zero + d, 32), :]
                if d == 8:
                    other = jnp.concatenate([g[8:], g[:8]], axis=0)
                pair_ref[k, 32 * d : 32 * d + 32, cut] = (g * other).astype(BF16)
            pair_ref[k, 512:528, cut] = (g[0:16] * g[16:32]).astype(BF16)
            pair_ref[k, 528:560, cut] = (g * last[0:1]).astype(BF16)
            tail = jnp.concatenate([last * last, jnp.zeros((8, 128), F32)], axis=0)
            pair_ref[k, 560:576, cut] = tail.astype(BF16)
        return grown

    def group(index, carry):
        base = index * GROUP
        which = [order_ref[0, base + k] for k in range(GROUP)]
        force = [force_ref[0, base + k] for k in range(GROUP)]
        count = [count_ref[0, base + k] for k in range(GROUP)]
        for k in range(GROUP):
            mine = drops_ref[jnp.minimum(which[k], cols - 1)].astype(F32)
            guest = guest_ref[jnp.clip(which[k] - cols, 0, guests - 1)].astype(F32)
            start = jnp.where(which[k] < cols, mine, guest[0:bins])
            start_ref[k, 0:bins, :] = start
            state_ref[k, 0:bins, :] = start

        zero = jnp.minimum(which[0], 0)

        def step(s, c):
            for k in range(GROUP):
                grown = grow(k, force[k], zero)
                change = jnp.dot(coef, pair_ref[k], preferred_element_type=F32)
                moved = grown + (change[0:40] + change[40:80])
                state_ref[k] = jnp.where(s < count[k], moved, state_ref[k])
            return c

        lax.fori_loop(0, count[0], step, 0)
        for k in range(GROUP):
            final = state_ref[k, 0:bins, :]
            weighted = mass[0:bins] * final
            heat = jnp.sum(mass[0:bins] * (final - start_ref[k, 0:bins, :]), axis=0, keepdims=True)
            echo = jnp.sum(weighted * weighted, axis=0, keepdims=True)
            heat_cell_ref[pl.ds(which[k], 1), :] = heat
            echo_cell_ref[pl.ds(which[k], 1), :] = echo

            result = state_ref[k].astype(BF16)
            guest = jnp.clip(which[k] - cols, 0, guests - 1)
            mine = which[k] < cols
            final_ref[jnp.where(mine, which[k], sent_ref[0, guest])] = final.astype(BF16)
            back_ref[jnp.where(mine, guests, guest)] = result
        return carry

    lax.fori_loop(0, cols // GROUP, group, 0)
    means = jnp.where(
        iota((CRM_LEV, cells), 1) // CRM_X == iota((CRM_LEV, cells), 0), F32(1.0 / CRM_X), 0.0
    )
    contract = (((1,), (1,)), ((), ()))
    heat = lax.dot_general(
        means, heat_cell_ref[...], contract, precision=HIGH, preferred_element_type=F32
    )
    heat = heat.astype(BF16).astype(F32)
    echo = lax.dot_general(
        means, echo_cell_ref[...], contract, precision=HIGH, preferred_element_type=F32
    )
    both = jnp.concatenate([heat, jnp.log(1.0 + echo)], axis=0)
    own_ref[...] = both[:, 0:cols]
    away_ref[...] = both[:, cols : 2 * cols]


def block_kernel(n_gcm, n_crm, own_ref, back_ref, rank_ref, slot_ref, heat_ref, send_ref):
    cols = own_ref.shape[1]
    odd = 2 * iota((cols, cols), 0) + 1
    home = (rank_ref[...] == odd).astype(F32)
    both = own_ref[...] + jnp.dot(
        back_ref[...], home, precision=HIGH, preferred_element_type=F32
    )
    heat = both[0:CRM_LEV]
    echo = both[CRM_LEV:]
    heat_ref[...] = heat
    contract = (((1,), (1,)), ((), ()))
    devices = send_ref.shape[0]
    slots = 2 * cols
    capacity = slots // devices
    onehot = (slot_ref[...] == iota((slots, cols), 0)).astype(F32)
    packed = lax.dot_general(echo, onehot, contract, precision=HIGH, preferred_element_type=F32)
    coarse = packed.astype(BF16).astype(F32)
    rest = packed - coarse
    middle = rest.astype(BF16).astype(F32)
    pieces = (coarse, middle, rest - middle)
    lane = iota((CRM_LEV, 128), 1)
    near = heat
    far = pltpu.roll(heat, 64, 1)
    sides = jnp.where(
        lane == 1, pltpu.roll(heat, 65, 1), jnp.where(lane == 62, pltpu.roll(heat, 63, 1), heat)
    )
    g = lax.axis_index("gcm")
    for d in range(devices):
        away = d // n_crm - g
        below = (away == 1) | (away == 1 - n_gcm)
        above = (away == -1) | (away == n_gcm - 1)
        block = jnp.where(below, far, jnp.where(above, near, sides))
        tile, offset = divmod(d * capacity, 128)
        for i, piece in enumerate(pieces):
            moved = pltpu.roll(
                piece[:, 128 * tile : 128 * tile + 128], (64 + i * capacity - offset) % 128, 1
            )
            start = 64 + i * capacity
            block = jnp.where((lane >= start) & (lane < start + capacity), moved, block)
        send_ref[d] = block.astype(BF16)


def last_kernel(
    n_gcm, n_crm, base_ref, own_ref, got_ref, up_map_ref, drops_in, out_ref, power_ref, drops_out,
    *back_refs,
):
    cols = own_ref.shape[1]
    half = cols // 2
    element = iota((cols, 256), 0)
    col = iota((cols, 256), 1)
    phase = col % 4
    edge = (phase == 0) | (phase == 3)
    other = jnp.where(phase == 0, col // 4 - 1, col // 4 + 1)

    def spread(centre, start, west, west_lane, east, east_lane):
        inside = jnp.where(element == col // 4 + start, jnp.where(edge, 0.5, 1.0), 0.0)
        beside = edge & (element == other + start) & (other >= 0) & (other < half)
        middle = jnp.where(beside, 0.5, inside).astype(BF16)
        from_west = jnp.where((col == 0) & (element == west_lane), 0.5, 0.0).astype(BF16)
        from_east = jnp.where((col == 255) & (element == east_lane), 0.5, 0.0).astype(BF16)
        total = jnp.dot(centre, middle, preferred_element_type=F32)
        total += jnp.dot(west, from_west, preferred_element_type=F32)
        total += jnp.dot(east, from_east, preferred_element_type=F32)
        return total

    own = own_ref[...].astype(BF16)
    g = lax.axis_index("gcm")
    c = lax.axis_index("crm")
    north = jnp.where(g == 0, n_gcm - 1, g - 1) * n_crm
    south = jnp.where(g == n_gcm - 1, 0, g + 1) * n_crm
    west = jnp.where(c == 0, n_crm - 1, c - 1)
    east = jnp.where(c == n_crm - 1, 0, c + 1)
    up, down = got_ref[north + c], got_ref[south + c]
    left, right = got_ref[g * n_crm + west], got_ref[g * n_crm + east]
    up_left, up_right = got_ref[north + west], got_ref[north + east]
    down_left, down_right = got_ref[south + west], got_ref[south + east]
    above = spread(up, 0, up_left, half - 1, up_right, 0)
    near = spread(own, 0, left, half - 1, right, 0)
    far = spread(own, half, left, half - 2, right, 1)
    below = spread(down, 0, down_left, half - 1, down_right, 0)
    parts = (
        0.5 * (above + near), near, 0.5 * (near + far), far, 0.5 * (far + below),
    )
    up_map = up_map_ref[...]
    for part, ref in zip(parts, back_refs):
        ref[...] = DT_PHYS * jnp.dot(up_map, part, precision=HIGH, preferred_element_type=F32)

    devices = got_ref.shape[0]
    slots = power_ref.shape[1]
    capacity = slots // devices
    lane = iota((CRM_LEV, 128), 1)
    tiles = [jnp.zeros((CRM_LEV, 128), F32) for _ in range(slots // 128)]
    for d in range(devices):
        block = got_ref[d].astype(F32)
        fine = pltpu.roll(block, 128 - 2 * capacity, 1) + pltpu.roll(block, 128 - capacity, 1)
        tile, offset = divmod(d * capacity, 128)
        moved = pltpu.roll(block + fine, (offset - 64) % 128, 1)
        tiles[tile] = jnp.where((lane >= offset) & (lane < offset + capacity), moved, tiles[tile])
    power_ref[...] = jnp.concatenate(tiles, axis=1)

    def body(chunk, carry):
        levels = pl.ds(pl.multiple_of(chunk * CHUNK, CHUNK), CHUNK)
        shape = (CHUNK, 8, 256)
        row = iota(shape, 1)
        wide = [jnp.broadcast_to(ref[levels, :][:, None, :], shape) for ref in back_refs]
        back = jnp.where(
            row == 0,
            wide[0],
            jnp.where(
                row < 3,
                wide[1],
                jnp.where(row < 5, wide[2], jnp.where(row < 7, wide[3], wide[4])),
            ),
        )
        out_ref[levels] = base_ref[levels] + back
        return carry

    lax.fori_loop(0, base_ref.shape[0] // CHUNK, body, 0)


def call(kernel, outs, args, scratch=(), sems=(), flops=10_000_000, limit=16, through=()):
    spaces = {
        "s": pl.BlockSpec(memory_space=pltpu.SMEM),
        "v": pl.BlockSpec(memory_space=pltpu.VMEM),
        "h": pl.BlockSpec(memory_space=pl.ANY),
    }
    return pl.pallas_call(
        kernel,
        out_shape=[jax.ShapeDtypeStruct(s, t) for s, t in outs]
        + [jax.ShapeDtypeStruct(args[i][1].shape, args[i][1].dtype) for i in through],
        in_specs=[spaces[kind] for kind, _ in args],
        out_specs=[spaces["v"]] * len(outs) + [spaces["h"]] * len(through),
        input_output_aliases={i: len(outs) + n for n, i in enumerate(through)},
        scratch_shapes=[pltpu.VMEM(s, t) for s, t in scratch] + list(sems),
        compiler_params=pltpu.CompilerParams(vmem_limit_bytes=limit * MIB),
        cost_estimate=pl.CostEstimate(flops=flops, bytes_accessed=4_000_000, transcendentals=0),
    )(*[value for _, value in args])


def v(*values):
    return [("v", value) for value in values]


def shift(value, rows, cols):
    n_gcm = lax.axis_size("gcm")
    n_crm = lax.axis_size("crm")
    pairs = []
    for g in range(n_gcm):
        for c in range(n_crm):
            target = ((g + rows) % n_gcm) * n_crm + (c + cols) % n_crm
            pairs.append((g * n_crm + c, target))
    return lax.ppermute(value, ("gcm", "crm"), pairs)


def pair_table(bins):
    table = np.zeros((bins * bins, 576), np.float32)

    def put(column, i, j):
        table[i * bins + j, column] = 1.0
        table[j * bins + i, column] = 1.0

    for d in range(16):
        for b in range(32):
            put(32 * d + b, b, (b + d) % 32)
    for b in range(16):
        put(512 + b, b, b + 16)
    for b in range(32):
        put(528 + b, b, 32)
    put(560, 32, 32)
    return table


def to_partner(value):
    n_gcm = lax.axis_size("gcm")
    n_crm = lax.axis_size("crm")
    pairs = []
    for g in range(n_gcm):
        for c in range(n_crm):
            pairs.append((g * n_crm + c, (g ^ 1) * n_crm + c))
    return lax.ppermute(value, ("gcm", "crm"), pairs)


def shards(tracer, wind_x, wind_y, drops, owner, counts, collision, growth):
    devices = lax.axis_size("gcm") * lax.axis_size("crm")
    levels, row_count, col_count = tracer.shape
    col_total, bins, cells = drops.shape
    field = (tracer.shape, F32)
    strip = ((levels, row_count, 128), F32)
    rows = ((2, levels, col_count), F32)
    wide = col_count + 128
    down_map, up_map = level_tables(levels, CRM_LEV)

    row = ((1, col_total), jnp.int32)
    capacity = 2 * col_total // devices
    guests = col_total // 2
    tend, top, bot, to_right, to_left = call(
        first_kernel,
        [field, rows, rows] + [((levels // 4, 8, 128), F32)] * 2,
        [("h", tracer), ("h", wind_x), ("h", wind_y)],
        [field] * 3,
        [pltpu.SemaphoreType.DMA((3, levels // CHUNK))],
        limit=62,
    )
    from_left = shift(to_right, 0, 1)
    from_right = shift(to_left, 0, -1)
    count_row, _ = lax.optimization_barrier((counts[None, :], to_left))
    other_counts = to_partner(count_row)
    q_strip, u_strip, v_strip, tend_strip, top, bot = call(
        strip_kernel,
        [strip] * 4 + [((levels, wide + col_count), F32)] * 2,
        v(from_left, from_right, top, bot) + [("h", drops)],
    )
    sent, order, force, ordered, rank, slot = call(
        functools.partial(plan_kernel, capacity),
        [row] * 6,
        v(count_row, other_counts, owner.T) + [("h", top)],
    )
    (leaving,) = call(
        gather_kernel,
        [((guests, 40, cells), BF16)],
        [("s", sent)] + v(drops),
        [((8, 40, cells), F32)],
    )
    from_above = shift(bot, 1, 0)
    from_below = shift(top, -1, 0)
    leaving, from_above, from_below = lax.optimization_barrier((leaving, from_above, from_below))
    guest_drops = to_partner(leaving)
    coef, growth_rows = call(
        coef_kernel,
        [((80, 576), BF16), ((40, cells), F32)],
        v(collision, jnp.asarray(pair_table(bins), BF16), growth[None, :]) + [("h", top)],
        [((80, 576), F32), ((8, 128), F32)],
    )
    state, smooth, tend, top, bot = call(
        second_kernel,
        [field, field, ((levels, row_count, wide), F32)] + [((1, levels, wide), F32)] * 2,
        v(tracer, wind_x, wind_y, tend, q_strip, u_strip, v_strip, tend_strip)
        + v(from_above, from_below),
    )
    base, forcing = call(
        third_kernel,
        [field, ((CRM_LEV, col_total), F32)],
        v(tracer, state, smooth, tend, shift(bot, 1, 0), shift(top, -1, 0))
        + v(jnp.asarray(down_map, F32)) + [("h", coef), ("h", growth_rows)],
        [((levels, col_count), F32), ((levels, col_count), F32)],
    )

    other_forcing = to_partner(forcing)
    n_gcm = lax.axis_size("gcm")
    n_crm = lax.axis_size("crm")

    pairs = ((2 * CRM_LEV, col_total), F32)
    final, back, own, away = call(
        crm_kernel,
        [((col_total, bins, cells), BF16), ((guests + 1, 40, cells), BF16), pairs, pairs],
        [("s", order), ("s", force), ("s", ordered), ("s", sent)]
        + v(drops, guest_drops, forcing, other_forcing, coef, growth_rows),
        [((GROUP, 40, cells), F32), ((GROUP, 40, cells), F32), ((GROUP, 576, cells), BF16),
         ((2 * GROUP, 48, 128), F32), ((2 * col_total, cells), F32),
         ((2 * col_total, cells), F32), ((2 * col_total, cells), F32)],
        flops=10_000_000_000,
        limit=24,
    )
    returned = to_partner(away)
    returned, back = lax.optimization_barrier((returned, back))
    returned_drops = to_partner(back)
    heat, send = call(
        functools.partial(block_kernel, n_gcm, n_crm),
        [((CRM_LEV, col_total), F32), ((devices, CRM_LEV, 128), BF16)],
        v(own, returned, rank, slot),
    )
    got = lax.all_to_all(send, ("gcm", "crm"), split_axis=0, concat_axis=0, tiled=True)
    (drops_next,) = call(
        merge_kernel,
        [((col_total, bins, cells), BF16)],
        [("s", sent)] + v(final, returned_drops),
    )
    tracer_next, power, by_bin = call(
        functools.partial(last_kernel, n_gcm, n_crm),
        [field, ((CRM_LEV, devices * capacity), F32)],
        v(base, heat, got, jnp.asarray(up_map, F32))
        + [("h", drops_next.transpose(1, 0, 2))],
        [((levels, col_count), F32)] * 5,
        through=(4,),
    )
    drops_next = by_bin.transpose(1, 0, 2)
    return (tracer_next, drops_next, power)


def solution(mesh):
    return jax.shard_map(
        shards,
        mesh=mesh,
        in_specs=(
            P(None, "gcm", "crm"),
            P(None, "gcm", "crm"),
            P(None, "gcm", "crm"),
            P(("gcm", "crm"), None, None),
            P(("gcm", "crm"), None),
            P(("gcm", "crm")),
            P(),
            P(),
        ),
        out_specs=(P(None, "gcm", "crm"), P(("gcm", "crm"), None, None), P(None, ("gcm", "crm"))),
        check_vma=False,
    )
```

```python
import functools

import jax
import jax.numpy as jnp
import numpy as np
from jax import lax
from jax.experimental import pallas as pl
from jax.experimental.pallas import tpu as pltpu
from jax.sharding import PartitionSpec as P

CRM_X = 16
CRM_LEV = 16
DYN_STEPS = 2

DT_DYN = 0.04
DT_CRM = 0.05
DT_PHYS = 0.5
HIGH = lax.Precision.HIGHEST
F32 = jnp.float32
BF16 = jnp.bfloat16
GROUP = 16
CHUNK = 8
MIB = 1024 * 1024


def gll_tables():
    inv_root = 1.0 / np.sqrt(5.0)
    gll_nodes = np.array([-1.0, -inv_root, inv_root, 1.0])
    weights = np.array([1.0, 5.0, 5.0, 1.0]) / 6.0
    legendre = (5.0 * gll_nodes**3 - 3.0 * gll_nodes) / 2.0
    derivative = np.zeros((4, 4))
    for i in range(4):
        for j in range(4):
            if i != j:
                derivative[i, j] = legendre[i] / (legendre[j] * (gll_nodes[i] - gll_nodes[j]))
    derivative[0, 0] = -3.0
    derivative[3, 3] = 3.0
    return (2.0 * derivative, weights)


def level_tables(levels, crm_levels):
    spacing = levels / crm_levels
    centres = (np.arange(crm_levels) + 0.5) * spacing - 0.5
    hats = np.maximum(0.0, 1.0 - np.abs(np.arange(levels)[None, :] - centres[:, None]) / spacing)
    down_map = hats / hats.sum(axis=1, keepdims=True)
    up_map = hats.T / hats.T.sum(axis=1, keepdims=True)
    return (down_map, up_map)


DERIV, WEIGHTS = gll_tables()


def iota(shape, axis):
    return lax.broadcasted_iota(jnp.int32, shape, axis)


def derivative_terms(shape, axis):
    phase = iota(shape, axis) % 4
    terms = []
    for shift in range(-3, 4):
        value = jnp.zeros(shape, F32)
        for i in range(4):
            if 0 <= i + shift < 4:
                value = jnp.where(phase == i, F32(DERIV[i, i + shift]), value)
        terms.append((shift, value))
    return terms


def along(x, terms, axis):
    size = x.shape[axis]
    total = None
    for shift, value in terms:
        moved = x if shift == 0 else pltpu.roll(x, (-shift) % size, axis)
        part = value[None] * moved
        total = part if total is None else total + part
    return total


def tendency(x, u, v, row_terms, col_terms):
    halves = []
    for h in range(x.shape[2] // 128):
        cut = slice(128 * h, 128 * h + 128)
        q = x[:, :, cut]
        grad_x = along(q, row_terms, 1)
        grad_y = along(q, col_terms, 2)
        halves.append(-(u[:, :, cut] * grad_x + v[:, :, cut] * grad_y))
    return jnp.concatenate(halves, axis=2)


def put_rows(x, levels, top_ref, bot_ref, i):
    top_ref[i, levels, :] = x[:, 0, :]
    bot_ref[i, levels, :] = x[:, 7, :]


def first_kernel(
    q_hbm, u_hbm, v_hbm, tend_ref, top_ref, bot_ref, right_ref, left_ref, q_ref, u_ref, v_ref, sems
):
    row_terms = derivative_terms((8, 128), 0)
    col_terms = derivative_terms((8, 128), 1)
    lane = iota((8, 128), 1)
    chunks = q_ref.shape[0] // CHUNK

    def copies(chunk):
        levels = pl.ds(pl.multiple_of(chunk * CHUNK, CHUNK), CHUNK)
        return [
            pltpu.make_async_copy(src.at[levels], dst.at[levels], sems.at[i, chunk])
            for i, (src, dst) in enumerate(((q_hbm, q_ref), (u_hbm, u_ref), (v_hbm, v_ref)))
        ]

    for chunk in range(chunks):
        for copy in copies(chunk):
            copy.start()

    def body(chunk, carry):
        for copy in copies(chunk):
            copy.wait()
        for half in range(CHUNK // 4):
            right = jnp.zeros((8, 128), F32)
            left = jnp.zeros((8, 128), F32)
            for j in range(4):
                for f, ref in enumerate((q_ref, u_ref, v_ref)):
                    start = 32 * j + 8 * f
                    here = (lane >= start) & (lane < start + 8)
                    x = ref[chunk * CHUNK + half * 4 + j]
                    moved = pltpu.roll(x[:, 128:256], (start - 120) % 128, 1)
                    right = jnp.where(here, moved, right)
                    first = x[:, 0:128]
                    if start:
                        first = pltpu.roll(first, start, 1)
                    left = jnp.where(here, first, left)
            right_ref[chunk * (CHUNK // 4) + half] = right
            left_ref[chunk * (CHUNK // 4) + half] = left
        levels = pl.ds(pl.multiple_of(chunk * CHUNK, CHUNK), CHUNK)
        q = q_ref[levels]
        tend = tendency(q, u_ref[levels], v_ref[levels], row_terms, col_terms)
        tend_ref[levels] = tend
        put_rows(tend, levels, top_ref, bot_ref, 0)
        put_rows(q, levels, top_ref, bot_ref, 1)
        return carry

    lax.fori_loop(0, chunks, body, 0)


def strip_kernel(
    left_ref, right_ref, top_main, bot_main, after_ref,
    q_ref, u_ref, v_ref, tend_ref, top_ref, bot_ref,
):
    row_terms = derivative_terms((8, 128), 0)
    col_terms = derivative_terms((8, 128), 1)
    lane = iota((8, 128), 1)
    for out, main in ((top_ref, top_main), (bot_ref, bot_main)):
        out[:, 0:256] = main[0]
        out[:, 256:512] = main[1]

    def body(chunk, carry):
        tiles = [[], [], []]
        for half in range(CHUNK // 4):
            west = left_ref[chunk * (CHUNK // 4) + half]
            east = right_ref[chunk * (CHUNK // 4) + half]
            for j in range(4):
                for f in range(3):
                    start = 32 * j + 8 * f
                    a = pltpu.roll(east, 128 - start, 1) if start else east
                    b = pltpu.roll(west, (120 - start) % 128, 1)
                    tiles[f].append(jnp.where(lane < 8, a, jnp.where(lane >= 120, b, 0.0)))
        q, u, v = [jnp.stack(tile, axis=0) for tile in tiles]
        levels = pl.ds(pl.multiple_of(chunk * CHUNK, CHUNK), CHUNK)
        q_ref[levels] = q
        u_ref[levels] = u
        v_ref[levels] = v
        tend = tendency(q, u, v, row_terms, col_terms)
        tend_ref[levels] = tend
        shared = jnp.where((lane >= 8) & (lane < 24), pltpu.roll(q, 16, 2), tend)
        top_ref[levels, 512:640] = shared[:, 0, :]
        bot_ref[levels, 512:640] = shared[:, 7, :]
        return carry

    lax.fori_loop(0, q_ref.shape[0] // CHUNK, body, 0)


def assemble_chunk(x, up, down):
    shape = x.shape
    row = iota(shape, 1)
    partner = jnp.where(
        row == 0,
        jnp.broadcast_to(up[:, None, :], shape),
        jnp.where(
            row == 7,
            jnp.broadcast_to(down[:, None, :], shape),
            jnp.where(row == 3, pltpu.roll(x, 7, 1), pltpu.roll(x, 1, 1)),
        ),
    )
    x = jnp.where((row % 4 == 0) | (row % 4 == 3), 0.5 * (x + partner), x)
    col = iota(shape, 2)
    partner = jnp.where(
        col % 4 == 3, pltpu.roll(x, shape[2] - 1, 2), pltpu.roll(x, 1, 2)
    )
    return jnp.where((col % 4 == 0) | (col % 4 == 3), 0.5 * (x + partner), x)


def join(main, strip):
    return jnp.concatenate([main, strip], axis=2)


def second_kernel(
    q_ref, u_ref, v_ref, tend_ref, q_strip, u_strip, v_strip, tend_strip, up_ref, down_ref,
    state_ref, smooth_ref, next_ref, top_ref, bot_ref,
):
    row_terms = derivative_terms((8, 128), 0)
    col_terms = derivative_terms((8, 128), 1)

    def body(chunk, carry):
        levels = pl.ds(pl.multiple_of(chunk * CHUNK, CHUNK), CHUNK)
        q = join(q_ref[levels], q_strip[levels])
        rows = []
        for ref in (up_ref, down_ref):
            shared = ref[levels, 512:640]
            rows.append(jnp.concatenate([ref[levels, 0:256], shared], axis=1))
            rows.append(jnp.concatenate([ref[levels, 256:512], pltpu.roll(shared, 112, 1)], axis=1))
        change = assemble_chunk(join(tend_ref[levels], tend_strip[levels]), rows[0], rows[2])
        smooth = assemble_chunk(q, rows[1], rows[3])
        smooth_ref[levels] = smooth[:, :, 0:256]
        state = q + DT_DYN * change
        state_ref[levels] = state[:, :, 0:256]
        tend = tendency(
            state, join(u_ref[levels], u_strip[levels]), join(v_ref[levels], v_strip[levels]),
            row_terms, col_terms,
        )
        next_ref[levels] = tend
        put_rows(tend, levels, top_ref, bot_ref, 0)
        return carry

    lax.fori_loop(0, q_ref.shape[0] // CHUNK, body, 0)


def third_kernel(
    q_ref, state_ref, smooth_ref, tend_ref, up_ref, down_ref, down_map_ref, coef_ref, growth_ref,
    base_ref, forcing_ref, near_ref, far_ref,
):
    cols = forcing_ref.shape[1]
    half = cols // 2
    phase = iota((8, 256), 0) % 4
    row_weight = jnp.where((phase == 0) | (phase == 3), F32(WEIGHTS[0]), F32(WEIGHTS[1]))
    near_rows = jnp.where(iota((8, 256), 0) < 4, row_weight, 0.0)
    far_rows = row_weight - near_rows

    def body(chunk, carry):
        levels = pl.ds(pl.multiple_of(chunk * CHUNK, CHUNK), CHUNK)
        change = assemble_chunk(tend_ref[levels], up_ref[0, levels, :], down_ref[0, levels, :])
        moved = (state_ref[levels] + DT_DYN * change[:, :, 0:256]) - q_ref[levels]
        base_ref[levels] = smooth_ref[levels] + moved
        near_ref[levels, :] = jnp.sum(moved * near_rows[None], axis=1)
        far_ref[levels, :] = jnp.sum(moved * far_rows[None], axis=1)
        return carry

    lax.fori_loop(0, q_ref.shape[0] // CHUNK, body, 0)
    point = iota((256, cols), 0)
    element = iota((256, cols), 1)
    weight = jnp.where(
        (point % 4 == 0) | (point % 4 == 3), F32(WEIGHTS[0]), F32(WEIGHTS[1])
    ) * F32(0.25 / (DYN_STEPS * DT_DYN))
    near_cols = jnp.where(point // 4 == element, weight, 0.0)
    far_cols = jnp.where(point // 4 + half == element, weight, 0.0)
    means = jnp.dot(near_ref[...], near_cols, precision=HIGH, preferred_element_type=F32)
    means += jnp.dot(far_ref[...], far_cols, precision=HIGH, preferred_element_type=F32)
    forcing = jnp.dot(down_map_ref[...], means, precision=HIGH, preferred_element_type=F32)
    forcing_ref[...] = forcing.astype(BF16).astype(F32)


def coef_kernel(
    collision_ref, table_ref, growth_ref, after_ref, coef_ref, growth_out_ref, wide_ref, line_ref
):
    bins = collision_ref.shape[0]
    total = jnp.dot(collision_ref[...], table_ref[...], preferred_element_type=F32) * DT_CRM
    coarse = total.astype(BF16).astype(F32)
    wide_ref[...] = jnp.zeros(wide_ref.shape, F32)
    wide_ref[0:bins, :] = coarse
    wide_ref[40 : 40 + bins, :] = total - coarse
    coef_ref[...] = wide_ref[...].astype(BF16)
    line_ref[...] = jnp.zeros(line_ref.shape, F32)
    line_ref[0:1, 0:bins] = growth_ref[...]
    rows = jnp.broadcast_to(line_ref[0:1, :], (128, 128)).T[0:40]
    for h in range(growth_out_ref.shape[1] // 128):
        growth_out_ref[:, 128 * h : 128 * h + 128] = rows


def rank_row(values):
    total = values.shape[1]
    across = jnp.broadcast_to(values, (total, total))
    down = across.T
    earlier = iota((total, total), 0) < iota((total, total), 1)
    ahead = (down > across) | ((down == across) & earlier)
    return jnp.sum(ahead.astype(F32), axis=0, keepdims=True)


def plan_kernel(
    capacity, count_ref, other_ref, owner_ref, after_ref,
    sent_ref, order_ref, force_ref, ordered_ref, rank_ref, slot_ref,
):
    cols = count_ref.shape[1]
    counts = count_ref[...].astype(F32)
    others = other_ref[...].astype(F32)
    rank = rank_row(counts)
    other_rank = rank_row(others)
    square = (cols, cols)
    index = iota(square, 0).astype(F32)
    odd = 2.0 * iota(square, 1).astype(F32) + 1.0
    down_rank = jnp.broadcast_to(rank, square).T
    sent = jnp.sum(jnp.where(down_rank == odd, index, 0.0), axis=0, keepdims=True)
    sent_ref[...] = sent.astype(jnp.int32)
    rank_ref[...] = rank.astype(jnp.int32)

    is_odd = rank.astype(jnp.int32) % 2 == 1
    other_odd = other_rank.astype(jnp.int32) % 2 == 1
    listed = jnp.concatenate(
        [jnp.where(is_odd, -1.0, counts), jnp.where(other_odd, others, -1.0)], axis=1
    )
    lane = iota((1, cols), 1).astype(F32)
    name = jnp.concatenate([lane, cols + 0.5 * (other_rank - 1.0)], axis=1)
    wide = (2 * cols, 2 * cols)
    place = jnp.broadcast_to(rank_row(listed), wide).T[:, 0:cols]
    here = place == iota((2 * cols, cols), 1).astype(F32)
    force = iota((2 * cols, cols), 0).astype(F32)
    name = jnp.broadcast_to(name, wide).T[:, 0:cols]
    value = jnp.broadcast_to(listed, wide).T[:, 0:cols]
    for what, ref in ((name, order_ref), (force, force_ref), (value, ordered_ref)):
        total = jnp.sum(jnp.where(here, what, 0.0), axis=0, keepdims=True)
        ref[...] = total.astype(jnp.int32)

    owners = jnp.broadcast_to(owner_ref[...].astype(F32), square)
    same = (owners.T == owners) & (iota(square, 0) < iota(square, 1))
    earlier = jnp.sum(same.astype(F32), axis=0, keepdims=True)
    slot_ref[...] = owner_ref[...] * capacity + earlier.astype(jnp.int32)


def gather_kernel(sent_ref, drops_ref, out_ref, wide_ref):
    bins = drops_ref.shape[1]
    wide_ref[...] = jnp.zeros(wide_ref.shape, F32)

    def body(p, carry):
        for k in range(8):
            wide_ref[k, 0:bins, :] = drops_ref[sent_ref[0, 8 * p + k]].astype(F32)
        for k in range(8):
            out_ref[8 * p + k] = wide_ref[k].astype(BF16)
        return carry

    lax.fori_loop(0, out_ref.shape[0] // 8, body, 0)


def merge_kernel(sent_ref, final_ref, back_ref, out_ref):
    out_ref[...] = final_ref[...]

    def body(p, carry):
        row = back_ref[p].astype(F32)[0 : out_ref.shape[1]]
        out_ref[sent_ref[0, p]] = row.astype(BF16)
        return carry

    lax.fori_loop(0, back_ref.shape[0] - 1, body, 0)


def crm_kernel(
    order_ref, force_ref, count_ref, sent_ref,
    drops_ref, guest_ref, forcing_ref, other_ref, coef_ref, growth_ref,
    final_ref, back_ref, own_ref, away_ref,
    state_ref, start_ref, pair_ref, twice_ref, cell_ref, heat_cell_ref, echo_cell_ref,
):
    bins = drops_ref.shape[1]
    cells = drops_ref.shape[2]
    cols = drops_ref.shape[0]
    guests = guest_ref.shape[0]
    coef = coef_ref[...]
    growth = growth_ref[...]
    state_ref[...] = jnp.zeros(state_ref.shape, F32)
    heat_cell_ref[...] = jnp.zeros(heat_cell_ref.shape, F32)
    echo_cell_ref[...] = jnp.zeros(echo_cell_ref.shape, F32)
    mass = (iota((40, cells), 0) + 1).astype(F32) / F32(bins)
    spread = (iota((CRM_LEV, cells), 1) // CRM_X == iota((CRM_LEV, cells), 0)).astype(BF16)
    for i, ref in enumerate((forcing_ref, other_ref)):
        rows = jnp.dot(ref[...].T.astype(BF16), spread, preferred_element_type=F32)
        cell_ref[cols * i : cols * i + cols, :] = DT_CRM * rows

    def grow(k, which, zero):
        grown = state_ref[k] + growth * cell_ref[pl.ds(which, 1), :]
        for h in range(cells // 128):
            cut = slice(128 * h, 128 * h + 128)
            g = grown[0:32, cut]
            last = grown[32:40, cut]
            twice_ref[2 * k + h, 0:32, :] = g
            twice_ref[2 * k + h, 32:48, :] = g[0:16]
            for d in range(16):
                other = g if d % 8 == 0 else twice_ref[2 * k + h, pl.ds(zero + d, 32), :]
                if d == 8:
                    other = jnp.concatenate([g[8:], g[:8]], axis=0)
                pair_ref[k, 32 * d : 32 * d + 32, cut] = (g * other).astype(BF16)
            pair_ref[k, 512:528, cut] = (g[0:16] * g[16:32]).astype(BF16)
            pair_ref[k, 528:560, cut] = (g * last[0:1]).astype(BF16)
            tail = jnp.concatenate([last * last, jnp.zeros((8, 128), F32)], axis=0)
            pair_ref[k, 560:576, cut] = tail.astype(BF16)
        return grown

    def group(index, carry):
        base = index * GROUP
        which = [order_ref[0, base + k] for k in range(GROUP)]
        force = [force_ref[0, base + k] for k in range(GROUP)]
        count = [count_ref[0, base + k] for k in range(GROUP)]
        for k in range(GROUP):
            mine = drops_ref[jnp.minimum(which[k], cols - 1)].astype(F32)
            guest = guest_ref[jnp.clip(which[k] - cols, 0, guests - 1)].astype(F32)
            start = jnp.where(which[k] < cols, mine, guest[0:bins])
            start_ref[k, 0:bins, :] = start
            state_ref[k, 0:bins, :] = start

        zero = jnp.minimum(which[0], 0)

        def substeps(width):
            def step(s, c):
                for k in range(width):
                    grown = grow(k, force[k], zero)
                    change = jnp.dot(coef, pair_ref[k], preferred_element_type=F32)
                    moved = grown + (change[0:40] + change[40:80])
                    state_ref[k] = jnp.where(s < count[k], moved, state_ref[k])
                return c

            return step

        half = count[GROUP // 2]
        lax.fori_loop(0, half, substeps(GROUP), 0)
        lax.fori_loop(half, count[0], substeps(GROUP // 2), 0)
        for k in range(GROUP):
            final = state_ref[k, 0:bins, :]
            weighted = mass[0:bins] * final
            heat = jnp.sum(mass[0:bins] * (final - start_ref[k, 0:bins, :]), axis=0, keepdims=True)
            echo = jnp.sum(weighted * weighted, axis=0, keepdims=True)
            heat_cell_ref[pl.ds(which[k], 1), :] = heat
            echo_cell_ref[pl.ds(which[k], 1), :] = echo

            result = state_ref[k].astype(BF16)
            guest = jnp.clip(which[k] - cols, 0, guests - 1)
            mine = which[k] < cols
            final_ref[jnp.where(mine, which[k], sent_ref[0, guest])] = final.astype(BF16)
            back_ref[jnp.where(mine, guests, guest)] = result
        return carry

    lax.fori_loop(0, cols // GROUP, group, 0)
    means = jnp.where(
        iota((CRM_LEV, cells), 1) // CRM_X == iota((CRM_LEV, cells), 0), F32(1.0 / CRM_X), 0.0
    )
    contract = (((1,), (1,)), ((), ()))
    heat = lax.dot_general(
        means, heat_cell_ref[...], contract, precision=HIGH, preferred_element_type=F32
    )
    heat = heat.astype(BF16).astype(F32)
    echo = lax.dot_general(
        means, echo_cell_ref[...], contract, precision=HIGH, preferred_element_type=F32
    )
    both = jnp.concatenate([heat, jnp.log(1.0 + echo)], axis=0)
    own_ref[...] = both[:, 0:cols]
    away_ref[...] = both[:, cols : 2 * cols]


def block_kernel(n_gcm, n_crm, own_ref, back_ref, rank_ref, slot_ref, heat_ref, send_ref):
    cols = own_ref.shape[1]
    odd = 2 * iota((cols, cols), 0) + 1
    home = (rank_ref[...] == odd).astype(F32)
    both = own_ref[...] + jnp.dot(
        back_ref[...], home, precision=HIGH, preferred_element_type=F32
    )
    heat = both[0:CRM_LEV]
    echo = both[CRM_LEV:]
    heat_ref[...] = heat
    contract = (((1,), (1,)), ((), ()))
    devices = send_ref.shape[0]
    slots = 2 * cols
    capacity = slots // devices
    onehot = (slot_ref[...] == iota((slots, cols), 0)).astype(F32)
    packed = lax.dot_general(echo, onehot, contract, precision=HIGH, preferred_element_type=F32)
    coarse = packed.astype(BF16).astype(F32)
    rest = packed - coarse
    middle = rest.astype(BF16).astype(F32)
    pieces = (coarse, middle, rest - middle)
    lane = iota((CRM_LEV, 128), 1)
    near = heat
    far = pltpu.roll(heat, 64, 1)
    sides = jnp.where(
        lane == 1, pltpu.roll(heat, 65, 1), jnp.where(lane == 62, pltpu.roll(heat, 63, 1), heat)
    )
    g = lax.axis_index("gcm")
    for d in range(devices):
        away = d // n_crm - g
        below = (away == 1) | (away == 1 - n_gcm)
        above = (away == -1) | (away == n_gcm - 1)
        block = jnp.where(below, far, jnp.where(above, near, sides))
        tile, offset = divmod(d * capacity, 128)
        for i, piece in enumerate(pieces):
            moved = pltpu.roll(
                piece[:, 128 * tile : 128 * tile + 128], (64 + i * capacity - offset) % 128, 1
            )
            start = 64 + i * capacity
            block = jnp.where((lane >= start) & (lane < start + capacity), moved, block)
        send_ref[d] = block.astype(BF16)


def last_kernel(
    n_gcm, n_crm, base_ref, own_ref, got_ref, up_map_ref, drops_in, out_ref, power_ref, drops_out,
    *back_refs,
):
    cols = own_ref.shape[1]
    half = cols // 2
    element = iota((cols, 256), 0)
    col = iota((cols, 256), 1)
    phase = col % 4
    edge = (phase == 0) | (phase == 3)
    other = jnp.where(phase == 0, col // 4 - 1, col // 4 + 1)

    def spread(centre, start, west, west_lane, east, east_lane):
        inside = jnp.where(element == col // 4 + start, jnp.where(edge, 0.5, 1.0), 0.0)
        beside = edge & (element == other + start) & (other >= 0) & (other < half)
        middle = jnp.where(beside, 0.5, inside).astype(BF16)
        from_west = jnp.where((col == 0) & (element == west_lane), 0.5, 0.0).astype(BF16)
        from_east = jnp.where((col == 255) & (element == east_lane), 0.5, 0.0).astype(BF16)
        total = jnp.dot(centre, middle, preferred_element_type=F32)
        total += jnp.dot(west, from_west, preferred_element_type=F32)
        total += jnp.dot(east, from_east, preferred_element_type=F32)
        return total

    own = own_ref[...].astype(BF16)
    g = lax.axis_index("gcm")
    c = lax.axis_index("crm")
    north = jnp.where(g == 0, n_gcm - 1, g - 1) * n_crm
    south = jnp.where(g == n_gcm - 1, 0, g + 1) * n_crm
    west = jnp.where(c == 0, n_crm - 1, c - 1)
    east = jnp.where(c == n_crm - 1, 0, c + 1)
    up, down = got_ref[north + c], got_ref[south + c]
    left, right = got_ref[g * n_crm + west], got_ref[g * n_crm + east]
    up_left, up_right = got_ref[north + west], got_ref[north + east]
    down_left, down_right = got_ref[south + west], got_ref[south + east]
    above = spread(up, 0, up_left, half - 1, up_right, 0)
    near = spread(own, 0, left, half - 1, right, 0)
    far = spread(own, half, left, half - 2, right, 1)
    below = spread(down, 0, down_left, half - 1, down_right, 0)
    parts = (
        0.5 * (above + near), near, 0.5 * (near + far), far, 0.5 * (far + below),
    )
    up_map = up_map_ref[...]
    for part, ref in zip(parts, back_refs):
        ref[...] = DT_PHYS * jnp.dot(up_map, part, precision=HIGH, preferred_element_type=F32)

    devices = got_ref.shape[0]
    slots = power_ref.shape[1]
    capacity = slots // devices
    lane = iota((CRM_LEV, 128), 1)
    tiles = [jnp.zeros((CRM_LEV, 128), F32) for _ in range(slots // 128)]
    for d in range(devices):
        block = got_ref[d].astype(F32)
        fine = pltpu.roll(block, 128 - 2 * capacity, 1) + pltpu.roll(block, 128 - capacity, 1)
        tile, offset = divmod(d * capacity, 128)
        moved = pltpu.roll(block + fine, (offset - 64) % 128, 1)
        tiles[tile] = jnp.where((lane >= offset) & (lane < offset + capacity), moved, tiles[tile])
    power_ref[...] = jnp.concatenate(tiles, axis=1)

    def body(chunk, carry):
        levels = pl.ds(pl.multiple_of(chunk * CHUNK, CHUNK), CHUNK)
        shape = (CHUNK, 8, 256)
        row = iota(shape, 1)
        wide = [jnp.broadcast_to(ref[levels, :][:, None, :], shape) for ref in back_refs]
        back = jnp.where(
            row == 0,
            wide[0],
            jnp.where(
                row < 3,
                wide[1],
                jnp.where(row < 5, wide[2], jnp.where(row < 7, wide[3], wide[4])),
            ),
        )
        out_ref[levels] = base_ref[levels] + back
        return carry

    lax.fori_loop(0, base_ref.shape[0] // CHUNK, body, 0)


def call(kernel, outs, args, scratch=(), sems=(), flops=10_000_000, limit=16, through=()):
    spaces = {
        "s": pl.BlockSpec(memory_space=pltpu.SMEM),
        "v": pl.BlockSpec(memory_space=pltpu.VMEM),
        "h": pl.BlockSpec(memory_space=pl.ANY),
    }
    return pl.pallas_call(
        kernel,
        out_shape=[jax.ShapeDtypeStruct(s, t) for s, t in outs]
        + [jax.ShapeDtypeStruct(args[i][1].shape, args[i][1].dtype) for i in through],
        in_specs=[spaces[kind] for kind, _ in args],
        out_specs=[spaces["v"]] * len(outs) + [spaces["h"]] * len(through),
        input_output_aliases={i: len(outs) + n for n, i in enumerate(through)},
        scratch_shapes=[pltpu.VMEM(s, t) for s, t in scratch] + list(sems),
        compiler_params=pltpu.CompilerParams(vmem_limit_bytes=limit * MIB),
        cost_estimate=pl.CostEstimate(flops=flops, bytes_accessed=4_000_000, transcendentals=0),
    )(*[value for _, value in args])


def v(*values):
    return [("v", value) for value in values]


def shift(value, rows, cols):
    n_gcm = lax.axis_size("gcm")
    n_crm = lax.axis_size("crm")
    pairs = []
    for g in range(n_gcm):
        for c in range(n_crm):
            target = ((g + rows) % n_gcm) * n_crm + (c + cols) % n_crm
            pairs.append((g * n_crm + c, target))
    return lax.ppermute(value, ("gcm", "crm"), pairs)


def pair_table(bins):
    table = np.zeros((bins * bins, 576), np.float32)

    def put(column, i, j):
        table[i * bins + j, column] = 1.0
        table[j * bins + i, column] = 1.0

    for d in range(16):
        for b in range(32):
            put(32 * d + b, b, (b + d) % 32)
    for b in range(16):
        put(512 + b, b, b + 16)
    for b in range(32):
        put(528 + b, b, 32)
    put(560, 32, 32)
    return table


def to_partner(value):
    n_gcm = lax.axis_size("gcm")
    n_crm = lax.axis_size("crm")
    pairs = []
    for g in range(n_gcm):
        for c in range(n_crm):
            pairs.append((g * n_crm + c, (g ^ 1) * n_crm + c))
    return lax.ppermute(value, ("gcm", "crm"), pairs)


def shards(tracer, wind_x, wind_y, drops, owner, counts, collision, growth):
    devices = lax.axis_size("gcm") * lax.axis_size("crm")
    levels, row_count, col_count = tracer.shape
    col_total, bins, cells = drops.shape
    field = (tracer.shape, F32)
    strip = ((levels, row_count, 128), F32)
    rows = ((2, levels, col_count), F32)
    wide = col_count + 128
    down_map, up_map = level_tables(levels, CRM_LEV)

    row = ((1, col_total), jnp.int32)
    capacity = 2 * col_total // devices
    guests = col_total // 2
    tend, top, bot, to_right, to_left = call(
        first_kernel,
        [field, rows, rows] + [((levels // 4, 8, 128), F32)] * 2,
        [("h", tracer), ("h", wind_x), ("h", wind_y)],
        [field] * 3,
        [pltpu.SemaphoreType.DMA((3, levels // CHUNK))],
        limit=62,
    )
    from_left = shift(to_right, 0, 1)
    from_right = shift(to_left, 0, -1)
    count_row, _ = lax.optimization_barrier((counts[None, :], to_left))
    other_counts = to_partner(count_row)
    q_strip, u_strip, v_strip, tend_strip, top, bot = call(
        strip_kernel,
        [strip] * 4 + [((levels, wide + col_count), F32)] * 2,
        v(from_left, from_right, top, bot) + [("h", drops)],
    )
    sent, order, force, ordered, rank, slot = call(
        functools.partial(plan_kernel, capacity),
        [row] * 6,
        v(count_row, other_counts, owner.T) + [("h", top)],
    )
    (leaving,) = call(
        gather_kernel,
        [((guests, 40, cells), BF16)],
        [("s", sent)] + v(drops),
        [((8, 40, cells), F32)],
    )
    from_above = shift(bot, 1, 0)
    from_below = shift(top, -1, 0)
    leaving, from_above, from_below = lax.optimization_barrier((leaving, from_above, from_below))
    guest_drops = to_partner(leaving)
    coef, growth_rows = call(
        coef_kernel,
        [((80, 576), BF16), ((40, cells), F32)],
        v(collision, jnp.asarray(pair_table(bins), BF16), growth[None, :]) + [("h", top)],
        [((80, 576), F32), ((8, 128), F32)],
    )
    state, smooth, tend, top, bot = call(
        second_kernel,
        [field, field, ((levels, row_count, wide), F32)] + [((1, levels, wide), F32)] * 2,
        v(tracer, wind_x, wind_y, tend, q_strip, u_strip, v_strip, tend_strip)
        + v(from_above, from_below),
    )
    base, forcing = call(
        third_kernel,
        [field, ((CRM_LEV, col_total), F32)],
        v(tracer, state, smooth, tend, shift(bot, 1, 0), shift(top, -1, 0))
        + v(jnp.asarray(down_map, F32)) + [("h", coef), ("h", growth_rows)],
        [((levels, col_count), F32), ((levels, col_count), F32)],
    )

    other_forcing = to_partner(forcing)
    n_gcm = lax.axis_size("gcm")
    n_crm = lax.axis_size("crm")

    pairs = ((2 * CRM_LEV, col_total), F32)
    final, back, own, away = call(
        crm_kernel,
        [((col_total, bins, cells), BF16), ((guests + 1, 40, cells), BF16), pairs, pairs],
        [("s", order), ("s", force), ("s", ordered), ("s", sent)]
        + v(drops, guest_drops, forcing, other_forcing, coef, growth_rows),
        [((GROUP, 40, cells), F32), ((GROUP, 40, cells), F32), ((GROUP, 576, cells), BF16),
         ((2 * GROUP, 48, 128), F32), ((2 * col_total, cells), F32),
         ((2 * col_total, cells), F32), ((2 * col_total, cells), F32)],
        flops=10_000_000_000,
        limit=24,
    )
    returned = to_partner(away)
    returned, back = lax.optimization_barrier((returned, back))
    returned_drops = to_partner(back)
    heat, send = call(
        functools.partial(block_kernel, n_gcm, n_crm),
        [((CRM_LEV, col_total), F32), ((devices, CRM_LEV, 128), BF16)],
        v(own, returned, rank, slot),
    )
    got = lax.all_to_all(send, ("gcm", "crm"), split_axis=0, concat_axis=0, tiled=True)
    (drops_next,) = call(
        merge_kernel,
        [((col_total, bins, cells), BF16)],
        [("s", sent)] + v(final, returned_drops),
    )
    tracer_next, power, by_bin = call(
        functools.partial(last_kernel, n_gcm, n_crm),
        [field, ((CRM_LEV, devices * capacity), F32)],
        v(base, heat, got, jnp.asarray(up_map, F32))
        + [("h", drops_next.transpose(1, 0, 2))],
        [((levels, col_count), F32)] * 5,
        through=(4,),
    )
    drops_next = by_bin.transpose(1, 0, 2)
    return (tracer_next, drops_next, power)


def solution(mesh):
    return jax.shard_map(
        shards,
        mesh=mesh,
        in_specs=(
            P(None, "gcm", "crm"),
            P(None, "gcm", "crm"),
            P(None, "gcm", "crm"),
            P(("gcm", "crm"), None, None),
            P(("gcm", "crm"), None),
            P(("gcm", "crm")),
            P(),
            P(),
        ),
        out_specs=(P(None, "gcm", "crm"), P(("gcm", "crm"), None, None), P(None, ("gcm", "crm"))),
        check_vma=False,
    )
```

```python
import functools

import jax
import jax.numpy as jnp
import numpy as np
from jax import lax
from jax.experimental import pallas as pl
from jax.experimental.pallas import tpu as pltpu
from jax.sharding import PartitionSpec as P

CRM_X = 16
CRM_LEV = 16
DYN_STEPS = 2

DT_DYN = 0.04
DT_CRM = 0.05
DT_PHYS = 0.5
HIGH = lax.Precision.HIGHEST
F32 = jnp.float32
BF16 = jnp.bfloat16
GROUP = 32
CHUNK = 8
MIB = 1024 * 1024


def gll_tables():
    inv_root = 1.0 / np.sqrt(5.0)
    gll_nodes = np.array([-1.0, -inv_root, inv_root, 1.0])
    weights = np.array([1.0, 5.0, 5.0, 1.0]) / 6.0
    legendre = (5.0 * gll_nodes**3 - 3.0 * gll_nodes) / 2.0
    derivative = np.zeros((4, 4))
    for i in range(4):
        for j in range(4):
            if i != j:
                derivative[i, j] = legendre[i] / (legendre[j] * (gll_nodes[i] - gll_nodes[j]))
    derivative[0, 0] = -3.0
    derivative[3, 3] = 3.0
    return (2.0 * derivative, weights)


def level_tables(levels, crm_levels):
    spacing = levels / crm_levels
    centres = (np.arange(crm_levels) + 0.5) * spacing - 0.5
    hats = np.maximum(0.0, 1.0 - np.abs(np.arange(levels)[None, :] - centres[:, None]) / spacing)
    down_map = hats / hats.sum(axis=1, keepdims=True)
    up_map = hats.T / hats.T.sum(axis=1, keepdims=True)
    return (down_map, up_map)


DERIV, WEIGHTS = gll_tables()


def iota(shape, axis):
    return lax.broadcasted_iota(jnp.int32, shape, axis)


def derivative_terms(shape, axis):
    phase = iota(shape, axis) % 4
    terms = []
    for shift in range(-3, 4):
        value = jnp.zeros(shape, F32)
        for i in range(4):
            if 0 <= i + shift < 4:
                value = jnp.where(phase == i, F32(DERIV[i, i + shift]), value)
        terms.append((shift, value))
    return terms


def along(x, terms, axis):
    size = x.shape[axis]
    total = None
    for shift, value in terms:
        moved = x if shift == 0 else pltpu.roll(x, (-shift) % size, axis)
        part = value[None] * moved
        total = part if total is None else total + part
    return total


def tendency(x, u, v, row_terms, col_terms):
    halves = []
    for h in range(x.shape[2] // 128):
        cut = slice(128 * h, 128 * h + 128)
        q = x[:, :, cut]
        grad_x = along(q, row_terms, 1)
        grad_y = along(q, col_terms, 2)
        halves.append(-(u[:, :, cut] * grad_x + v[:, :, cut] * grad_y))
    return jnp.concatenate(halves, axis=2)


def put_rows(x, levels, top_ref, bot_ref, i):
    top_ref[i, levels, :] = x[:, 0, :]
    bot_ref[i, levels, :] = x[:, 7, :]


def first_kernel(
    q_hbm, u_hbm, v_hbm, tend_ref, top_ref, bot_ref, right_ref, left_ref, q_ref, u_ref, v_ref, sems
):
    row_terms = derivative_terms((8, 128), 0)
    col_terms = derivative_terms((8, 128), 1)
    lane = iota((8, 128), 1)
    chunks = q_ref.shape[0] // CHUNK

    def copies(chunk):
        levels = pl.ds(pl.multiple_of(chunk * CHUNK, CHUNK), CHUNK)
        return [
            pltpu.make_async_copy(src.at[levels], dst.at[levels], sems.at[i, chunk])
            for i, (src, dst) in enumerate(((q_hbm, q_ref), (u_hbm, u_ref), (v_hbm, v_ref)))
        ]

    for chunk in range(chunks):
        for copy in copies(chunk):
            copy.start()

    def body(chunk, carry):
        for copy in copies(chunk):
            copy.wait()
        for half in range(CHUNK // 4):
            right = jnp.zeros((8, 128), F32)
            left = jnp.zeros((8, 128), F32)
            for j in range(4):
                for f, ref in enumerate((q_ref, u_ref, v_ref)):
                    start = 32 * j + 8 * f
                    here = (lane >= start) & (lane < start + 8)
                    x = ref[chunk * CHUNK + half * 4 + j]
                    moved = pltpu.roll(x[:, 128:256], (start - 120) % 128, 1)
                    right = jnp.where(here, moved, right)
                    first = x[:, 0:128]
                    if start:
                        first = pltpu.roll(first, start, 1)
                    left = jnp.where(here, first, left)
            right_ref[chunk * (CHUNK // 4) + half] = right
            left_ref[chunk * (CHUNK // 4) + half] = left
        levels = pl.ds(pl.multiple_of(chunk * CHUNK, CHUNK), CHUNK)
        q = q_ref[levels]
        tend = tendency(q, u_ref[levels], v_ref[levels], row_terms, col_terms)
        tend_ref[levels] = tend
        put_rows(tend, levels, top_ref, bot_ref, 0)
        put_rows(q, levels, top_ref, bot_ref, 1)
        return carry

    lax.fori_loop(0, chunks, body, 0)


def strip_kernel(
    left_ref, right_ref, top_main, bot_main, after_ref,
    q_ref, u_ref, v_ref, tend_ref, top_ref, bot_ref,
):
    row_terms = derivative_terms((8, 128), 0)
    col_terms = derivative_terms((8, 128), 1)
    lane = iota((8, 128), 1)
    for out, main in ((top_ref, top_main), (bot_ref, bot_main)):
        out[:, 0:256] = main[0]
        out[:, 256:512] = main[1]

    def body(chunk, carry):
        tiles = [[], [], []]
        for half in range(CHUNK // 4):
            west = left_ref[chunk * (CHUNK // 4) + half]
            east = right_ref[chunk * (CHUNK // 4) + half]
            for j in range(4):
                for f in range(3):
                    start = 32 * j + 8 * f
                    a = pltpu.roll(east, 128 - start, 1) if start else east
                    b = pltpu.roll(west, (120 - start) % 128, 1)
                    tiles[f].append(jnp.where(lane < 8, a, jnp.where(lane >= 120, b, 0.0)))
        q, u, v = [jnp.stack(tile, axis=0) for tile in tiles]
        levels = pl.ds(pl.multiple_of(chunk * CHUNK, CHUNK), CHUNK)
        q_ref[levels] = q
        u_ref[levels] = u
        v_ref[levels] = v
        tend = tendency(q, u, v, row_terms, col_terms)
        tend_ref[levels] = tend
        shared = jnp.where((lane >= 8) & (lane < 24), pltpu.roll(q, 16, 2), tend)
        top_ref[levels, 512:640] = shared[:, 0, :]
        bot_ref[levels, 512:640] = shared[:, 7, :]
        return carry

    lax.fori_loop(0, q_ref.shape[0] // CHUNK, body, 0)


def assemble_chunk(x, up, down):
    shape = x.shape
    row = iota(shape, 1)
    partner = jnp.where(
        row == 0,
        jnp.broadcast_to(up[:, None, :], shape),
        jnp.where(
            row == 7,
            jnp.broadcast_to(down[:, None, :], shape),
            jnp.where(row == 3, pltpu.roll(x, 7, 1), pltpu.roll(x, 1, 1)),
        ),
    )
    x = jnp.where((row % 4 == 0) | (row % 4 == 3), 0.5 * (x + partner), x)
    col = iota(shape, 2)
    partner = jnp.where(
        col % 4 == 3, pltpu.roll(x, shape[2] - 1, 2), pltpu.roll(x, 1, 2)
    )
    return jnp.where((col % 4 == 0) | (col % 4 == 3), 0.5 * (x + partner), x)


def join(main, strip):
    return jnp.concatenate([main, strip], axis=2)


def second_kernel(
    q_ref, u_ref, v_ref, tend_ref, q_strip, u_strip, v_strip, tend_strip, up_ref, down_ref,
    state_ref, smooth_ref, next_ref, top_ref, bot_ref,
):
    row_terms = derivative_terms((8, 128), 0)
    col_terms = derivative_terms((8, 128), 1)

    def body(chunk, carry):
        levels = pl.ds(pl.multiple_of(chunk * CHUNK, CHUNK), CHUNK)
        q = join(q_ref[levels], q_strip[levels])
        rows = []
        for ref in (up_ref, down_ref):
            shared = ref[levels, 512:640]
            rows.append(jnp.concatenate([ref[levels, 0:256], shared], axis=1))
            rows.append(jnp.concatenate([ref[levels, 256:512], pltpu.roll(shared, 112, 1)], axis=1))
        change = assemble_chunk(join(tend_ref[levels], tend_strip[levels]), rows[0], rows[2])
        smooth = assemble_chunk(q, rows[1], rows[3])
        smooth_ref[levels] = smooth[:, :, 0:256]
        state = q + DT_DYN * change
        state_ref[levels] = state[:, :, 0:256]
        tend = tendency(
            state, join(u_ref[levels], u_strip[levels]), join(v_ref[levels], v_strip[levels]),
            row_terms, col_terms,
        )
        next_ref[levels] = tend
        put_rows(tend, levels, top_ref, bot_ref, 0)
        return carry

    lax.fori_loop(0, q_ref.shape[0] // CHUNK, body, 0)


def third_kernel(
    q_ref, state_ref, smooth_ref, tend_ref, up_ref, down_ref, down_map_ref, coef_ref, growth_ref,
    base_ref, forcing_ref, near_ref, far_ref,
):
    cols = forcing_ref.shape[1]
    half = cols // 2
    phase = iota((8, 256), 0) % 4
    row_weight = jnp.where((phase == 0) | (phase == 3), F32(WEIGHTS[0]), F32(WEIGHTS[1]))
    near_rows = jnp.where(iota((8, 256), 0) < 4, row_weight, 0.0)
    far_rows = row_weight - near_rows

    def body(chunk, carry):
        levels = pl.ds(pl.multiple_of(chunk * CHUNK, CHUNK), CHUNK)
        change = assemble_chunk(tend_ref[levels], up_ref[0, levels, :], down_ref[0, levels, :])
        moved = (state_ref[levels] + DT_DYN * change[:, :, 0:256]) - q_ref[levels]
        base_ref[levels] = smooth_ref[levels] + moved
        near_ref[levels, :] = jnp.sum(moved * near_rows[None], axis=1)
        far_ref[levels, :] = jnp.sum(moved * far_rows[None], axis=1)
        return carry

    lax.fori_loop(0, q_ref.shape[0] // CHUNK, body, 0)
    point = iota((256, cols), 0)
    element = iota((256, cols), 1)
    weight = jnp.where(
        (point % 4 == 0) | (point % 4 == 3), F32(WEIGHTS[0]), F32(WEIGHTS[1])
    ) * F32(0.25 / (DYN_STEPS * DT_DYN))
    near_cols = jnp.where(point // 4 == element, weight, 0.0)
    far_cols = jnp.where(point // 4 + half == element, weight, 0.0)
    means = jnp.dot(near_ref[...], near_cols, precision=HIGH, preferred_element_type=F32)
    means += jnp.dot(far_ref[...], far_cols, precision=HIGH, preferred_element_type=F32)
    forcing = jnp.dot(down_map_ref[...], means, precision=HIGH, preferred_element_type=F32)
    forcing_ref[...] = forcing.astype(BF16).astype(F32)


def coef_kernel(
    collision_ref, table_ref, growth_ref, after_ref, coef_ref, growth_out_ref, wide_ref, line_ref
):
    bins = collision_ref.shape[0]
    total = jnp.dot(collision_ref[...], table_ref[...], preferred_element_type=F32) * DT_CRM
    coarse = total.astype(BF16).astype(F32)
    wide_ref[...] = jnp.zeros(wide_ref.shape, F32)
    wide_ref[0:bins, :] = coarse
    wide_ref[40 : 40 + bins, :] = total - coarse
    coef_ref[...] = wide_ref[...].astype(BF16)
    line_ref[...] = jnp.zeros(line_ref.shape, F32)
    line_ref[0:1, 0:bins] = growth_ref[...]
    rows = jnp.broadcast_to(line_ref[0:1, :], (128, 128)).T[0:40]
    for h in range(growth_out_ref.shape[1] // 128):
        growth_out_ref[:, 128 * h : 128 * h + 128] = rows


def rank_row(values):
    total = values.shape[1]
    across = jnp.broadcast_to(values, (total, total))
    down = across.T
    earlier = iota((total, total), 0) < iota((total, total), 1)
    ahead = (down > across) | ((down == across) & earlier)
    return jnp.sum(ahead.astype(F32), axis=0, keepdims=True)


def plan_kernel(
    capacity, count_ref, other_ref, owner_ref, after_ref,
    sent_ref, order_ref, force_ref, ordered_ref, rank_ref, slot_ref,
):
    cols = count_ref.shape[1]
    counts = count_ref[...].astype(F32)
    others = other_ref[...].astype(F32)
    rank = rank_row(counts)
    other_rank = rank_row(others)
    square = (cols, cols)
    index = iota(square, 0).astype(F32)
    odd = 2.0 * iota(square, 1).astype(F32) + 1.0
    down_rank = jnp.broadcast_to(rank, square).T
    sent = jnp.sum(jnp.where(down_rank == odd, index, 0.0), axis=0, keepdims=True)
    sent_ref[...] = sent.astype(jnp.int32)
    rank_ref[...] = rank.astype(jnp.int32)

    is_odd = rank.astype(jnp.int32) % 2 == 1
    other_odd = other_rank.astype(jnp.int32) % 2 == 1
    listed = jnp.concatenate(
        [jnp.where(is_odd, -1.0, counts), jnp.where(other_odd, others, -1.0)], axis=1
    )
    lane = iota((1, cols), 1).astype(F32)
    name = jnp.concatenate([lane, cols + 0.5 * (other_rank - 1.0)], axis=1)
    wide = (2 * cols, 2 * cols)
    place = jnp.broadcast_to(rank_row(listed), wide).T[:, 0:cols]
    here = place == iota((2 * cols, cols), 1).astype(F32)
    force = iota((2 * cols, cols), 0).astype(F32)
    name = jnp.broadcast_to(name, wide).T[:, 0:cols]
    value = jnp.broadcast_to(listed, wide).T[:, 0:cols]
    for what, ref in ((name, order_ref), (force, force_ref), (value, ordered_ref)):
        total = jnp.sum(jnp.where(here, what, 0.0), axis=0, keepdims=True)
        ref[...] = total.astype(jnp.int32)

    owners = jnp.broadcast_to(owner_ref[...].astype(F32), square)
    same = (owners.T == owners) & (iota(square, 0) < iota(square, 1))
    earlier = jnp.sum(same.astype(F32), axis=0, keepdims=True)
    slot_ref[...] = owner_ref[...] * capacity + earlier.astype(jnp.int32)


def gather_kernel(sent_ref, drops_ref, out_ref, wide_ref):
    bins = drops_ref.shape[1]
    wide_ref[...] = jnp.zeros(wide_ref.shape, F32)

    def body(p, carry):
        for k in range(8):
            wide_ref[k, 0:bins, :] = drops_ref[sent_ref[0, 8 * p + k]].astype(F32)
        for k in range(8):
            out_ref[8 * p + k] = wide_ref[k].astype(BF16)
        return carry

    lax.fori_loop(0, out_ref.shape[0] // 8, body, 0)


def merge_kernel(sent_ref, final_ref, back_ref, out_ref):
    out_ref[...] = final_ref[...]

    def body(p, carry):
        row = back_ref[p].astype(F32)[0 : out_ref.shape[1]]
        out_ref[sent_ref[0, p]] = row.astype(BF16)
        return carry

    lax.fori_loop(0, back_ref.shape[0] - 1, body, 0)


def crm_kernel(
    order_ref, force_ref, count_ref, sent_ref,
    drops_ref, guest_ref, forcing_ref, other_ref, coef_ref, growth_ref,
    final_ref, back_ref, own_ref, away_ref,
    state_ref, start_ref, pair_ref, twice_ref, cell_ref, heat_cell_ref, echo_cell_ref,
):
    bins = drops_ref.shape[1]
    cells = drops_ref.shape[2]
    cols = drops_ref.shape[0]
    guests = guest_ref.shape[0]
    coef = coef_ref[...]
    growth = growth_ref[...]
    state_ref[...] = jnp.zeros(state_ref.shape, F32)
    heat_cell_ref[...] = jnp.zeros(heat_cell_ref.shape, F32)
    echo_cell_ref[...] = jnp.zeros(echo_cell_ref.shape, F32)
    mass = (iota((40, cells), 0) + 1).astype(F32) / F32(bins)
    spread = (iota((CRM_LEV, cells), 1) // CRM_X == iota((CRM_LEV, cells), 0)).astype(BF16)
    for i, ref in enumerate((forcing_ref, other_ref)):
        rows = jnp.dot(ref[...].T.astype(BF16), spread, preferred_element_type=F32)
        cell_ref[cols * i : cols * i + cols, :] = DT_CRM * rows

    def grow(k, which, zero):
        grown = state_ref[k] + growth * cell_ref[pl.ds(which, 1), :]
        for h in range(cells // 128):
            cut = slice(128 * h, 128 * h + 128)
            g = grown[0:32, cut]
            last = grown[32:40, cut]
            twice_ref[2 * k + h, 0:32, :] = g
            twice_ref[2 * k + h, 32:48, :] = g[0:16]
            for d in range(16):
                other = g if d % 8 == 0 else twice_ref[2 * k + h, pl.ds(zero + d, 32), :]
                if d == 8:
                    other = jnp.concatenate([g[8:], g[:8]], axis=0)
                pair_ref[k, 32 * d : 32 * d + 32, cut] = (g * other).astype(BF16)
            pair_ref[k, 512:528, cut] = (g[0:16] * g[16:32]).astype(BF16)
            pair_ref[k, 528:560, cut] = (g * last[0:1]).astype(BF16)
            tail = jnp.concatenate([last * last, jnp.zeros((8, 128), F32)], axis=0)
            pair_ref[k, 560:576, cut] = tail.astype(BF16)
        return grown

    def group(index, carry):
        base = index * GROUP
        which = [order_ref[0, base + k] for k in range(GROUP)]
        force = [force_ref[0, base + k] for k in range(GROUP)]
        count = [count_ref[0, base + k] for k in range(GROUP)]
        for k in range(GROUP):
            mine = drops_ref[jnp.minimum(which[k], cols - 1)].astype(F32)
            guest = guest_ref[jnp.clip(which[k] - cols, 0, guests - 1)].astype(F32)
            start = jnp.where(which[k] < cols, mine, guest[0:bins])
            start_ref[k, 0:bins, :] = start
            state_ref[k, 0:bins, :] = start

        zero = jnp.minimum(which[0], 0)

        def substeps(width):
            def step(s, c):
                for k in range(width):
                    grown = grow(k, force[k], zero)
                    change = jnp.dot(coef, pair_ref[k], preferred_element_type=F32)
                    moved = grown + (change[0:40] + change[40:80])
                    state_ref[k] = jnp.where(s < count[k], moved, state_ref[k])
                return c

            return step

        half, quarter = count[GROUP // 2], count[GROUP // 4]
        lax.fori_loop(0, half, substeps(GROUP), 0)
        lax.fori_loop(half, quarter, substeps(GROUP // 2), 0)
        lax.fori_loop(quarter, count[0], substeps(GROUP // 4), 0)
        for k in range(GROUP):
            final = state_ref[k, 0:bins, :]
            weighted = mass[0:bins] * final
            heat = jnp.sum(mass[0:bins] * (final - start_ref[k, 0:bins, :]), axis=0, keepdims=True)
            echo = jnp.sum(weighted * weighted, axis=0, keepdims=True)
            heat_cell_ref[pl.ds(which[k], 1), :] = heat
            echo_cell_ref[pl.ds(which[k], 1), :] = echo

            result = state_ref[k].astype(BF16)
            guest = jnp.clip(which[k] - cols, 0, guests - 1)
            mine = which[k] < cols
            final_ref[jnp.where(mine, which[k], sent_ref[0, guest])] = final.astype(BF16)
            back_ref[jnp.where(mine, guests, guest)] = result
        return carry

    lax.fori_loop(0, cols // GROUP, group, 0)
    means = jnp.where(
        iota((CRM_LEV, cells), 1) // CRM_X == iota((CRM_LEV, cells), 0), F32(1.0 / CRM_X), 0.0
    )
    contract = (((1,), (1,)), ((), ()))
    heat = lax.dot_general(
        means, heat_cell_ref[...], contract, precision=HIGH, preferred_element_type=F32
    )
    heat = heat.astype(BF16).astype(F32)
    echo = lax.dot_general(
        means, echo_cell_ref[...], contract, precision=HIGH, preferred_element_type=F32
    )
    both = jnp.concatenate([heat, jnp.log(1.0 + echo)], axis=0)
    own_ref[...] = both[:, 0:cols]
    away_ref[...] = both[:, cols : 2 * cols]


def block_kernel(n_gcm, n_crm, own_ref, back_ref, rank_ref, slot_ref, heat_ref, send_ref):
    cols = own_ref.shape[1]
    odd = 2 * iota((cols, cols), 0) + 1
    home = (rank_ref[...] == odd).astype(F32)
    both = own_ref[...] + jnp.dot(
        back_ref[...], home, precision=HIGH, preferred_element_type=F32
    )
    heat = both[0:CRM_LEV]
    echo = both[CRM_LEV:]
    heat_ref[...] = heat
    contract = (((1,), (1,)), ((), ()))
    devices = send_ref.shape[0]
    slots = 2 * cols
    capacity = slots // devices
    onehot = (slot_ref[...] == iota((slots, cols), 0)).astype(F32)
    packed = lax.dot_general(echo, onehot, contract, precision=HIGH, preferred_element_type=F32)
    coarse = packed.astype(BF16).astype(F32)
    rest = packed - coarse
    middle = rest.astype(BF16).astype(F32)
    pieces = (coarse, middle, rest - middle)
    lane = iota((CRM_LEV, 128), 1)
    near = heat
    far = pltpu.roll(heat, 64, 1)
    sides = jnp.where(
        lane == 1, pltpu.roll(heat, 65, 1), jnp.where(lane == 62, pltpu.roll(heat, 63, 1), heat)
    )
    g = lax.axis_index("gcm")
    for d in range(devices):
        away = d // n_crm - g
        below = (away == 1) | (away == 1 - n_gcm)
        above = (away == -1) | (away == n_gcm - 1)
        block = jnp.where(below, far, jnp.where(above, near, sides))
        tile, offset = divmod(d * capacity, 128)
        for i, piece in enumerate(pieces):
            moved = pltpu.roll(
                piece[:, 128 * tile : 128 * tile + 128], (64 + i * capacity - offset) % 128, 1
            )
            start = 64 + i * capacity
            block = jnp.where((lane >= start) & (lane < start + capacity), moved, block)
        send_ref[d] = block.astype(BF16)


def last_kernel(
    n_gcm, n_crm, base_ref, own_ref, got_ref, up_map_ref, drops_in, out_ref, power_ref, drops_out,
    *back_refs,
):
    cols = own_ref.shape[1]
    half = cols // 2
    element = iota((cols, 256), 0)
    col = iota((cols, 256), 1)
    phase = col % 4
    edge = (phase == 0) | (phase == 3)
    other = jnp.where(phase == 0, col // 4 - 1, col // 4 + 1)

    def spread(centre, start, west, west_lane, east, east_lane):
        inside = jnp.where(element == col // 4 + start, jnp.where(edge, 0.5, 1.0), 0.0)
        beside = edge & (element == other + start) & (other >= 0) & (other < half)
        middle = jnp.where(beside, 0.5, inside).astype(BF16)
        from_west = jnp.where((col == 0) & (element == west_lane), 0.5, 0.0).astype(BF16)
        from_east = jnp.where((col == 255) & (element == east_lane), 0.5, 0.0).astype(BF16)
        total = jnp.dot(centre, middle, preferred_element_type=F32)
        total += jnp.dot(west, from_west, preferred_element_type=F32)
        total += jnp.dot(east, from_east, preferred_element_type=F32)
        return total

    own = own_ref[...].astype(BF16)
    g = lax.axis_index("gcm")
    c = lax.axis_index("crm")
    north = jnp.where(g == 0, n_gcm - 1, g - 1) * n_crm
    south = jnp.where(g == n_gcm - 1, 0, g + 1) * n_crm
    west = jnp.where(c == 0, n_crm - 1, c - 1)
    east = jnp.where(c == n_crm - 1, 0, c + 1)
    up, down = got_ref[north + c], got_ref[south + c]
    left, right = got_ref[g * n_crm + west], got_ref[g * n_crm + east]
    up_left, up_right = got_ref[north + west], got_ref[north + east]
    down_left, down_right = got_ref[south + west], got_ref[south + east]
    above = spread(up, 0, up_left, half - 1, up_right, 0)
    near = spread(own, 0, left, half - 1, right, 0)
    far = spread(own, half, left, half - 2, right, 1)
    below = spread(down, 0, down_left, half - 1, down_right, 0)
    parts = (
        0.5 * (above + near), near, 0.5 * (near + far), far, 0.5 * (far + below),
    )
    up_map = up_map_ref[...]
    for part, ref in zip(parts, back_refs):
        ref[...] = DT_PHYS * jnp.dot(up_map, part, precision=HIGH, preferred_element_type=F32)

    devices = got_ref.shape[0]
    slots = power_ref.shape[1]
    capacity = slots // devices
    lane = iota((CRM_LEV, 128), 1)
    tiles = [jnp.zeros((CRM_LEV, 128), F32) for _ in range(slots // 128)]
    for d in range(devices):
        block = got_ref[d].astype(F32)
        fine = pltpu.roll(block, 128 - 2 * capacity, 1) + pltpu.roll(block, 128 - capacity, 1)
        tile, offset = divmod(d * capacity, 128)
        moved = pltpu.roll(block + fine, (offset - 64) % 128, 1)
        tiles[tile] = jnp.where((lane >= offset) & (lane < offset + capacity), moved, tiles[tile])
    power_ref[...] = jnp.concatenate(tiles, axis=1)

    def body(chunk, carry):
        levels = pl.ds(pl.multiple_of(chunk * CHUNK, CHUNK), CHUNK)
        shape = (CHUNK, 8, 256)
        row = iota(shape, 1)
        wide = [jnp.broadcast_to(ref[levels, :][:, None, :], shape) for ref in back_refs]
        back = jnp.where(
            row == 0,
            wide[0],
            jnp.where(
                row < 3,
                wide[1],
                jnp.where(row < 5, wide[2], jnp.where(row < 7, wide[3], wide[4])),
            ),
        )
        out_ref[levels] = base_ref[levels] + back
        return carry

    lax.fori_loop(0, base_ref.shape[0] // CHUNK, body, 0)


def call(kernel, outs, args, scratch=(), sems=(), flops=10_000_000, limit=16, through=()):
    spaces = {
        "s": pl.BlockSpec(memory_space=pltpu.SMEM),
        "v": pl.BlockSpec(memory_space=pltpu.VMEM),
        "h": pl.BlockSpec(memory_space=pl.ANY),
    }
    return pl.pallas_call(
        kernel,
        out_shape=[jax.ShapeDtypeStruct(s, t) for s, t in outs]
        + [jax.ShapeDtypeStruct(args[i][1].shape, args[i][1].dtype) for i in through],
        in_specs=[spaces[kind] for kind, _ in args],
        out_specs=[spaces["v"]] * len(outs) + [spaces["h"]] * len(through),
        input_output_aliases={i: len(outs) + n for n, i in enumerate(through)},
        scratch_shapes=[pltpu.VMEM(s, t) for s, t in scratch] + list(sems),
        compiler_params=pltpu.CompilerParams(vmem_limit_bytes=limit * MIB),
        cost_estimate=pl.CostEstimate(flops=flops, bytes_accessed=4_000_000, transcendentals=0),
    )(*[value for _, value in args])


def v(*values):
    return [("v", value) for value in values]


def shift(value, rows, cols):
    n_gcm = lax.axis_size("gcm")
    n_crm = lax.axis_size("crm")
    pairs = []
    for g in range(n_gcm):
        for c in range(n_crm):
            target = ((g + rows) % n_gcm) * n_crm + (c + cols) % n_crm
            pairs.append((g * n_crm + c, target))
    return lax.ppermute(value, ("gcm", "crm"), pairs)


def pair_table(bins):
    table = np.zeros((bins * bins, 576), np.float32)

    def put(column, i, j):
        table[i * bins + j, column] = 1.0
        table[j * bins + i, column] = 1.0

    for d in range(16):
        for b in range(32):
            put(32 * d + b, b, (b + d) % 32)
    for b in range(16):
        put(512 + b, b, b + 16)
    for b in range(32):
        put(528 + b, b, 32)
    put(560, 32, 32)
    return table


def to_partner(value):
    n_gcm = lax.axis_size("gcm")
    n_crm = lax.axis_size("crm")
    pairs = []
    for g in range(n_gcm):
        for c in range(n_crm):
            pairs.append((g * n_crm + c, (g ^ 1) * n_crm + c))
    return lax.ppermute(value, ("gcm", "crm"), pairs)


def shards(tracer, wind_x, wind_y, drops, owner, counts, collision, growth):
    devices = lax.axis_size("gcm") * lax.axis_size("crm")
    levels, row_count, col_count = tracer.shape
    col_total, bins, cells = drops.shape
    field = (tracer.shape, F32)
    strip = ((levels, row_count, 128), F32)
    rows = ((2, levels, col_count), F32)
    wide = col_count + 128
    down_map, up_map = level_tables(levels, CRM_LEV)

    row = ((1, col_total), jnp.int32)
    capacity = 2 * col_total // devices
    guests = col_total // 2
    tend, top, bot, to_right, to_left = call(
        first_kernel,
        [field, rows, rows] + [((levels // 4, 8, 128), F32)] * 2,
        [("h", tracer), ("h", wind_x), ("h", wind_y)],
        [field] * 3,
        [pltpu.SemaphoreType.DMA((3, levels // CHUNK))],
        limit=62,
    )
    from_left = shift(to_right, 0, 1)
    from_right = shift(to_left, 0, -1)
    count_row, _ = lax.optimization_barrier((counts[None, :], to_left))
    other_counts = to_partner(count_row)
    q_strip, u_strip, v_strip, tend_strip, top, bot = call(
        strip_kernel,
        [strip] * 4 + [((levels, wide + col_count), F32)] * 2,
        v(from_left, from_right, top, bot) + [("h", drops)],
    )
    sent, order, force, ordered, rank, slot = call(
        functools.partial(plan_kernel, capacity),
        [row] * 6,
        v(count_row, other_counts, owner.T) + [("h", top)],
    )
    (leaving,) = call(
        gather_kernel,
        [((guests, 40, cells), BF16)],
        [("s", sent)] + v(drops),
        [((8, 40, cells), F32)],
    )
    from_above = shift(bot, 1, 0)
    from_below = shift(top, -1, 0)
    leaving, from_above, from_below = lax.optimization_barrier((leaving, from_above, from_below))
    guest_drops = to_partner(leaving)
    coef, growth_rows = call(
        coef_kernel,
        [((80, 576), BF16), ((40, cells), F32)],
        v(collision, jnp.asarray(pair_table(bins), BF16), growth[None, :]) + [("h", top)],
        [((80, 576), F32), ((8, 128), F32)],
    )
    state, smooth, tend, top, bot = call(
        second_kernel,
        [field, field, ((levels, row_count, wide), F32)] + [((1, levels, wide), F32)] * 2,
        v(tracer, wind_x, wind_y, tend, q_strip, u_strip, v_strip, tend_strip)
        + v(from_above, from_below),
    )
    base, forcing = call(
        third_kernel,
        [field, ((CRM_LEV, col_total), F32)],
        v(tracer, state, smooth, tend, shift(bot, 1, 0), shift(top, -1, 0))
        + v(jnp.asarray(down_map, F32)) + [("h", coef), ("h", growth_rows)],
        [((levels, col_count), F32), ((levels, col_count), F32)],
    )

    other_forcing = to_partner(forcing)
    n_gcm = lax.axis_size("gcm")
    n_crm = lax.axis_size("crm")

    pairs = ((2 * CRM_LEV, col_total), F32)
    final, back, own, away = call(
        crm_kernel,
        [((col_total, bins, cells), BF16), ((guests + 1, 40, cells), BF16), pairs, pairs],
        [("s", order), ("s", force), ("s", ordered), ("s", sent)]
        + v(drops, guest_drops, forcing, other_forcing, coef, growth_rows),
        [((GROUP, 40, cells), F32), ((GROUP, 40, cells), F32), ((GROUP, 576, cells), BF16),
         ((2 * GROUP, 48, 128), F32), ((2 * col_total, cells), F32),
         ((2 * col_total, cells), F32), ((2 * col_total, cells), F32)],
        flops=10_000_000_000,
        limit=32,
    )
    returned = to_partner(away)
    returned, back = lax.optimization_barrier((returned, back))
    returned_drops = to_partner(back)
    heat, send = call(
        functools.partial(block_kernel, n_gcm, n_crm),
        [((CRM_LEV, col_total), F32), ((devices, CRM_LEV, 128), BF16)],
        v(own, returned, rank, slot),
    )
    got = lax.all_to_all(send, ("gcm", "crm"), split_axis=0, concat_axis=0, tiled=True)
    (drops_next,) = call(
        merge_kernel,
        [((col_total, bins, cells), BF16)],
        [("s", sent)] + v(final, returned_drops),
    )
    tracer_next, power, by_bin = call(
        functools.partial(last_kernel, n_gcm, n_crm),
        [field, ((CRM_LEV, devices * capacity), F32)],
        v(base, heat, got, jnp.asarray(up_map, F32))
        + [("h", drops_next.transpose(1, 0, 2))],
        [((levels, col_count), F32)] * 5,
        through=(4,),
    )
    drops_next = by_bin.transpose(1, 0, 2)
    return (tracer_next, drops_next, power)


def solution(mesh):
    return jax.shard_map(
        shards,
        mesh=mesh,
        in_specs=(
            P(None, "gcm", "crm"),
            P(None, "gcm", "crm"),
            P(None, "gcm", "crm"),
            P(("gcm", "crm"), None, None),
            P(("gcm", "crm"), None),
            P(("gcm", "crm")),
            P(),
            P(),
        ),
        out_specs=(P(None, "gcm", "crm"), P(("gcm", "crm"), None, None), P(None, ("gcm", "crm"))),
        check_vma=False,
    )
```
